32 devices in a mesh: seq: 8 (over y, x, core), head: 4 (over z).
Axes of the slice: x: 2, y: 2, z: 4, core: 2. Of those that a mesh axis runs over, the one named last changes fastest.
Arguments:
- queries: bfloat16 [3072, 4096], P('seq', 'head'), may hold values from -108 to 108
- keys_in: bfloat16 [3072, 4096], P('seq', 'head'), may hold values from -4 to 4
- values: bfloat16 [3072, 4096], P('seq', 'head'), may hold values from -6 to 6
- out_grad: bfloat16 [3072, 4096], P('seq', 'head'), may hold values from -6 to 6
- out_weight: bfloat16 [4096, 4096], P('head'), may hold values from -0.09375 to 0.09375
- doc_ids: int32 [3072], P('seq'), may hold values from 0 to 7, never falling along the last dimension, each value on 1 to 1920 neighbouring positions
Outputs:
- query_grad: bfloat16 [3072, 4096], P('seq', 'head')
- key_grad: bfloat16 [3072, 4096], P('seq', 'head')
- value_grad: bfloat16 [3072, 4096], P('seq', 'head')
The draws below stay inside these ranges and needn't reach their ends.
Inputs may be any that keep to these rules, and one draw needn't show every extreme that they name: `doc_ids`: document ids never fall along the rows.
All inputs are finite; a program needn't handle non-finite values.
Results may differ from the reference program's by a relative error of at most 0.0085.
Values may be sent and summed in bfloat16 or wider, within the bound.
No kernel may reach another device: no remote copies, remote signals or barrier semaphores. Data moves between devices by JAX's collectives and lax.ppermute only.
A program may use at most 192 MiB of HBM per device.

```python
import math
import jax
import jax.numpy as jnp
import numpy as np
from jax import lax

D = 4096
HEADS = 32
HD = 128
S_DEV = 384
TOKENS = 3072


def shared_keys(key):
    return jnp.clip(jax.random.normal(jax.random.fold_in(key, 11), (TOKENS, HEADS * HD), jnp.float32), -4.0, 4.0)


def draw_keys_in(key, part):
    base_keys = shared_keys(key)
    return base_keys.astype(jnp.bfloat16)


def draw_queries(key, part):
    drawn = jnp.clip(jax.random.normal(jax.random.fold_in(key, 13), (TOKENS, HEADS * HD), jnp.float32), -4.0, 4.0)
    return drawn.astype(jnp.bfloat16)


def block_levels(stream_key, dims, split, smallest, largest):
    gain, own = 1.0, jax.random.fold_in(stream_key, 6)
    for position, shards_of in split:
        draws = jnp.exp(jax.random.uniform(jax.random.fold_in(own, position), (shards_of,), jnp.float32, smallest / len(split), largest / len(split)))
        gain = gain * jnp.repeat(draws, dims[position] // shards_of).reshape([-1 if axis == position else 1 for axis in range(len(dims))])
    return gain


def split_up(amount, total, most, lean):
    loads = [(1 << 20) // math.isqrt(grade ** lean) + 1 for grade in range(2, amount + 1)]
    spare, given = total - most - (amount - 1), [1] * (amount - 1)
    while spare > 0:
        free = [i for i in range(amount - 1) if given[i] < most]
        whole, remaining = sum([loads[i] for i in free]), spare
        for i in free:
            extra = min(most - given[i], max(1, remaining * loads[i] // whole), spare)
            given[i] = given[i] + extra
            spare = spare - extra
    return np.array([most] + given)


def uneven_parts(stream_key, count, total, most, skew):
    if count == 2:
        one = jax.random.randint(stream_key, (), max(1, total - most), min(most, total - 1) + 1)
        return jnp.stack([one, total - one])
    tallies = jnp.asarray(split_up(count, total, most, skew), jnp.int32)
    twos = (count - 1) // 2
    donor, taker = tallies[1:1 + 2 * twos:2], tallies[2:2 + 2 * twos:2]
    slack = jnp.minimum(donor - 1, most - taker)
    shifted = jax.random.randint(jax.random.fold_in(stream_key, 1), (twos,), 0, 1 << 20) % (slack + 1)
    tallies = tallies.at[1:1 + 2 * twos:2].set(donor - shifted).at[2:2 + 2 * twos:2].set(taker + shifted)
    return tallies[jax.random.permutation(jax.random.fold_in(stream_key, 2), count)]


def bell_draw(stream_key, shape, spread, limit, shards=(), held_as=jnp.bfloat16):
    result = spread * jax.random.normal(stream_key, shape, jnp.float32)
    if shards:
        result = result * block_levels(stream_key, shape, shards, -0.22, 0.18)
    return jnp.clip(result, -limit, limit).astype(held_as)


def setup_inputs(seed: int = 0) -> dict:
    key_list = jax.random.split(jax.random.key(seed), 7)
    return {
        "queries": draw_queries(jax.random.fold_in(key_list[6], 71), 0),
        "keys_in": draw_keys_in(jax.random.fold_in(key_list[6], 71), 0),
        "values": bell_draw(key_list[2], (TOKENS, HEADS * HD), 1.0, 6.0, ((0, 8), (1, 4))),
        "out_grad": bell_draw(key_list[3], (TOKENS, D), 1.0, 6.0, ((0, 8), (1, 4))),
        "out_weight": bell_draw(key_list[4], (HEADS * HD, D), D ** -0.5, 0.09375, ((0, 4),)),
        "doc_ids": jnp.searchsorted(jnp.cumsum(uneven_parts(key_list[5], 8, TOKENS, TOKENS // 2 + S_DEV, 2)), jnp.arange(TOKENS), side="right").astype(jnp.int32),
    }


def reference(queries, keys_in, values, out_grad, out_weight, doc_ids):
    grad_attn = jnp.dot(out_grad, out_weight.T, preferred_element_type=jnp.float32).astype(jnp.bfloat16)
    scale = HD ** -0.5
    positions = jnp.arange(TOKENS, dtype=jnp.int32)
    allowed = (positions[None, :] <= positions[:, None]) & (doc_ids[None, :] == doc_ids[:, None])

    def one_head(head_index):
        offset = (head_index * HD).astype(jnp.int32)
        query_h = lax.dynamic_slice_in_dim(queries, offset, HD, 1)
        key_h = lax.dynamic_slice_in_dim(keys_in, offset, HD, 1)
        value_h = lax.dynamic_slice_in_dim(values, offset, HD, 1)
        grad_h = lax.dynamic_slice_in_dim(grad_attn, offset, HD, 1)
        scores = jnp.dot(query_h, key_h.T, preferred_element_type=jnp.float32) * scale
        masked = jnp.where(allowed, scores, -1e30)
        row_max = jnp.max(masked, axis=1)
        row_total = jnp.sum(jnp.where(allowed, jnp.exp(masked - row_max[:, None]), 0.0), axis=1)
        log_total = row_max + jnp.log(row_total)
        probs = jnp.where(allowed, jnp.exp(masked - log_total[:, None]), 0.0)
        grad_probs = jnp.dot(grad_h, value_h.T, preferred_element_type=jnp.float32)
        row_dot = jnp.sum(probs * grad_probs, axis=1)
        grad_scores = (probs * (grad_probs - row_dot[:, None])).astype(jnp.bfloat16)
        query_grad = (scale * jnp.dot(grad_scores, key_h, preferred_element_type=jnp.float32)).astype(jnp.bfloat16)
        key_grad = (scale * jnp.dot(grad_scores.T, query_h, preferred_element_type=jnp.float32)).astype(jnp.bfloat16)
        value_grad = jnp.dot(probs.astype(jnp.bfloat16).T, grad_h, preferred_element_type=jnp.float32).astype(jnp.bfloat16)
        return query_grad, key_grad, value_grad

    query_all, key_all, value_all = lax.map(one_head, jnp.arange(HEADS, dtype=jnp.int32))

    def flatten(stacked):
        return jnp.transpose(stacked, (1, 0, 2)).reshape(TOKENS, HEADS * HD)

    return flatten(query_all), flatten(key_all), flatten(value_all)
```

```python
import functools
import math

import jax
import jax.numpy as jnp
from jax import lax
from jax.experimental import pallas as pl
from jax.experimental.pallas import tpu as pltpu
from jax.sharding import PartitionSpec as P

HD = 128
NEG_LARGE = -1e30
VMEM_LIMIT = 56 * 1024 * 1024

NN = (((1,), (0,)), ((), ()))


def dot32(a, b):
    return lax.dot_general(a, b, NN, preferred_element_type=jnp.float32)


def block_size(total, wanted):
    size = min(wanted, total)
    while total % size or size % 128:
        size -= 128
    return size


def pack_kernel(*refs):
    half = len(refs) // 2
    for src, dst in zip(refs[:half], refs[half:]):
        dst[...] = src[...]


def pack_heads(arrays, peers):
    rows, width = arrays[0].shape
    heads = width // HD
    return pl.pallas_call(
        pack_kernel,
        grid=(peers,),
        in_specs=[pl.BlockSpec((rows, HD), lambda p: (0, lax.rem(p, heads)))] * len(arrays),
        out_specs=[pl.BlockSpec((rows, HD), lambda p: (p, 0))] * len(arrays),
        out_shape=[jax.ShapeDtypeStruct((peers * rows, HD), a.dtype) for a in arrays],
    )(*arrays)


def unpack_heads(arrays, rows, heads):
    return pl.pallas_call(
        pack_kernel,
        grid=(heads,),
        in_specs=[pl.BlockSpec((rows, HD), lambda p: (p, 0))] * len(arrays),
        out_specs=[pl.BlockSpec((rows, HD), lambda p: (0, p))] * len(arrays),
        out_shape=[jax.ShapeDtypeStruct((rows, heads * HD), a.dtype) for a in arrays],
    )(*arrays)


def visible(first_row, q0, k0, shape):
    key_pos = k0 + lax.broadcasted_iota(jnp.int32, shape, 0)
    query_pos = q0 + lax.broadcasted_iota(jnp.int32, shape, 1)
    return (key_pos >= first_row) & (key_pos <= query_pos)


def forward_kernel(bq, bk, first_s, first_ref, q_ref, k_ref, v_ref, out_ref, log_ref, vt_ref):
    total = q_ref.shape[0]
    factor = HD ** (-0.5) * math.log2(math.e)
    vt_ref[...] = v_ref[...].T

    @pl.loop(0, total // bq)
    def _(qi):
        q0 = pl.multiple_of(qi * bq, bq)
        qt = q_ref[pl.ds(q0, bq), :].T
        first_row = first_ref[:, pl.ds(q0, bq)]
        low = first_s[q0] // bk
        last_first = first_s[q0 + bq - 1]

        def step(ki, carry):
            top, total_p, acc = carry
            k0 = pl.multiple_of(ki * bk, bk)
            s = dot32(k_ref[pl.ds(k0, bk), :], qt) * factor
            inner = (k0 >= last_first) & (k0 + bk - 1 <= q0)
            s = lax.cond(
                inner,
                lambda x: x,
                lambda x: jnp.where(visible(first_row, q0, k0, (bk, bq)), x, NEG_LARGE),
                s,
            )
            new_top = jnp.maximum(top, jnp.max(s, axis=0, keepdims=True))
            p = jnp.exp2(s - new_top)
            fix = jnp.exp2(top - new_top)
            high = p.astype(jnp.bfloat16)
            rest = (p - high.astype(jnp.float32)).astype(jnp.bfloat16)
            vt = vt_ref[:, pl.ds(k0, bk)]
            acc = acc * fix + (dot32(vt, high) + dot32(vt, rest))
            return new_top, total_p * fix + jnp.sum(p, axis=0, keepdims=True), acc

        init = (
            jnp.full((1, bq), NEG_LARGE, jnp.float32),
            jnp.zeros((1, bq), jnp.float32),
            jnp.zeros((HD, bq), jnp.float32),
        )
        top, total_p, acc = lax.fori_loop(low, (q0 + bq + bk - 1) // bk, step, init)
        out_ref[:, pl.ds(q0, bq)] = acc / total_p
        log_ref[:, pl.ds(q0, bq)] = top + jnp.log2(total_p)


def backward_kernel(bq, bk, first_s, first_ref, q_ref, k_ref, v_ref, g_ref, out_ref, log_ref,
                    dq_ref, dk_ref, dv_ref, kt_ref, dk_acc, dv_acc, dq_acc):
    total = q_ref.shape[0]
    scale = HD ** (-0.5)
    factor = scale * math.log2(math.e)
    kt_ref[...] = k_ref[...].T
    dk_acc[...] = jnp.zeros_like(dk_acc)
    dv_acc[...] = jnp.zeros_like(dv_acc)

    @pl.loop(0, total // bq)
    def _(qi):
        q0 = pl.multiple_of(qi * bq, bq)
        q = q_ref[pl.ds(q0, bq), :]
        g = g_ref[pl.ds(q0, bq), :]
        qt = q.T
        gt = g.T
        first_row = first_ref[:, pl.ds(q0, bq)]
        log_row = log_ref[:, pl.ds(q0, bq)]
        dot_row = jnp.sum(gt.astype(jnp.float32) * out_ref[:, pl.ds(q0, bq)], axis=0, keepdims=True)
        low = first_s[q0] // bk
        last_first = first_s[q0 + bq - 1]
        dq_acc[...] = jnp.zeros_like(dq_acc)

        @pl.loop(low, (q0 + bq + bk - 1) // bk)
        def _(ki):
            k0 = pl.multiple_of(ki * bk, bk)
            rows = pl.ds(k0, bk)
            s = dot32(k_ref[rows, :], qt) * factor
            p = jnp.exp2(s - log_row)
            inner = (k0 >= last_first) & (k0 + bk - 1 <= q0)
            p = lax.cond(
                inner,
                lambda x: x,
                lambda x: jnp.where(visible(first_row, q0, k0, (bk, bq)), x, 0.0),
                p,
            )
            dv_acc[rows, :] += dot32(p.astype(jnp.bfloat16), g)
            dp = dot32(v_ref[rows, :], gt)
            ds = (p * (dp - dot_row)).astype(jnp.bfloat16)
            dk_acc[rows, :] += dot32(ds, q)
            dq_acc[...] += dot32(kt_ref[:, rows], ds)

        dq_ref[pl.ds(q0, bq), :] = (scale * dq_acc[...]).T.astype(dq_ref.dtype)

    dk_ref[...] = (scale * dk_acc[...]).astype(dk_ref.dtype)
    dv_ref[...] = dv_acc[...].astype(dv_ref.dtype)


def vmem(count):
    return [pl.BlockSpec(memory_space=pltpu.VMEM)] * count


def attention_forward(first, q, k, v):
    total = q.shape[0]
    bq, bk = block_size(total, 512), block_size(total, 256)
    return pl.pallas_call(
        functools.partial(forward_kernel, bq, bk),
        in_specs=[pl.BlockSpec(memory_space=pltpu.SMEM)] + vmem(4),
        out_specs=vmem(2),
        out_shape=[
            jax.ShapeDtypeStruct((HD, total), jnp.float32),
            jax.ShapeDtypeStruct((1, total), jnp.float32),
        ],
        scratch_shapes=[pltpu.VMEM((HD, total), jnp.bfloat16)],
        compiler_params=pltpu.CompilerParams(vmem_limit_bytes=VMEM_LIMIT),
    )(first, first.reshape(1, total), q, k, v)


def attention_backward(first, q, k, v, g, out, log_total):
    total = q.shape[0]
    bq, bk = block_size(total, 512), block_size(total, 256)
    return pl.pallas_call(
        functools.partial(backward_kernel, bq, bk),
        in_specs=[pl.BlockSpec(memory_space=pltpu.SMEM)] + vmem(7),
        out_specs=vmem(3),
        out_shape=[jax.ShapeDtypeStruct((total, HD), jnp.bfloat16)] * 3,
        scratch_shapes=[
            pltpu.VMEM((HD, total), jnp.bfloat16),
            pltpu.VMEM((total, HD), jnp.float32),
            pltpu.VMEM((total, HD), jnp.float32),
            pltpu.VMEM((HD, bq), jnp.float32),
        ],
        compiler_params=pltpu.CompilerParams(vmem_limit_bytes=VMEM_LIMIT),
    )(first, first.reshape(1, total), q, k, v, g, out, log_total)


def per_device(peers, queries, keys_in, values, out_grad, out_weight, doc_ids):
    rows, width = queries.shape
    heads = width // HD

    def swap(x):
        return lax.all_to_all(x, "seq", 0, 0, tiled=True)

    all_grad = lax.all_gather(out_grad, "head", axis=1, tiled=True)
    docs = lax.all_gather(doc_ids, "seq", axis=0, tiled=True)
    place = jnp.arange(docs.shape[0], dtype=jnp.int32)
    edge = jnp.concatenate([jnp.zeros((1,), jnp.bool_), docs[1:] != docs[:-1]])
    first = lax.cummax(jnp.where(edge, place, 0))
    q, k, v = (swap(x) for x in pack_heads([queries, keys_in, values], peers))
    out, log_total = attention_forward(first, q, k, v)
    grad = lax.dot_general(
        all_grad, out_weight, (((1,), (1,)), ((), ())), preferred_element_type=jnp.float32
    ).astype(jnp.bfloat16)
    (g,) = pack_heads([grad], peers)
    g = swap(g)
    grads = attention_backward(first, q, k, v, g, out, log_total)
    return tuple(unpack_heads([swap(x) for x in grads], rows, heads))


def solution(mesh):
    in_specs = (
        P("seq", "head"),
        P("seq", "head"),
        P("seq", "head"),
        P("seq", "head"),
        P("head", None),
        P("seq"),
    )
    out_specs = (P("seq", "head"), P("seq", "head"), P("seq", "head"))
    return jax.shard_map(
        functools.partial(per_device, mesh.shape["seq"]),
        mesh=mesh, in_specs=in_specs, out_specs=out_specs, check_vma=False,
    )
```

```python
import functools
import math

import jax
import jax.numpy as jnp
from jax import lax
from jax.experimental import pallas as pl
from jax.experimental.pallas import tpu as pltpu
from jax.sharding import PartitionSpec as P

HD = 128
DOC_VALUES = 8
DOC_ROWS = 16
NEG_LARGE = -1e30
VMEM_LIMIT = 56 * 1024 * 1024
PARAMS = pltpu.CompilerParams(vmem_limit_bytes=VMEM_LIMIT)

NN = (((1,), (0,)), ((), ()))
NT = (((1,), (1,)), ((), ()))
SMEM_SPEC = pl.BlockSpec(memory_space=pltpu.SMEM)
VMEM_SPEC = pl.BlockSpec(memory_space=pltpu.VMEM)


def dot32(a, b, dims=NN):
    return lax.dot_general(a, b, dims, preferred_element_type=jnp.float32)


def block_size(total, wanted):
    size = min(wanted, total)
    while total % size or size % 128:
        size -= 128
    return size


def aligned(index, size):
    return pl.ds(pl.multiple_of(index * size, size), size)


def pack_kernel(heads, rows, me_s, q_ref, k_ref, v_ref, doc_ref, *outs):
    own = lax.rem(me_s[0], heads)
    docs = doc_ref[...].astype(jnp.float32)
    docs = jnp.concatenate([docs, jnp.zeros((DOC_ROWS - docs.shape[0], HD), jnp.float32)], axis=0)
    docs = docs.astype(jnp.bfloat16)
    for d, out in enumerate(outs):
        columns = aligned(own ^ d, HD)
        for part, ref in enumerate((q_ref, k_ref, v_ref)):
            out[part * rows:(part + 1) * rows, :] = ref[:, columns]
        out[3 * rows:, :] = docs


def pack_heads(me, q, k, v, doc_ids):
    rows, width = q.shape
    heads = width // HD
    return pl.pallas_call(
        functools.partial(pack_kernel, heads, rows),
        in_specs=[SMEM_SPEC] + [VMEM_SPEC] * 4,
        out_specs=[VMEM_SPEC] * heads,
        out_shape=[jax.ShapeDtypeStruct((3 * rows + DOC_ROWS, HD), q.dtype)] * heads,
        compiler_params=PARAMS,
    )(me, q, k, v, doc_ids.reshape(rows // HD, HD))


def unpack_kernel(heads, rows, me_s, *refs):
    own = lax.rem(me_s[0], heads)
    for d in range(heads):
        columns = aligned(own ^ d, HD)
        for part in range(3):
            refs[heads + part][:, columns] = refs[d][part * rows:(part + 1) * rows, :]


def unpack_heads(me, blocks, rows):
    heads = len(blocks)
    return pl.pallas_call(
        functools.partial(unpack_kernel, heads, rows),
        in_specs=[SMEM_SPEC] + [VMEM_SPEC] * heads,
        out_specs=[VMEM_SPEC] * 3,
        out_shape=[jax.ShapeDtypeStruct((rows, heads * HD), blocks[0].dtype)] * 3,
        compiler_params=PARAMS,
    )(me, *blocks)


def project_kernel(first, where_s, *refs):
    if first:
        o_ref, w_ref, out_ref = refs
        out_ref[...] = dot32(o_ref[...], w_ref[...], NT)
    else:
        o_ref, w_ref, acc_ref, out_ref = refs
        out_ref[...] = acc_ref[...] + dot32(o_ref[...], w_ref[...], NT)


def project_last_kernel(where_s, o_ref, w_ref, acc_ref, *outs):
    step = pl.program_id(0)
    both = (acc_ref[...] + dot32(o_ref[...], w_ref[...], NT)).astype(jnp.bfloat16)
    odd = where_s[1] == 1
    near = jnp.where(odd, both[:, HD:], both[:, :HD])
    far = jnp.where(odd, both[:, :HD], both[:, HD:])
    for j in range(len(outs) // 2):

        @pl.when(step == j)
        def _():
            outs[2 * j][...] = near
            outs[2 * j + 1][...] = far


def project(me, block, weight, features, acc, last):
    rows, width = features.shape
    pairs = weight.shape[0] // (2 * HD)
    where = jnp.stack([block, lax.rem(me, 2), lax.rem(me // 2, pairs)])
    feature_spec = pl.BlockSpec((rows, width), lambda j, w: (0, 0))
    weight_spec = pl.BlockSpec((2 * HD, width), lambda j, w: (w[2] ^ j, w[0]))
    acc_spec = pl.BlockSpec((rows, 2 * HD), lambda j, w: (0, w[2] ^ j))
    cost = pl.CostEstimate(
        flops=2 * rows * width * weight.shape[0],
        bytes_accessed=2 * width * weight.shape[0] + 8 * rows * weight.shape[0],
        transcendentals=0,
    )
    if last:
        kernel = project_last_kernel
        out_specs = [pl.BlockSpec((rows, HD), lambda j, w: (0, 0))] * (2 * pairs)
        out_shape = [jax.ShapeDtypeStruct((rows, HD), jnp.bfloat16)] * (2 * pairs)
    else:
        kernel = functools.partial(project_kernel, acc is None)
        out_specs = acc_spec
        out_shape = jax.ShapeDtypeStruct((rows, weight.shape[0]), jnp.float32)
    return pl.pallas_call(
        kernel,
        grid_spec=pltpu.PrefetchScalarGridSpec(
            num_scalar_prefetch=1,
            grid=(pairs,),
            in_specs=[feature_spec, weight_spec] + ([] if acc is None else [acc_spec]),
            out_specs=out_specs,
        ),
        out_shape=out_shape,
        compiler_params=PARAMS,
        cost_estimate=cost,
    )(where, features, weight, *([] if acc is None else [acc]))


def visible(first_row, q0, k0, shape):
    key_pos = k0 + lax.broadcasted_iota(jnp.int32, shape, 0)
    query_pos = q0 + lax.broadcasted_iota(jnp.int32, (1, shape[1]), 1)
    return (key_pos >= first_row) & (key_pos <= query_pos)


def block_ranges(first_row, q0, bq, bk):
    low = jnp.min(first_row) // bk
    high = (q0 + bq + bk - 1) // bk
    mid_low = jnp.minimum((jnp.max(first_row) + bk - 1) // bk, high)
    mid_high = jnp.maximum((q0 + 1) // bk, mid_low)
    return low, mid_low, mid_high, high


def edge_block(index, low, mid_low, mid_high):
    return jnp.where(index < mid_low - low, low + index, index - (mid_low - low) + mid_high)


def forward_kernel(peers, rows, bq, bk, me_s, *refs):
    blocks = refs[:peers]
    q_ref, k_ref, v_ref, first_ref, out_ref, log_ref, vt_ref, doc_ref = refs[peers:]
    total = q_ref.shape[0]
    factor = HD ** (-0.5) * math.log2(math.e)
    for d, block in enumerate(blocks):
        place = me_s[0] ^ d
        for part, ref in enumerate((q_ref, k_ref, v_ref)):
            ref[aligned(place, rows), :] = block[part * rows:(part + 1) * rows, :]
        docs = block[3 * rows:, :].astype(jnp.float32)
        for t in range(rows // HD):
            doc_ref[:, aligned(place * (rows // HD) + t, HD)] = docs[t:t + 1, :]
    docs = doc_ref[...]
    first = jnp.zeros(docs.shape, jnp.float32)
    for value in range(1, DOC_VALUES):
        before = jnp.sum((docs < value).astype(jnp.float32))
        first = jnp.where(docs >= value, before, first)
    first_ref[...] = first.astype(jnp.int32)
    vt_ref[...] = v_ref[...].T

    @pl.loop(0, total // bq)
    def _(qi):
        queries = aligned(qi, bq)
        q0 = qi * bq
        qt = q_ref[queries, :].T
        first_row = first_ref[:, queries]
        low, mid_low, mid_high, high = block_ranges(first_row, q0, bq, bk)

        def step(ki, carry, edge):
            top, total_p, acc = carry
            keys = aligned(ki, bk)
            s = dot32(k_ref[keys, :], qt) * factor
            if edge:
                s = jnp.where(visible(first_row, q0, ki * bk, (bk, bq)), s, NEG_LARGE)
            new_top = jnp.maximum(top, jnp.max(s, axis=0, keepdims=True))
            p = jnp.exp2(s - new_top)
            fix = jnp.exp2(top - new_top)
            high_p = p.astype(jnp.bfloat16)
            rest = (p - high_p.astype(jnp.float32)).astype(jnp.bfloat16)
            vt = vt_ref[:, keys]
            acc = acc * fix + (dot32(vt, high_p) + dot32(vt, rest))
            return new_top, total_p * fix + jnp.sum(p, axis=0, keepdims=True), acc

        def edge_step(index, carry):
            return step(edge_block(index, low, mid_low, mid_high), carry, True)

        state = (
            jnp.full((1, bq), NEG_LARGE, jnp.float32),
            jnp.zeros((1, bq), jnp.float32),
            jnp.zeros((HD, bq), jnp.float32),
        )
        state = lax.fori_loop(mid_low, mid_high, lambda ki, c: step(ki, c, False), state)
        edges = mid_low - low + high - mid_high
        top, total_p, acc = lax.fori_loop(0, edges, edge_step, state)
        out_ref[:, queries] = acc / total_p
        log_ref[:, queries] = top + jnp.log2(total_p)


def backward_kernel(peers, heads, rows, bq, bk, me_s, q_ref, k_ref, v_ref, first_ref, out_ref, log_ref,
                    *refs):
    blocks = refs[:peers]
    results = refs[peers:peers + heads]
    g_ref, kt_ref, dq_ref, dk_acc, dv_acc, dq_acc = refs[peers + heads:]
    total = q_ref.shape[0]
    scale = HD ** (-0.5)
    factor = scale * math.log2(math.e)
    me = me_s[0]
    for d, block in enumerate(blocks):
        g_ref[aligned(me ^ d, rows), :] = block[...]
    kt_ref[...] = k_ref[...].T
    dk_acc[...] = jnp.zeros_like(dk_acc)
    dv_acc[...] = jnp.zeros_like(dv_acc)
    own_first = (me // heads) * heads * rows
    own_last = own_first + heads * rows

    @pl.loop(0, total // bq)
    def _(qi):
        queries = aligned(qi, bq)
        q0 = qi * bq
        q = q_ref[queries, :]
        g = g_ref[queries, :]
        qt = q.T
        gt = g.T
        first_row = first_ref[:, queries]
        log_row = log_ref[:, queries]
        dot_row = jnp.sum(gt.astype(jnp.float32) * out_ref[:, queries], axis=0, keepdims=True)
        low, mid_low, mid_high, high = block_ranges(first_row, q0, bq, bk)
        dq_acc[...] = jnp.zeros_like(dq_acc)
        if heads < peers:
            wanted = (q0 + bq > own_first) & (q0 < own_last)
            low = jnp.where(wanted, low, jnp.maximum(low, own_first // bk))
            high = jnp.where(wanted, high, jnp.minimum(high, (own_last + bk - 1) // bk))
            high = jnp.maximum(low, high)
            mid_low = jnp.clip(mid_low, low, high)
            mid_high = jnp.clip(mid_high, mid_low, high)

        def step(ki, edge):
            keys = aligned(ki, bk)
            p = jnp.exp2(dot32(k_ref[keys, :], qt) * factor - log_row)
            if edge:
                p = jnp.where(visible(first_row, q0, ki * bk, (bk, bq)), p, 0.0)
            dv_acc[keys, :] += dot32(p.astype(jnp.bfloat16), g)
            dp = dot32(v_ref[keys, :], gt)
            ds = (p * (dp - dot_row)).astype(jnp.bfloat16)
            dk_acc[keys, :] += dot32(ds, q)
            dq_acc[...] += dot32(kt_ref[:, keys], ds)

        @pl.loop(mid_low, mid_high)
        def _(ki):
            step(ki, False)

        @pl.loop(0, mid_low - low + high - mid_high)
        def _(index):
            step(edge_block(index, low, mid_low, mid_high), True)

        dq_ref[queries, :] = (scale * dq_acc[...]).T.astype(dq_ref.dtype)

    for d, result in enumerate(results):
        own = aligned(me ^ d, rows)
        result[:rows, :] = dq_ref[own, :]
        result[rows:2 * rows, :] = (scale * dk_acc[own, :]).astype(result.dtype)
        result[2 * rows:, :] = dv_acc[own, :].astype(result.dtype)


def attention_cost(total, products):
    return pl.CostEstimate(
        flops=products * total * total * HD // 2,
        bytes_accessed=16 * total * HD,
        transcendentals=total * total // 4,
    )


def attention_forward(me, blocks, rows):
    peers = len(blocks)
    total = peers * rows
    bq, bk = block_size(total, 512), block_size(total, 256)
    return pl.pallas_call(
        functools.partial(forward_kernel, peers, rows, bq, bk),
        in_specs=[SMEM_SPEC] + [VMEM_SPEC] * peers,
        out_specs=[VMEM_SPEC] * 6,
        out_shape=[jax.ShapeDtypeStruct((total, HD), jnp.bfloat16)] * 3
        + [
            jax.ShapeDtypeStruct((1, total), jnp.int32),
            jax.ShapeDtypeStruct((HD, total), jnp.float32),
            jax.ShapeDtypeStruct((1, total), jnp.float32),
        ],
        scratch_shapes=[
            pltpu.VMEM((HD, total), jnp.bfloat16),
            pltpu.VMEM((1, total), jnp.float32),
        ],
        compiler_params=PARAMS,
        cost_estimate=attention_cost(total, 3),
    )(me, *blocks)


def attention_backward(me, heads, state, blocks):
    peers, rows = len(blocks), blocks[0].shape[0]
    total = peers * rows
    bq, bk = block_size(total, 512), block_size(total, 256)
    return pl.pallas_call(
        functools.partial(backward_kernel, peers, heads, rows, bq, bk),
        in_specs=[SMEM_SPEC] + [VMEM_SPEC] * (6 + peers),
        out_specs=[VMEM_SPEC] * heads,
        out_shape=[jax.ShapeDtypeStruct((3 * rows, HD), jnp.bfloat16)] * heads,
        scratch_shapes=[
            pltpu.VMEM((total, HD), jnp.bfloat16),
            pltpu.VMEM((HD, total), jnp.bfloat16),
            pltpu.VMEM((total, HD), jnp.bfloat16),
            pltpu.VMEM((total, HD), jnp.float32),
            pltpu.VMEM((total, HD), jnp.float32),
            pltpu.VMEM((HD, bq), jnp.float32),
        ],
        compiler_params=PARAMS,
        cost_estimate=attention_cost(total, 5),
    )(me, *state, *blocks)


def per_device(peers, groups, queries, keys_in, values, out_grad, out_weight, doc_ids):
    rows, width = queries.shape
    heads = width // HD
    me = lax.axis_index("seq")
    me_vector = me.reshape(1)

    def exchange(x, d):
        return x if d == 0 else lax.ppermute(x, "seq", [(i, i ^ d) for i in range(peers)])

    def pass_on(x):
        return lax.ppermute(x, "head", [(i, (i + 1) % groups) for i in range(groups)])

    packed = pack_heads(me_vector, queries, keys_in, values, doc_ids)
    received = [exchange(packed[d % heads], d) for d in range(peers)]
    state = attention_forward(me_vector, received, rows)

    features, acc = out_grad, None
    for step in range(groups):
        block = lax.rem(lax.axis_index("head") + groups - step, groups)
        last = step == groups - 1
        acc = project(me, block, out_weight, features, acc, last)
        if not last:
            features = pass_on(features)
    grads = [exchange(acc[d % heads], d) for d in range(peers)]

    results = attention_backward(me_vector, heads, state, grads)
    returned = [exchange(results[d], d) for d in range(heads)]
    return tuple(unpack_heads(me_vector, returned, rows))


def solution(mesh):
    in_specs = (
        P("seq", "head"),
        P("seq", "head"),
        P("seq", "head"),
        P("seq", "head"),
        P("head", None),
        P("seq"),
    )
    out_specs = (P("seq", "head"), P("seq", "head"), P("seq", "head"))
    return jax.shard_map(
        functools.partial(per_device, mesh.shape["seq"], mesh.shape["head"]),
        mesh=mesh, in_specs=in_specs, out_specs=out_specs, check_vma=False,
    )
```

```python
import functools
import math

import jax
import jax.numpy as jnp
from jax import lax
from jax.experimental import pallas as pl
from jax.experimental.pallas import tpu as pltpu
from jax.sharding import PartitionSpec as P

HD = 128
DOC_VALUES = 8
DOC_ROWS = 16
NEG_LARGE = -1e30
VMEM_LIMIT = 56 * 1024 * 1024
PARAMS = pltpu.CompilerParams(vmem_limit_bytes=VMEM_LIMIT)

NN = (((1,), (0,)), ((), ()))
NT = (((1,), (1,)), ((), ()))
SMEM_SPEC = pl.BlockSpec(memory_space=pltpu.SMEM)
VMEM_SPEC = pl.BlockSpec(memory_space=pltpu.VMEM)


def dot32(a, b, dims=NN):
    return lax.dot_general(a, b, dims, preferred_element_type=jnp.float32)


def block_size(total, wanted):
    size = min(wanted, total)
    while total % size or size % 128:
        size -= 128
    return size


def aligned(index, size):
    return pl.ds(pl.multiple_of(index * size, size), size)


def pack_kernel(heads, rows, me_s, q_ref, k_ref, v_ref, doc_ref, *outs):
    own = lax.rem(me_s[0], heads)
    docs = doc_ref[...].astype(jnp.float32)
    docs = jnp.concatenate([docs, jnp.zeros((DOC_ROWS - docs.shape[0], HD), jnp.float32)], axis=0)
    docs = docs.astype(jnp.bfloat16)
    for d, out in enumerate(outs):
        columns = aligned(own ^ d, HD)
        for part, ref in enumerate((q_ref, k_ref, v_ref)):
            out[part * rows:(part + 1) * rows, :] = ref[:, columns]
        out[3 * rows:, :] = docs


def pack_heads(me, q, k, v, doc_ids):
    rows, width = q.shape
    heads = width // HD
    return pl.pallas_call(
        functools.partial(pack_kernel, heads, rows),
        in_specs=[SMEM_SPEC] + [VMEM_SPEC] * 4,
        out_specs=[VMEM_SPEC] * heads,
        out_shape=[jax.ShapeDtypeStruct((3 * rows + DOC_ROWS, HD), q.dtype)] * heads,
        compiler_params=PARAMS,
    )(me, q, k, v, doc_ids.reshape(rows // HD, HD))


def unpack_kernel(heads, rows, me_s, *refs):
    own = lax.rem(me_s[0], heads)
    for d in range(heads):
        columns = aligned(own ^ d, HD)
        for part in range(3):
            refs[heads + part][:, columns] = refs[d][part * rows:(part + 1) * rows, :]


def unpack_heads(me, blocks, rows):
    heads = len(blocks)
    return pl.pallas_call(
        functools.partial(unpack_kernel, heads, rows),
        in_specs=[SMEM_SPEC] + [VMEM_SPEC] * heads,
        out_specs=[VMEM_SPEC] * 3,
        out_shape=[jax.ShapeDtypeStruct((rows, heads * HD), blocks[0].dtype)] * 3,
        compiler_params=PARAMS,
    )(me, *blocks)


def project_kernel(first, where_s, *refs):
    if first:
        o_ref, w_ref, out_ref = refs
        out_ref[...] = dot32(o_ref[...], w_ref[...], NT)
    else:
        o_ref, w_ref, acc_ref, out_ref = refs
        out_ref[...] = acc_ref[...] + dot32(o_ref[...], w_ref[...], NT)


def project_last_kernel(where_s, o_ref, w_ref, acc_ref, *outs):
    step = pl.program_id(0)
    both = (acc_ref[...] + dot32(o_ref[...], w_ref[...], NT)).astype(jnp.bfloat16)
    odd = where_s[1] == 1
    near = jnp.where(odd, both[:, HD:], both[:, :HD])
    far = jnp.where(odd, both[:, :HD], both[:, HD:])
    for j in range(len(outs) // 2):

        @pl.when(step == j)
        def _():
            outs[2 * j][...] = near
            outs[2 * j + 1][...] = far


def project(me, block, weight, features, acc, last):
    rows, width = features.shape
    pairs = weight.shape[0] // (2 * HD)
    where = jnp.stack([block, lax.rem(me, 2), lax.rem(me // 2, pairs)])
    feature_spec = pl.BlockSpec((rows, width), lambda j, w: (0, 0))
    weight_spec = pl.BlockSpec((2 * HD, width), lambda j, w: (w[2] ^ j, w[0]))
    acc_spec = pl.BlockSpec((rows, 2 * HD), lambda j, w: (0, w[2] ^ j))
    cost = pl.CostEstimate(
        flops=2 * rows * width * weight.shape[0],
        bytes_accessed=2 * width * weight.shape[0] + 8 * rows * weight.shape[0],
        transcendentals=0,
    )
    if last:
        kernel = project_last_kernel
        out_specs = [pl.BlockSpec((rows, HD), lambda j, w: (0, 0))] * (2 * pairs)
        out_shape = [jax.ShapeDtypeStruct((rows, HD), jnp.bfloat16)] * (2 * pairs)
    else:
        kernel = functools.partial(project_kernel, acc is None)
        out_specs = acc_spec
        out_shape = jax.ShapeDtypeStruct((rows, weight.shape[0]), jnp.float32)
    return pl.pallas_call(
        kernel,
        grid_spec=pltpu.PrefetchScalarGridSpec(
            num_scalar_prefetch=1,
            grid=(pairs,),
            in_specs=[feature_spec, weight_spec] + ([] if acc is None else [acc_spec]),
            out_specs=out_specs,
        ),
        out_shape=out_shape,
        compiler_params=PARAMS,
        cost_estimate=cost,
    )(where, features, weight, *([] if acc is None else [acc]))


def visible(first_row, q0, k0, shape):
    key_pos = k0 + lax.broadcasted_iota(jnp.int32, shape, 0)
    query_pos = q0 + lax.broadcasted_iota(jnp.int32, (1, shape[1]), 1)
    return (key_pos >= first_row) & (key_pos <= query_pos)


def block_ranges(first_row, q0, bq, bk):
    low = jnp.min(first_row) // bk
    high = (q0 + bq + bk - 1) // bk
    mid_low = jnp.minimum((jnp.max(first_row) + bk - 1) // bk, high)
    mid_high = jnp.maximum((q0 + 1) // bk, mid_low)
    return low, mid_low, mid_high, high


def edge_block(index, low, mid_low, mid_high):
    return jnp.where(index < mid_low - low, low + index, index - (mid_low - low) + mid_high)


def forward_kernel(peers, rows, bq, bk, me_s, *refs):
    blocks = refs[:peers]
    q_ref, k_ref, v_ref, first_ref, out_ref, log_ref, vt_ref, doc_ref = refs[peers:]
    total = q_ref.shape[0]
    factor = HD ** (-0.5) * math.log2(math.e)
    for d, block in enumerate(blocks):
        place = me_s[0] ^ d
        for part, ref in enumerate((q_ref, k_ref, v_ref)):
            ref[aligned(place, rows), :] = block[part * rows:(part + 1) * rows, :]
        docs = block[3 * rows:, :].astype(jnp.float32)
        for t in range(rows // HD):
            doc_ref[:, aligned(place * (rows // HD) + t, HD)] = docs[t:t + 1, :]
    docs = doc_ref[...]
    first = jnp.zeros(docs.shape, jnp.float32)
    for value in range(1, DOC_VALUES):
        before = jnp.sum((docs < value).astype(jnp.float32))
        first = jnp.where(docs >= value, before, first)
    first_ref[...] = first.astype(jnp.int32)
    vt_ref[...] = v_ref[...].T

    @pl.loop(0, total // bq)
    def _(qi):
        queries = aligned(qi, bq)
        q0 = qi * bq
        qt = q_ref[queries, :].T
        first_row = first_ref[:, queries]
        low, mid_low, mid_high, high = block_ranges(first_row, q0, bq, bk)

        def step(ki, carry, edge):
            top, total_p, acc = carry
            keys = aligned(ki, bk)
            s = dot32(k_ref[keys, :], qt) * factor
            if edge:
                s = jnp.where(visible(first_row, q0, ki * bk, (bk, bq)), s, NEG_LARGE)
            new_top = jnp.maximum(top, jnp.max(s, axis=0, keepdims=True))
            p = jnp.exp2(s - new_top)
            fix = jnp.exp2(top - new_top)
            high_p = p.astype(jnp.bfloat16)
            rest = (p - high_p.astype(jnp.float32)).astype(jnp.bfloat16)
            vt = vt_ref[:, keys]
            acc = acc * fix + (dot32(vt, high_p) + dot32(vt, rest))
            return new_top, total_p * fix + jnp.sum(p, axis=0, keepdims=True), acc

        def edge_step(index, carry):
            return step(edge_block(index, low, mid_low, mid_high), carry, True)

        state = (
            jnp.full((1, bq), NEG_LARGE, jnp.float32),
            jnp.zeros((1, bq), jnp.float32),
            jnp.zeros((HD, bq), jnp.float32),
        )
        state = lax.fori_loop(mid_low, mid_high, lambda ki, c: step(ki, c, False), state)
        edges = mid_low - low + high - mid_high
        top, total_p, acc = lax.fori_loop(0, edges, edge_step, state)
        out_ref[:, queries] = acc / total_p
        log_ref[:, queries] = top + jnp.log2(total_p)


def backward_kernel(peers, heads, rows, bq, bk, me_s, q_ref, k_ref, v_ref, first_ref, out_ref, log_ref,
                    *refs):
    blocks = refs[:peers]
    results = refs[peers:peers + heads]
    g_ref, kt_ref, dq_ref, dk_acc, dv_acc, dq_acc = refs[peers + heads:]
    total = q_ref.shape[0]
    scale = HD ** (-0.5)
    factor = scale * math.log2(math.e)
    me = me_s[0]
    for d, block in enumerate(blocks):
        g_ref[aligned(me ^ d, rows), :] = block[...]
    kt_ref[...] = k_ref[...].T
    dk_acc[...] = jnp.zeros_like(dk_acc)
    dv_acc[...] = jnp.zeros_like(dv_acc)
    own_first = (me // heads) * heads * rows
    own_last = own_first + heads * rows

    @pl.loop(0, total // bq)
    def _(qi):
        queries = aligned(qi, bq)
        q0 = qi * bq
        q = q_ref[queries, :]
        g = g_ref[queries, :]
        qt = q.T
        gt = g.T
        first_row = first_ref[:, queries]
        log_row = log_ref[:, queries]
        dot_row = jnp.sum(gt.astype(jnp.float32) * out_ref[:, queries], axis=0, keepdims=True)
        low, mid_low, mid_high, high = block_ranges(first_row, q0, bq, bk)
        dq_acc[...] = jnp.zeros_like(dq_acc)
        if heads < peers:
            wanted = (q0 + bq > own_first) & (q0 < own_last)
            low = jnp.where(wanted, low, jnp.maximum(low, own_first // bk))
            high = jnp.where(wanted, high, jnp.minimum(high, (own_last + bk - 1) // bk))
            high = jnp.maximum(low, high)
            mid_low = jnp.clip(mid_low, low, high)
            mid_high = jnp.clip(mid_high, mid_low, high)

        def step(ki, edge):
            keys = aligned(ki, bk)
            p = jnp.exp2(dot32(k_ref[keys, :], qt) * factor - log_row)
            if edge:
                p = jnp.where(visible(first_row, q0, ki * bk, (bk, bq)), p, 0.0)
            dv_acc[keys, :] += dot32(p.astype(jnp.bfloat16), g)
            dp = dot32(v_ref[keys, :], gt)
            ds = (p * (dp - dot_row)).astype(jnp.bfloat16)
            dk_acc[keys, :] += dot32(ds, q)
            dq_acc[...] += dot32(kt_ref[:, keys], ds)

        @pl.loop(mid_low, mid_high)
        def _(ki):
            step(ki, False)

        @pl.loop(0, mid_low - low + high - mid_high)
        def _(index):
            step(edge_block(index, low, mid_low, mid_high), True)

        dq_ref[queries, :] = (scale * dq_acc[...]).T.astype(dq_ref.dtype)

    for d, result in enumerate(results):
        own = aligned(me ^ d, rows)
        result[:rows, :] = dq_ref[own, :]
        result[rows:2 * rows, :] = (scale * dk_acc[own, :]).astype(result.dtype)
        result[2 * rows:, :] = dv_acc[own, :].astype(result.dtype)


def attention_cost(total, products):
    return pl.CostEstimate(
        flops=products * total * total * HD // 2,
        bytes_accessed=16 * total * HD,
        transcendentals=total * total // 4,
    )


def attention_forward(me, blocks, rows):
    peers = len(blocks)
    total = peers * rows
    bq, bk = block_size(total, 512), block_size(total, 256)
    return pl.pallas_call(
        functools.partial(forward_kernel, peers, rows, bq, bk),
        in_specs=[SMEM_SPEC] + [VMEM_SPEC] * peers,
        out_specs=[VMEM_SPEC] * 6,
        out_shape=[jax.ShapeDtypeStruct((total, HD), jnp.bfloat16)] * 3
        + [
            jax.ShapeDtypeStruct((1, total), jnp.int32),
            jax.ShapeDtypeStruct((HD, total), jnp.float32),
            jax.ShapeDtypeStruct((1, total), jnp.float32),
        ],
        scratch_shapes=[
            pltpu.VMEM((HD, total), jnp.bfloat16),
            pltpu.VMEM((1, total), jnp.float32),
        ],
        compiler_params=PARAMS,
        cost_estimate=attention_cost(total, 3),
    )(me, *blocks)


def attention_backward(me, heads, state, blocks):
    peers, rows = len(blocks), blocks[0].shape[0]
    total = peers * rows
    bq, bk = block_size(total, 512), block_size(total, 256)
    return pl.pallas_call(
        functools.partial(backward_kernel, peers, heads, rows, bq, bk),
        in_specs=[SMEM_SPEC] + [VMEM_SPEC] * (6 + peers),
        out_specs=[VMEM_SPEC] * heads,
        out_shape=[jax.ShapeDtypeStruct((3 * rows, HD), jnp.bfloat16)] * heads,
        scratch_shapes=[
            pltpu.VMEM((total, HD), jnp.bfloat16),
            pltpu.VMEM((HD, total), jnp.bfloat16),
            pltpu.VMEM((total, HD), jnp.bfloat16),
            pltpu.VMEM((total, HD), jnp.float32),
            pltpu.VMEM((total, HD), jnp.float32),
            pltpu.VMEM((HD, bq), jnp.float32),
        ],
        compiler_params=PARAMS,
        cost_estimate=attention_cost(total, 5),
    )(me, *state, *blocks)


def per_device(peers, groups, queries, keys_in, values, out_grad, out_weight, doc_ids):
    rows, width = queries.shape
    heads = width // HD
    me = lax.axis_index("seq")
    me_vector = me.reshape(1)

    def exchange(x, d):
        return x if d == 0 else lax.ppermute(x, "seq", [(i, i ^ d) for i in range(peers)])

    def pass_on(x):
        return lax.ppermute(x, "head", [(i, (i + 1) % groups) for i in range(groups)])

    packed = list(pack_heads(me_vector, queries, keys_in, values, doc_ids))
    received = [exchange(packed[d % heads], d) for d in range(peers)]

    after = lax.optimization_barrier
    features, acc = out_grad, None
    for step in range(groups):
        block = lax.rem(lax.axis_index("head") + groups - step, groups)
        last = step == groups - 1
        if step == 0:
            features, packed[0] = after((features, packed[0]))
        if not last:
            passed = pass_on(features)
        if step == groups - 2:
            received[0], features = after((received[0], features))
            state = list(attention_forward(me_vector, received, rows))
            features, state[1] = after((features, state[1]))
        acc = project(me, block, out_weight, features, acc, last)
        if not last:
            features = passed
            if step < groups - 2:
                low = 1 + step * (peers - 1) // (groups - 2)
                high = 1 + (step + 1) * (peers - 1) // (groups - 2)
                features, acc, received[low:high] = after((features, acc, received[low:high]))
    grads = [exchange(acc[d % heads], d) for d in range(peers)]

    results = attention_backward(me_vector, heads, state, grads)
    returned = [exchange(results[d], d) for d in range(heads)]
    return tuple(unpack_heads(me_vector, returned, rows))


def solution(mesh):
    in_specs = (
        P("seq", "head"),
        P("seq", "head"),
        P("seq", "head"),
        P("seq", "head"),
        P("head", None),
        P("seq"),
    )
    out_specs = (P("seq", "head"), P("seq", "head"), P("seq", "head"))
    return jax.shard_map(
        functools.partial(per_device, mesh.shape["seq"], mesh.shape["head"]),
        mesh=mesh, in_specs=in_specs, out_specs=out_specs, check_vma=False,
    )
```

```python
import functools
import math

import jax
import jax.numpy as jnp
from jax import lax
from jax.experimental import pallas as pl
from jax.experimental.pallas import tpu as pltpu
from jax.sharding import PartitionSpec as P

HD = 128
DOC_VALUES = 8
DOC_ROWS = 16
NEG_LARGE = -1e30
VMEM_LIMIT = 56 * 1024 * 1024
PARAMS = pltpu.CompilerParams(vmem_limit_bytes=VMEM_LIMIT)

NN = (((1,), (0,)), ((), ()))
NT = (((1,), (1,)), ((), ()))
SMEM_SPEC = pl.BlockSpec(memory_space=pltpu.SMEM)
VMEM_SPEC = pl.BlockSpec(memory_space=pltpu.VMEM)


def dot32(a, b, dims=NN):
    return lax.dot_general(a, b, dims, preferred_element_type=jnp.float32)


def block_size(total, wanted):
    size = min(wanted, total)
    while total % size or size % 128:
        size -= 128
    return size


def aligned(index, size):
    return pl.ds(pl.multiple_of(index * size, size), size)


def pack_kernel(heads, rows, me_s, q_ref, k_ref, v_ref, doc_ref, *outs):
    own = lax.rem(me_s[0], heads)
    docs = doc_ref[...].astype(jnp.float32)
    docs = jnp.concatenate([docs, jnp.zeros((DOC_ROWS - docs.shape[0], HD), jnp.float32)], axis=0)
    docs = docs.astype(jnp.bfloat16)
    for d, out in enumerate(outs):
        columns = aligned(own ^ d, HD)
        for part, ref in enumerate((q_ref, k_ref, v_ref)):
            out[part * rows:(part + 1) * rows, :] = ref[:, columns]
        out[3 * rows:, :] = docs


def pack_heads(me, q, k, v, doc_ids):
    rows, width = q.shape
    heads = width // HD
    return pl.pallas_call(
        functools.partial(pack_kernel, heads, rows),
        in_specs=[SMEM_SPEC] + [VMEM_SPEC] * 4,
        out_specs=[VMEM_SPEC] * heads,
        out_shape=[jax.ShapeDtypeStruct((3 * rows + DOC_ROWS, HD), q.dtype)] * heads,
        compiler_params=PARAMS,
    )(me, q, k, v, doc_ids.reshape(rows // HD, HD))


def unpack_kernel(heads, rows, me_s, *refs):
    own = lax.rem(me_s[0], heads)
    for d in range(heads):
        columns = aligned(own ^ d, HD)
        for part in range(3):
            refs[heads + part][:, columns] = refs[d][part * rows:(part + 1) * rows, :]


def unpack_heads(me, blocks, rows):
    heads = len(blocks)
    return pl.pallas_call(
        functools.partial(unpack_kernel, heads, rows),
        in_specs=[SMEM_SPEC] + [VMEM_SPEC] * heads,
        out_specs=[VMEM_SPEC] * 3,
        out_shape=[jax.ShapeDtypeStruct((rows, heads * HD), blocks[0].dtype)] * 3,
        compiler_params=PARAMS,
    )(me, *blocks)


def project_kernel(first, where_s, *refs):
    if first:
        o_ref, w_ref, out_ref = refs
        out_ref[...] = dot32(o_ref[...], w_ref[...], NT)
    else:
        o_ref, w_ref, acc_ref, out_ref = refs
        out_ref[...] = acc_ref[...] + dot32(o_ref[...], w_ref[...], NT)


def project_last_kernel(where_s, o_ref, w_ref, acc_ref, *outs):
    step = pl.program_id(0)
    both = (acc_ref[...] + dot32(o_ref[...], w_ref[...], NT)).astype(jnp.bfloat16)
    odd = where_s[1] == 1
    near = jnp.where(odd, both[:, HD:], both[:, :HD])
    far = jnp.where(odd, both[:, :HD], both[:, HD:])
    for j in range(len(outs) // 2):

        @pl.when(step == j)
        def _():
            outs[2 * j][...] = near
            outs[2 * j + 1][...] = far


def project(me, block, weight, features, acc, last):
    rows, width = features.shape
    pairs = weight.shape[0] // (2 * HD)
    where = jnp.stack([block, lax.rem(me, 2), lax.rem(me // 2, pairs)])
    feature_spec = pl.BlockSpec((rows, width), lambda j, w: (0, 0))
    weight_spec = pl.BlockSpec((2 * HD, width), lambda j, w: (w[2] ^ j, w[0]))
    acc_spec = pl.BlockSpec((rows, 2 * HD), lambda j, w: (0, w[2] ^ j))
    cost = pl.CostEstimate(
        flops=2 * rows * width * weight.shape[0],
        bytes_accessed=2 * width * weight.shape[0] + 8 * rows * weight.shape[0],
        transcendentals=0,
    )
    if last:
        kernel = project_last_kernel
        out_specs = [pl.BlockSpec((rows, HD), lambda j, w: (0, 0))] * (2 * pairs)
        out_shape = [jax.ShapeDtypeStruct((rows, HD), jnp.bfloat16)] * (2 * pairs)
    else:
        kernel = functools.partial(project_kernel, acc is None)
        out_specs = acc_spec
        out_shape = jax.ShapeDtypeStruct((rows, weight.shape[0]), jnp.float32)
    return pl.pallas_call(
        kernel,
        grid_spec=pltpu.PrefetchScalarGridSpec(
            num_scalar_prefetch=1,
            grid=(pairs,),
            in_specs=[feature_spec, weight_spec] + ([] if acc is None else [acc_spec]),
            out_specs=out_specs,
        ),
        out_shape=out_shape,
        compiler_params=PARAMS,
        cost_estimate=cost,
    )(where, features, weight, *([] if acc is None else [acc]))


def visible(first_row, q0, k0, shape):
    key = lax.broadcasted_iota(jnp.int32, shape, 0)
    last_row = q0 - k0 + lax.broadcasted_iota(jnp.int32, (1, shape[1]), 1)
    return (key >= first_row - k0) & (key <= last_row)


def plan_size(total, bq, bk):
    return sum(((q + 1) * bq + bk - 1) // bk for q in range(total // bq)) + 2


def fill_plan(lows, total, bq, bk, own, plan_q, plan_k, count_ref):
    def put(qi):
        def at(ki, count):
            plan_q[count] = qi
            plan_k[count] = ki
            return count + 1

        return at

    count = 0
    for qi, low in enumerate(lows):
        high = ((qi + 1) * bq + bk - 1) // bk
        if own is not None:
            wanted = ((qi + 1) * bq > own[0]) & (qi * bq < own[1])
            low = jnp.where(wanted, low, jnp.maximum(low, own[0] // bk))
            high = jnp.where(wanted, high, jnp.minimum(high, (own[1] + bk - 1) // bk))
        count = lax.fori_loop(low, high, put(qi), count)
    count_ref[0] = (count + 1) // 2
    for spare in range(2):
        plan_q[count + spare] = 0
        plan_k[count + spare] = total // bk - 1


def pipelined(plan_q, plan_k, count_ref, early, late, buffers):
    early(plan_q[0], plan_k[0], buffers[0])

    @pl.loop(0, count_ref[0])
    def _(i):
        for turn in range(2):
            now = 2 * i + turn
            late(plan_q[now], plan_k[now], buffers[turn])
            early(plan_q[now + 1], plan_k[now + 1], buffers[1 - turn])


def forward_kernel(peers, heads, rows, bq, bk, me_s, *refs):
    blocks = refs[:peers]
    q_ref, k_ref, v_ref, first_ref, out_ref, log_ref, plan_q, plan_k, count_ref = refs[peers:peers + 9]
    own_q, own_k, own_count, qt_ref, vt_ref, doc_ref, sum_ref, s0, top0, s1, top1 = refs[peers + 9:]
    total = q_ref.shape[0]
    factor = HD ** (-0.5) * math.log2(math.e)
    me = me_s[0]
    for d, block in enumerate(blocks):
        place = me ^ d
        for part, ref in enumerate((q_ref, k_ref, v_ref)):
            ref[aligned(place, rows), :] = block[part * rows:(part + 1) * rows, :]
        docs = block[3 * rows:, :].astype(jnp.float32)
        for t in range(rows // HD):
            doc_ref[:, aligned(place * (rows // HD) + t, HD)] = docs[t:t + 1, :]
    docs = doc_ref[...]
    first = jnp.zeros(docs.shape, jnp.float32)
    for value in range(1, DOC_VALUES):
        before = jnp.sum((docs < value).astype(jnp.float32))
        first = jnp.where(docs >= value, before, first)
    first = first.astype(jnp.int32)
    first_ref[...] = first
    lows = [jnp.min(first[:, qi * bq:(qi + 1) * bq]) // bk for qi in range(total // bq)]
    fill_plan(lows, total, bq, bk, None, own_q, own_k, own_count)
    group = (me // heads) * heads * rows
    own = None if heads == peers else (group, group + heads * rows)
    fill_plan(lows, total, bq, bk, own, plan_q, plan_k, count_ref)
    qt_ref[...] = q_ref[...].T
    vt_ref[...] = v_ref[...].T
    out_ref[...] = jnp.zeros_like(out_ref)
    log_ref[...] = jnp.full_like(log_ref, NEG_LARGE)
    sum_ref[...] = jnp.zeros_like(sum_ref)

    def early(qi, ki, buffer):
        s_ref, top_ref = buffer
        keys, queries = aligned(ki, bk), aligned(qi, bq)
        s = dot32(k_ref[keys, :], qt_ref[:, queries]) * factor
        s = jnp.where(visible(first_ref[:, queries], qi * bq, ki * bk, (bk, bq)), s, NEG_LARGE)
        s_ref[...] = s
        top_ref[...] = jnp.max(s, axis=0, keepdims=True)

    def late(qi, ki, buffer):
        s_ref, top_ref = buffer
        keys, queries = aligned(ki, bk), aligned(qi, bq)
        top = log_ref[:, queries]
        new_top = jnp.maximum(top, top_ref[...])
        p = jnp.exp2(s_ref[...] - new_top)
        fix = jnp.exp2(top - new_top)
        high = p.astype(jnp.bfloat16)
        rest = (p - high.astype(jnp.float32)).astype(jnp.bfloat16)
        vt = vt_ref[:, keys]
        out_ref[:, queries] = out_ref[:, queries] * fix + (dot32(vt, high) + dot32(vt, rest))
        sum_ref[:, queries] = sum_ref[:, queries] * fix + jnp.sum(p, axis=0, keepdims=True)
        log_ref[:, queries] = new_top

    pipelined(own_q, own_k, own_count, early, late, ((s0, top0), (s1, top1)))
    total_p = sum_ref[...]
    out_ref[...] = out_ref[...] / total_p
    log_ref[...] = log_ref[...] + jnp.log2(total_p)


def backward_kernel(peers, heads, rows, bq, bk, me_s, plan_q, plan_k, count_ref, q_ref, k_ref, v_ref,
                    first_ref, out_ref, log_ref, *refs):
    blocks = refs[:peers]
    results = refs[peers:peers + heads]
    g_ref, qt_ref, gt_ref, kt_ref, dot_ref, dk_acc, dv_acc, dq_acc, p0, ds0, p1, ds1 = refs[peers + heads:]
    scale = HD ** (-0.5)
    factor = scale * math.log2(math.e)
    me = me_s[0]
    for d, block in enumerate(blocks):
        g_ref[aligned(me ^ d, rows), :] = block[...]
    qt_ref[...] = q_ref[...].T
    gt_ref[...] = g_ref[...].T
    kt_ref[...] = k_ref[...].T
    dot_ref[...] = jnp.sum(gt_ref[...].astype(jnp.float32) * out_ref[...], axis=0, keepdims=True)
    dk_acc[...] = jnp.zeros_like(dk_acc)
    dv_acc[...] = jnp.zeros_like(dv_acc)
    dq_acc[...] = jnp.zeros_like(dq_acc)

    def early(qi, ki, buffer):
        p_ref, ds_ref = buffer
        keys, queries = aligned(ki, bk), aligned(qi, bq)
        p = jnp.exp2(dot32(k_ref[keys, :], qt_ref[:, queries]) * factor - log_ref[:, queries])
        p = jnp.where(visible(first_ref[:, queries], qi * bq, ki * bk, (bk, bq)), p, 0.0)
        p_ref[...] = p.astype(jnp.bfloat16)
        dp = dot32(v_ref[keys, :], gt_ref[:, queries])
        ds_ref[...] = (p * (dp - dot_ref[:, queries])).astype(jnp.bfloat16)

    def late(qi, ki, buffer):
        p_ref, ds_ref = buffer
        keys, queries = aligned(ki, bk), aligned(qi, bq)
        dv_acc[keys, :] += dot32(p_ref[...], g_ref[queries, :])
        dk_acc[keys, :] += dot32(ds_ref[...], q_ref[queries, :])
        dq_acc[:, queries] += dot32(kt_ref[:, keys], ds_ref[...])

    pipelined(plan_q, plan_k, count_ref, early, late, ((p0, ds0), (p1, ds1)))
    for d, result in enumerate(results):
        own = aligned(me ^ d, rows)
        result[:rows, :] = (scale * dq_acc[:, own]).T.astype(result.dtype)
        result[rows:2 * rows, :] = (scale * dk_acc[own, :]).astype(result.dtype)
        result[2 * rows:, :] = dv_acc[own, :].astype(result.dtype)


def attention_cost(total, products):
    return pl.CostEstimate(
        flops=products * total * total * HD // 2,
        bytes_accessed=16 * total * HD,
        transcendentals=total * total // 4,
    )


def attention_forward(me, blocks, rows, heads):
    peers = len(blocks)
    total = peers * rows
    bq, bk = block_size(total, 512), block_size(total, 256)
    size = plan_size(total, bq, bk)
    return pl.pallas_call(
        functools.partial(forward_kernel, peers, heads, rows, bq, bk),
        in_specs=[SMEM_SPEC] + [VMEM_SPEC] * peers,
        out_specs=[VMEM_SPEC] * 6 + [SMEM_SPEC] * 3,
        out_shape=[jax.ShapeDtypeStruct((total, HD), jnp.bfloat16)] * 3
        + [
            jax.ShapeDtypeStruct((1, total), jnp.int32),
            jax.ShapeDtypeStruct((HD, total), jnp.float32),
            jax.ShapeDtypeStruct((1, total), jnp.float32),
            jax.ShapeDtypeStruct((size,), jnp.int32),
            jax.ShapeDtypeStruct((size,), jnp.int32),
            jax.ShapeDtypeStruct((1,), jnp.int32),
        ],
        scratch_shapes=[
            pltpu.SMEM((size,), jnp.int32),
            pltpu.SMEM((size,), jnp.int32),
            pltpu.SMEM((1,), jnp.int32),
            pltpu.VMEM((HD, total), jnp.bfloat16),
            pltpu.VMEM((HD, total), jnp.bfloat16),
            pltpu.VMEM((1, total), jnp.float32),
            pltpu.VMEM((1, total), jnp.float32),
        ]
        + [pltpu.VMEM((bk, bq), jnp.float32), pltpu.VMEM((1, bq), jnp.float32)] * 2,
        compiler_params=PARAMS,
        cost_estimate=attention_cost(total, 3),
    )(me, *blocks)


def attention_backward(me, heads, state, blocks):
    peers, rows = len(blocks), blocks[0].shape[0]
    total = peers * rows
    bq, bk = block_size(total, 512), block_size(total, 256)
    return pl.pallas_call(
        functools.partial(backward_kernel, peers, heads, rows, bq, bk),
        in_specs=[SMEM_SPEC] * 4 + [VMEM_SPEC] * (6 + peers),
        out_specs=[VMEM_SPEC] * heads,
        out_shape=[jax.ShapeDtypeStruct((3 * rows, HD), jnp.bfloat16)] * heads,
        scratch_shapes=[
            pltpu.VMEM((total, HD), jnp.bfloat16),
            pltpu.VMEM((HD, total), jnp.bfloat16),
            pltpu.VMEM((HD, total), jnp.bfloat16),
            pltpu.VMEM((HD, total), jnp.bfloat16),
            pltpu.VMEM((1, total), jnp.float32),
            pltpu.VMEM((total, HD), jnp.float32),
            pltpu.VMEM((total, HD), jnp.float32),
            pltpu.VMEM((HD, total), jnp.float32),
        ]
        + [pltpu.VMEM((bk, bq), jnp.bfloat16)] * 4,
        compiler_params=PARAMS,
        cost_estimate=attention_cost(total, 5),
    )(me, *state[6:], *state[:6], *blocks)


def per_device(peers, groups, queries, keys_in, values, out_grad, out_weight, doc_ids):
    rows, width = queries.shape
    heads = width // HD
    me = lax.axis_index("seq")
    me_vector = me.reshape(1)

    def exchange(x, d):
        return x if d == 0 else lax.ppermute(x, "seq", [(i, i ^ d) for i in range(peers)])

    def pass_on(x):
        return lax.ppermute(x, "head", [(i, (i + 1) % groups) for i in range(groups)])

    order = [*range(peers - 2, 0, -2), *range(peers - 1, 0, -2)]

    def exchange_all(blocks, wanted):
        moved = {d: exchange(blocks[d % heads], d) for d in order if d < wanted}
        return [blocks[0]] + [moved[d] for d in range(1, wanted)]

    packed = list(pack_heads(me_vector, queries, keys_in, values, doc_ids))
    received = exchange_all(packed, peers)

    after = lax.optimization_barrier
    features, acc = out_grad, None
    for step in range(groups):
        block = lax.rem(lax.axis_index("head") + groups - step, groups)
        last = step == groups - 1
        if step == 0:
            features, packed[0] = after((features, packed[0]))
        if not last:
            passed = pass_on(features)
        if step == groups - 2:
            received[0], features = after((received[0], features))
            state = list(attention_forward(me_vector, received, rows, heads))
            features, state[1] = after((features, state[1]))
        acc = project(me, block, out_weight, features, acc, last)
        if not last:
            features = passed
            if step < groups - 2:
                batch = order[step * len(order) // (groups - 2):(step + 1) * len(order) // (groups - 2)]
                features, acc, here = after((features, acc, [received[d] for d in batch]))
                for d, block in zip(batch, here):
                    received[d] = block
    grads = exchange_all(acc, peers)

    results = attention_backward(me_vector, heads, state, grads)
    returned = exchange_all(results, heads)
    return tuple(unpack_heads(me_vector, returned, rows))


def solution(mesh):
    in_specs = (
        P("seq", "head"),
        P("seq", "head"),
        P("seq", "head"),
        P("seq", "head"),
        P("head", None),
        P("seq"),
    )
    out_specs = (P("seq", "head"), P("seq", "head"), P("seq", "head"))
    return jax.shard_map(
        functools.partial(per_device, mesh.shape["seq"], mesh.shape["head"]),
        mesh=mesh, in_specs=in_specs, out_specs=out_specs, check_vma=False,
    )
```

```python
import functools
import math

import jax
import jax.numpy as jnp
from jax import lax
from jax.experimental import pallas as pl
from jax.experimental.pallas import tpu as pltpu
from jax.sharding import PartitionSpec as P

HD = 128
DOC_VALUES = 8
DOC_ROWS = 16
NEG_LARGE = -1e30
VMEM_LIMIT = 56 * 1024 * 1024
PARAMS = pltpu.CompilerParams(vmem_limit_bytes=VMEM_LIMIT)

NN = (((1,), (0,)), ((), ()))
NT = (((1,), (1,)), ((), ()))
SMEM_SPEC = pl.BlockSpec(memory_space=pltpu.SMEM)
VMEM_SPEC = pl.BlockSpec(memory_space=pltpu.VMEM)


def dot32(a, b, dims=NN):
    return lax.dot_general(a, b, dims, preferred_element_type=jnp.float32)


def block_size(total, wanted):
    size = min(wanted, total)
    while total % size or size % 128:
        size -= 128
    return size


def aligned(index, size):
    return pl.ds(pl.multiple_of(index * size, size), size)


def pack_kernel(heads, rows, me_s, q_ref, k_ref, v_ref, doc_ref, *outs):
    own = lax.rem(me_s[0], heads)
    docs = doc_ref[...].astype(jnp.float32)
    docs = jnp.concatenate([docs, jnp.zeros((DOC_ROWS - docs.shape[0], HD), jnp.float32)], axis=0)
    docs = docs.astype(jnp.bfloat16)
    for d, out in enumerate(outs):
        columns = aligned(own ^ d, HD)
        for part, ref in enumerate((q_ref, k_ref, v_ref)):
            out[part * rows:(part + 1) * rows, :] = ref[:, columns]
        out[3 * rows:, :] = docs


def pack_heads(me, q, k, v, doc_ids):
    rows, width = q.shape
    heads = width // HD
    return pl.pallas_call(
        functools.partial(pack_kernel, heads, rows),
        in_specs=[SMEM_SPEC] + [VMEM_SPEC] * 4,
        out_specs=[VMEM_SPEC] * heads,
        out_shape=[jax.ShapeDtypeStruct((3 * rows + DOC_ROWS, HD), q.dtype)] * heads,
        compiler_params=PARAMS,
    )(me, q, k, v, doc_ids.reshape(rows // HD, HD))


def unpack_kernel(heads, rows, me_s, *refs):
    own = lax.rem(me_s[0], heads)
    for d in range(heads):
        columns = aligned(own ^ d, HD)
        for part in range(3):
            refs[heads + part][:, columns] = refs[d][part * rows:(part + 1) * rows, :]


def unpack_heads(me, blocks, rows):
    heads = len(blocks)
    return pl.pallas_call(
        functools.partial(unpack_kernel, heads, rows),
        in_specs=[SMEM_SPEC] + [VMEM_SPEC] * heads,
        out_specs=[VMEM_SPEC] * 3,
        out_shape=[jax.ShapeDtypeStruct((rows, heads * HD), blocks[0].dtype)] * 3,
        compiler_params=PARAMS,
    )(me, *blocks)


def project_kernel(first, o_ref, w_ref, *refs):
    out_ref = refs[-1]
    for pair in range(w_ref.shape[1] // (2 * HD)):
        columns = slice(pair * 2 * HD, (pair + 1) * 2 * HD)
        both = dot32(o_ref[...], w_ref[:, columns])
        out_ref[:, columns] = both if first else refs[0][:, columns] + both


def project_last_kernel(me_s, o_ref, w_ref, acc_ref, *outs):
    pairs = len(outs) // 2
    odd = lax.rem(me_s[0], 2) == 1
    for j in range(pairs):
        columns = aligned(lax.rem(me_s[0] // 2, pairs) ^ j, 2 * HD)
        both = (acc_ref[:, columns] + dot32(o_ref[...], w_ref[:, columns])).astype(jnp.bfloat16)
        outs[2 * j][...] = jnp.where(odd, both[:, HD:], both[:, :HD])
        outs[2 * j + 1][...] = jnp.where(odd, both[:, :HD], both[:, HD:])


def project(me, weight, features, acc, last):
    rows, width = features.shape
    columns = weight.shape[1]
    cost = pl.CostEstimate(
        flops=2 * rows * width * columns,
        bytes_accessed=2 * width * columns + 8 * rows * columns,
        transcendentals=0,
    )
    if last:
        return pl.pallas_call(
            project_last_kernel,
            in_specs=[SMEM_SPEC] + [VMEM_SPEC] * 3,
            out_specs=[VMEM_SPEC] * (columns // HD),
            out_shape=[jax.ShapeDtypeStruct((rows, HD), jnp.bfloat16)] * (columns // HD),
            compiler_params=PARAMS,
            cost_estimate=cost,
        )(me, features, weight, acc)
    operands = (features, weight) + (() if acc is None else (acc,))
    return pl.pallas_call(
        functools.partial(project_kernel, acc is None),
        in_specs=[VMEM_SPEC] * len(operands),
        out_specs=VMEM_SPEC,
        out_shape=jax.ShapeDtypeStruct((rows, columns), jnp.float32),
        compiler_params=PARAMS,
        cost_estimate=cost,
    )(*operands)


def visible(first_row, q0, k0, shape):
    key = lax.broadcasted_iota(jnp.int32, shape, 0)
    last_row = q0 - k0 + lax.broadcasted_iota(jnp.int32, (1, shape[1]), 1)
    return (key >= first_row - k0) & (key <= last_row)


def plan_size(total, bq, bk):
    return sum(((q + 1) * bq + bk - 1) // bk for q in range(total // bq)) + 2


def fill_plan(lows, total, bq, bk, own, plan_q, plan_k, count_ref):
    def put(qi):
        def at(ki, count):
            plan_q[count] = qi
            plan_k[count] = ki
            return count + 1

        return at

    count = 0
    for qi, low in enumerate(lows):
        high = ((qi + 1) * bq + bk - 1) // bk
        if own is not None:
            wanted = ((qi + 1) * bq > own[0]) & (qi * bq < own[1])
            low = jnp.where(wanted, low, jnp.maximum(low, own[0] // bk))
            high = jnp.where(wanted, high, jnp.minimum(high, (own[1] + bk - 1) // bk))
        count = lax.fori_loop(low, high, put(qi), count)
    count_ref[0] = (count + 1) // 2
    for spare in range(2):
        plan_q[count + spare] = 0
        plan_k[count + spare] = total // bk - 1


def pipelined(plan_q, plan_k, count_ref, early, late, buffers):
    early(plan_q[0], plan_k[0], buffers[0])

    @pl.loop(0, count_ref[0])
    def _(i):
        for turn in range(2):
            now = 2 * i + turn
            late(plan_q[now], plan_k[now], buffers[turn])
            early(plan_q[now + 1], plan_k[now + 1], buffers[1 - turn])


def forward_kernel(peers, heads, rows, bq, bk, me_s, *refs):
    blocks = refs[:peers]
    q_ref, k_ref, v_ref, qt_ref, kt_ref, first_ref, out_ref, log_ref = refs[peers:peers + 8]
    plan_q, plan_k, count_ref, own_q, own_k, own_count = refs[peers + 8:peers + 14]
    vt_ref, doc_ref, sum_ref, s0, top0, s1, top1 = refs[peers + 14:]
    total = q_ref.shape[0]
    factor = HD ** (-0.5) * math.log2(math.e)
    me = me_s[0]
    for d, block in enumerate(blocks):
        place = me ^ d
        for part, ref in enumerate((q_ref, k_ref, v_ref)):
            ref[aligned(place, rows), :] = block[part * rows:(part + 1) * rows, :]
        docs = block[3 * rows:, :].astype(jnp.float32)
        for t in range(rows // HD):
            doc_ref[:, aligned(place * (rows // HD) + t, HD)] = docs[t:t + 1, :]
    docs = doc_ref[...]
    first = jnp.zeros(docs.shape, jnp.float32)
    for value in range(1, DOC_VALUES):
        before = jnp.sum((docs < value).astype(jnp.float32))
        first = jnp.where(docs >= value, before, first)
    first = first.astype(jnp.int32)
    first_ref[...] = first
    lows = [jnp.min(first[:, qi * bq:(qi + 1) * bq]) // bk for qi in range(total // bq)]
    fill_plan(lows, total, bq, bk, None, own_q, own_k, own_count)
    group = (me // heads) * heads * rows
    own = None if heads == peers else (group, group + heads * rows)
    fill_plan(lows, total, bq, bk, own, plan_q, plan_k, count_ref)
    qt_ref[...] = q_ref[...].T
    kt_ref[...] = k_ref[...].T
    vt_ref[...] = v_ref[...].T
    out_ref[...] = jnp.zeros_like(out_ref)
    log_ref[...] = jnp.full_like(log_ref, NEG_LARGE)
    sum_ref[...] = jnp.zeros_like(sum_ref)

    def early(qi, ki, buffer):
        s_ref, top_ref = buffer
        keys, queries = aligned(ki, bk), aligned(qi, bq)
        s = dot32(k_ref[keys, :], qt_ref[:, queries]) * factor
        s = jnp.where(visible(first_ref[:, queries], qi * bq, ki * bk, (bk, bq)), s, NEG_LARGE)
        s_ref[...] = s
        top_ref[...] = jnp.max(s, axis=0, keepdims=True)

    def late(qi, ki, buffer):
        s_ref, top_ref = buffer
        keys, queries = aligned(ki, bk), aligned(qi, bq)
        top = log_ref[:, queries]
        new_top = jnp.maximum(top, top_ref[...])
        p = jnp.exp2(s_ref[...] - new_top)
        fix = jnp.exp2(top - new_top)
        high = p.astype(jnp.bfloat16)
        rest = (p - high.astype(jnp.float32)).astype(jnp.bfloat16)
        vt = vt_ref[:, keys]
        out_ref[:, queries] = out_ref[:, queries] * fix + (dot32(vt, high) + dot32(vt, rest))
        sum_ref[:, queries] = sum_ref[:, queries] * fix + jnp.sum(p, axis=0, keepdims=True)
        log_ref[:, queries] = new_top

    pipelined(own_q, own_k, own_count, early, late, ((s0, top0), (s1, top1)))
    total_p = sum_ref[...]
    out_ref[...] = out_ref[...] / total_p
    log_ref[...] = log_ref[...] + jnp.log2(total_p)


def backward_kernel(peers, heads, rows, bq, bk, me_s, plan_q, plan_k, count_ref, q_ref, k_ref, v_ref,
                    qt_ref, kt_ref, first_ref, out_ref, log_ref, *refs):
    blocks = refs[:peers]
    results = refs[peers:peers + heads]
    g_ref, gt_ref, dot_ref, dk_acc, dv_acc, dq_acc, p0, ds0, p1, ds1 = refs[peers + heads:]
    scale = HD ** (-0.5)
    factor = scale * math.log2(math.e)
    me = me_s[0]
    for d, block in enumerate(blocks):
        g_ref[aligned(me ^ d, rows), :] = block[...]
    gt_ref[...] = g_ref[...].T
    dot_ref[...] = jnp.sum(gt_ref[...].astype(jnp.float32) * out_ref[...], axis=0, keepdims=True)
    dk_acc[...] = jnp.zeros_like(dk_acc)
    dv_acc[...] = jnp.zeros_like(dv_acc)
    dq_acc[...] = jnp.zeros_like(dq_acc)

    def early(qi, ki, buffer):
        p_ref, ds_ref = buffer
        keys, queries = aligned(ki, bk), aligned(qi, bq)
        p = jnp.exp2(dot32(k_ref[keys, :], qt_ref[:, queries]) * factor - log_ref[:, queries])
        p = jnp.where(visible(first_ref[:, queries], qi * bq, ki * bk, (bk, bq)), p, 0.0)
        p_ref[...] = p.astype(jnp.bfloat16)
        dp = dot32(v_ref[keys, :], gt_ref[:, queries])
        ds_ref[...] = (p * (dp - dot_ref[:, queries])).astype(jnp.bfloat16)

    def late(qi, ki, buffer):
        p_ref, ds_ref = buffer
        keys, queries = aligned(ki, bk), aligned(qi, bq)
        dv_acc[keys, :] += dot32(p_ref[...], g_ref[queries, :])
        dk_acc[keys, :] += dot32(ds_ref[...], q_ref[queries, :])
        dq_acc[:, queries] += dot32(kt_ref[:, keys], ds_ref[...])

    pipelined(plan_q, plan_k, count_ref, early, late, ((p0, ds0), (p1, ds1)))
    for d, result in enumerate(results):
        own = aligned(me ^ d, rows)
        result[:rows, :] = (scale * dq_acc[:, own]).astype(result.dtype).T
        result[rows:2 * rows, :] = (scale * dk_acc[own, :]).astype(result.dtype)
        result[2 * rows:, :] = dv_acc[own, :].astype(result.dtype)


def attention_cost(total, products):
    return pl.CostEstimate(
        flops=products * total * total * HD // 2,
        bytes_accessed=16 * total * HD,
        transcendentals=total * total // 4,
    )


def attention_forward(me, blocks, rows, heads):
    peers = len(blocks)
    total = peers * rows
    bq, bk = block_size(total, 512), block_size(total, 256)
    size = plan_size(total, bq, bk)
    return pl.pallas_call(
        functools.partial(forward_kernel, peers, heads, rows, bq, bk),
        in_specs=[SMEM_SPEC] + [VMEM_SPEC] * peers,
        out_specs=[VMEM_SPEC] * 8 + [SMEM_SPEC] * 3,
        out_shape=[jax.ShapeDtypeStruct((total, HD), jnp.bfloat16)] * 3
        + [jax.ShapeDtypeStruct((HD, total), jnp.bfloat16)] * 2
        + [
            jax.ShapeDtypeStruct((1, total), jnp.int32),
            jax.ShapeDtypeStruct((HD, total), jnp.float32),
            jax.ShapeDtypeStruct((1, total), jnp.float32),
            jax.ShapeDtypeStruct((size,), jnp.int32),
            jax.ShapeDtypeStruct((size,), jnp.int32),
            jax.ShapeDtypeStruct((1,), jnp.int32),
        ],
        scratch_shapes=[
            pltpu.SMEM((size,), jnp.int32),
            pltpu.SMEM((size,), jnp.int32),
            pltpu.SMEM((1,), jnp.int32),
            pltpu.VMEM((HD, total), jnp.bfloat16),
            pltpu.VMEM((1, total), jnp.float32),
            pltpu.VMEM((1, total), jnp.float32),
        ]
        + [pltpu.VMEM((bk, bq), jnp.float32), pltpu.VMEM((1, bq), jnp.float32)] * 2,
        compiler_params=PARAMS,
        cost_estimate=attention_cost(total, 3),
    )(me, *blocks)


def attention_backward(me, heads, state, blocks):
    peers, rows = len(blocks), blocks[0].shape[0]
    total = peers * rows
    bq, bk = block_size(total, 512), block_size(total, 256)
    return pl.pallas_call(
        functools.partial(backward_kernel, peers, heads, rows, bq, bk),
        in_specs=[SMEM_SPEC] * 4 + [VMEM_SPEC] * (8 + peers),
        out_specs=[VMEM_SPEC] * heads,
        out_shape=[jax.ShapeDtypeStruct((3 * rows, HD), jnp.bfloat16)] * heads,
        scratch_shapes=[
            pltpu.VMEM((total, HD), jnp.bfloat16),
            pltpu.VMEM((HD, total), jnp.bfloat16),
            pltpu.VMEM((1, total), jnp.float32),
            pltpu.VMEM((total, HD), jnp.float32),
            pltpu.VMEM((total, HD), jnp.float32),
            pltpu.VMEM((HD, total), jnp.float32),
        ]
        + [pltpu.VMEM((bk, bq), jnp.bfloat16)] * 4,
        compiler_params=PARAMS,
        cost_estimate=attention_cost(total, 5),
    )(me, *state[8:], *state[:8], *blocks)


def per_device(peers, groups, queries, keys_in, values, out_grad, out_weight, doc_ids):
    rows, width = queries.shape
    heads = width // HD
    me = lax.axis_index("seq")
    me_vector = me.reshape(1)

    def exchange(x, d):
        return x if d == 0 else lax.ppermute(x, "seq", [(i, i ^ d) for i in range(peers)])

    def pass_on(x):
        return lax.ppermute(x, "head", [(i, (i + 1) % groups) for i in range(groups)])

    order = [*range(peers - 2, 0, -2), *range(peers - 1, 0, -2)]

    def exchange_all(blocks, wanted):
        moved = {d: exchange(blocks[d % heads], d) for d in order if d < wanted}
        return [blocks[0]] + [moved[d] for d in range(1, wanted)]

    packed = list(pack_heads(me_vector, queries, keys_in, values, doc_ids))
    received = exchange_all(packed, peers)

    after = lax.optimization_barrier
    features, acc = out_grad, None
    weights = []
    for step in range(groups):
        block = lax.rem(lax.axis_index("head") + groups - step, groups)
        weights.append(lax.dynamic_slice_in_dim(out_weight, block * width, width, 1).T)
    for step in range(groups):
        last = step == groups - 1
        if not last:
            passed = pass_on(features)
        if step == groups - 2:
            received[0], features = after((received[0], features))
            state = list(attention_forward(me_vector, received, rows, heads))
            features, state[1] = after((features, state[1]))
        acc = project(me_vector, weights[step], features, acc, last)
        if not last:
            features = passed
            if step < groups - 2:
                batch = order[step * len(order) // (groups - 2):(step + 1) * len(order) // (groups - 2)]
                here = [received[d] for d in batch]
                features, acc, here, weights[2:] = after((features, acc, here, weights[2:]))
                for d, block in zip(batch, here):
                    received[d] = block
    grads = exchange_all(acc, peers)

    results = attention_backward(me_vector, heads, state, grads)
    returned = exchange_all(results, heads)
    return tuple(unpack_heads(me_vector, returned, rows))


def solution(mesh):
    in_specs = (
        P("seq", "head"),
        P("seq", "head"),
        P("seq", "head"),
        P("seq", "head"),
        P("head", None),
        P("seq"),
    )
    out_specs = (P("seq", "head"), P("seq", "head"), P("seq", "head"))
    return jax.shard_map(
        functools.partial(per_device, mesh.shape["seq"], mesh.shape["head"]),
        mesh=mesh, in_specs=in_specs, out_specs=out_specs, check_vma=False,
    )
```

```python
import functools
import math

import jax
import jax.numpy as jnp
from jax import lax
from jax.experimental import pallas as pl
from jax.experimental.pallas import tpu as pltpu
from jax.sharding import PartitionSpec as P

HD = 128
DOC_VALUES = 8
DOC_ROWS = 16
NEG_LARGE = -1e30
VMEM_SPARE = 6 * 1024 * 1024

NN = (((1,), (0,)), ((), ()))
NT = (((1,), (1,)), ((), ()))
SMEM_SPEC = pl.BlockSpec(memory_space=pltpu.SMEM)
VMEM_SPEC = pl.BlockSpec(memory_space=pltpu.VMEM)


def dot32(a, b, dims=NN):
    return lax.dot_general(a, b, dims, preferred_element_type=jnp.float32)


def block_size(total, wanted):
    size = min(wanted, total)
    while total % size or size % 128:
        size -= 128
    return size


def aligned(index, size):
    return pl.ds(pl.multiple_of(index * size, size), size)


def params(arrays, scratch=()):
    total = sum(math.prod(a.shape) * jnp.dtype(a.dtype).itemsize for a in (*arrays, *scratch))
    return pltpu.CompilerParams(vmem_limit_bytes=total + VMEM_SPARE)


def pack_kernel(heads, rows, me_s, q_ref, k_ref, v_ref, doc_ref, *outs):
    own = lax.rem(me_s[0], heads)
    docs = doc_ref[...].astype(jnp.float32)
    docs = jnp.concatenate([docs, jnp.zeros((DOC_ROWS - docs.shape[0], HD), jnp.float32)], axis=0)
    docs = docs.astype(jnp.bfloat16)
    for d, out in enumerate(outs):
        columns = aligned(own ^ d, HD)
        for part, ref in enumerate((q_ref, k_ref, v_ref)):
            out[part * rows:(part + 1) * rows, :] = ref[:, columns]
        out[3 * rows:, :] = docs


def pack_heads(me, q, k, v, doc_ids):
    rows, width = q.shape
    heads = width // HD
    out_shape = [jax.ShapeDtypeStruct((3 * rows + DOC_ROWS, HD), q.dtype)] * heads
    return pl.pallas_call(
        functools.partial(pack_kernel, heads, rows),
        in_specs=[SMEM_SPEC] + [VMEM_SPEC] * 4,
        out_specs=[VMEM_SPEC] * heads,
        out_shape=out_shape,
        compiler_params=params([q, k, v, *out_shape]),
    )(me, q, k, v, doc_ids.reshape(rows // HD, HD))


def unpack_kernel(heads, rows, me_s, *refs):
    own = lax.rem(me_s[0], heads)
    for d in range(heads):
        columns = aligned(own ^ d, HD)
        for part in range(3):
            refs[heads + part][:, columns] = refs[d][part * rows:(part + 1) * rows, :]


def unpack_heads(me, blocks, rows):
    heads = len(blocks)
    return pl.pallas_call(
        functools.partial(unpack_kernel, heads, rows),
        in_specs=[SMEM_SPEC] + [VMEM_SPEC] * heads,
        out_specs=[VMEM_SPEC] * 3,
        out_shape=[jax.ShapeDtypeStruct((rows, heads * HD), blocks[0].dtype)] * 3,
        compiler_params=params([*blocks, *blocks]),
    )(me, *blocks)


def project_kernel(first, o_ref, w_ref, *refs):
    out_ref = refs[-1]
    for pair in range(w_ref.shape[0] // (2 * HD)):
        part = slice(pair * 2 * HD, (pair + 1) * 2 * HD)
        both = dot32(o_ref[...], w_ref[part, :], NT)
        out_ref[:, part] = both if first else refs[0][:, part] + both


def project_last_kernel(me_s, o_ref, w_ref, acc_ref, *outs):
    pairs = len(outs) // 2
    odd = lax.rem(me_s[0], 2) == 1
    for j in range(pairs):
        part = aligned(lax.rem(me_s[0] // 2, pairs) ^ j, 2 * HD)
        both = (acc_ref[:, part] + dot32(o_ref[...], w_ref[part, :], NT)).astype(jnp.bfloat16)
        outs[2 * j][...] = jnp.where(odd, both[:, HD:], both[:, :HD])
        outs[2 * j + 1][...] = jnp.where(odd, both[:, :HD], both[:, HD:])


def project(me, weight, features, acc, last):
    rows, width = features.shape
    columns = weight.shape[0]
    heads = columns // HD
    total = jax.ShapeDtypeStruct((rows, columns), jnp.float32)
    cost = pl.CostEstimate(
        flops=2 * rows * width * columns,
        bytes_accessed=2 * width * columns + 8 * rows * columns,
        transcendentals=0,
    )
    if last:
        return pl.pallas_call(
            project_last_kernel,
            in_specs=[SMEM_SPEC] + [VMEM_SPEC] * 3,
            out_specs=[VMEM_SPEC] * heads,
            out_shape=[jax.ShapeDtypeStruct((rows, HD), jnp.bfloat16)] * heads,
            compiler_params=params([features, weight, total, total]),
            cost_estimate=cost,
        )(me, features, weight, acc)
    operands = (features, weight) + (() if acc is None else (acc,))
    return pl.pallas_call(
        functools.partial(project_kernel, acc is None),
        in_specs=[VMEM_SPEC] * len(operands),
        out_specs=VMEM_SPEC,
        out_shape=total,
        compiler_params=params([features, weight, total, total]),
        cost_estimate=cost,
    )(*operands)


def visible(first_row, q0, k0, shape):
    key = lax.broadcasted_iota(jnp.int32, shape, 0)
    last_row = q0 - k0 + lax.broadcasted_iota(jnp.int32, (1, shape[1]), 1)
    return (key >= first_row - k0) & (key <= last_row)


def plan_size(total, bq, bk):
    return sum(((q + 1) * bq + bk - 1) // bk for q in range(total // bq)) + 2


def fill_plan(lows, total, bq, bk, own, plan_q, plan_k, count_ref):
    def put(qi):
        def at(ki, count):
            plan_q[count] = qi
            plan_k[count] = ki
            return count + 1

        return at

    count = 0
    for qi, low in enumerate(lows):
        high = ((qi + 1) * bq + bk - 1) // bk
        if own is not None:
            wanted = ((qi + 1) * bq > own[0]) & (qi * bq < own[1])
            low = jnp.where(wanted, low, jnp.maximum(low, own[0] // bk))
            high = jnp.where(wanted, high, jnp.minimum(high, (own[1] + bk - 1) // bk))
        count = lax.fori_loop(low, high, put(qi), count)
    count_ref[0] = (count + 1) // 2
    for spare in range(2):
        plan_q[count + spare] = 0
        plan_k[count + spare] = total // bk - 1


def pipelined(plan_q, plan_k, count_ref, early, late, buffers):
    early(plan_q[0], plan_k[0], buffers[0])

    @pl.loop(0, count_ref[0])
    def _(i):
        for turn in range(2):
            now = 2 * i + turn
            late(plan_q[now], plan_k[now], buffers[turn])
            early(plan_q[now + 1], plan_k[now + 1], buffers[1 - turn])


def forward_kernel(peers, heads, rows, bq, bk, me_s, *refs):
    blocks = refs[:peers]
    q_ref, k_ref, v_ref, qt_ref, kt_ref, first_ref, out_ref, log_ref = refs[peers:peers + 8]
    plan_q, plan_k, count_ref, own_q, own_k, own_count = refs[peers + 8:peers + 14]
    vt_ref, doc_ref, sum_ref, s0, top0, s1, top1 = refs[peers + 14:]
    total = q_ref.shape[0]
    factor = HD ** (-0.5) * math.log2(math.e)
    me = me_s[0]
    for d, block in enumerate(blocks):
        place = me ^ d
        for part, ref in enumerate((q_ref, k_ref, v_ref)):
            ref[aligned(place, rows), :] = block[part * rows:(part + 1) * rows, :]
        docs = block[3 * rows:, :].astype(jnp.float32)
        for t in range(rows // HD):
            doc_ref[:, aligned(place * (rows // HD) + t, HD)] = docs[t:t + 1, :]
    docs = doc_ref[...]
    first = jnp.zeros(docs.shape, jnp.float32)
    for value in range(1, DOC_VALUES):
        before = jnp.sum((docs < value).astype(jnp.float32))
        first = jnp.where(docs >= value, before, first)
    first = first.astype(jnp.int32)
    first_ref[...] = first
    lows = [jnp.min(first[:, qi * bq:(qi + 1) * bq]) // bk for qi in range(total // bq)]
    fill_plan(lows, total, bq, bk, None, own_q, own_k, own_count)
    group = (me // heads) * heads * rows
    own = None if heads == peers else (group, group + heads * rows)
    fill_plan(lows, total, bq, bk, own, plan_q, plan_k, count_ref)
    qt_ref[...] = q_ref[...].T
    kt_ref[...] = k_ref[...].T
    vt_ref[...] = v_ref[...].T
    out_ref[...] = jnp.zeros_like(out_ref)
    log_ref[...] = jnp.full_like(log_ref, NEG_LARGE)
    sum_ref[...] = jnp.zeros_like(sum_ref)

    def early(qi, ki, buffer):
        s_ref, top_ref = buffer
        keys, queries = aligned(ki, bk), aligned(qi, bq)
        s = dot32(k_ref[keys, :], qt_ref[:, queries]) * factor
        s = jnp.where(visible(first_ref[:, queries], qi * bq, ki * bk, (bk, bq)), s, NEG_LARGE)
        s_ref[...] = s
        top_ref[...] = jnp.max(s, axis=0, keepdims=True)

    def late(qi, ki, buffer):
        s_ref, top_ref = buffer
        keys, queries = aligned(ki, bk), aligned(qi, bq)
        top = log_ref[:, queries]
        new_top = jnp.maximum(top, top_ref[...])
        p = jnp.exp2(s_ref[...] - new_top)
        fix = jnp.exp2(top - new_top)
        high = p.astype(jnp.bfloat16)
        rest = (p - high.astype(jnp.float32)).astype(jnp.bfloat16)
        vt = vt_ref[:, keys]
        out_ref[:, queries] = out_ref[:, queries] * fix + (dot32(vt, high) + dot32(vt, rest))
        sum_ref[:, queries] = sum_ref[:, queries] * fix + jnp.sum(p, axis=0, keepdims=True)
        log_ref[:, queries] = new_top

    pipelined(own_q, own_k, own_count, early, late, ((s0, top0), (s1, top1)))
    total_p = sum_ref[...]
    out_ref[...] = out_ref[...] / total_p
    log_ref[...] = log_ref[...] + jnp.log2(total_p)


def backward_kernel(peers, heads, rows, bq, bk, me_s, plan_q, plan_k, count_ref, q_ref, k_ref, v_ref,
                    qt_ref, kt_ref, first_ref, out_ref, log_ref, *refs):
    blocks = refs[:peers]
    results = refs[peers:peers + heads]
    g_ref, gt_ref, dot_ref, dk_acc, dv_acc, dq_acc, p0, ds0, p1, ds1 = refs[peers + heads:]
    scale = HD ** (-0.5)
    factor = scale * math.log2(math.e)
    me = me_s[0]
    for d, block in enumerate(blocks):
        g_ref[aligned(me ^ d, rows), :] = block[...]
    gt_ref[...] = g_ref[...].T
    dot_ref[...] = jnp.sum(gt_ref[...].astype(jnp.float32) * out_ref[...], axis=0, keepdims=True)
    dk_acc[...] = jnp.zeros_like(dk_acc)
    dv_acc[...] = jnp.zeros_like(dv_acc)
    dq_acc[...] = jnp.zeros_like(dq_acc)

    def early(qi, ki, buffer):
        p_ref, ds_ref = buffer
        keys, queries = aligned(ki, bk), aligned(qi, bq)
        p = jnp.exp2(dot32(k_ref[keys, :], qt_ref[:, queries]) * factor - log_ref[:, queries])
        p = jnp.where(visible(first_ref[:, queries], qi * bq, ki * bk, (bk, bq)), p, 0.0)
        p_ref[...] = p.astype(jnp.bfloat16)
        dp = dot32(v_ref[keys, :], gt_ref[:, queries])
        ds_ref[...] = (p * (dp - dot_ref[:, queries])).astype(jnp.bfloat16)

    def late(qi, ki, buffer):
        p_ref, ds_ref = buffer
        keys, queries = aligned(ki, bk), aligned(qi, bq)
        dv_acc[keys, :] += dot32(p_ref[...], g_ref[queries, :])
        dk_acc[keys, :] += dot32(ds_ref[...], q_ref[queries, :])
        dq_acc[:, queries] += dot32(kt_ref[:, keys], ds_ref[...])

    pipelined(plan_q, plan_k, count_ref, early, late, ((p0, ds0), (p1, ds1)))
    for d, result in enumerate(results):
        own = aligned(me ^ d, rows)
        result[:rows, :] = (scale * dq_acc[:, own]).astype(result.dtype).T
        result[rows:2 * rows, :] = (scale * dk_acc[own, :]).astype(result.dtype)
        result[2 * rows:, :] = dv_acc[own, :].astype(result.dtype)


def attention_cost(total, products):
    return pl.CostEstimate(
        flops=products * total * total * HD // 2,
        bytes_accessed=16 * total * HD,
        transcendentals=total * total // 4,
    )


def attention_forward(me, blocks, rows, heads):
    peers = len(blocks)
    total = peers * rows
    bq, bk = block_size(total, 512), block_size(total, 256)
    size = plan_size(total, bq, bk)
    vectors = [
        *[jax.ShapeDtypeStruct((total, HD), jnp.bfloat16)] * 3,
        *[jax.ShapeDtypeStruct((HD, total), jnp.bfloat16)] * 2,
        jax.ShapeDtypeStruct((1, total), jnp.int32),
        jax.ShapeDtypeStruct((HD, total), jnp.float32),
        jax.ShapeDtypeStruct((1, total), jnp.float32),
    ]
    plan = [(size,), (size,), (1,)]
    scratch = [
        pltpu.VMEM((HD, total), jnp.bfloat16),
        pltpu.VMEM((1, total), jnp.float32),
        pltpu.VMEM((1, total), jnp.float32),
        *[pltpu.VMEM((bk, bq), jnp.float32), pltpu.VMEM((1, bq), jnp.float32)] * 2,
    ]
    return pl.pallas_call(
        functools.partial(forward_kernel, peers, heads, rows, bq, bk),
        in_specs=[SMEM_SPEC] + [VMEM_SPEC] * peers,
        out_specs=[VMEM_SPEC] * len(vectors) + [SMEM_SPEC] * 3,
        out_shape=vectors + [jax.ShapeDtypeStruct(shape, jnp.int32) for shape in plan],
        scratch_shapes=[pltpu.SMEM(shape, jnp.int32) for shape in plan] + scratch,
        compiler_params=params([*blocks, *vectors], scratch),
        cost_estimate=attention_cost(total, 3),
    )(me, *blocks)


def attention_backward(me, heads, state, blocks):
    peers, rows = len(blocks), blocks[0].shape[0]
    total = peers * rows
    bq, bk = block_size(total, 512), block_size(total, 256)
    vectors, plan = state[:8], state[8:]
    out_shape = [jax.ShapeDtypeStruct((3 * rows, HD), jnp.bfloat16)] * heads
    scratch = [
        pltpu.VMEM((total, HD), jnp.bfloat16),
        pltpu.VMEM((HD, total), jnp.bfloat16),
        pltpu.VMEM((1, total), jnp.float32),
        pltpu.VMEM((total, HD), jnp.float32),
        pltpu.VMEM((total, HD), jnp.float32),
        pltpu.VMEM((HD, total), jnp.float32),
        *[pltpu.VMEM((bk, bq), jnp.bfloat16)] * 4,
    ]
    return pl.pallas_call(
        functools.partial(backward_kernel, peers, heads, rows, bq, bk),
        in_specs=[SMEM_SPEC] * 4 + [VMEM_SPEC] * (8 + peers),
        out_specs=[VMEM_SPEC] * heads,
        out_shape=out_shape,
        scratch_shapes=scratch,
        compiler_params=params([*vectors, *blocks, *out_shape], scratch),
        cost_estimate=attention_cost(total, 5),
    )(me, *plan, *vectors, *blocks)


def per_device(peers, groups, queries, keys_in, values, out_grad, out_weight, doc_ids):
    rows, width = queries.shape
    heads = width // HD
    me = lax.axis_index("seq")
    me_vector = me.reshape(1)

    def exchange(x, d):
        return x if d == 0 else lax.ppermute(x, "seq", [(i, i ^ d) for i in range(peers)])

    def pass_on(x):
        return lax.ppermute(x, "head", [(i, (i + 1) % groups) for i in range(groups)])

    order = [*range(peers - 2, 0, -2), *range(peers - 1, 0, -2)]

    def exchange_all(blocks, wanted):
        moved = {d: exchange(blocks[d % heads], d) for d in order if d < wanted}
        return [blocks[0]] + [moved[d] for d in range(1, wanted)]

    packed = list(pack_heads(me_vector, queries, keys_in, values, doc_ids))
    received = exchange_all(packed, peers)

    after = lax.optimization_barrier
    features, acc = out_grad, None
    weights = []
    for step in range(groups):
        block = lax.rem(lax.axis_index("head") + groups - step, groups)
        weights.append(lax.dynamic_slice_in_dim(out_weight, block * width, width, 1))
    for step in range(groups):
        last = step == groups - 1
        if not last:
            passed = pass_on(features)
        if step == groups - 2:
            received[0], features = after((received[0], features))
            state = list(attention_forward(me_vector, received, rows, heads))
            features, state[1] = after((features, state[1]))
        acc = project(me_vector, weights[step], features, acc, last)
        if not last:
            features = passed
            if step < groups - 2:
                batch = order[step * len(order) // (groups - 2):(step + 1) * len(order) // (groups - 2)]
                here = [received[d] for d in batch]
                features, acc, here, weights[2:] = after((features, acc, here, weights[2:]))
                for d, block in zip(batch, here):
                    received[d] = block
    grads = exchange_all(acc, peers)

    results = attention_backward(me_vector, heads, state, grads)
    returned = exchange_all(results, heads)
    return tuple(unpack_heads(me_vector, returned, rows))


def solution(mesh):
    in_specs = (
        P("seq", "head"),
        P("seq", "head"),
        P("seq", "head"),
        P("seq", "head"),
        P("head", None),
        P("seq"),
    )
    out_specs = (P("seq", "head"), P("seq", "head"), P("seq", "head"))
    return jax.shard_map(
        functools.partial(per_device, mesh.shape["seq"], mesh.shape["head"]),
        mesh=mesh, in_specs=in_specs, out_specs=out_specs, check_vma=False,
    )
```

```python
import functools
import math

import jax
import jax.numpy as jnp
from jax import lax
from jax.experimental import pallas as pl
from jax.experimental.pallas import tpu as pltpu
from jax.sharding import PartitionSpec as P

HD = 128
DOC_VALUES = 8
DOC_ROWS = 16
ONES_ROWS = 16
NEG_LARGE = -1e30
VMEM_SPARE = 6 * 1024 * 1024

NN = (((1,), (0,)), ((), ()))
NT = (((1,), (1,)), ((), ()))
SMEM_SPEC = pl.BlockSpec(memory_space=pltpu.SMEM)
VMEM_SPEC = pl.BlockSpec(memory_space=pltpu.VMEM)


def dot32(a, b, dims=NN):
    return lax.dot_general(a, b, dims, preferred_element_type=jnp.float32)


def block_size(total, wanted):
    size = min(wanted, total)
    while total % size or size % 128:
        size -= 128
    return size


def aligned(index, size):
    return pl.ds(pl.multiple_of(index * size, size), size)


def params(arrays, scratch=()):
    total = sum(math.prod(a.shape) * jnp.dtype(a.dtype).itemsize for a in (*arrays, *scratch))
    return pltpu.CompilerParams(vmem_limit_bytes=total + VMEM_SPARE)


def pack_kernel(heads, rows, me_s, q_ref, k_ref, v_ref, doc_ref, *outs):
    own = lax.rem(me_s[0], heads)
    docs = doc_ref[...].astype(jnp.float32)
    docs = jnp.concatenate([docs, jnp.zeros((DOC_ROWS - docs.shape[0], HD), jnp.float32)], axis=0)
    docs = docs.astype(jnp.bfloat16)
    for d, out in enumerate(outs):
        columns = aligned(own ^ d, HD)
        for part, ref in enumerate((q_ref, k_ref, v_ref)):
            out[part * rows:(part + 1) * rows, :] = ref[:, columns]
        out[3 * rows:, :] = docs


def pack_heads(me, q, k, v, doc_ids):
    rows, width = q.shape
    heads = width // HD
    out_shape = [jax.ShapeDtypeStruct((3 * rows + DOC_ROWS, HD), q.dtype)] * heads
    return pl.pallas_call(
        functools.partial(pack_kernel, heads, rows),
        in_specs=[SMEM_SPEC] + [VMEM_SPEC] * 4,
        out_specs=[VMEM_SPEC] * heads,
        out_shape=out_shape,
        compiler_params=params([q, k, v, *out_shape]),
    )(me, q, k, v, doc_ids.reshape(rows // HD, HD))


def unpack_kernel(heads, rows, me_s, *refs):
    own = lax.rem(me_s[0], heads)
    for d in range(heads):
        columns = aligned(own ^ d, HD)
        for part in range(3):
            refs[heads + part][:, columns] = refs[d][part * rows:(part + 1) * rows, :]


def unpack_heads(me, blocks, rows):
    heads = len(blocks)
    return pl.pallas_call(
        functools.partial(unpack_kernel, heads, rows),
        in_specs=[SMEM_SPEC] + [VMEM_SPEC] * heads,
        out_specs=[VMEM_SPEC] * 3,
        out_shape=[jax.ShapeDtypeStruct((rows, heads * HD), blocks[0].dtype)] * 3,
        compiler_params=params([*blocks, *blocks]),
    )(me, *blocks)


def project_kernel(first, o_ref, w_ref, *refs):
    out_ref = refs[-1]
    for pair in range(w_ref.shape[0] // (2 * HD)):
        part = slice(pair * 2 * HD, (pair + 1) * 2 * HD)
        both = dot32(o_ref[...], w_ref[part, :], NT)
        out_ref[:, part] = both if first else refs[0][:, part] + both


def project_last_kernel(me_s, o_ref, w_ref, acc_ref, *outs):
    pairs = len(outs) // 2
    odd = lax.rem(me_s[0], 2) == 1
    for j in range(pairs):
        part = aligned(lax.rem(me_s[0] // 2, pairs) ^ j, 2 * HD)
        both = (acc_ref[:, part] + dot32(o_ref[...], w_ref[part, :], NT)).astype(jnp.bfloat16)
        outs[2 * j][...] = jnp.where(odd, both[:, HD:], both[:, :HD])
        outs[2 * j + 1][...] = jnp.where(odd, both[:, :HD], both[:, HD:])


def project(me, weight, features, acc, last):
    rows, width = features.shape
    columns = weight.shape[0]
    heads = columns // HD
    total = jax.ShapeDtypeStruct((rows, columns), jnp.float32)
    cost = pl.CostEstimate(
        flops=2 * rows * width * columns,
        bytes_accessed=2 * width * columns + 8 * rows * columns,
        transcendentals=0,
    )
    if last:
        return pl.pallas_call(
            project_last_kernel,
            in_specs=[SMEM_SPEC] + [VMEM_SPEC] * 3,
            out_specs=[VMEM_SPEC] * heads,
            out_shape=[jax.ShapeDtypeStruct((rows, HD), jnp.bfloat16)] * heads,
            compiler_params=params([features, weight, total, total]),
            cost_estimate=cost,
        )(me, features, weight, acc)
    operands = (features, weight) + (() if acc is None else (acc,))
    return pl.pallas_call(
        functools.partial(project_kernel, acc is None),
        in_specs=[VMEM_SPEC] * len(operands),
        out_specs=VMEM_SPEC,
        out_shape=total,
        compiler_params=params([features, weight, total, total]),
        cost_estimate=cost,
    )(*operands)


def visible(first_row, q0, k0, shape):
    key = lax.broadcasted_iota(jnp.int32, shape, 0)
    last_row = q0 - k0 + lax.broadcasted_iota(jnp.int32, (1, shape[1]), 1)
    return (key >= first_row - k0) & (key <= last_row)


def block_sizes(total):
    return (
        (block_size(total, 256), block_size(total, 256)),
        (block_size(total, 256), block_size(total, 512)),
    )


def plan_size(total, bq, bk):
    return sum(((q + 1) * bq + bk - 1) // bk for q in range(total // bq)) + 2


def fill_plan(lows, total, bq, bk, own, plan_q, plan_k, count_ref):
    def put(qi):
        def at(ki, count):
            plan_q[count] = qi
            plan_k[count] = ki
            return count + 1

        return at

    count = 0
    for qi, low in enumerate(lows):
        low, high = low // bk, ((qi + 1) * bq + bk - 1) // bk
        if own is not None:
            wanted = ((qi + 1) * bq > own[0]) & (qi * bq < own[1])
            low = jnp.where(wanted, low, jnp.maximum(low, own[0] // bk))
            high = jnp.where(wanted, high, jnp.minimum(high, (own[1] + bk - 1) // bk))
        count = lax.fori_loop(low, high, put(qi), count)
    count_ref[0] = (count + 1) // 2
    for spare in range(2):
        plan_q[count + spare] = 0
        plan_k[count + spare] = total // bk - 1


def pipelined(plan_q, plan_k, count_ref, early, late, buffers):
    early(plan_q[0], plan_k[0], buffers[0])

    @pl.loop(0, count_ref[0])
    def _(i):
        for turn in range(2):
            now = 2 * i + turn
            late(plan_q[now], plan_k[now], buffers[turn])
            early(plan_q[now + 1], plan_k[now + 1], buffers[1 - turn])


def forward_kernel(peers, heads, rows, bq, bk, me_s, *refs):
    blocks = refs[:peers]
    q_ref, k_ref, v_ref, qt_ref, kt_ref, first_ref, out_ref, log_ref = refs[peers:peers + 8]
    plan_q, plan_k, count_ref, own_q, own_k, own_count = refs[peers + 8:peers + 14]
    vt_ref, doc_ref, sum_ref, s0, top0, s1, top1 = refs[peers + 14:]
    total = q_ref.shape[0]
    factor = HD ** (-0.5) * math.log2(math.e)
    me = me_s[0]
    for d, block in enumerate(blocks):
        place = me ^ d
        for part, ref in enumerate((q_ref, k_ref, v_ref)):
            ref[aligned(place, rows), :] = block[part * rows:(part + 1) * rows, :]
        docs = block[3 * rows:, :].astype(jnp.float32)
        for t in range(rows // HD):
            doc_ref[:, aligned(place * (rows // HD) + t, HD)] = docs[t:t + 1, :]
    docs = doc_ref[...]
    first = jnp.zeros(docs.shape, jnp.float32)
    for value in range(1, DOC_VALUES):
        before = jnp.sum((docs < value).astype(jnp.float32))
        first = jnp.where(docs >= value, before, first)
    first = first.astype(jnp.int32)
    first_ref[...] = first
    lows = [jnp.min(first[:, qi * bq:(qi + 1) * bq]) for qi in range(total // bq)]
    fill_plan(lows, total, bq, bk, None, own_q, own_k, own_count)
    group = (me // heads) * heads * rows
    own = None if heads == peers else (group, group + heads * rows)
    back_q, back_k = block_sizes(total)[1]
    lows = [jnp.min(first[:, qi * back_q:(qi + 1) * back_q]) for qi in range(total // back_q)]
    fill_plan(lows, total, back_q, back_k, own, plan_q, plan_k, count_ref)
    qt_ref[...] = q_ref[...].T
    kt_ref[...] = k_ref[...].T
    vt_ref[:HD, :] = v_ref[...].T
    vt_ref[HD:, :] = jnp.ones((ONES_ROWS, total), jnp.bfloat16)
    out_ref[...] = jnp.zeros_like(out_ref)
    log_ref[...] = jnp.full_like(log_ref, NEG_LARGE)
    sum_ref[...] = jnp.zeros_like(sum_ref)

    def early(qi, ki, buffer):
        s_ref, top_ref = buffer
        keys, queries = aligned(ki, bk), aligned(qi, bq)
        s = dot32(k_ref[keys, :], qt_ref[:, queries]) * factor
        s = jnp.where(visible(first_ref[:, queries], qi * bq, ki * bk, (bk, bq)), s, NEG_LARGE)
        s_ref[...] = s
        top_ref[...] = jnp.max(s, axis=0, keepdims=True)

    def late(qi, ki, buffer):
        s_ref, top_ref = buffer
        keys, queries = aligned(ki, bk), aligned(qi, bq)
        top = log_ref[:, queries]
        new_top = jnp.maximum(top, top_ref[...])
        p = jnp.exp2(s_ref[...] - new_top)
        fix = jnp.exp2(top - new_top)
        high = p.astype(jnp.bfloat16)
        rest = (p - high.astype(jnp.float32)).astype(jnp.bfloat16)
        vt = vt_ref[:, keys]
        sums = dot32(vt, high) + dot32(vt, rest)
        out_ref[:, queries] = out_ref[:, queries] * fix + sums[:HD, :]
        sum_ref[:, queries] = sum_ref[:, queries] * fix + sums[HD:HD + 1, :]
        log_ref[:, queries] = new_top

    pipelined(own_q, own_k, own_count, early, late, ((s0, top0), (s1, top1)))
    total_p = sum_ref[...]
    out_ref[...] = out_ref[...] / total_p
    log_ref[...] = log_ref[...] + jnp.log2(total_p)


def backward_kernel(peers, heads, rows, bq, bk, me_s, plan_q, plan_k, count_ref, q_ref, k_ref, v_ref,
                    qt_ref, kt_ref, first_ref, out_ref, log_ref, *refs):
    blocks = refs[:peers]
    results = refs[peers:peers + heads]
    g_ref, gt_ref, dot_ref, dk_acc, dv_acc, dq_acc, p0, ds0, p1, ds1 = refs[peers + heads:]
    scale = HD ** (-0.5)
    factor = scale * math.log2(math.e)
    me = me_s[0]
    for d, block in enumerate(blocks):
        g_ref[aligned(me ^ d, rows), :] = block[...]
    gt_ref[...] = g_ref[...].T
    dot_ref[...] = jnp.sum(gt_ref[...].astype(jnp.float32) * out_ref[...], axis=0, keepdims=True)
    dk_acc[...] = jnp.zeros_like(dk_acc)
    dv_acc[...] = jnp.zeros_like(dv_acc)
    dq_acc[...] = jnp.zeros_like(dq_acc)

    def early(qi, ki, buffer):
        p_ref, ds_ref = buffer
        keys, queries = aligned(ki, bk), aligned(qi, bq)
        p = jnp.exp2(dot32(k_ref[keys, :], qt_ref[:, queries]) * factor - log_ref[:, queries])
        p = jnp.where(visible(first_ref[:, queries], qi * bq, ki * bk, (bk, bq)), p, 0.0)
        p_ref[...] = p.astype(jnp.bfloat16)
        dp = dot32(v_ref[keys, :], gt_ref[:, queries])
        ds_ref[...] = (p * (dp - dot_ref[:, queries])).astype(jnp.bfloat16)

    def late(qi, ki, buffer):
        p_ref, ds_ref = buffer
        keys, queries = aligned(ki, bk), aligned(qi, bq)
        dv_acc[keys, :] += dot32(p_ref[...], g_ref[queries, :])
        dk_acc[keys, :] += dot32(ds_ref[...], q_ref[queries, :])
        dq_acc[:, queries] += dot32(kt_ref[:, keys], ds_ref[...])

    pipelined(plan_q, plan_k, count_ref, early, late, ((p0, ds0), (p1, ds1)))
    for d, result in enumerate(results):
        own = aligned(me ^ d, rows)
        result[:rows, :] = (scale * dq_acc[:, own]).astype(result.dtype).T
        result[rows:2 * rows, :] = (scale * dk_acc[own, :]).astype(result.dtype)
        result[2 * rows:, :] = dv_acc[own, :].astype(result.dtype)


def attention_cost(total, products):
    return pl.CostEstimate(
        flops=products * total * total * HD // 2,
        bytes_accessed=16 * total * HD,
        transcendentals=total * total // 4,
    )


def attention_forward(me, blocks, rows, heads):
    peers = len(blocks)
    total = peers * rows
    (bq, bk), back = block_sizes(total)
    plan = [(plan_size(total, *back),)] * 2 + [(1,)]
    own_plan = [(plan_size(total, bq, bk),)] * 2 + [(1,)]
    vectors = [
        *[jax.ShapeDtypeStruct((total, HD), jnp.bfloat16)] * 3,
        *[jax.ShapeDtypeStruct((HD, total), jnp.bfloat16)] * 2,
        jax.ShapeDtypeStruct((1, total), jnp.int32),
        jax.ShapeDtypeStruct((HD, total), jnp.float32),
        jax.ShapeDtypeStruct((1, total), jnp.float32),
    ]
    scratch = [
        pltpu.VMEM((HD + ONES_ROWS, total), jnp.bfloat16),
        pltpu.VMEM((1, total), jnp.float32),
        pltpu.VMEM((1, total), jnp.float32),
        *[pltpu.VMEM((bk, bq), jnp.float32), pltpu.VMEM((1, bq), jnp.float32)] * 2,
    ]
    return pl.pallas_call(
        functools.partial(forward_kernel, peers, heads, rows, bq, bk),
        in_specs=[SMEM_SPEC] + [VMEM_SPEC] * peers,
        out_specs=[VMEM_SPEC] * len(vectors) + [SMEM_SPEC] * 3,
        out_shape=vectors + [jax.ShapeDtypeStruct(shape, jnp.int32) for shape in plan],
        scratch_shapes=[pltpu.SMEM(shape, jnp.int32) for shape in own_plan] + scratch,
        compiler_params=params([*blocks, *vectors], scratch),
        cost_estimate=attention_cost(total, 3),
    )(me, *blocks)


def attention_backward(me, heads, state, blocks):
    peers, rows = len(blocks), blocks[0].shape[0]
    total = peers * rows
    bq, bk = block_sizes(total)[1]
    vectors, plan = state[:8], state[8:]
    out_shape = [jax.ShapeDtypeStruct((3 * rows, HD), jnp.bfloat16)] * heads
    scratch = [
        pltpu.VMEM((total, HD), jnp.bfloat16),
        pltpu.VMEM((HD, total), jnp.bfloat16),
        pltpu.VMEM((1, total), jnp.float32),
        pltpu.VMEM((total, HD), jnp.float32),
        pltpu.VMEM((total, HD), jnp.float32),
        pltpu.VMEM((HD, total), jnp.float32),
        *[pltpu.VMEM((bk, bq), jnp.bfloat16)] * 4,
    ]
    return pl.pallas_call(
        functools.partial(backward_kernel, peers, heads, rows, bq, bk),
        in_specs=[SMEM_SPEC] * 4 + [VMEM_SPEC] * (8 + peers),
        out_specs=[VMEM_SPEC] * heads,
        out_shape=out_shape,
        scratch_shapes=scratch,
        compiler_params=params([*vectors, *blocks, *out_shape], scratch),
        cost_estimate=attention_cost(total, 5),
    )(me, *plan, *vectors, *blocks)


def per_device(peers, groups, queries, keys_in, values, out_grad, out_weight, doc_ids):
    rows, width = queries.shape
    heads = width // HD
    me = lax.axis_index("seq")
    me_vector = me.reshape(1)

    def exchange(x, d):
        return x if d == 0 else lax.ppermute(x, "seq", [(i, i ^ d) for i in range(peers)])

    def pass_on(x):
        return lax.ppermute(x, "head", [(i, (i + 1) % groups) for i in range(groups)])

    order = [*range(peers - 2, 0, -2), *range(peers - 1, 0, -2)]

    def exchange_all(blocks, wanted):
        moved = {d: exchange(blocks[d % heads], d) for d in order if d < wanted}
        return [blocks[0]] + [moved[d] for d in range(1, wanted)]

    packed = list(pack_heads(me_vector, queries, keys_in, values, doc_ids))
    received = exchange_all(packed, peers)

    after = lax.optimization_barrier
    features, acc = out_grad, None
    weights = []
    for step in range(groups):
        block = lax.rem(lax.axis_index("head") + groups - step, groups)
        weights.append(lax.dynamic_slice_in_dim(out_weight, block * width, width, 1))
    for step in range(groups):
        last = step == groups - 1
        if not last:
            passed = pass_on(features)
        if step == groups - 2:
            received[0], features = after((received[0], features))
            state = list(attention_forward(me_vector, received, rows, heads))
            features, state[1] = after((features, state[1]))
        acc = project(me_vector, weights[step], features, acc, last)
        if not last:
            features = passed
            if step < groups - 2:
                batch = order[step * len(order) // (groups - 2):(step + 1) * len(order) // (groups - 2)]
                here = [received[d] for d in batch]
                features, acc, here, weights[2:] = after((features, acc, here, weights[2:]))
                for d, block in zip(batch, here):
                    received[d] = block
    grads = exchange_all(acc, peers)

    results = attention_backward(me_vector, heads, state, grads)
    returned = exchange_all(results, heads)
    return tuple(unpack_heads(me_vector, returned, rows))


def solution(mesh):
    in_specs = (
        P("seq", "head"),
        P("seq", "head"),
        P("seq", "head"),
        P("seq", "head"),
        P("head", None),
        P("seq"),
    )
    out_specs = (P("seq", "head"), P("seq", "head"), P("seq", "head"))
    return jax.shard_map(
        functools.partial(per_device, mesh.shape["seq"], mesh.shape["head"]),
        mesh=mesh, in_specs=in_specs, out_specs=out_specs, check_vma=False,
    )
```

```python
import functools
import math

import jax
import jax.numpy as jnp
from jax import lax
from jax.experimental import pallas as pl
from jax.experimental.pallas import tpu as pltpu
from jax.sharding import PartitionSpec as P

HD = 128
DOC_VALUES = 8
DOC_ROWS = 16
ONES_ROWS = 16
NEG_LARGE = -1e30
VMEM_SPARE = 6 * 1024 * 1024

NN = (((1,), (0,)), ((), ()))
NT = (((1,), (1,)), ((), ()))
SMEM_SPEC = pl.BlockSpec(memory_space=pltpu.SMEM)
VMEM_SPEC = pl.BlockSpec(memory_space=pltpu.VMEM)


def dot32(a, b, dims=NN):
    return lax.dot_general(a, b, dims, preferred_element_type=jnp.float32)


def block_size(total, wanted):
    size = min(wanted, total)
    while total % size or size % 128:
        size -= 128
    return size


def aligned(index, size):
    return pl.ds(pl.multiple_of(index * size, size), size)


def params(arrays, scratch=()):
    total = sum(math.prod(a.shape) * jnp.dtype(a.dtype).itemsize for a in (*arrays, *scratch))
    return pltpu.CompilerParams(vmem_limit_bytes=total + VMEM_SPARE)


def pack_kernel(heads, rows, me_s, q_ref, k_ref, v_ref, doc_ref, *refs):
    outs, done = refs[:heads], refs[heads]
    own = lax.rem(me_s[0], heads)
    copies = []
    for d, out in enumerate(outs):
        columns = aligned(own ^ d, HD)
        for part, ref in enumerate((q_ref, k_ref, v_ref)):
            place = out.at[pl.ds(part * rows, rows), :]
            copies.append(pltpu.make_async_copy(ref.at[:, columns], place, done.at[d, part]))
            copies[-1].start()
    docs = doc_ref[...].astype(jnp.float32)
    docs = jnp.concatenate([docs, jnp.zeros((DOC_ROWS - docs.shape[0], HD), jnp.float32)], axis=0)
    docs = docs.astype(jnp.bfloat16)
    for out in outs:
        out[3 * rows:, :] = docs
    for copy in copies:
        copy.wait()


def pack_heads(me, q, k, v, doc_ids):
    rows, width = q.shape
    heads = width // HD
    out_shape = [jax.ShapeDtypeStruct((3 * rows + DOC_ROWS, HD), q.dtype)] * heads
    return pl.pallas_call(
        functools.partial(pack_kernel, heads, rows),
        in_specs=[SMEM_SPEC] + [pl.BlockSpec(memory_space=pltpu.HBM)] * 3 + [VMEM_SPEC],
        out_specs=[VMEM_SPEC] * heads,
        out_shape=out_shape,
        scratch_shapes=[pltpu.SemaphoreType.DMA((heads, 3))],
        compiler_params=params(out_shape),
    )(me, q, k, v, doc_ids.reshape(rows // HD, HD))


def unpack_kernel(heads, rows, me_s, *refs):
    own = lax.rem(me_s[0], heads)
    for d in range(heads):
        columns = aligned(own ^ d, HD)
        for part in range(3):
            refs[heads + part][:, columns] = refs[d][part * rows:(part + 1) * rows, :]


def unpack_heads(me, blocks, rows):
    heads = len(blocks)
    return pl.pallas_call(
        functools.partial(unpack_kernel, heads, rows),
        in_specs=[SMEM_SPEC] + [VMEM_SPEC] * heads,
        out_specs=[VMEM_SPEC] * 3,
        out_shape=[jax.ShapeDtypeStruct((rows, heads * HD), blocks[0].dtype)] * 3,
        compiler_params=params([*blocks, *blocks]),
    )(me, *blocks)


def project_kernel(first, o_ref, w_ref, *refs):
    out_ref = refs[-1]
    for pair in range(w_ref.shape[0] // (2 * HD)):
        part = slice(pair * 2 * HD, (pair + 1) * 2 * HD)
        both = dot32(o_ref[...], w_ref[part, :], NT)
        out_ref[:, part] = both if first else refs[0][:, part] + both


def project_last_kernel(me_s, o_ref, w_ref, acc_ref, *outs):
    pairs = len(outs) // 2
    odd = lax.rem(me_s[0], 2) == 1
    for j in range(pairs):
        part = aligned(lax.rem(me_s[0] // 2, pairs) ^ j, 2 * HD)
        both = (acc_ref[:, part] + dot32(o_ref[...], w_ref[part, :], NT)).astype(jnp.bfloat16)
        outs[2 * j][...] = jnp.where(odd, both[:, HD:], both[:, :HD])
        outs[2 * j + 1][...] = jnp.where(odd, both[:, :HD], both[:, HD:])


def project(me, weight, features, acc, last):
    rows, width = features.shape
    columns = weight.shape[0]
    heads = columns // HD
    total = jax.ShapeDtypeStruct((rows, columns), jnp.float32)
    cost = pl.CostEstimate(
        flops=2 * rows * width * columns,
        bytes_accessed=2 * width * columns + 8 * rows * columns,
        transcendentals=0,
    )
    if last:
        return pl.pallas_call(
            project_last_kernel,
            in_specs=[SMEM_SPEC] + [VMEM_SPEC] * 3,
            out_specs=[VMEM_SPEC] * heads,
            out_shape=[jax.ShapeDtypeStruct((rows, HD), jnp.bfloat16)] * heads,
            compiler_params=params([features, weight, total, total]),
            cost_estimate=cost,
        )(me, features, weight, acc)
    operands = (features, weight) + (() if acc is None else (acc,))
    return pl.pallas_call(
        functools.partial(project_kernel, acc is None),
        in_specs=[VMEM_SPEC] * len(operands),
        out_specs=VMEM_SPEC,
        out_shape=total,
        compiler_params=params([features, weight, total, total]),
        cost_estimate=cost,
    )(*operands)


def visible(first_row, q0, k0, shape):
    key = lax.broadcasted_iota(jnp.int32, shape, 0)
    last_row = q0 - k0 + lax.broadcasted_iota(jnp.int32, (1, shape[1]), 1)
    return (key >= first_row - k0) & (key <= last_row)


def block_sizes(total):
    return (
        (block_size(total, 256), block_size(total, 256)),
        (block_size(total, 256), block_size(total, 256)),
    )


def plan_size(total, bq, bk):
    return sum(((q + 1) * bq + bk - 1) // bk for q in range(total // bq)) + 2


def fill_plan(lows, total, bq, bk, own, plan_q, plan_k, count_ref):
    def put(qi):
        def at(ki, count):
            plan_q[count] = qi
            plan_k[count] = ki
            return count + 1

        return at

    count = 0
    for qi, low in enumerate(lows):
        low, high = low // bk, ((qi + 1) * bq + bk - 1) // bk
        if own is not None:
            wanted = ((qi + 1) * bq > own[0]) & (qi * bq < own[1])
            low = jnp.where(wanted, low, jnp.maximum(low, own[0] // bk))
            high = jnp.where(wanted, high, jnp.minimum(high, (own[1] + bk - 1) // bk))
        count = lax.fori_loop(low, high, put(qi), count)
    count_ref[0] = (count + 1) // 2
    for spare in range(2):
        plan_q[count + spare] = 0
        plan_k[count + spare] = total // bk - 1


def pipelined(plan_q, plan_k, count_ref, early, late, buffers):
    early(plan_q[0], plan_k[0], buffers[0])

    @pl.loop(0, count_ref[0])
    def _(i):
        for turn in range(2):
            now = 2 * i + turn
            late(plan_q[now], plan_k[now], buffers[turn])
            early(plan_q[now + 1], plan_k[now + 1], buffers[1 - turn])


def forward_kernel(peers, heads, rows, bq, bk, me_s, *refs):
    blocks = refs[:peers]
    q_ref, k_ref, v_ref, qt_ref, kt_ref, first_ref, out_ref, log_ref = refs[peers:peers + 8]
    plan_q, plan_k, count_ref, own_q, own_k, own_count = refs[peers + 8:peers + 14]
    vt_ref, doc_ref, sum_ref, s0, top0, s1, top1 = refs[peers + 14:]
    total = q_ref.shape[0]
    factor = HD ** (-0.5) * math.log2(math.e)
    me = me_s[0]
    for d, block in enumerate(blocks):
        place = me ^ d
        for part, ref in enumerate((q_ref, k_ref, v_ref)):
            ref[aligned(place, rows), :] = block[part * rows:(part + 1) * rows, :]
        docs = block[3 * rows:, :].astype(jnp.float32)
        for t in range(rows // HD):
            doc_ref[:, aligned(place * (rows // HD) + t, HD)] = docs[t:t + 1, :]
    docs = doc_ref[...]
    first = jnp.zeros(docs.shape, jnp.float32)
    for value in range(1, DOC_VALUES):
        before = jnp.sum((docs < value).astype(jnp.float32))
        first = jnp.where(docs >= value, before, first)
    first = first.astype(jnp.int32)
    first_ref[...] = first
    lows = [jnp.min(first[:, qi * bq:(qi + 1) * bq]) for qi in range(total // bq)]
    fill_plan(lows, total, bq, bk, None, own_q, own_k, own_count)
    group = (me // heads) * heads * rows
    own = None if heads == peers else (group, group + heads * rows)
    back_q, back_k = block_sizes(total)[1]
    lows = [jnp.min(first[:, qi * back_q:(qi + 1) * back_q]) for qi in range(total // back_q)]
    fill_plan(lows, total, back_q, back_k, own, plan_q, plan_k, count_ref)
    qt_ref[...] = q_ref[...].T
    kt_ref[...] = k_ref[...].T
    vt_ref[:HD, :] = v_ref[...].T
    vt_ref[HD:, :] = jnp.ones((ONES_ROWS, total), jnp.bfloat16)
    out_ref[...] = jnp.zeros_like(out_ref)
    log_ref[...] = jnp.full_like(log_ref, NEG_LARGE)
    sum_ref[...] = jnp.zeros_like(sum_ref)

    def early(qi, ki, buffer):
        s_ref, top_ref = buffer
        keys, queries = aligned(ki, bk), aligned(qi, bq)
        s = dot32(k_ref[keys, :], qt_ref[:, queries]) * factor
        s = jnp.where(visible(first_ref[:, queries], qi * bq, ki * bk, (bk, bq)), s, NEG_LARGE)
        s_ref[...] = s
        top_ref[...] = jnp.max(s, axis=0, keepdims=True)

    def late(qi, ki, buffer):
        s_ref, top_ref = buffer
        keys, queries = aligned(ki, bk), aligned(qi, bq)
        top = log_ref[:, queries]
        new_top = jnp.maximum(top, top_ref[...])
        p = jnp.exp2(s_ref[...] - new_top)
        fix = jnp.exp2(top - new_top)
        high = p.astype(jnp.bfloat16)
        rest = (p - high.astype(jnp.float32)).astype(jnp.bfloat16)
        vt = vt_ref[:, keys]
        sums = dot32(vt, high) + dot32(vt, rest)
        out_ref[:, queries] = out_ref[:, queries] * fix + sums[:HD, :]
        sum_ref[:, queries] = sum_ref[:, queries] * fix + sums[HD:HD + 1, :]
        log_ref[:, queries] = new_top

    pipelined(own_q, own_k, own_count, early, late, ((s0, top0), (s1, top1)))
    total_p = sum_ref[...]
    out_ref[...] = out_ref[...] / total_p
    log_ref[...] = math.log(2.0) * (log_ref[...] + jnp.log2(total_p))


def backward_kernel(peers, heads, rows, bq, bk, me_s, plan_q, plan_k, count_ref, q_ref, k_ref, v_ref,
                    qt_ref, kt_ref, first_ref, out_ref, log_ref, *refs):
    blocks = refs[:peers]
    results = refs[peers:peers + heads]
    g_ref, gt_ref, dot_ref, dk_acc, dv_acc, dq_acc, p0, ds0, p1, ds1 = refs[peers + heads:]
    scale = HD ** (-0.5)
    me = me_s[0]
    for d, block in enumerate(blocks):
        g_ref[aligned(me ^ d, rows), :] = block[...]
    gt_ref[...] = g_ref[...].T
    dot_ref[...] = jnp.sum(gt_ref[...].astype(jnp.float32) * out_ref[...], axis=0, keepdims=True)
    dk_acc[...] = jnp.zeros_like(dk_acc)
    dv_acc[...] = jnp.zeros_like(dv_acc)
    dq_acc[...] = jnp.zeros_like(dq_acc)

    def early(qi, ki, buffer):
        p_ref, ds_ref = buffer
        keys, queries = aligned(ki, bk), aligned(qi, bq)
        p = jnp.exp(dot32(k_ref[keys, :], qt_ref[:, queries]) * scale - log_ref[:, queries])
        p = jnp.where(visible(first_ref[:, queries], qi * bq, ki * bk, (bk, bq)), p, 0.0)
        p_ref[...] = p.astype(jnp.bfloat16)
        dp = dot32(v_ref[keys, :], gt_ref[:, queries])
        ds_ref[...] = (p * (dp - dot_ref[:, queries])).astype(jnp.bfloat16)

    def late(qi, ki, buffer):
        p_ref, ds_ref = buffer
        keys, queries = aligned(ki, bk), aligned(qi, bq)
        dv_acc[keys, :] += dot32(p_ref[...], g_ref[queries, :])
        dk_acc[keys, :] += dot32(ds_ref[...], q_ref[queries, :])
        dq_acc[:, queries] += dot32(kt_ref[:, keys], ds_ref[...])

    pipelined(plan_q, plan_k, count_ref, early, late, ((p0, ds0), (p1, ds1)))
    for d, result in enumerate(results):
        own = aligned(me ^ d, rows)
        result[:rows, :] = (scale * dq_acc[:, own]).astype(result.dtype).T
        result[rows:2 * rows, :] = (scale * dk_acc[own, :]).astype(result.dtype)
        result[2 * rows:, :] = dv_acc[own, :].astype(result.dtype)


def attention_cost(total, products):
    return pl.CostEstimate(
        flops=products * total * total * HD // 2,
        bytes_accessed=16 * total * HD,
        transcendentals=total * total // 4,
    )


def attention_forward(me, blocks, rows, heads):
    peers = len(blocks)
    total = peers * rows
    (bq, bk), back = block_sizes(total)
    plan = [(plan_size(total, *back),)] * 2 + [(1,)]
    own_plan = [(plan_size(total, bq, bk),)] * 2 + [(1,)]
    vectors = [
        *[jax.ShapeDtypeStruct((total, HD), jnp.bfloat16)] * 3,
        *[jax.ShapeDtypeStruct((HD, total), jnp.bfloat16)] * 2,
        jax.ShapeDtypeStruct((1, total), jnp.int32),
        jax.ShapeDtypeStruct((HD, total), jnp.float32),
        jax.ShapeDtypeStruct((1, total), jnp.float32),
    ]
    scratch = [
        pltpu.VMEM((HD + ONES_ROWS, total), jnp.bfloat16),
        pltpu.VMEM((1, total), jnp.float32),
        pltpu.VMEM((1, total), jnp.float32),
        *[pltpu.VMEM((bk, bq), jnp.float32), pltpu.VMEM((1, bq), jnp.float32)] * 2,
    ]
    return pl.pallas_call(
        functools.partial(forward_kernel, peers, heads, rows, bq, bk),
        in_specs=[SMEM_SPEC] + [VMEM_SPEC] * peers,
        out_specs=[VMEM_SPEC] * len(vectors) + [SMEM_SPEC] * 3,
        out_shape=vectors + [jax.ShapeDtypeStruct(shape, jnp.int32) for shape in plan],
        scratch_shapes=[pltpu.SMEM(shape, jnp.int32) for shape in own_plan] + scratch,
        compiler_params=params([*blocks, *vectors], scratch),
        cost_estimate=attention_cost(total, 3),
    )(me, *blocks)


def attention_backward(me, heads, state, blocks):
    peers, rows = len(blocks), blocks[0].shape[0]
    total = peers * rows
    bq, bk = block_sizes(total)[1]
    vectors, plan = state[:8], state[8:]
    out_shape = [jax.ShapeDtypeStruct((3 * rows, HD), jnp.bfloat16)] * heads
    scratch = [
        pltpu.VMEM((total, HD), jnp.bfloat16),
        pltpu.VMEM((HD, total), jnp.bfloat16),
        pltpu.VMEM((1, total), jnp.float32),
        pltpu.VMEM((total, HD), jnp.float32),
        pltpu.VMEM((total, HD), jnp.float32),
        pltpu.VMEM((HD, total), jnp.float32),
        *[pltpu.VMEM((bk, bq), jnp.bfloat16)] * 4,
    ]
    return pl.pallas_call(
        functools.partial(backward_kernel, peers, heads, rows, bq, bk),
        in_specs=[SMEM_SPEC] * 4 + [VMEM_SPEC] * (8 + peers),
        out_specs=[VMEM_SPEC] * heads,
        out_shape=out_shape,
        scratch_shapes=scratch,
        compiler_params=params([*vectors, *blocks, *out_shape], scratch),
        cost_estimate=attention_cost(total, 5),
    )(me, *plan, *vectors, *blocks)


def per_device(peers, groups, queries, keys_in, values, out_grad, out_weight, doc_ids):
    rows, width = queries.shape
    heads = width // HD
    me = lax.axis_index("seq")
    me_vector = me.reshape(1)

    def exchange(x, d):
        return x if d == 0 else lax.ppermute(x, "seq", [(i, i ^ d) for i in range(peers)])

    def pass_on(x):
        return lax.ppermute(x, "head", [(i, (i + 1) % groups) for i in range(groups)])

    order = [*range(peers - 2, 0, -2), *range(peers - 1, 0, -2)]

    def exchange_all(blocks, wanted):
        moved = {d: exchange(blocks[d % heads], d) for d in order if d < wanted}
        return [blocks[0]] + [moved[d] for d in range(1, wanted)]

    packed = list(pack_heads(me_vector, queries, keys_in, values, doc_ids))
    received = exchange_all(packed, peers)

    def share(step):
        return len(order) * step * (step + 1) // ((groups - 2) * (groups - 1))

    after = lax.optimization_barrier
    features, acc = out_grad, None
    weights = []
    for step in range(groups):
        block = lax.rem(lax.axis_index("head") + groups - step, groups)
        weights.append(lax.dynamic_slice_in_dim(out_weight, block * width, width, 1))
    for step in range(groups):
        last = step == groups - 1
        if not last:
            passed = pass_on(features)
        if step == groups - 2:
            received[0], features = after((received[0], features))
            state = list(attention_forward(me_vector, received, rows, heads))
            features, state[1] = after((features, state[1]))
        acc = project(me_vector, weights[step], features, acc, last)
        if not last:
            features = passed
            if step < groups - 2:
                batch = order[share(step):share(step + 1)]
                here = [received[d] for d in batch]
                features, acc, here, weights[2:] = after((features, acc, here, weights[2:]))
                for d, block in zip(batch, here):
                    received[d] = block
    grads = exchange_all(acc, peers)

    results = attention_backward(me_vector, heads, state, grads)
    returned = exchange_all(results, heads)
    return tuple(unpack_heads(me_vector, returned, rows))


def solution(mesh):
    in_specs = (
        P("seq", "head"),
        P("seq", "head"),
        P("seq", "head"),
        P("seq", "head"),
        P("head", None),
        P("seq"),
    )
    out_specs = (P("seq", "head"), P("seq", "head"), P("seq", "head"))
    return jax.shard_map(
        functools.partial(per_device, mesh.shape["seq"], mesh.shape["head"]),
        mesh=mesh, in_specs=in_specs, out_specs=out_specs, check_vma=False,
    )
```

```python
import functools
import math

import jax
import jax.numpy as jnp
from jax import lax
from jax.experimental import pallas as pl
from jax.experimental.pallas import tpu as pltpu
from jax.sharding import PartitionSpec as P

HD = 128
DOC_VALUES = 8
DOC_ROWS = 16
ONES_ROWS = 16
NEG_LARGE = -1e30
VMEM_SPARE = 6 * 1024 * 1024

NN = (((1,), (0,)), ((), ()))
NT = (((1,), (1,)), ((), ()))
SMEM_SPEC = pl.BlockSpec(memory_space=pltpu.SMEM)
VMEM_SPEC = pl.BlockSpec(memory_space=pltpu.VMEM)


def dot32(a, b, dims=NN):
    return lax.dot_general(a, b, dims, preferred_element_type=jnp.float32)


def block_size(total, wanted):
    size = min(wanted, total)
    while total % size or size % 128:
        size -= 128
    return size


def aligned(index, size):
    return pl.ds(pl.multiple_of(index * size, size), size)


def params(arrays, scratch=()):
    total = sum(math.prod(a.shape) * jnp.dtype(a.dtype).itemsize for a in (*arrays, *scratch))
    return pltpu.CompilerParams(vmem_limit_bytes=total + VMEM_SPARE)


def pack_kernel(heads, rows, me_s, q_ref, k_ref, v_ref, doc_ref, *refs):
    outs, done = refs[:heads], refs[heads]
    own = lax.rem(me_s[0], heads)
    copies = []
    for d, out in enumerate(outs):
        columns = aligned(own ^ d, HD)
        for part, ref in enumerate((q_ref, k_ref, v_ref)):
            place = out.at[pl.ds(part * rows, rows), :]
            copies.append(pltpu.make_async_copy(ref.at[:, columns], place, done.at[d, part]))
            copies[-1].start()
    docs = doc_ref[...].astype(jnp.float32)
    docs = jnp.concatenate([docs, jnp.zeros((DOC_ROWS - docs.shape[0], HD), jnp.float32)], axis=0)
    docs = docs.astype(jnp.bfloat16)
    for out in outs:
        out[3 * rows:, :] = docs
    for copy in copies:
        copy.wait()


def pack_heads(me, q, k, v, doc_ids):
    rows, width = q.shape
    heads = width // HD
    out_shape = [jax.ShapeDtypeStruct((3 * rows + DOC_ROWS, HD), q.dtype)] * heads
    return pl.pallas_call(
        functools.partial(pack_kernel, heads, rows),
        in_specs=[SMEM_SPEC] + [pl.BlockSpec(memory_space=pltpu.HBM)] * 3 + [VMEM_SPEC],
        out_specs=[VMEM_SPEC] * heads,
        out_shape=out_shape,
        scratch_shapes=[pltpu.SemaphoreType.DMA((heads, 3))],
        compiler_params=params(out_shape),
    )(me, q, k, v, doc_ids.reshape(rows // HD, HD))


def unpack_kernel(heads, rows, me_s, *refs):
    own = lax.rem(me_s[0], heads)
    for d in range(heads):
        columns = aligned(own ^ d, HD)
        for part in range(3):
            refs[heads + part][:, columns] = refs[d][part * rows:(part + 1) * rows, :]


def unpack_heads(me, blocks, rows):
    heads = len(blocks)
    return pl.pallas_call(
        functools.partial(unpack_kernel, heads, rows),
        in_specs=[SMEM_SPEC] + [VMEM_SPEC] * heads,
        out_specs=[VMEM_SPEC] * 3,
        out_shape=[jax.ShapeDtypeStruct((rows, heads * HD), blocks[0].dtype)] * 3,
        compiler_params=params([*blocks, *blocks]),
    )(me, *blocks)


def project_kernel(first, o_ref, w_ref, *refs):
    out_ref = refs[-1]
    for pair in range(w_ref.shape[0] // (2 * HD)):
        part = slice(pair * 2 * HD, (pair + 1) * 2 * HD)
        both = dot32(o_ref[...], w_ref[part, :], NT)
        out_ref[:, part] = both if first else refs[0][:, part] + both


def project_last_kernel(me_s, o_ref, w_ref, acc_ref, *outs):
    pairs = len(outs) // 2
    odd = lax.rem(me_s[0], 2) == 1
    for j in range(pairs):
        part = aligned(lax.rem(me_s[0] // 2, pairs) ^ j, 2 * HD)
        both = (acc_ref[:, part] + dot32(o_ref[...], w_ref[part, :], NT)).astype(jnp.bfloat16)
        outs[2 * j][...] = jnp.where(odd, both[:, HD:], both[:, :HD])
        outs[2 * j + 1][...] = jnp.where(odd, both[:, :HD], both[:, HD:])


def project(me, weight, features, acc, last):
    rows, width = features.shape
    columns = weight.shape[0]
    heads = columns // HD
    total = jax.ShapeDtypeStruct((rows, columns), jnp.float32)
    cost = pl.CostEstimate(
        flops=2 * rows * width * columns,
        bytes_accessed=2 * width * columns + 8 * rows * columns,
        transcendentals=0,
    )
    if last:
        return pl.pallas_call(
            project_last_kernel,
            in_specs=[SMEM_SPEC] + [VMEM_SPEC] * 3,
            out_specs=[VMEM_SPEC] * heads,
            out_shape=[jax.ShapeDtypeStruct((rows, HD), jnp.bfloat16)] * heads,
            compiler_params=params([features, weight, total, total]),
            cost_estimate=cost,
        )(me, features, weight, acc)
    operands = (features, weight) + (() if acc is None else (acc,))
    return pl.pallas_call(
        functools.partial(project_kernel, acc is None),
        in_specs=[VMEM_SPEC] * len(operands),
        out_specs=VMEM_SPEC,
        out_shape=total,
        compiler_params=params([features, weight, total, total]),
        cost_estimate=cost,
    )(*operands)


def at_or_before(q0, k0, shape):
    key = lax.broadcasted_iota(jnp.int32, shape, 0)
    return key <= q0 - k0 + lax.broadcasted_iota(jnp.int32, (1, shape[1]), 1)


def block_sizes(total):
    return (
        (block_size(total, 256), block_size(total, 256)),
        (block_size(total, 256), block_size(total, 256)),
    )


def plan_size(total, bq, bk):
    return sum(((q + 1) * bq + bk - 1) // bk for q in range(total // bq)) + 2


def fill_plan(lows, total, bq, bk, own, plan_q, plan_k, count_ref):
    def put(qi):
        def at(ki, count):
            plan_q[count] = qi
            plan_k[count] = ki
            return count + 1

        return at

    spans = []
    for qi, low in enumerate(lows):
        low, high = low // bk, ((qi + 1) * bq + bk - 1) // bk
        if own is not None:
            wanted = ((qi + 1) * bq > own[0]) & (qi * bq < own[1])
            low = jnp.where(wanted, low, jnp.maximum(low, own[0] // bk))
            high = jnp.where(wanted, high, jnp.minimum(high, (own[1] + bk - 1) // bk))
        whole = jnp.maximum(low, jnp.minimum(high, qi * bq // bk))
        spans.append((low, whole, high))
    count = 0
    for qi, (low, whole, high) in enumerate(spans):
        count = lax.fori_loop(low, whole, put(qi), count)
    count_ref[0] = jnp.maximum(count - 1, 0) // 2
    for qi, (low, whole, high) in enumerate(spans):
        count = lax.fori_loop(whole, high, put(qi), count)
    count_ref[1] = (count + 1) // 2
    for spare in range(2):
        plan_q[count + spare] = 0
        plan_k[count + spare] = total // bk - 1


def pipelined(plan_q, plan_k, count_ref, early, late, buffers):
    early(plan_q[0], plan_k[0], buffers[0], True)

    def turns(diagonal):
        def body(i, carry):
            for turn in range(2):
                now = 2 * i + turn
                late(plan_q[now], plan_k[now], buffers[turn])
                early(plan_q[now + 1], plan_k[now + 1], buffers[1 - turn], diagonal)
            return carry

        return body

    lax.fori_loop(0, count_ref[0], turns(False), 0)
    lax.fori_loop(count_ref[0], count_ref[1], turns(True), 0)


def forward_kernel(peers, heads, rows, bq, bk, me_s, *refs):
    blocks = refs[:peers]
    q_ref, v_ref, kx_ref, qtx_ref, kt_ref, out_ref, log_ref = refs[peers:peers + 7]
    plan_q, plan_k, count_ref, own_q, own_k, own_count = refs[peers + 7:peers + 13]
    vt_ref, doc_ref, sum_ref, s0, top0, s1, top1 = refs[peers + 13:]
    total = q_ref.shape[0]
    factor = HD ** (-0.5) * math.log2(math.e)
    me = me_s[0]
    for d, block in enumerate(blocks):
        place = me ^ d
        for part, ref in enumerate((q_ref, kx_ref.at[:, :HD], v_ref)):
            ref[aligned(place, rows), :] = block[part * rows:(part + 1) * rows, :]
        docs = block[3 * rows:, :].astype(jnp.float32)
        for t in range(rows // HD):
            doc_ref[:, aligned(place * (rows // HD) + t, HD)] = docs[t:t + 1, :]
    docs = doc_ref[...]
    first = jnp.zeros(docs.shape, jnp.float32)
    for value in range(1, DOC_VALUES):
        before = jnp.sum((docs < value).astype(jnp.float32))
        first = jnp.where(docs >= value, before, first)
    first = first.astype(jnp.int32)
    lows = [jnp.min(first[:, qi * bq:(qi + 1) * bq]) for qi in range(total // bq)]
    fill_plan(lows, total, bq, bk, None, own_q, own_k, own_count)
    group = (me // heads) * heads * rows
    own = None if heads == peers else (group, group + heads * rows)
    back_q, back_k = block_sizes(total)[1]
    lows = [jnp.min(first[:, qi * back_q:(qi + 1) * back_q]) for qi in range(total // back_q)]
    fill_plan(lows, total, back_q, back_k, own, plan_q, plan_k, count_ref)
    same = lax.broadcasted_iota(jnp.int32, (HD, total), 0).astype(jnp.float32) == docs
    qtx_ref[:HD, :] = q_ref[...].T
    qtx_ref[HD:, :] = jnp.where(same, 0.0, NEG_LARGE).astype(jnp.bfloat16)
    kx_ref[:, HD:] = jnp.where(same, 1.0, 0.0).astype(jnp.bfloat16).T
    kt_ref[...] = kx_ref[:, :HD].T
    vt_ref[:HD, :] = v_ref[...].T
    vt_ref[HD:, :] = jnp.ones((ONES_ROWS, total), jnp.bfloat16)
    out_ref[...] = jnp.zeros_like(out_ref)
    log_ref[...] = jnp.full_like(log_ref, NEG_LARGE)
    sum_ref[...] = jnp.zeros_like(sum_ref)

    def early(qi, ki, buffer, diagonal):
        s_ref, top_ref = buffer
        keys, queries = aligned(ki, bk), aligned(qi, bq)
        s = dot32(kx_ref[keys, :], qtx_ref[:, queries]) * factor
        if diagonal:
            s = jnp.where(at_or_before(qi * bq, ki * bk, (bk, bq)), s, NEG_LARGE)
        s_ref[...] = s
        top_ref[...] = jnp.max(s, axis=0, keepdims=True)

    def late(qi, ki, buffer):
        s_ref, top_ref = buffer
        keys, queries = aligned(ki, bk), aligned(qi, bq)
        top = log_ref[:, queries]
        new_top = jnp.maximum(top, top_ref[...])
        p = jnp.exp2(s_ref[...] - new_top)
        fix = jnp.exp2(top - new_top)
        high = p.astype(jnp.bfloat16)
        rest = (p - high.astype(jnp.float32)).astype(jnp.bfloat16)
        vt = vt_ref[:, keys]
        sums = dot32(vt, high) + dot32(vt, rest)
        out_ref[:, queries] = out_ref[:, queries] * fix + sums[:HD, :]
        sum_ref[:, queries] = sum_ref[:, queries] * fix + sums[HD:HD + 1, :]
        log_ref[:, queries] = new_top

    pipelined(own_q, own_k, own_count, early, late, ((s0, top0), (s1, top1)))
    total_p = sum_ref[...]
    out_ref[...] = out_ref[...] / total_p
    log_ref[...] = math.log(2.0) * (log_ref[...] + jnp.log2(total_p))


def backward_kernel(peers, heads, rows, bq, bk, me_s, plan_q, plan_k, count_ref, q_ref, v_ref,
                    kx_ref, qtx_ref, kt_ref, out_ref, log_ref, *refs):
    blocks = refs[:peers]
    results = refs[peers:peers + heads]
    g_ref, gt_ref, dot_ref, dk_acc, dv_acc, dq_acc, p0, ds0, p1, ds1 = refs[peers + heads:]
    scale = HD ** (-0.5)
    me = me_s[0]
    for d, block in enumerate(blocks):
        g_ref[aligned(me ^ d, rows), :] = block[...]
    gt_ref[...] = g_ref[...].T
    dot_ref[...] = jnp.sum(gt_ref[...].astype(jnp.float32) * out_ref[...], axis=0, keepdims=True)
    dk_acc[...] = jnp.zeros_like(dk_acc)
    dv_acc[...] = jnp.zeros_like(dv_acc)
    dq_acc[...] = jnp.zeros_like(dq_acc)

    def early(qi, ki, buffer, diagonal):
        p_ref, ds_ref = buffer
        keys, queries = aligned(ki, bk), aligned(qi, bq)
        p = jnp.exp(dot32(kx_ref[keys, :], qtx_ref[:, queries]) * scale - log_ref[:, queries])
        if diagonal:
            p = jnp.where(at_or_before(qi * bq, ki * bk, (bk, bq)), p, 0.0)
        p_ref[...] = p.astype(jnp.bfloat16)
        dp = dot32(v_ref[keys, :], gt_ref[:, queries])
        ds_ref[...] = (p * (dp - dot_ref[:, queries])).astype(jnp.bfloat16)

    def late(qi, ki, buffer):
        p_ref, ds_ref = buffer
        keys, queries = aligned(ki, bk), aligned(qi, bq)
        dv_acc[keys, :] += dot32(p_ref[...], g_ref[queries, :])
        dk_acc[keys, :] += dot32(ds_ref[...], q_ref[queries, :])
        dq_acc[:, queries] += dot32(kt_ref[:, keys], ds_ref[...])

    pipelined(plan_q, plan_k, count_ref, early, late, ((p0, ds0), (p1, ds1)))
    for d, result in enumerate(results):
        own = aligned(me ^ d, rows)
        result[:rows, :] = (scale * dq_acc[:, own]).astype(result.dtype).T
        result[rows:2 * rows, :] = (scale * dk_acc[own, :]).astype(result.dtype)
        result[2 * rows:, :] = dv_acc[own, :].astype(result.dtype)


def attention_cost(total, products):
    return pl.CostEstimate(
        flops=products * total * total * HD // 2,
        bytes_accessed=16 * total * HD,
        transcendentals=total * total // 4,
    )


def attention_forward(me, blocks, rows, heads):
    peers = len(blocks)
    total = peers * rows
    (bq, bk), back = block_sizes(total)
    plan = [(plan_size(total, *back),)] * 2 + [(2,)]
    own_plan = [(plan_size(total, bq, bk),)] * 2 + [(2,)]
    vectors = [
        *[jax.ShapeDtypeStruct((total, HD), jnp.bfloat16)] * 2,
        jax.ShapeDtypeStruct((total, 2 * HD), jnp.bfloat16),
        jax.ShapeDtypeStruct((2 * HD, total), jnp.bfloat16),
        jax.ShapeDtypeStruct((HD, total), jnp.bfloat16),
        jax.ShapeDtypeStruct((HD, total), jnp.float32),
        jax.ShapeDtypeStruct((1, total), jnp.float32),
    ]
    scratch = [
        pltpu.VMEM((HD + ONES_ROWS, total), jnp.bfloat16),
        pltpu.VMEM((1, total), jnp.float32),
        pltpu.VMEM((1, total), jnp.float32),
        *[pltpu.VMEM((bk, bq), jnp.float32), pltpu.VMEM((1, bq), jnp.float32)] * 2,
    ]
    return pl.pallas_call(
        functools.partial(forward_kernel, peers, heads, rows, bq, bk),
        in_specs=[SMEM_SPEC] + [VMEM_SPEC] * peers,
        out_specs=[VMEM_SPEC] * len(vectors) + [SMEM_SPEC] * 3,
        out_shape=vectors + [jax.ShapeDtypeStruct(shape, jnp.int32) for shape in plan],
        scratch_shapes=[pltpu.SMEM(shape, jnp.int32) for shape in own_plan] + scratch,
        compiler_params=params([*blocks, *vectors], scratch),
        cost_estimate=attention_cost(total, 3),
    )(me, *blocks)


def attention_backward(me, heads, state, blocks):
    peers, rows = len(blocks), blocks[0].shape[0]
    total = peers * rows
    bq, bk = block_sizes(total)[1]
    vectors, plan = state[:7], state[7:]
    out_shape = [jax.ShapeDtypeStruct((3 * rows, HD), jnp.bfloat16)] * heads
    scratch = [
        pltpu.VMEM((total, HD), jnp.bfloat16),
        pltpu.VMEM((HD, total), jnp.bfloat16),
        pltpu.VMEM((1, total), jnp.float32),
        pltpu.VMEM((total, HD), jnp.float32),
        pltpu.VMEM((total, HD), jnp.float32),
        pltpu.VMEM((HD, total), jnp.float32),
        *[pltpu.VMEM((bk, bq), jnp.bfloat16)] * 4,
    ]
    return pl.pallas_call(
        functools.partial(backward_kernel, peers, heads, rows, bq, bk),
        in_specs=[SMEM_SPEC] * 4 + [VMEM_SPEC] * (7 + peers),
        out_specs=[VMEM_SPEC] * heads,
        out_shape=out_shape,
        scratch_shapes=scratch,
        compiler_params=params([*vectors, *blocks, *out_shape], scratch),
        cost_estimate=attention_cost(total, 5),
    )(me, *plan, *vectors, *blocks)


def per_device(peers, groups, queries, keys_in, values, out_grad, out_weight, doc_ids):
    rows, width = queries.shape
    heads = width // HD
    me = lax.axis_index("seq")
    me_vector = me.reshape(1)

    def exchange(x, d):
        return x if d == 0 else lax.ppermute(x, "seq", [(i, i ^ d) for i in range(peers)])

    def pass_on(x):
        return lax.ppermute(x, "head", [(i, (i + 1) % groups) for i in range(groups)])

    order = [*range(2, peers, 2), *range(peers - 1, 0, -2)]

    def exchange_all(blocks, wanted):
        moved = {d: exchange(blocks[d % heads], d) for d in order if d < wanted}
        return [blocks[0]] + [moved[d] for d in range(1, wanted)]

    packed = list(pack_heads(me_vector, queries, keys_in, values, doc_ids))
    received = exchange_all(packed, peers)

    def share(step):
        return len(order) * step * (step + 1) // ((groups - 2) * (groups - 1))

    after = lax.optimization_barrier
    features, acc = out_grad, None
    weights = []
    for step in range(groups):
        block = lax.rem(lax.axis_index("head") + groups - step, groups)
        weights.append(lax.dynamic_slice_in_dim(out_weight, block * width, width, 1))
    for step in range(groups):
        last = step == groups - 1
        if not last:
            passed = pass_on(features)
        if step == groups - 2:
            received[0], features = after((received[0], features))
            state = list(attention_forward(me_vector, received, rows, heads))
            features, state[1] = after((features, state[1]))
        acc = project(me_vector, weights[step], features, acc, last)
        if not last:
            features = passed
            if step < groups - 2:
                batch = order[share(step):share(step + 1)]
                here = [received[d] for d in batch]
                features, acc, here, weights[2:] = after((features, acc, here, weights[2:]))
                for d, block in zip(batch, here):
                    received[d] = block
    grads = exchange_all(acc, peers)

    results = attention_backward(me_vector, heads, state, grads)
    returned = exchange_all(results, heads)
    return tuple(unpack_heads(me_vector, returned, rows))


def solution(mesh):
    in_specs = (
        P("seq", "head"),
        P("seq", "head"),
        P("seq", "head"),
        P("seq", "head"),
        P("head", None),
        P("seq"),
    )
    out_specs = (P("seq", "head"), P("seq", "head"), P("seq", "head"))
    return jax.shard_map(
        functools.partial(per_device, mesh.shape["seq"], mesh.shape["head"]),
        mesh=mesh, in_specs=in_specs, out_specs=out_specs, check_vma=False,
    )
```

```python
import functools
import math

import jax
import jax.numpy as jnp
from jax import lax
from jax.experimental import pallas as pl
from jax.experimental.pallas import tpu as pltpu
from jax.sharding import PartitionSpec as P

HD = 128
DOC_VALUES = 8
DOC_ROWS = 16
ONES_ROWS = 16
NEG_LARGE = -1e30
VMEM_SPARE = 6 * 1024 * 1024
LIST_BYTES = 16 * 1024 * 1024

NN = (((1,), (0,)), ((), ()))
NT = (((1,), (1,)), ((), ()))
SMEM_SPEC = pl.BlockSpec(memory_space=pltpu.SMEM)
VMEM_SPEC = pl.BlockSpec(memory_space=pltpu.VMEM)


def dot32(a, b, dims=NN):
    return lax.dot_general(a, b, dims, preferred_element_type=jnp.float32)


def block_size(total, wanted):
    size = min(wanted, total)
    while total % size or size % 128:
        size -= 128
    return size


def aligned(index, size):
    return pl.ds(pl.multiple_of(index * size, size), size)


def params(arrays, scratch=()):
    total = sum(math.prod(a.shape) * jnp.dtype(a.dtype).itemsize for a in (*arrays, *scratch))
    return pltpu.CompilerParams(vmem_limit_bytes=total + VMEM_SPARE)


def pack_kernel(heads, rows, me_s, q_ref, k_ref, v_ref, doc_ref, *refs):
    outs, done = refs[:heads], refs[heads]
    own = lax.rem(me_s[0], heads)
    copies = []
    for d, out in enumerate(outs):
        columns = aligned(own ^ d, HD)
        for part, ref in enumerate((q_ref, k_ref, v_ref)):
            place = out.at[pl.ds(part * rows, rows), :]
            copies.append(pltpu.make_async_copy(ref.at[:, columns], place, done.at[d, part]))
            copies[-1].start()
    docs = doc_ref[...].astype(jnp.float32)
    docs = jnp.concatenate([docs, jnp.zeros((DOC_ROWS - docs.shape[0], HD), jnp.float32)], axis=0)
    docs = docs.astype(jnp.bfloat16)
    for out in outs:
        out[3 * rows:, :] = docs
    for copy in copies:
        copy.wait()


def pack_heads(me, q, k, v, doc_ids):
    rows, width = q.shape
    heads = width // HD
    out_shape = [jax.ShapeDtypeStruct((3 * rows + DOC_ROWS, HD), q.dtype)] * heads
    return pl.pallas_call(
        functools.partial(pack_kernel, heads, rows),
        in_specs=[SMEM_SPEC] + [pl.BlockSpec(memory_space=pltpu.HBM)] * 3 + [VMEM_SPEC],
        out_specs=[VMEM_SPEC] * heads,
        out_shape=out_shape,
        scratch_shapes=[pltpu.SemaphoreType.DMA((heads, 3))],
        compiler_params=params(out_shape),
    )(me, q, k, v, doc_ids.reshape(rows // HD, HD))


def unpack_kernel(heads, rows, me_s, *refs):
    own = lax.rem(me_s[0], heads)
    for d in range(heads):
        columns = aligned(own ^ d, HD)
        for part in range(3):
            refs[heads + part][:, columns] = refs[d][part * rows:(part + 1) * rows, :]


def unpack_heads(me, blocks, rows):
    heads = len(blocks)
    return pl.pallas_call(
        functools.partial(unpack_kernel, heads, rows),
        in_specs=[SMEM_SPEC] + [VMEM_SPEC] * heads,
        out_specs=[VMEM_SPEC] * 3,
        out_shape=[jax.ShapeDtypeStruct((rows, heads * HD), blocks[0].dtype)] * 3,
        compiler_params=params([*blocks, *blocks]),
    )(me, *blocks)


def project_kernel(first, o_ref, w_ref, *refs):
    out_ref = refs[-1]
    for pair in range(w_ref.shape[0] // (2 * HD)):
        part = slice(pair * 2 * HD, (pair + 1) * 2 * HD)
        both = dot32(o_ref[...], w_ref[part, :], NT)
        out_ref[:, part] = both if first else refs[0][:, part] + both


def project_last_kernel(me_s, o_ref, w_ref, acc_ref, *outs):
    pairs = len(outs) // 2
    odd = lax.rem(me_s[0], 2) == 1
    for j in range(pairs):
        part = aligned(lax.rem(me_s[0] // 2, pairs) ^ j, 2 * HD)
        both = (acc_ref[:, part] + dot32(o_ref[...], w_ref[part, :], NT)).astype(jnp.bfloat16)
        outs[2 * j][...] = jnp.where(odd, both[:, HD:], both[:, :HD])
        outs[2 * j + 1][...] = jnp.where(odd, both[:, :HD], both[:, HD:])


def project(me, weight, features, acc, last):
    rows, width = features.shape
    columns = weight.shape[0]
    heads = columns // HD
    total = jax.ShapeDtypeStruct((rows, columns), jnp.float32)
    cost = pl.CostEstimate(
        flops=2 * rows * width * columns,
        bytes_accessed=2 * width * columns + 8 * rows * columns,
        transcendentals=0,
    )
    if last:
        return pl.pallas_call(
            project_last_kernel,
            in_specs=[SMEM_SPEC] + [VMEM_SPEC] * 3,
            out_specs=[VMEM_SPEC] * heads,
            out_shape=[jax.ShapeDtypeStruct((rows, HD), jnp.bfloat16)] * heads,
            compiler_params=params([features, weight, total, total]),
            cost_estimate=cost,
        )(me, features, weight, acc)
    operands = (features, weight) + (() if acc is None else (acc,))
    return pl.pallas_call(
        functools.partial(project_kernel, acc is None),
        in_specs=[VMEM_SPEC] * len(operands),
        out_specs=VMEM_SPEC,
        out_shape=total,
        compiler_params=params([features, weight, total, total]),
        cost_estimate=cost,
    )(*operands)


def at_or_before(q0, k0, shape):
    key = lax.broadcasted_iota(jnp.int32, shape, 0)
    return key <= q0 - k0 + lax.broadcasted_iota(jnp.int32, (1, shape[1]), 1)


def block_sizes(total):
    return (
        (block_size(total, 256), block_size(total, 256)),
        (block_size(total, 256), block_size(total, 256)),
    )


def plan_size(total, bq, bk):
    return sum(((q + 1) * bq + bk - 1) // bk for q in range(total // bq)) + 2


def fill_plan(lows, total, bq, bk, own, plan_q, plan_k, count_ref):
    def put(qi):
        def at(ki, count):
            plan_q[count] = qi
            plan_k[count] = ki
            return count + 1

        return at

    spans = []
    for qi, low in enumerate(lows):
        low, high = low // bk, ((qi + 1) * bq + bk - 1) // bk
        if own is not None:
            wanted = ((qi + 1) * bq > own[0]) & (qi * bq < own[1])
            low = jnp.where(wanted, low, jnp.maximum(low, own[0] // bk))
            high = jnp.where(wanted, high, jnp.minimum(high, (own[1] + bk - 1) // bk))
        whole = jnp.maximum(low, jnp.minimum(high, qi * bq // bk))
        spans.append((low, whole, high))
    count = 0
    for qi, (low, whole, high) in enumerate(spans):
        count = lax.fori_loop(low, whole, put(qi), count)
    count_ref[0] = jnp.maximum(count - 1, 0) // 2
    for qi, (low, whole, high) in enumerate(spans):
        count = lax.fori_loop(whole, high, put(qi), count)
    count_ref[1] = (count + 1) // 2
    for spare in range(2):
        plan_q[count + spare] = 0
        plan_k[count + spare] = total // bk - 1


def pipelined(plan_q, plan_k, count_ref, early, late, buffers):
    early(0, plan_q[0], plan_k[0], buffers[0], True)

    def turns(diagonal):
        def body(i, carry):
            for turn in range(2):
                now = 2 * i + turn
                late(now, plan_q[now], plan_k[now], buffers[turn])
                early(now + 1, plan_q[now + 1], plan_k[now + 1], buffers[1 - turn], diagonal)
            return carry

        return body

    lax.fori_loop(0, count_ref[0], turns(False), 0)
    lax.fori_loop(count_ref[0], count_ref[1], turns(True), 0)


def forward_kernel(peers, heads, rows, bq, bk, kept, me_s, *refs):
    blocks = refs[:peers]
    if kept:
        p_list, top_list = refs[peers + 7:peers + 9]
        refs = refs[:peers + 7] + refs[peers + 9:]
    q_ref, v_ref, kx_ref, qtx_ref, kt_ref, out_ref, log_ref = refs[peers:peers + 7]
    plan_q, plan_k, count_ref, own_q, own_k, own_count = refs[peers + 7:peers + 13]
    vt_ref, doc_ref, sum_ref, s0, top0, s1, top1 = refs[peers + 13:]
    total = q_ref.shape[0]
    factor = HD ** (-0.5) * math.log2(math.e)
    me = me_s[0]
    for d, block in enumerate(blocks):
        place = me ^ d
        for part, ref in enumerate((q_ref, kx_ref.at[:, :HD], v_ref)):
            ref[aligned(place, rows), :] = block[part * rows:(part + 1) * rows, :]
        docs = block[3 * rows:, :].astype(jnp.float32)
        for t in range(rows // HD):
            doc_ref[:, aligned(place * (rows // HD) + t, HD)] = docs[t:t + 1, :]
    docs = doc_ref[...]
    first = jnp.zeros(docs.shape, jnp.float32)
    for value in range(1, DOC_VALUES):
        before = jnp.sum((docs < value).astype(jnp.float32))
        first = jnp.where(docs >= value, before, first)
    first = first.astype(jnp.int32)
    lows = [jnp.min(first[:, qi * bq:(qi + 1) * bq]) for qi in range(total // bq)]
    fill_plan(lows, total, bq, bk, None, own_q, own_k, own_count)
    group = (me // heads) * heads * rows
    own = None if heads == peers else (group, group + heads * rows)
    back_q, back_k = block_sizes(total)[1]
    lows = [jnp.min(first[:, qi * back_q:(qi + 1) * back_q]) for qi in range(total // back_q)]
    fill_plan(lows, total, back_q, back_k, own, plan_q, plan_k, count_ref)
    same = lax.broadcasted_iota(jnp.int32, (HD, total), 0).astype(jnp.float32) == docs
    qtx_ref[:HD, :] = q_ref[...].T
    qtx_ref[HD:, :] = jnp.where(same, 0.0, NEG_LARGE).astype(jnp.bfloat16)
    kx_ref[:, HD:] = jnp.where(same, 1.0, 0.0).astype(jnp.bfloat16).T
    kt_ref[...] = kx_ref[:, :HD].T
    vt_ref[:HD, :] = v_ref[...].T
    vt_ref[HD:, :] = jnp.ones((ONES_ROWS, total), jnp.bfloat16)
    out_ref[...] = jnp.zeros_like(out_ref)
    log_ref[...] = jnp.full_like(log_ref, NEG_LARGE)
    sum_ref[...] = jnp.zeros_like(sum_ref)

    def early(now, qi, ki, buffer, diagonal):
        s_ref, top_ref = buffer
        keys, queries = aligned(ki, bk), aligned(qi, bq)
        s = dot32(kx_ref[keys, :], qtx_ref[:, queries]) * factor
        if diagonal:
            s = jnp.where(at_or_before(qi * bq, ki * bk, (bk, bq)), s, NEG_LARGE)
        s_ref[...] = s
        top_ref[...] = jnp.max(s, axis=0, keepdims=True)

    def late(now, qi, ki, buffer):
        s_ref, top_ref = buffer
        keys, queries = aligned(ki, bk), aligned(qi, bq)
        top = log_ref[:, queries]
        new_top = jnp.maximum(top, top_ref[...])
        p = jnp.exp2(s_ref[...] - new_top)
        fix = jnp.exp2(top - new_top)
        high = p.astype(jnp.bfloat16)
        rest = (p - high.astype(jnp.float32)).astype(jnp.bfloat16)
        if kept:
            p_list[now] = high
            top_list[now] = new_top
        vt = vt_ref[:, keys]
        sums = dot32(vt, high) + dot32(vt, rest)
        out_ref[:, queries] = out_ref[:, queries] * fix + sums[:HD, :]
        sum_ref[:, queries] = sum_ref[:, queries] * fix + sums[HD:HD + 1, :]
        log_ref[:, queries] = new_top

    pipelined(own_q, own_k, own_count, early, late, ((s0, top0), (s1, top1)))
    total_p = sum_ref[...]
    out_ref[...] = out_ref[...] / total_p
    log_ref[...] = log_ref[...] + jnp.log2(total_p)


def backward_kernel(peers, heads, rows, bq, bk, kept, me_s, plan_q, plan_k, count_ref, q_ref, v_ref,
                    kx_ref, qtx_ref, kt_ref, out_ref, log_ref, *refs):
    if kept:
        p_list, top_list = refs[:2]
        refs = refs[2:]
    blocks = refs[:peers]
    results = refs[peers:peers + heads]
    g_ref, gt_ref, dot_ref, dk_acc, dv_acc, dq_acc, p0, ds0, p1, ds1 = refs[peers + heads:]
    scale = HD ** (-0.5)
    factor = scale * math.log2(math.e)
    me = me_s[0]
    for d, block in enumerate(blocks):
        g_ref[aligned(me ^ d, rows), :] = block[...]
    gt_ref[...] = g_ref[...].T
    dot_ref[...] = jnp.sum(gt_ref[...].astype(jnp.float32) * out_ref[...], axis=0, keepdims=True)
    dk_acc[...] = jnp.zeros_like(dk_acc)
    dv_acc[...] = jnp.zeros_like(dv_acc)
    dq_acc[...] = jnp.zeros_like(dq_acc)

    def early(now, qi, ki, buffer, diagonal):
        p_ref, ds_ref = buffer
        keys, queries = aligned(ki, bk), aligned(qi, bq)
        log_row = log_ref[:, queries]
        if kept:
            p = p_list[now].astype(jnp.float32) * jnp.exp2(top_list[now] - log_row)
        else:
            p = jnp.exp2(dot32(kx_ref[keys, :], qtx_ref[:, queries]) * factor - log_row)
            if diagonal:
                p = jnp.where(at_or_before(qi * bq, ki * bk, (bk, bq)), p, 0.0)
        p_ref[...] = p.astype(jnp.bfloat16)
        dp = dot32(v_ref[keys, :], gt_ref[:, queries])
        ds_ref[...] = (p * (dp - dot_ref[:, queries])).astype(jnp.bfloat16)

    def late(now, qi, ki, buffer):
        p_ref, ds_ref = buffer
        keys, queries = aligned(ki, bk), aligned(qi, bq)
        dv_acc[keys, :] += dot32(p_ref[...], g_ref[queries, :])
        dk_acc[keys, :] += dot32(ds_ref[...], q_ref[queries, :])
        dq_acc[:, queries] += dot32(kt_ref[:, keys], ds_ref[...])

    pipelined(plan_q, plan_k, count_ref, early, late, ((p0, ds0), (p1, ds1)))
    for d, result in enumerate(results):
        own = aligned(me ^ d, rows)
        result[:rows, :] = (scale * dq_acc[:, own]).astype(result.dtype).T
        result[rows:2 * rows, :] = (scale * dk_acc[own, :]).astype(result.dtype)
        result[2 * rows:, :] = dv_acc[own, :].astype(result.dtype)


def keeps_list(total, peers, heads):
    forward, backward = block_sizes(total)
    size = plan_size(total, *forward) * math.prod(forward) * 2
    return forward == backward and heads == peers and size <= LIST_BYTES


def attention_cost(total, products):
    return pl.CostEstimate(
        flops=products * total * total * HD // 2,
        bytes_accessed=16 * total * HD,
        transcendentals=total * total // 4,
    )


def attention_forward(me, blocks, rows, heads):
    peers = len(blocks)
    total = peers * rows
    (bq, bk), back = block_sizes(total)
    plan = [(plan_size(total, *back),)] * 2 + [(2,)]
    own_plan = [(plan_size(total, bq, bk),)] * 2 + [(2,)]
    vectors = [
        *[jax.ShapeDtypeStruct((total, HD), jnp.bfloat16)] * 2,
        jax.ShapeDtypeStruct((total, 2 * HD), jnp.bfloat16),
        jax.ShapeDtypeStruct((2 * HD, total), jnp.bfloat16),
        jax.ShapeDtypeStruct((HD, total), jnp.bfloat16),
        jax.ShapeDtypeStruct((HD, total), jnp.float32),
        jax.ShapeDtypeStruct((1, total), jnp.float32),
    ]
    kept = keeps_list(total, peers, heads)
    if kept:
        vectors.append(jax.ShapeDtypeStruct((*own_plan[0], bk, bq), jnp.bfloat16))
        vectors.append(jax.ShapeDtypeStruct((*own_plan[0], 1, bq), jnp.float32))
    scratch = [
        pltpu.VMEM((HD + ONES_ROWS, total), jnp.bfloat16),
        pltpu.VMEM((1, total), jnp.float32),
        pltpu.VMEM((1, total), jnp.float32),
        *[pltpu.VMEM((bk, bq), jnp.float32), pltpu.VMEM((1, bq), jnp.float32)] * 2,
    ]
    return pl.pallas_call(
        functools.partial(forward_kernel, peers, heads, rows, bq, bk, kept),
        in_specs=[SMEM_SPEC] + [VMEM_SPEC] * peers,
        out_specs=[VMEM_SPEC] * len(vectors) + [SMEM_SPEC] * 3,
        out_shape=vectors + [jax.ShapeDtypeStruct(shape, jnp.int32) for shape in plan],
        scratch_shapes=[pltpu.SMEM(shape, jnp.int32) for shape in own_plan] + scratch,
        compiler_params=params([*blocks, *vectors], scratch),
        cost_estimate=attention_cost(total, 3),
    )(me, *blocks)


def attention_backward(me, heads, state, blocks):
    peers, rows = len(blocks), blocks[0].shape[0]
    total = peers * rows
    bq, bk = block_sizes(total)[1]
    vectors, plan = state[:-3], state[-3:]
    kept = keeps_list(total, peers, heads)
    out_shape = [jax.ShapeDtypeStruct((3 * rows, HD), jnp.bfloat16)] * heads
    scratch = [
        pltpu.VMEM((total, HD), jnp.bfloat16),
        pltpu.VMEM((HD, total), jnp.bfloat16),
        pltpu.VMEM((1, total), jnp.float32),
        pltpu.VMEM((total, HD), jnp.float32),
        pltpu.VMEM((total, HD), jnp.float32),
        pltpu.VMEM((HD, total), jnp.float32),
        *[pltpu.VMEM((bk, bq), jnp.bfloat16)] * 4,
    ]
    return pl.pallas_call(
        functools.partial(backward_kernel, peers, heads, rows, bq, bk, kept),
        in_specs=[SMEM_SPEC] * 4 + [VMEM_SPEC] * (len(vectors) + peers),
        out_specs=[VMEM_SPEC] * heads,
        out_shape=out_shape,
        scratch_shapes=scratch,
        compiler_params=params([*vectors, *blocks, *out_shape], scratch),
        cost_estimate=attention_cost(total, 5),
    )(me, *plan, *vectors, *blocks)


def per_device(peers, groups, queries, keys_in, values, out_grad, out_weight, doc_ids):
    rows, width = queries.shape
    heads = width // HD
    me = lax.axis_index("seq")
    me_vector = me.reshape(1)

    def exchange(x, d):
        return x if d == 0 else lax.ppermute(x, "seq", [(i, i ^ d) for i in range(peers)])

    def pass_on(x):
        return lax.ppermute(x, "head", [(i, (i + 1) % groups) for i in range(groups)])

    order = [*range(2, peers, 2), *range(peers - 1, 0, -2)]

    def exchange_all(blocks, wanted):
        moved = {d: exchange(blocks[d % heads], d) for d in order if d < wanted}
        return [blocks[0]] + [moved[d] for d in range(1, wanted)]

    packed = list(pack_heads(me_vector, queries, keys_in, values, doc_ids))
    received = exchange_all(packed, peers)

    def share(step):
        return len(order) * step * (step + 1) // ((groups - 2) * (groups - 1))

    after = lax.optimization_barrier
    features, acc = out_grad, None
    weights = []
    for step in range(groups):
        block = lax.rem(lax.axis_index("head") + groups - step, groups)
        weights.append(lax.dynamic_slice_in_dim(out_weight, block * width, width, 1))
    for step in range(groups):
        last = step == groups - 1
        if not last:
            passed = pass_on(features)
        if step == groups - 2:
            received[0], features = after((received[0], features))
            state = list(attention_forward(me_vector, received, rows, heads))
            features, state[1] = after((features, state[1]))
        acc = project(me_vector, weights[step], features, acc, last)
        if not last:
            features = passed
            if step < groups - 2:
                batch = order[share(step):share(step + 1)]
                here = [received[d] for d in batch]
                features, acc, here, weights[2:] = after((features, acc, here, weights[2:]))
                for d, block in zip(batch, here):
                    received[d] = block
    grads = exchange_all(acc, peers)

    results = attention_backward(me_vector, heads, state, grads)
    returned = exchange_all(results, heads)
    return tuple(unpack_heads(me_vector, returned, rows))


def solution(mesh):
    in_specs = (
        P("seq", "head"),
        P("seq", "head"),
        P("seq", "head"),
        P("seq", "head"),
        P("head", None),
        P("seq"),
    )
    out_specs = (P("seq", "head"), P("seq", "head"), P("seq", "head"))
    return jax.shard_map(
        functools.partial(per_device, mesh.shape["seq"], mesh.shape["head"]),
        mesh=mesh, in_specs=in_specs, out_specs=out_specs, check_vma=False,
    )
```

```python
import functools
import math

import jax
import jax.numpy as jnp
from jax import lax
from jax.experimental import pallas as pl
from jax.experimental.pallas import tpu as pltpu
from jax.sharding import PartitionSpec as P

HD = 128
DOC_VALUES = 8
DOC_ROWS = 16
ONES_ROWS = 16
NEG_LARGE = -1e30
VMEM_SPARE = 6 * 1024 * 1024
LIST_BYTES = 16 * 1024 * 1024

NN = (((1,), (0,)), ((), ()))
NT = (((1,), (1,)), ((), ()))
SMEM_SPEC = pl.BlockSpec(memory_space=pltpu.SMEM)
VMEM_SPEC = pl.BlockSpec(memory_space=pltpu.VMEM)


def dot32(a, b, dims=NN):
    return lax.dot_general(a, b, dims, preferred_element_type=jnp.float32)


def block_size(total, wanted):
    size = min(wanted, total)
    while total % size or size % 128:
        size -= 128
    return size


def aligned(index, size):
    return pl.ds(pl.multiple_of(index * size, size), size)


def params(arrays, scratch=()):
    total = sum(math.prod(a.shape) * jnp.dtype(a.dtype).itemsize for a in (*arrays, *scratch))
    return pltpu.CompilerParams(vmem_limit_bytes=total + VMEM_SPARE)


def pack_kernel(heads, rows, me_s, q_ref, k_ref, v_ref, doc_ref, *refs):
    outs, done = refs[:heads], refs[heads]
    own = lax.rem(me_s[0], heads)
    copies = []
    for d, out in enumerate(outs):
        columns = aligned(own ^ d, HD)
        for part, ref in enumerate((q_ref, k_ref, v_ref)):
            place = out.at[pl.ds(part * rows, rows), :]
            copies.append(pltpu.make_async_copy(ref.at[:, columns], place, done.at[d, part]))
            copies[-1].start()
    docs = doc_ref[...].astype(jnp.float32)
    docs = jnp.concatenate([docs, jnp.zeros((DOC_ROWS - docs.shape[0], HD), jnp.float32)], axis=0)
    docs = docs.astype(jnp.bfloat16)
    for out in outs:
        out[3 * rows:, :] = docs
    for copy in copies:
        copy.wait()


def pack_heads(me, q, k, v, doc_ids):
    rows, width = q.shape
    heads = width // HD
    out_shape = [jax.ShapeDtypeStruct((3 * rows + DOC_ROWS, HD), q.dtype)] * heads
    return pl.pallas_call(
        functools.partial(pack_kernel, heads, rows),
        in_specs=[SMEM_SPEC] + [pl.BlockSpec(memory_space=pltpu.HBM)] * 3 + [VMEM_SPEC],
        out_specs=[VMEM_SPEC] * heads,
        out_shape=out_shape,
        scratch_shapes=[pltpu.SemaphoreType.DMA((heads, 3))],
        compiler_params=params(out_shape),
    )(me, q, k, v, doc_ids.reshape(rows // HD, HD))


def unpack_kernel(heads, rows, me_s, *refs):
    own = lax.rem(me_s[0], heads)
    for d in range(heads):
        columns = aligned(own ^ d, HD)
        for part in range(3):
            refs[heads + part][:, columns] = refs[d][part * rows:(part + 1) * rows, :]


def unpack_heads(me, blocks, rows):
    heads = len(blocks)
    return pl.pallas_call(
        functools.partial(unpack_kernel, heads, rows),
        in_specs=[SMEM_SPEC] + [VMEM_SPEC] * heads,
        out_specs=[VMEM_SPEC] * 3,
        out_shape=[jax.ShapeDtypeStruct((rows, heads * HD), blocks[0].dtype)] * 3,
        compiler_params=params([*blocks, *blocks]),
    )(me, *blocks)


def project_kernel(first, o_ref, w_ref, *refs):
    out_ref = refs[-1]
    for pair in range(w_ref.shape[0] // (2 * HD)):
        part = slice(pair * 2 * HD, (pair + 1) * 2 * HD)
        both = dot32(o_ref[...], w_ref[part, :], NT)
        out_ref[:, part] = both if first else refs[0][:, part] + both


def project_last_kernel(me_s, o_ref, w_ref, acc_ref, upper_ref, *outs):
    pairs = len(outs) // 2
    odd = lax.rem(me_s[0], 2) == 1
    cut = upper_ref.shape[0]
    for j in range(pairs):
        part = aligned(lax.rem(me_s[0] // 2, pairs) ^ j, 2 * HD)
        lower = acc_ref[:, part] + dot32(o_ref[...], w_ref[part, :], NT)
        for place, value in ((slice(0, cut), upper_ref[:, part]), (slice(cut, None), lower)):
            both = value.astype(jnp.bfloat16)
            outs[2 * j][place, :] = jnp.where(odd, both[:, HD:], both[:, :HD])
            outs[2 * j + 1][place, :] = jnp.where(odd, both[:, :HD], both[:, HD:])


def project(me, weight, features, acc, upper=None):
    rows, width = features.shape
    columns = weight.shape[0]
    heads = columns // HD
    total = jax.ShapeDtypeStruct((rows, columns), jnp.float32)
    cost = pl.CostEstimate(
        flops=2 * rows * width * columns,
        bytes_accessed=2 * width * columns + 8 * rows * columns,
        transcendentals=0,
    )
    if upper is not None:
        return pl.pallas_call(
            project_last_kernel,
            in_specs=[SMEM_SPEC] + [VMEM_SPEC] * 4,
            out_specs=[VMEM_SPEC] * heads,
            out_shape=[jax.ShapeDtypeStruct((upper.shape[0] + rows, HD), jnp.bfloat16)] * heads,
            compiler_params=params([features, weight, total, upper, upper]),
            cost_estimate=cost,
        )(me, features, weight, acc, upper)
    operands = (features, weight) + (() if acc is None else (acc,))
    return pl.pallas_call(
        functools.partial(project_kernel, acc is None),
        in_specs=[VMEM_SPEC] * len(operands),
        out_specs=VMEM_SPEC,
        out_shape=total,
        compiler_params=params([features, weight, total, total]),
        cost_estimate=cost,
    )(*operands)


def at_or_before(q0, k0, shape):
    key = lax.broadcasted_iota(jnp.int32, shape, 0)
    return key <= q0 - k0 + lax.broadcasted_iota(jnp.int32, (1, shape[1]), 1)


def block_sizes(total):
    return (
        (block_size(total, 256), block_size(total, 256)),
        (block_size(total, 256), block_size(total, 256)),
    )


def plan_size(total, bq, bk):
    return sum(((q + 1) * bq + bk - 1) // bk for q in range(total // bq)) + 2


def fill_plan(lows, total, bq, bk, own, plan_q, plan_k, count_ref):
    def put(qi):
        def at(ki, count):
            plan_q[count] = qi
            plan_k[count] = ki
            return count + 1

        return at

    spans = []
    for qi, low in enumerate(lows):
        low, high = low // bk, ((qi + 1) * bq + bk - 1) // bk
        if own is not None:
            wanted = ((qi + 1) * bq > own[0]) & (qi * bq < own[1])
            low = jnp.where(wanted, low, jnp.maximum(low, own[0] // bk))
            high = jnp.where(wanted, high, jnp.minimum(high, (own[1] + bk - 1) // bk))
        whole = jnp.maximum(low, jnp.minimum(high, qi * bq // bk))
        spans.append((low, whole, high))
    count = 0
    for qi, (low, whole, high) in enumerate(spans):
        count = lax.fori_loop(low, whole, put(qi), count)
    count_ref[0] = jnp.maximum(count - 1, 0) // 2
    for qi, (low, whole, high) in enumerate(spans):
        count = lax.fori_loop(whole, high, put(qi), count)
    count_ref[1] = (count + 1) // 2
    for spare in range(2):
        plan_q[count + spare] = 0
        plan_k[count + spare] = total // bk - 1


def pipelined(plan_q, plan_k, count_ref, early, late, buffers):
    early(0, plan_q[0], plan_k[0], buffers[0], True)

    def turns(diagonal):
        def body(i, carry):
            for turn in range(2):
                now = 2 * i + turn
                late(now, plan_q[now], plan_k[now], buffers[turn])
                early(now + 1, plan_q[now + 1], plan_k[now + 1], buffers[1 - turn], diagonal)
            return carry

        return body

    lax.fori_loop(0, count_ref[0], turns(False), 0)
    lax.fori_loop(count_ref[0], count_ref[1], turns(True), 0)


def forward_kernel(peers, heads, rows, bq, bk, kept, me_s, *refs):
    blocks = refs[:peers]
    if kept:
        p_list, top_list = refs[peers + 7:peers + 9]
        refs = refs[:peers + 7] + refs[peers + 9:]
    q_ref, v_ref, kx_ref, qtx_ref, kt_ref, out_ref, log_ref = refs[peers:peers + 7]
    plan_q, plan_k, count_ref, own_q, own_k, own_count = refs[peers + 7:peers + 13]
    vt_ref, doc_ref, sum_ref, s0, top0, s1, top1 = refs[peers + 13:]
    total = q_ref.shape[0]
    factor = HD ** (-0.5) * math.log2(math.e)
    me = me_s[0]
    for d, block in enumerate(blocks):
        place = me ^ d
        for part, ref in enumerate((q_ref, kx_ref.at[:, :HD], v_ref)):
            ref[aligned(place, rows), :] = block[part * rows:(part + 1) * rows, :]
        docs = block[3 * rows:, :].astype(jnp.float32)
        for t in range(rows // HD):
            doc_ref[:, aligned(place * (rows // HD) + t, HD)] = docs[t:t + 1, :]
    docs = doc_ref[...]
    first = jnp.zeros(docs.shape, jnp.float32)
    for value in range(1, DOC_VALUES):
        before = jnp.sum((docs < value).astype(jnp.float32))
        first = jnp.where(docs >= value, before, first)
    first = first.astype(jnp.int32)
    lows = [jnp.min(first[:, qi * bq:(qi + 1) * bq]) for qi in range(total // bq)]
    fill_plan(lows, total, bq, bk, None, own_q, own_k, own_count)
    group = (me // heads) * heads * rows
    own = None if heads == peers else (group, group + heads * rows)
    back_q, back_k = block_sizes(total)[1]
    lows = [jnp.min(first[:, qi * back_q:(qi + 1) * back_q]) for qi in range(total // back_q)]
    fill_plan(lows, total, back_q, back_k, own, plan_q, plan_k, count_ref)
    same = lax.broadcasted_iota(jnp.int32, (HD, total), 0).astype(jnp.float32) == docs
    qtx_ref[:HD, :] = q_ref[...].T
    qtx_ref[HD:, :] = jnp.where(same, 0.0, NEG_LARGE).astype(jnp.bfloat16)
    kx_ref[:, HD:] = jnp.where(same, 1.0, 0.0).astype(jnp.bfloat16).T
    kt_ref[...] = kx_ref[:, :HD].T
    vt_ref[:HD, :] = v_ref[...].T
    vt_ref[HD:, :] = jnp.ones((ONES_ROWS, total), jnp.bfloat16)
    out_ref[...] = jnp.zeros_like(out_ref)
    log_ref[...] = jnp.full_like(log_ref, NEG_LARGE)
    sum_ref[...] = jnp.zeros_like(sum_ref)

    def early(now, qi, ki, buffer, diagonal):
        s_ref, top_ref = buffer
        keys, queries = aligned(ki, bk), aligned(qi, bq)
        s = dot32(kx_ref[keys, :], qtx_ref[:, queries]) * factor
        if diagonal:
            s = jnp.where(at_or_before(qi * bq, ki * bk, (bk, bq)), s, NEG_LARGE)
        s_ref[...] = s
        top_ref[...] = jnp.max(s, axis=0, keepdims=True)

    def late(now, qi, ki, buffer):
        s_ref, top_ref = buffer
        keys, queries = aligned(ki, bk), aligned(qi, bq)
        top = log_ref[:, queries]
        new_top = jnp.maximum(top, top_ref[...])
        p = jnp.exp2(s_ref[...] - new_top)
        fix = jnp.exp2(top - new_top)
        high = p.astype(jnp.bfloat16)
        vt = vt_ref[:, keys]
        sums = dot32(vt, high)
        if kept:
            p_list[now] = high
            top_list[now] = new_top
        else:
            sums = sums + dot32(vt, (p - high.astype(jnp.float32)).astype(jnp.bfloat16))
        out_ref[:, queries] = out_ref[:, queries] * fix + sums[:HD, :]
        sum_ref[:, queries] = sum_ref[:, queries] * fix + sums[HD:HD + 1, :]
        log_ref[:, queries] = new_top

    pipelined(own_q, own_k, own_count, early, late, ((s0, top0), (s1, top1)))
    total_p = sum_ref[...]
    out_ref[...] = out_ref[...] / total_p
    log_ref[...] = log_ref[...] + jnp.log2(total_p)


def backward_kernel(peers, heads, rows, bq, bk, kept, me_s, plan_q, plan_k, count_ref, q_ref, v_ref,
                    kx_ref, qtx_ref, kt_ref, out_ref, log_ref, *refs):
    if kept:
        p_list, top_list = refs[:2]
        refs = refs[2:]
    blocks = refs[:peers]
    results = refs[peers:peers + heads]
    g_ref, gt_ref, dot_ref, dk_acc, dv_acc, dq_acc, p0, ds0, p1, ds1 = refs[peers + heads:]
    scale = HD ** (-0.5)
    factor = scale * math.log2(math.e)
    me = me_s[0]
    for d, block in enumerate(blocks):
        g_ref[aligned(me ^ d, rows), :] = block[...]
    gt_ref[...] = g_ref[...].T
    dot_ref[...] = jnp.sum(gt_ref[...].astype(jnp.float32) * out_ref[...], axis=0, keepdims=True)
    dk_acc[...] = jnp.zeros_like(dk_acc)
    dv_acc[...] = jnp.zeros_like(dv_acc)
    dq_acc[...] = jnp.zeros_like(dq_acc)

    def early(now, qi, ki, buffer, diagonal):
        p_ref, ds_ref = buffer
        keys, queries = aligned(ki, bk), aligned(qi, bq)
        log_row = log_ref[:, queries]
        if kept:
            p = p_list[now].astype(jnp.float32) * jnp.exp2(top_list[now] - log_row)
        else:
            p = jnp.exp2(dot32(kx_ref[keys, :], qtx_ref[:, queries]) * factor - log_row)
            if diagonal:
                p = jnp.where(at_or_before(qi * bq, ki * bk, (bk, bq)), p, 0.0)
        p_ref[...] = p.astype(jnp.bfloat16)
        dp = dot32(v_ref[keys, :], gt_ref[:, queries])
        ds_ref[...] = (p * (dp - dot_ref[:, queries])).astype(jnp.bfloat16)

    def late(now, qi, ki, buffer):
        p_ref, ds_ref = buffer
        keys, queries = aligned(ki, bk), aligned(qi, bq)
        dv_acc[keys, :] += dot32(p_ref[...], g_ref[queries, :])
        dk_acc[keys, :] += dot32(ds_ref[...], q_ref[queries, :])
        dq_acc[:, queries] += dot32(kt_ref[:, keys], ds_ref[...])

    pipelined(plan_q, plan_k, count_ref, early, late, ((p0, ds0), (p1, ds1)))
    for d, result in enumerate(results):
        own = aligned(me ^ d, rows)
        result[:rows, :] = (scale * dq_acc[:, own]).astype(result.dtype).T
        result[rows:2 * rows, :] = (scale * dk_acc[own, :]).astype(result.dtype)
        result[2 * rows:, :] = dv_acc[own, :].astype(result.dtype)


def keeps_list(total, peers, heads):
    forward, backward = block_sizes(total)
    size = plan_size(total, *forward) * math.prod(forward) * 2
    return forward == backward and heads == peers and size <= LIST_BYTES


def attention_cost(total, products):
    return pl.CostEstimate(
        flops=products * total * total * HD // 2,
        bytes_accessed=16 * total * HD,
        transcendentals=total * total // 4,
    )


def attention_forward(me, blocks, rows, heads):
    peers = len(blocks)
    total = peers * rows
    (bq, bk), back = block_sizes(total)
    plan = [(plan_size(total, *back),)] * 2 + [(2,)]
    own_plan = [(plan_size(total, bq, bk),)] * 2 + [(2,)]
    vectors = [
        *[jax.ShapeDtypeStruct((total, HD), jnp.bfloat16)] * 2,
        jax.ShapeDtypeStruct((total, 2 * HD), jnp.bfloat16),
        jax.ShapeDtypeStruct((2 * HD, total), jnp.bfloat16),
        jax.ShapeDtypeStruct((HD, total), jnp.bfloat16),
        jax.ShapeDtypeStruct((HD, total), jnp.float32),
        jax.ShapeDtypeStruct((1, total), jnp.float32),
    ]
    kept = keeps_list(total, peers, heads)
    if kept:
        vectors.append(jax.ShapeDtypeStruct((*own_plan[0], bk, bq), jnp.bfloat16))
        vectors.append(jax.ShapeDtypeStruct((*own_plan[0], 1, bq), jnp.float32))
    scratch = [
        pltpu.VMEM((HD + ONES_ROWS, total), jnp.bfloat16),
        pltpu.VMEM((1, total), jnp.float32),
        pltpu.VMEM((1, total), jnp.float32),
        *[pltpu.VMEM((bk, bq), jnp.float32), pltpu.VMEM((1, bq), jnp.float32)] * 2,
    ]
    return pl.pallas_call(
        functools.partial(forward_kernel, peers, heads, rows, bq, bk, kept),
        in_specs=[SMEM_SPEC] + [VMEM_SPEC] * peers,
        out_specs=[VMEM_SPEC] * len(vectors) + [SMEM_SPEC] * 3,
        out_shape=vectors + [jax.ShapeDtypeStruct(shape, jnp.int32) for shape in plan],
        scratch_shapes=[pltpu.SMEM(shape, jnp.int32) for shape in own_plan] + scratch,
        compiler_params=params([*blocks, *vectors], scratch),
        cost_estimate=attention_cost(total, 3),
    )(me, *blocks)


def attention_backward(me, heads, state, blocks):
    peers, rows = len(blocks), blocks[0].shape[0]
    total = peers * rows
    bq, bk = block_sizes(total)[1]
    vectors, plan = state[:-3], state[-3:]
    kept = keeps_list(total, peers, heads)
    out_shape = [jax.ShapeDtypeStruct((3 * rows, HD), jnp.bfloat16)] * heads
    scratch = [
        pltpu.VMEM((total, HD), jnp.bfloat16),
        pltpu.VMEM((HD, total), jnp.bfloat16),
        pltpu.VMEM((1, total), jnp.float32),
        pltpu.VMEM((total, HD), jnp.float32),
        pltpu.VMEM((total, HD), jnp.float32),
        pltpu.VMEM((HD, total), jnp.float32),
        *[pltpu.VMEM((bk, bq), jnp.bfloat16)] * 4,
    ]
    return pl.pallas_call(
        functools.partial(backward_kernel, peers, heads, rows, bq, bk, kept),
        in_specs=[SMEM_SPEC] * 4 + [VMEM_SPEC] * (len(vectors) + peers),
        out_specs=[VMEM_SPEC] * heads,
        out_shape=out_shape,
        scratch_shapes=scratch,
        compiler_params=params([*vectors, *blocks, *out_shape], scratch),
        cost_estimate=attention_cost(total, 5),
    )(me, *plan, *vectors, *blocks)


def per_device(peers, groups, queries, keys_in, values, out_grad, out_weight, doc_ids):
    rows, width = queries.shape
    heads = width // HD
    me = lax.axis_index("seq")
    me_vector = me.reshape(1)

    def exchange(x, d):
        return x if d == 0 else lax.ppermute(x, "seq", [(i, i ^ d) for i in range(peers)])

    def pass_on(x):
        return lax.ppermute(x, "head", [(i, (i + 1) % groups) for i in range(groups)])

    order = [*range(2, peers, 2), *range(peers - 1, 0, -2)]

    def exchange_all(blocks, wanted):
        moved = {d: exchange(blocks[d % heads], d) for d in order if d < wanted}
        return [blocks[0]] + [moved[d] for d in range(1, wanted)]

    packed = list(pack_heads(me_vector, queries, keys_in, values, doc_ids))
    received = exchange_all(packed, peers)

    after = lax.optimization_barrier
    weights = []
    for step in range(groups):
        block = lax.rem(lax.axis_index("head") + groups - step, groups)
        weights.append(lax.dynamic_slice_in_dim(out_weight, block * width, width, 1))

    cut = 2 * rows // 3 // 16 * 16
    upper, lower = out_grad[:cut], out_grad[cut:]
    upper_acc, lower_acc = None, None
    gates = [0, 1] + [1 + (len(order) - 2) * step // max(groups - 3, 1) for step in range(1, groups - 2)]
    for step in range(groups):
        passed_upper = pass_on(upper) if step < groups - 1 else None
        passed_lower = pass_on(lower) if step > 0 else None
        if step == groups - 2:
            received[0], upper, lower = after((received[0], upper, lower))
            state = list(attention_forward(me_vector, received, rows, heads))
            upper, lower, state[1] = after((upper, lower, state[1]))
        upper_acc = project(me_vector, weights[step], upper, upper_acc)
        if step > 0:
            lower_acc = project(me_vector, weights[step - 1], lower, lower_acc)
            lower = passed_lower
        if step < groups - 1:
            upper = passed_upper
            batch = order[gates[step]:gates[step + 1]] if step < groups - 2 else []
            here = [received[d] for d in batch]
            fixed = [upper_acc] + ([lower_acc] if step > 0 else [])
            upper, lower, fixed, here, weights[2:] = after((upper, lower, fixed, here, weights[2:]))
            upper_acc = fixed[0]
            lower_acc = fixed[1] if step > 0 else None
            for d, block in zip(batch, here):
                received[d] = block
    acc = project(me_vector, weights[-1], lower, lower_acc, upper_acc)
    grads = exchange_all(acc, peers)

    results = attention_backward(me_vector, heads, state, grads)
    returned = exchange_all(results, heads)
    return tuple(unpack_heads(me_vector, returned, rows))


def solution(mesh):
    in_specs = (
        P("seq", "head"),
        P("seq", "head"),
        P("seq", "head"),
        P("seq", "head"),
        P("head", None),
        P("seq"),
    )
    out_specs = (P("seq", "head"), P("seq", "head"), P("seq", "head"))
    return jax.shard_map(
        functools.partial(per_device, mesh.shape["seq"], mesh.shape["head"]),
        mesh=mesh, in_specs=in_specs, out_specs=out_specs, check_vma=False,
    )
```

```python
import functools
import math

import jax
import jax.numpy as jnp
from jax import lax
from jax.experimental import pallas as pl
from jax.experimental.pallas import tpu as pltpu
from jax.sharding import PartitionSpec as P

HD = 128
DOC_VALUES = 8
DOC_ROWS = 16
ONES_ROWS = 16
NEG_LARGE = -1e30
VMEM_SPARE = 6 * 1024 * 1024
LIST_BYTES = 16 * 1024 * 1024

NN = (((1,), (0,)), ((), ()))
NT = (((1,), (1,)), ((), ()))
SMEM_SPEC = pl.BlockSpec(memory_space=pltpu.SMEM)
VMEM_SPEC = pl.BlockSpec(memory_space=pltpu.VMEM)


def dot32(a, b, dims=NN):
    return lax.dot_general(a, b, dims, preferred_element_type=jnp.float32)


def block_size(total, wanted):
    size = min(wanted, total)
    while total % size or size % 128:
        size -= 128
    return size


def aligned(index, size):
    return pl.ds(pl.multiple_of(index * size, size), size)


def params(arrays, scratch=()):
    total = sum(math.prod(a.shape) * jnp.dtype(a.dtype).itemsize for a in (*arrays, *scratch))
    return pltpu.CompilerParams(vmem_limit_bytes=total + VMEM_SPARE)


def pack_kernel(heads, rows, me_s, q_ref, k_ref, v_ref, doc_ref, *refs):
    outs, done = refs[:heads], refs[heads]
    own = lax.rem(me_s[0], heads)
    copies = []
    for d, out in enumerate(outs):
        columns = aligned(own ^ d, HD)
        for part, ref in enumerate((q_ref, k_ref, v_ref)):
            place = out.at[pl.ds(part * rows, rows), :]
            copies.append(pltpu.make_async_copy(ref.at[:, columns], place, done.at[d, part]))
            copies[-1].start()
    docs = doc_ref[...].astype(jnp.float32)
    docs = jnp.concatenate([docs, jnp.zeros((DOC_ROWS - docs.shape[0], HD), jnp.float32)], axis=0)
    docs = docs.astype(jnp.bfloat16)
    for out in outs:
        out[3 * rows:, :] = docs
    for copy in copies:
        copy.wait()


def pack_heads(me, q, k, v, doc_ids):
    rows, width = q.shape
    heads = width // HD
    out_shape = [jax.ShapeDtypeStruct((3 * rows + DOC_ROWS, HD), q.dtype)] * heads
    return pl.pallas_call(
        functools.partial(pack_kernel, heads, rows),
        in_specs=[SMEM_SPEC] + [pl.BlockSpec(memory_space=pltpu.HBM)] * 3 + [VMEM_SPEC],
        out_specs=[VMEM_SPEC] * heads,
        out_shape=out_shape,
        scratch_shapes=[pltpu.SemaphoreType.DMA((heads, 3))],
        compiler_params=params(out_shape),
    )(me, q, k, v, doc_ids.reshape(rows // HD, HD))


def unpack_kernel(heads, rows, me_s, *refs):
    own = lax.rem(me_s[0], heads)
    for d in range(heads):
        columns = aligned(own ^ d, HD)
        for part in range(3):
            refs[heads + part][:, columns] = refs[d][part * rows:(part + 1) * rows, :]


def unpack_heads(me, blocks, rows):
    heads = len(blocks)
    return pl.pallas_call(
        functools.partial(unpack_kernel, heads, rows),
        in_specs=[SMEM_SPEC] + [VMEM_SPEC] * heads,
        out_specs=[VMEM_SPEC] * 3,
        out_shape=[jax.ShapeDtypeStruct((rows, heads * HD), blocks[0].dtype)] * 3,
        compiler_params=params([*blocks, *blocks]),
    )(me, *blocks)


def project_kernel(first, o_ref, w_ref, *refs):
    out_ref = refs[-1]
    for pair in range(w_ref.shape[0] // (2 * HD)):
        part = slice(pair * 2 * HD, (pair + 1) * 2 * HD)
        both = dot32(o_ref[...], w_ref[part, :], NT)
        out_ref[:, part] = both if first else refs[0][:, part] + both


def project_last_kernel(me_s, o_ref, w_ref, acc_ref, *outs):
    pairs = len(outs) // 2
    odd = lax.rem(me_s[0], 2) == 1
    for j in range(pairs):
        part = aligned(lax.rem(me_s[0] // 2, pairs) ^ j, 2 * HD)
        both = (acc_ref[:, part] + dot32(o_ref[...], w_ref[part, :], NT)).astype(jnp.bfloat16)
        outs[2 * j][...] = jnp.where(odd, both[:, HD:], both[:, :HD])
        outs[2 * j + 1][...] = jnp.where(odd, both[:, :HD], both[:, HD:])


def project(me, weight, features, acc, last):
    rows, width = features.shape
    columns = weight.shape[0]
    heads = columns // HD
    total = jax.ShapeDtypeStruct((rows, columns), jnp.float32)
    cost = pl.CostEstimate(
        flops=2 * rows * width * columns,
        bytes_accessed=2 * width * columns + 8 * rows * columns,
        transcendentals=0,
    )
    if last:
        return pl.pallas_call(
            project_last_kernel,
            in_specs=[SMEM_SPEC] + [VMEM_SPEC] * 3,
            out_specs=[VMEM_SPEC] * heads,
            out_shape=[jax.ShapeDtypeStruct((rows, HD), jnp.bfloat16)] * heads,
            compiler_params=params([features, weight, total, total]),
            cost_estimate=cost,
        )(me, features, weight, acc)
    operands = (features, weight) + (() if acc is None else (acc,))
    return pl.pallas_call(
        functools.partial(project_kernel, acc is None),
        in_specs=[VMEM_SPEC] * len(operands),
        out_specs=VMEM_SPEC,
        out_shape=total,
        compiler_params=params([features, weight, total, total]),
        cost_estimate=cost,
    )(*operands)


def at_or_before(q0, k0, shape):
    key = lax.broadcasted_iota(jnp.int32, shape, 0)
    return key <= q0 - k0 + lax.broadcasted_iota(jnp.int32, (1, shape[1]), 1)


def block_sizes(total):
    return (
        (block_size(total, 256), block_size(total, 256)),
        (block_size(total, 256), block_size(total, 256)),
    )


def plan_size(total, bq, bk):
    return sum(((q + 1) * bq + bk - 1) // bk for q in range(total // bq)) + 2


def fill_plan(lows, total, bq, bk, own, plan_q, plan_k, count_ref):
    def put(qi):
        def at(ki, count):
            plan_q[count] = qi
            plan_k[count] = ki
            return count + 1

        return at

    spans = []
    for qi, low in enumerate(lows):
        low, high = low // bk, ((qi + 1) * bq + bk - 1) // bk
        if own is not None:
            wanted = ((qi + 1) * bq > own[0]) & (qi * bq < own[1])
            low = jnp.where(wanted, low, jnp.maximum(low, own[0] // bk))
            high = jnp.where(wanted, high, jnp.minimum(high, (own[1] + bk - 1) // bk))
        whole = jnp.maximum(low, jnp.minimum(high, qi * bq // bk))
        spans.append((low, whole, high))
    count = 0
    for qi, (low, whole, high) in enumerate(spans):
        count = lax.fori_loop(low, whole, put(qi), count)
    count_ref[0] = jnp.maximum(count - 1, 0) // 2
    for qi, (low, whole, high) in enumerate(spans):
        count = lax.fori_loop(whole, high, put(qi), count)
    count_ref[1] = (count + 1) // 2
    for spare in range(2):
        plan_q[count + spare] = 0
        plan_k[count + spare] = total // bk - 1


def pipelined(plan_q, plan_k, count_ref, early, late, buffers):
    early(0, plan_q[0], plan_k[0], buffers[0], True)

    def turns(diagonal):
        def body(i, carry):
            for turn in range(2):
                now = 2 * i + turn
                late(now, plan_q[now], plan_k[now], buffers[turn])
                early(now + 1, plan_q[now + 1], plan_k[now + 1], buffers[1 - turn], diagonal)
            return carry

        return body

    lax.fori_loop(0, count_ref[0], turns(False), 0)
    lax.fori_loop(count_ref[0], count_ref[1], turns(True), 0)


def forward_kernel(peers, heads, rows, bq, bk, kept, me_s, *refs):
    blocks = refs[:peers]
    if kept:
        p_list, top_list = refs[peers + 6:peers + 8]
        refs = refs[:peers + 6] + refs[peers + 8:]
    v_ref, qx_ref, kx_ref, kt_ref, rows_ref, log_ref = refs[peers:peers + 6]
    plan_q, plan_k, count_ref, own_q, own_k, own_count = refs[peers + 6:peers + 12]
    vt_ref, out_ref, doc_ref, sum_ref, s0, top0, s1, top1 = refs[peers + 12:]
    total = v_ref.shape[0]
    factor = HD ** (-0.5) * math.log2(math.e)
    me = me_s[0]
    for d, block in enumerate(blocks):
        place = me ^ d
        for part, ref in enumerate((qx_ref.at[:, :HD], kx_ref.at[:, :HD], v_ref)):
            ref[aligned(place, rows), :] = block[part * rows:(part + 1) * rows, :]
        docs = block[3 * rows:, :].astype(jnp.float32)
        for t in range(rows // HD):
            doc_ref[:, aligned(place * (rows // HD) + t, HD)] = docs[t:t + 1, :]
    docs = doc_ref[...]
    first = jnp.zeros(docs.shape, jnp.float32)
    for value in range(1, DOC_VALUES):
        before = jnp.sum((docs < value).astype(jnp.float32))
        first = jnp.where(docs >= value, before, first)
    first = first.astype(jnp.int32)
    lows = [jnp.min(first[:, qi * bq:(qi + 1) * bq]) for qi in range(total // bq)]
    fill_plan(lows, total, bq, bk, None, own_q, own_k, own_count)
    group = (me // heads) * heads * rows
    own = None if heads == peers else (group, group + heads * rows)
    back_q, back_k = block_sizes(total)[1]
    lows = [jnp.min(first[:, qi * back_q:(qi + 1) * back_q]) for qi in range(total // back_q)]
    fill_plan(lows, total, back_q, back_k, own, plan_q, plan_k, count_ref)
    same = lax.broadcasted_iota(jnp.int32, (HD, total), 0).astype(jnp.float32) == docs
    ones = jnp.where(same, 1.0, 0.0).astype(jnp.bfloat16).T
    kx_ref[:, HD:] = ones
    qx_ref[:, HD:] = ((1.0 - ones.astype(jnp.float32)) * NEG_LARGE).astype(jnp.bfloat16)
    kt_ref[...] = kx_ref[:, :HD].T
    vt_ref[:HD, :] = v_ref[...].T
    vt_ref[HD:, :] = jnp.ones((ONES_ROWS, total), jnp.bfloat16)
    out_ref[...] = jnp.zeros_like(out_ref)
    log_ref[...] = jnp.full_like(log_ref, NEG_LARGE)
    sum_ref[...] = jnp.zeros_like(sum_ref)

    def early(now, qi, ki, buffer, diagonal):
        s_ref, top_ref = buffer
        keys, queries = aligned(ki, bk), aligned(qi, bq)
        s = dot32(kx_ref[keys, :], qx_ref[queries, :], NT) * factor
        if diagonal:
            s = jnp.where(at_or_before(qi * bq, ki * bk, (bk, bq)), s, NEG_LARGE)
        s_ref[...] = s
        top_ref[...] = jnp.max(s, axis=0, keepdims=True)

    def late(now, qi, ki, buffer):
        s_ref, top_ref = buffer
        keys, queries = aligned(ki, bk), aligned(qi, bq)
        top = log_ref[:, queries]
        new_top = jnp.maximum(top, top_ref[...])
        p = jnp.exp2(s_ref[...] - new_top)
        fix = jnp.exp2(top - new_top)
        high = p.astype(jnp.bfloat16)
        vt = vt_ref[:, keys]
        sums = dot32(vt, high)
        if kept:
            p_list[now] = high
            top_list[now] = new_top
        else:
            sums = sums + dot32(vt, (p - high.astype(jnp.float32)).astype(jnp.bfloat16))
        out_ref[:, queries] = out_ref[:, queries] * fix + sums[:HD, :]
        sum_ref[:, queries] = sum_ref[:, queries] * fix + sums[HD:HD + 1, :]
        log_ref[:, queries] = new_top

    pipelined(own_q, own_k, own_count, early, late, ((s0, top0), (s1, top1)))
    total_p = sum_ref[...]
    rows_ref[...] = (out_ref[...] / total_p).T
    log_ref[...] = log_ref[...] + jnp.log2(total_p)


def backward_kernel(peers, heads, rows, bq, bk, kept, me_s, plan_q, plan_k, count_ref, v_ref,
                    qx_ref, kx_ref, kt_ref, rows_ref, log_ref, *refs):
    if kept:
        p_list, top_list = refs[:2]
        refs = refs[2:]
    blocks = refs[:peers]
    results = refs[peers:peers + heads]
    g_ref, dot_ref, dk_acc, dv_acc, dq_acc, p0, ds0, p1, ds1 = refs[peers + heads:]
    scale = HD ** (-0.5)
    factor = scale * math.log2(math.e)
    me = me_s[0]
    for d, block in enumerate(blocks):
        g_ref[aligned(me ^ d, rows), :] = block[...]
    ones = jnp.ones((ONES_ROWS, HD), jnp.bfloat16)
    for start in range(0, g_ref.shape[0], bq):
        part = slice(start, start + bq)
        left = g_ref[part, :].astype(jnp.float32) * rows_ref[part, :]
        dots = 0.0
        for _ in range(3):
            term = left.astype(jnp.bfloat16)
            left = left - term.astype(jnp.float32)
            dots = dots + dot32(ones, term, NT)
        dot_ref[:, part] = dots[:1, :]
    dk_acc[...] = jnp.zeros_like(dk_acc)
    dv_acc[...] = jnp.zeros_like(dv_acc)
    dq_acc[...] = jnp.zeros_like(dq_acc)

    def early(now, qi, ki, buffer, diagonal):
        p_ref, ds_ref = buffer
        keys, queries = aligned(ki, bk), aligned(qi, bq)
        log_row = log_ref[:, queries]
        if kept:
            p = p_list[now].astype(jnp.float32) * jnp.exp2(top_list[now] - log_row)
        else:
            p = jnp.exp2(dot32(kx_ref[keys, :], qx_ref[queries, :], NT) * factor - log_row)
            if diagonal:
                p = jnp.where(at_or_before(qi * bq, ki * bk, (bk, bq)), p, 0.0)
        p_ref[...] = p.astype(jnp.bfloat16)
        dp = dot32(v_ref[keys, :], g_ref[queries, :], NT)
        ds_ref[...] = (p * (dp - dot_ref[:, queries])).astype(jnp.bfloat16)

    def late(now, qi, ki, buffer):
        p_ref, ds_ref = buffer
        keys, queries = aligned(ki, bk), aligned(qi, bq)
        dv_acc[keys, :] += dot32(p_ref[...], g_ref[queries, :])
        dk_acc[keys, :] += dot32(ds_ref[...], qx_ref[queries, :HD])
        dq_acc[:, queries] += dot32(kt_ref[:, keys], ds_ref[...])

    pipelined(plan_q, plan_k, count_ref, early, late, ((p0, ds0), (p1, ds1)))
    for d, result in enumerate(results):
        own = aligned(me ^ d, rows)
        result[:rows, :] = (scale * dq_acc[:, own]).astype(result.dtype).T
        result[rows:2 * rows, :] = (scale * dk_acc[own, :]).astype(result.dtype)
        result[2 * rows:, :] = dv_acc[own, :].astype(result.dtype)


def keeps_list(total, peers, heads):
    forward, backward = block_sizes(total)
    size = plan_size(total, *forward) * math.prod(forward) * 2
    return forward == backward and heads == peers and size <= LIST_BYTES


def attention_cost(total, products):
    return pl.CostEstimate(
        flops=products * total * total * HD // 2,
        bytes_accessed=16 * total * HD,
        transcendentals=total * total // 4,
    )


def attention_forward(me, blocks, rows, heads):
    peers = len(blocks)
    total = peers * rows
    (bq, bk), back = block_sizes(total)
    plan = [(plan_size(total, *back),)] * 2 + [(2,)]
    own_plan = [(plan_size(total, bq, bk),)] * 2 + [(2,)]
    vectors = [
        jax.ShapeDtypeStruct((total, HD), jnp.bfloat16),
        *[jax.ShapeDtypeStruct((total, 2 * HD), jnp.bfloat16)] * 2,
        jax.ShapeDtypeStruct((HD, total), jnp.bfloat16),
        jax.ShapeDtypeStruct((total, HD), jnp.float32),
        jax.ShapeDtypeStruct((1, total), jnp.float32),
    ]
    kept = keeps_list(total, peers, heads)
    if kept:
        vectors.append(jax.ShapeDtypeStruct((*own_plan[0], bk, bq), jnp.bfloat16))
        vectors.append(jax.ShapeDtypeStruct((*own_plan[0], 1, bq), jnp.float32))
    scratch = [
        pltpu.VMEM((HD + ONES_ROWS, total), jnp.bfloat16),
        pltpu.VMEM((HD, total), jnp.float32),
        pltpu.VMEM((1, total), jnp.float32),
        pltpu.VMEM((1, total), jnp.float32),
        *[pltpu.VMEM((bk, bq), jnp.float32), pltpu.VMEM((1, bq), jnp.float32)] * 2,
    ]
    return pl.pallas_call(
        functools.partial(forward_kernel, peers, heads, rows, bq, bk, kept),
        in_specs=[SMEM_SPEC] + [VMEM_SPEC] * peers,
        out_specs=[VMEM_SPEC] * len(vectors) + [SMEM_SPEC] * 3,
        out_shape=vectors + [jax.ShapeDtypeStruct(shape, jnp.int32) for shape in plan],
        scratch_shapes=[pltpu.SMEM(shape, jnp.int32) for shape in own_plan] + scratch,
        compiler_params=params([*blocks, *vectors], scratch),
        cost_estimate=attention_cost(total, 3),
    )(me, *blocks)


def attention_backward(me, heads, state, blocks):
    peers, rows = len(blocks), blocks[0].shape[0]
    total = peers * rows
    bq, bk = block_sizes(total)[1]
    vectors, plan = state[:-3], state[-3:]
    kept = keeps_list(total, peers, heads)
    out_shape = [jax.ShapeDtypeStruct((3 * rows, HD), jnp.bfloat16)] * heads
    scratch = [
        pltpu.VMEM((total, HD), jnp.bfloat16),
        pltpu.VMEM((1, total), jnp.float32),
        pltpu.VMEM((total, HD), jnp.float32),
        pltpu.VMEM((total, HD), jnp.float32),
        pltpu.VMEM((HD, total), jnp.float32),
        *[pltpu.VMEM((bk, bq), jnp.bfloat16)] * 4,
    ]
    return pl.pallas_call(
        functools.partial(backward_kernel, peers, heads, rows, bq, bk, kept),
        in_specs=[SMEM_SPEC] * 4 + [VMEM_SPEC] * (len(vectors) + peers),
        out_specs=[VMEM_SPEC] * heads,
        out_shape=out_shape,
        scratch_shapes=scratch,
        compiler_params=params([*vectors, *blocks, *out_shape], scratch),
        cost_estimate=attention_cost(total, 5),
    )(me, *plan, *vectors, *blocks)


def per_device(peers, groups, queries, keys_in, values, out_grad, out_weight, doc_ids):
    rows, width = queries.shape
    heads = width // HD
    me = lax.axis_index("seq")
    me_vector = me.reshape(1)

    def exchange(x, d):
        return x if d == 0 else lax.ppermute(x, "seq", [(i, i ^ d) for i in range(peers)])

    def pass_on(x):
        return lax.ppermute(x, "head", [(i, (i + 1) % groups) for i in range(groups)])

    order = [*range(2, peers, 2), *range(peers - 1, 0, -2)]

    def exchange_all(blocks, wanted):
        moved = {d: exchange(blocks[d % heads], d) for d in order if d < wanted}
        return [blocks[0]] + [moved[d] for d in range(1, wanted)]

    packed = list(pack_heads(me_vector, queries, keys_in, values, doc_ids))
    received = exchange_all(packed, peers)

    def share(step):
        return len(order) * step * (step + 1) // ((groups - 2) * (groups - 1))

    after = lax.optimization_barrier
    features, acc = out_grad, None
    weights = []
    for step in range(groups):
        block = lax.rem(lax.axis_index("head") + groups - step, groups)
        weights.append(lax.dynamic_slice_in_dim(out_weight, block * width, width, 1))
    for step in range(groups):
        last = step == groups - 1
        if not last:
            passed = pass_on(features)
        if step == groups - 2:
            received[0], features = after((received[0], features))
            state = list(attention_forward(me_vector, received, rows, heads))
            features, state[1] = after((features, state[1]))
        acc = project(me_vector, weights[step], features, acc, last)
        if not last:
            features = passed
            if step < groups - 2:
                batch = order[share(step):share(step + 1)]
                here = [received[d] for d in batch]
                features, acc, here, weights[2:] = after((features, acc, here, weights[2:]))
                for d, block in zip(batch, here):
                    received[d] = block
    grads = exchange_all(acc, peers)

    results = attention_backward(me_vector, heads, state, grads)
    returned = exchange_all(results, heads)
    return tuple(unpack_heads(me_vector, returned, rows))


def solution(mesh):
    in_specs = (
        P("seq", "head"),
        P("seq", "head"),
        P("seq", "head"),
        P("seq", "head"),
        P("head", None),
        P("seq"),
    )
    out_specs = (P("seq", "head"), P("seq", "head"), P("seq", "head"))
    return jax.shard_map(
        functools.partial(per_device, mesh.shape["seq"], mesh.shape["head"]),
        mesh=mesh, in_specs=in_specs, out_specs=out_specs, check_vma=False,
    )
```

```python
import functools
import math

import jax
import jax.numpy as jnp
from jax import lax
from jax.experimental import pallas as pl
from jax.experimental.pallas import tpu as pltpu
from jax.sharding import PartitionSpec as P

HD = 128
DOC_VALUES = 8
DOC_ROWS = 16
ONES_ROWS = 16
NEG_LARGE = -1e30
VMEM_SPARE = 6 * 1024 * 1024
LIST_BYTES = 16 * 1024 * 1024

NN = (((1,), (0,)), ((), ()))
NT = (((1,), (1,)), ((), ()))
SMEM_SPEC = pl.BlockSpec(memory_space=pltpu.SMEM)
VMEM_SPEC = pl.BlockSpec(memory_space=pltpu.VMEM)


def dot32(a, b, dims=NN):
    return lax.dot_general(a, b, dims, preferred_element_type=jnp.float32)


def block_size(total, wanted):
    size = min(wanted, total)
    while total % size or size % 128:
        size -= 128
    return size


def aligned(index, size):
    return pl.ds(pl.multiple_of(index * size, size), size)


def params(arrays, scratch=()):
    total = sum(math.prod(a.shape) * jnp.dtype(a.dtype).itemsize for a in (*arrays, *scratch))
    return pltpu.CompilerParams(vmem_limit_bytes=total + VMEM_SPARE)


def pack_kernel(heads, rows, me_s, q_ref, k_ref, v_ref, doc_ref, *refs):
    outs, done = refs[:heads], refs[heads]
    own = lax.rem(me_s[0], heads)
    copies = []
    for d, out in enumerate(outs):
        columns = aligned(own ^ d, HD)
        for part, ref in enumerate((q_ref, k_ref, v_ref)):
            place = out.at[pl.ds(part * rows, rows), :]
            copies.append(pltpu.make_async_copy(ref.at[:, columns], place, done.at[d, part]))
            copies[-1].start()
    docs = doc_ref[...].astype(jnp.float32)
    docs = jnp.concatenate([docs, jnp.zeros((DOC_ROWS - docs.shape[0], HD), jnp.float32)], axis=0)
    docs = docs.astype(jnp.bfloat16)
    for out in outs:
        out[3 * rows:, :] = docs
    for copy in copies:
        copy.wait()


def pack_heads(me, q, k, v, doc_ids):
    rows, width = q.shape
    heads = width // HD
    out_shape = [jax.ShapeDtypeStruct((3 * rows + DOC_ROWS, HD), q.dtype)] * heads
    return pl.pallas_call(
        functools.partial(pack_kernel, heads, rows),
        in_specs=[SMEM_SPEC] + [pl.BlockSpec(memory_space=pltpu.HBM)] * 3 + [VMEM_SPEC],
        out_specs=[VMEM_SPEC] * heads,
        out_shape=out_shape,
        scratch_shapes=[pltpu.SemaphoreType.DMA((heads, 3))],
        compiler_params=params(out_shape),
    )(me, q, k, v, doc_ids.reshape(rows // HD, HD))


def unpack_kernel(heads, rows, me_s, *refs):
    own = lax.rem(me_s[0], heads)
    for d in range(heads):
        columns = aligned(own ^ d, HD)
        for part in range(3):
            refs[heads + part][:, columns] = refs[d][part * rows:(part + 1) * rows, :]


def unpack_heads(me, blocks, rows):
    heads = len(blocks)
    return pl.pallas_call(
        functools.partial(unpack_kernel, heads, rows),
        in_specs=[SMEM_SPEC] + [VMEM_SPEC] * heads,
        out_specs=[VMEM_SPEC] * 3,
        out_shape=[jax.ShapeDtypeStruct((rows, heads * HD), blocks[0].dtype)] * 3,
        compiler_params=params([*blocks, *blocks]),
    )(me, *blocks)


def project_kernel(count, *refs):
    features, weights, rest = refs[:count], refs[count:2 * count], refs[2 * count:]
    out_ref = rest[-1]
    for pair in range(out_ref.shape[1] // (2 * HD)):
        part = slice(pair * 2 * HD, (pair + 1) * 2 * HD)
        both = sum(dot32(o_ref[...], w_ref[part, :], NT) for o_ref, w_ref in zip(features, weights))
        out_ref[:, part] = both if len(rest) == 1 else rest[0][:, part] + both


def project_last_kernel(count, me_s, *refs):
    features, weights, acc_ref, outs = refs[:count], refs[count:2 * count], refs[2 * count], refs[2 * count + 1:]
    pairs = len(outs) // 2
    odd = lax.rem(me_s[0], 2) == 1
    for j in range(pairs):
        part = aligned(lax.rem(me_s[0] // 2, pairs) ^ j, 2 * HD)
        both = acc_ref[:, part]
        for o_ref, w_ref in zip(features, weights):
            both = both + dot32(o_ref[...], w_ref[part, :], NT)
        both = both.astype(jnp.bfloat16)
        outs[2 * j][...] = jnp.where(odd, both[:, HD:], both[:, :HD])
        outs[2 * j + 1][...] = jnp.where(odd, both[:, :HD], both[:, HD:])


def project(me, weights, features, acc, last):
    rows, width = features[0].shape
    columns = weights[0].shape[0]
    heads, count = columns // HD, len(features)
    total = jax.ShapeDtypeStruct((rows, columns), jnp.float32)
    cost = pl.CostEstimate(
        flops=2 * count * rows * width * columns,
        bytes_accessed=2 * count * width * columns + 8 * rows * columns,
        transcendentals=0,
    )
    operands = (*features, *weights) + (() if acc is None else (acc,))
    if last:
        return pl.pallas_call(
            functools.partial(project_last_kernel, count),
            in_specs=[SMEM_SPEC] + [VMEM_SPEC] * len(operands),
            out_specs=[VMEM_SPEC] * heads,
            out_shape=[jax.ShapeDtypeStruct((rows, HD), jnp.bfloat16)] * heads,
            compiler_params=params([*operands, total]),
            cost_estimate=cost,
        )(me, *operands)
    return pl.pallas_call(
        functools.partial(project_kernel, count),
        in_specs=[VMEM_SPEC] * len(operands),
        out_specs=VMEM_SPEC,
        out_shape=total,
        compiler_params=params([*operands, total]),
        cost_estimate=cost,
    )(*operands)


def at_or_before(q0, k0, shape):
    key = lax.broadcasted_iota(jnp.int32, shape, 0)
    return key <= q0 - k0 + lax.broadcasted_iota(jnp.int32, (1, shape[1]), 1)


def block_sizes(total):
    return (
        (block_size(total, 256), block_size(total, 256)),
        (block_size(total, 256), block_size(total, 256)),
    )


def plan_size(total, bq, bk):
    return sum(((q + 1) * bq + bk - 1) // bk for q in range(total // bq)) + 2


def fill_plan(lows, total, bq, bk, own, plan_q, plan_k, count_ref):
    def put(qi):
        def at(ki, count):
            plan_q[count] = qi
            plan_k[count] = ki
            return count + 1

        return at

    spans = []
    for qi, low in enumerate(lows):
        low, high = low // bk, ((qi + 1) * bq + bk - 1) // bk
        if own is not None:
            wanted = ((qi + 1) * bq > own[0]) & (qi * bq < own[1])
            low = jnp.where(wanted, low, jnp.maximum(low, own[0] // bk))
            high = jnp.where(wanted, high, jnp.minimum(high, (own[1] + bk - 1) // bk))
        whole = jnp.maximum(low, jnp.minimum(high, qi * bq // bk))
        spans.append((low, whole, high))
    count = 0
    for qi, (low, whole, high) in enumerate(spans):
        count = lax.fori_loop(low, whole, put(qi), count)
    count_ref[0] = jnp.maximum(count - 1, 0) // 2
    for qi, (low, whole, high) in enumerate(spans):
        count = lax.fori_loop(whole, high, put(qi), count)
    count_ref[1] = (count + 1) // 2
    for spare in range(2):
        plan_q[count + spare] = 0
        plan_k[count + spare] = total // bk - 1


def pipelined(plan_q, plan_k, count_ref, early, late, buffers):
    early(0, plan_q[0], plan_k[0], buffers[0], True)

    def turns(diagonal):
        def body(i, carry):
            for turn in range(2):
                now = 2 * i + turn
                late(now, plan_q[now], plan_k[now], buffers[turn])
                early(now + 1, plan_q[now + 1], plan_k[now + 1], buffers[1 - turn], diagonal)
            return carry

        return body

    lax.fori_loop(0, count_ref[0], turns(False), 0)
    lax.fori_loop(count_ref[0], count_ref[1], turns(True), 0)


def forward_kernel(peers, heads, rows, bq, bk, kept, me_s, *refs):
    blocks = refs[:peers]
    if kept:
        p_list, top_list = refs[peers + 6:peers + 8]
        refs = refs[:peers + 6] + refs[peers + 8:]
    v_ref, qx_ref, kx_ref, kt_ref, rows_ref, log_ref = refs[peers:peers + 6]
    plan_q, plan_k, count_ref, own_q, own_k, own_count = refs[peers + 6:peers + 12]
    vt_ref, out_ref, doc_ref, sum_ref, s0, top0, s1, top1 = refs[peers + 12:]
    total = v_ref.shape[0]
    factor = HD ** (-0.5) * math.log2(math.e)
    me = me_s[0]
    for d, block in enumerate(blocks):
        place = me ^ d
        for part, ref in enumerate((qx_ref.at[:, :HD], kx_ref.at[:, :HD], v_ref)):
            ref[aligned(place, rows), :] = block[part * rows:(part + 1) * rows, :]
        docs = block[3 * rows:, :].astype(jnp.float32)
        for t in range(rows // HD):
            doc_ref[:, aligned(place * (rows // HD) + t, HD)] = docs[t:t + 1, :]
    docs = doc_ref[...]
    first = jnp.zeros(docs.shape, jnp.float32)
    for value in range(1, DOC_VALUES):
        before = jnp.sum((docs < value).astype(jnp.float32))
        first = jnp.where(docs >= value, before, first)
    first = first.astype(jnp.int32)
    lows = [jnp.min(first[:, qi * bq:(qi + 1) * bq]) for qi in range(total // bq)]
    fill_plan(lows, total, bq, bk, None, own_q, own_k, own_count)
    group = (me // heads) * heads * rows
    own = None if heads == peers else (group, group + heads * rows)
    back_q, back_k = block_sizes(total)[1]
    lows = [jnp.min(first[:, qi * back_q:(qi + 1) * back_q]) for qi in range(total // back_q)]
    fill_plan(lows, total, back_q, back_k, own, plan_q, plan_k, count_ref)
    same = lax.broadcasted_iota(jnp.int32, (HD, total), 0).astype(jnp.float32) == docs
    ones = jnp.where(same, 1.0, 0.0).astype(jnp.bfloat16).T
    kx_ref[:, HD:] = ones
    qx_ref[:, HD:] = ((1.0 - ones.astype(jnp.float32)) * NEG_LARGE).astype(jnp.bfloat16)
    kt_ref[...] = kx_ref[:, :HD].T
    vt_ref[:HD, :] = v_ref[...].T
    vt_ref[HD:, :] = jnp.ones((ONES_ROWS, total), jnp.bfloat16)
    out_ref[...] = jnp.zeros_like(out_ref)
    log_ref[...] = jnp.full_like(log_ref, NEG_LARGE)
    sum_ref[...] = jnp.zeros_like(sum_ref)

    def early(now, qi, ki, buffer, diagonal):
        s_ref, top_ref = buffer
        keys, queries = aligned(ki, bk), aligned(qi, bq)
        s = dot32(kx_ref[keys, :], qx_ref[queries, :], NT) * factor
        if diagonal:
            s = jnp.where(at_or_before(qi * bq, ki * bk, (bk, bq)), s, NEG_LARGE)
        s_ref[...] = s
        top_ref[...] = jnp.max(s, axis=0, keepdims=True)

    def late(now, qi, ki, buffer):
        s_ref, top_ref = buffer
        keys, queries = aligned(ki, bk), aligned(qi, bq)
        top = log_ref[:, queries]
        new_top = jnp.maximum(top, top_ref[...])
        p = jnp.exp2(s_ref[...] - new_top)
        fix = jnp.exp2(top - new_top)
        high = p.astype(jnp.bfloat16)
        vt = vt_ref[:, keys]
        sums = dot32(vt, high)
        if kept:
            p_list[now] = high
            top_list[now] = new_top
        else:
            sums = sums + dot32(vt, (p - high.astype(jnp.float32)).astype(jnp.bfloat16))
        out_ref[:, queries] = out_ref[:, queries] * fix + sums[:HD, :]
        sum_ref[:, queries] = sum_ref[:, queries] * fix + sums[HD:HD + 1, :]
        log_ref[:, queries] = new_top

    pipelined(own_q, own_k, own_count, early, late, ((s0, top0), (s1, top1)))
    total_p = sum_ref[...]
    rows_ref[...] = (out_ref[...] / total_p).T
    log_ref[...] = log_ref[...] + jnp.log2(total_p)


def backward_kernel(peers, heads, rows, bq, bk, kept, me_s, plan_q, plan_k, count_ref, v_ref,
                    qx_ref, kx_ref, kt_ref, rows_ref, log_ref, *refs):
    if kept:
        p_list, top_list = refs[:2]
        refs = refs[2:]
    blocks = refs[:peers]
    results = refs[peers:peers + heads]
    g_ref, dot_ref, dk_acc, dv_acc, dq_acc, p0, ds0, p1, ds1 = refs[peers + heads:]
    scale = HD ** (-0.5)
    factor = scale * math.log2(math.e)
    me = me_s[0]
    for d, block in enumerate(blocks):
        g_ref[aligned(me ^ d, rows), :] = block[...]
    ones = jnp.ones((ONES_ROWS, HD), jnp.bfloat16)
    for start in range(0, g_ref.shape[0], bq):
        part = slice(start, start + bq)
        left = g_ref[part, :].astype(jnp.float32) * rows_ref[part, :]
        dots = 0.0
        for _ in range(3):
            term = left.astype(jnp.bfloat16)
            left = left - term.astype(jnp.float32)
            dots = dots + dot32(ones, term, NT)
        dot_ref[:, part] = dots[:1, :]
    dk_acc[...] = jnp.zeros_like(dk_acc)
    dv_acc[...] = jnp.zeros_like(dv_acc)
    dq_acc[...] = jnp.zeros_like(dq_acc)

    def early(now, qi, ki, buffer, diagonal):
        p_ref, ds_ref = buffer
        keys, queries = aligned(ki, bk), aligned(qi, bq)
        log_row = log_ref[:, queries]
        if kept:
            p = p_list[now].astype(jnp.float32) * jnp.exp2(top_list[now] - log_row)
        else:
            p = jnp.exp2(dot32(kx_ref[keys, :], qx_ref[queries, :], NT) * factor - log_row)
            if diagonal:
                p = jnp.where(at_or_before(qi * bq, ki * bk, (bk, bq)), p, 0.0)
        p_ref[...] = p.astype(jnp.bfloat16)
        dp = dot32(v_ref[keys, :], g_ref[queries, :], NT)
        ds_ref[...] = (p * (dp - dot_ref[:, queries])).astype(jnp.bfloat16)

    def late(now, qi, ki, buffer):
        p_ref, ds_ref = buffer
        keys, queries = aligned(ki, bk), aligned(qi, bq)
        dv_acc[keys, :] += dot32(p_ref[...], g_ref[queries, :])
        dk_acc[keys, :] += dot32(ds_ref[...], qx_ref[queries, :HD])
        dq_acc[:, queries] += dot32(kt_ref[:, keys], ds_ref[...])

    pipelined(plan_q, plan_k, count_ref, early, late, ((p0, ds0), (p1, ds1)))
    for d, result in enumerate(results):
        own = aligned(me ^ d, rows)
        result[:rows, :] = (scale * dq_acc[:, own]).astype(result.dtype).T
        result[rows:2 * rows, :] = (scale * dk_acc[own, :]).astype(result.dtype)
        result[2 * rows:, :] = dv_acc[own, :].astype(result.dtype)


def keeps_list(total, peers, heads):
    forward, backward = block_sizes(total)
    size = plan_size(total, *forward) * math.prod(forward) * 2
    return forward == backward and heads == peers and size <= LIST_BYTES


def attention_cost(total, products):
    return pl.CostEstimate(
        flops=products * total * total * HD // 2,
        bytes_accessed=16 * total * HD,
        transcendentals=total * total // 4,
    )


def attention_forward(me, blocks, rows, heads):
    peers = len(blocks)
    total = peers * rows
    (bq, bk), back = block_sizes(total)
    plan = [(plan_size(total, *back),)] * 2 + [(2,)]
    own_plan = [(plan_size(total, bq, bk),)] * 2 + [(2,)]
    vectors = [
        jax.ShapeDtypeStruct((total, HD), jnp.bfloat16),
        *[jax.ShapeDtypeStruct((total, 2 * HD), jnp.bfloat16)] * 2,
        jax.ShapeDtypeStruct((HD, total), jnp.bfloat16),
        jax.ShapeDtypeStruct((total, HD), jnp.float32),
        jax.ShapeDtypeStruct((1, total), jnp.float32),
    ]
    kept = keeps_list(total, peers, heads)
    if kept:
        vectors.append(jax.ShapeDtypeStruct((*own_plan[0], bk, bq), jnp.bfloat16))
        vectors.append(jax.ShapeDtypeStruct((*own_plan[0], 1, bq), jnp.float32))
    scratch = [
        pltpu.VMEM((HD + ONES_ROWS, total), jnp.bfloat16),
        pltpu.VMEM((HD, total), jnp.float32),
        pltpu.VMEM((1, total), jnp.float32),
        pltpu.VMEM((1, total), jnp.float32),
        *[pltpu.VMEM((bk, bq), jnp.float32), pltpu.VMEM((1, bq), jnp.float32)] * 2,
    ]
    return pl.pallas_call(
        functools.partial(forward_kernel, peers, heads, rows, bq, bk, kept),
        in_specs=[SMEM_SPEC] + [VMEM_SPEC] * peers,
        out_specs=[VMEM_SPEC] * len(vectors) + [SMEM_SPEC] * 3,
        out_shape=vectors + [jax.ShapeDtypeStruct(shape, jnp.int32) for shape in plan],
        scratch_shapes=[pltpu.SMEM(shape, jnp.int32) for shape in own_plan] + scratch,
        compiler_params=params([*blocks, *vectors], scratch),
        cost_estimate=attention_cost(total, 3),
    )(me, *blocks)


def attention_backward(me, heads, state, blocks):
    peers, rows = len(blocks), blocks[0].shape[0]
    total = peers * rows
    bq, bk = block_sizes(total)[1]
    vectors, plan = state[:-3], state[-3:]
    kept = keeps_list(total, peers, heads)
    out_shape = [jax.ShapeDtypeStruct((3 * rows, HD), jnp.bfloat16)] * heads
    scratch = [
        pltpu.VMEM((total, HD), jnp.bfloat16),
        pltpu.VMEM((1, total), jnp.float32),
        pltpu.VMEM((total, HD), jnp.float32),
        pltpu.VMEM((total, HD), jnp.float32),
        pltpu.VMEM((HD, total), jnp.float32),
        *[pltpu.VMEM((bk, bq), jnp.bfloat16)] * 4,
    ]
    return pl.pallas_call(
        functools.partial(backward_kernel, peers, heads, rows, bq, bk, kept),
        in_specs=[SMEM_SPEC] * 4 + [VMEM_SPEC] * (len(vectors) + peers),
        out_specs=[VMEM_SPEC] * heads,
        out_shape=out_shape,
        scratch_shapes=scratch,
        compiler_params=params([*vectors, *blocks, *out_shape], scratch),
        cost_estimate=attention_cost(total, 5),
    )(me, *plan, *vectors, *blocks)


def per_device(peers, groups, queries, keys_in, values, out_grad, out_weight, doc_ids):
    rows, width = queries.shape
    heads = width // HD
    me = lax.axis_index("seq")
    me_vector = me.reshape(1)

    def exchange(x, d):
        return x if d == 0 else lax.ppermute(x, "seq", [(i, i ^ d) for i in range(peers)])

    def pass_on(x, way):
        return lax.ppermute(x, "head", [(i, i + way) for i in range(groups) if 0 <= i + way < groups])

    order = [*range(2, peers, 2), *range(peers - 1, 0, -2)]

    def exchange_all(blocks, wanted):
        moved = {d: exchange(blocks[d % heads], d) for d in order if d < wanted}
        return [blocks[0]] + [moved[d] for d in range(1, wanted)]

    packed = list(pack_heads(me_vector, queries, keys_in, values, doc_ids))
    received = exchange_all(packed, peers)

    def share(step):
        return len(order) * step * (step + 1) // ((groups - 2) * (groups - 1))

    after = lax.optimization_barrier
    weights = []
    for step in range(groups):
        block = lax.rem(lax.axis_index("head") + groups - step, groups)
        weights.append(lax.dynamic_slice_in_dim(out_weight, block * width, width, 1))
    features, acc = [out_grad, out_grad], None
    for step in range(groups):
        last = step == groups - 1
        if not last:
            passed = [pass_on(features[0], 1), pass_on(features[1], -1)]
        if step == groups - 2:
            received[0], features = after((received[0], features))
            state = list(attention_forward(me_vector, received, rows, heads))
            features, state[1] = after((features, state[1]))
        if step == 0:
            acc = project(me_vector, weights[:1], features[:1], acc, last)
        else:
            acc = project(me_vector, [weights[step], weights[groups - step]], features, acc, last)
        if not last:
            features = passed
            if step < groups - 2:
                batch = order[share(step):share(step + 1)]
                here = [received[d] for d in batch]
                features, acc, here, weights[1:] = after((features, acc, here, weights[1:]))
                for d, block in zip(batch, here):
                    received[d] = block
    grads = exchange_all(acc, peers)

    results = attention_backward(me_vector, heads, state, grads)
    returned = exchange_all(results, heads)
    return tuple(unpack_heads(me_vector, returned, rows))


def solution(mesh):
    in_specs = (
        P("seq", "head"),
        P("seq", "head"),
        P("seq", "head"),
        P("seq", "head"),
        P("head", None),
        P("seq"),
    )
    out_specs = (P("seq", "head"), P("seq", "head"), P("seq", "head"))
    return jax.shard_map(
        functools.partial(per_device, mesh.shape["seq"], mesh.shape["head"]),
        mesh=mesh, in_specs=in_specs, out_specs=out_specs, check_vma=False,
    )
```

```python
import functools
import math

import jax
import jax.numpy as jnp
from jax import lax
from jax.experimental import pallas as pl
from jax.experimental.pallas import tpu as pltpu
from jax.sharding import PartitionSpec as P

HD = 128
DOC_VALUES = 8
DOC_ROWS = 16
ONES_ROWS = 16
STRIP = 64
NEG_LARGE = -1e30
VMEM_SPARE = 6 * 1024 * 1024
LIST_BYTES = 16 * 1024 * 1024

NN = (((1,), (0,)), ((), ()))
NT = (((1,), (1,)), ((), ()))
SMEM_SPEC = pl.BlockSpec(memory_space=pltpu.SMEM)
VMEM_SPEC = pl.BlockSpec(memory_space=pltpu.VMEM)


def dot32(a, b, dims=NN):
    return lax.dot_general(a, b, dims, preferred_element_type=jnp.float32)


def block_size(total, wanted):
    size = min(wanted, total)
    while total % size or size % 128:
        size -= 128
    return size


def aligned(index, size):
    return pl.ds(pl.multiple_of(index * size, size), size)


def params(arrays, scratch=()):
    total = sum(math.prod(a.shape) * jnp.dtype(a.dtype).itemsize for a in (*arrays, *scratch))
    return pltpu.CompilerParams(vmem_limit_bytes=total + VMEM_SPARE)


def pack_kernel(heads, rows, me_s, q_ref, k_ref, v_ref, doc_ref, *refs):
    outs, done = refs[:heads], refs[heads]
    own = lax.rem(me_s[0], heads)
    copies = []
    for d, out in enumerate(outs):
        columns = aligned(own ^ d, HD)
        for part, ref in enumerate((q_ref, k_ref, v_ref)):
            place = out.at[pl.ds(part * rows, rows), :]
            copies.append(pltpu.make_async_copy(ref.at[:, columns], place, done.at[d, part]))
            copies[-1].start()
    docs = doc_ref[...].astype(jnp.float32)
    docs = jnp.concatenate([docs, jnp.zeros((DOC_ROWS - docs.shape[0], HD), jnp.float32)], axis=0)
    docs = docs.astype(jnp.bfloat16)
    for out in outs:
        out[3 * rows:, :] = docs
    for copy in copies:
        copy.wait()


def pack_heads(me, q, k, v, doc_ids):
    rows, width = q.shape
    heads = width // HD
    out_shape = [jax.ShapeDtypeStruct((3 * rows + DOC_ROWS, HD), q.dtype)] * heads
    return pl.pallas_call(
        functools.partial(pack_kernel, heads, rows),
        in_specs=[SMEM_SPEC] + [pl.BlockSpec(memory_space=pltpu.HBM)] * 3 + [VMEM_SPEC],
        out_specs=[VMEM_SPEC] * heads,
        out_shape=out_shape,
        scratch_shapes=[pltpu.SemaphoreType.DMA((heads, 3))],
        compiler_params=params(out_shape),
    )(me, q, k, v, doc_ids.reshape(rows // HD, HD))


def unpack_kernel(heads, rows, me_s, *refs):
    own = lax.rem(me_s[0], heads)
    for d in range(heads):
        columns = aligned(own ^ d, HD)
        for part in range(3):
            refs[heads + part][:, columns] = refs[d][part * rows:(part + 1) * rows, :]


def unpack_heads(me, blocks, rows):
    heads = len(blocks)
    return pl.pallas_call(
        functools.partial(unpack_kernel, heads, rows),
        in_specs=[SMEM_SPEC] + [VMEM_SPEC] * heads,
        out_specs=[VMEM_SPEC] * 3,
        out_shape=[jax.ShapeDtypeStruct((rows, heads * HD), blocks[0].dtype)] * 3,
        compiler_params=params([*blocks, *blocks]),
    )(me, *blocks)


def project_kernel(first, o_ref, w_ref, *refs):
    out_ref = refs[-1]
    for pair in range(w_ref.shape[0] // (2 * HD)):
        part = slice(pair * 2 * HD, (pair + 1) * 2 * HD)
        both = dot32(o_ref[...], w_ref[part, :], NT)
        out_ref[:, part] = both if first else refs[0][:, part] + both


def project_last_kernel(me_s, o_ref, w_ref, acc_ref, *outs):
    pairs = len(outs) // 2
    odd = lax.rem(me_s[0], 2) == 1
    for j in range(pairs):
        part = aligned(lax.rem(me_s[0] // 2, pairs) ^ j, 2 * HD)
        both = (acc_ref[:, part] + dot32(o_ref[...], w_ref[part, :], NT)).astype(jnp.bfloat16)
        outs[2 * j][...] = jnp.where(odd, both[:, HD:], both[:, :HD])
        outs[2 * j + 1][...] = jnp.where(odd, both[:, :HD], both[:, HD:])


def project(me, weight, features, acc, last):
    rows, width = features.shape
    columns = weight.shape[0]
    heads = columns // HD
    total = jax.ShapeDtypeStruct((rows, columns), jnp.float32)
    cost = pl.CostEstimate(
        flops=2 * rows * width * columns,
        bytes_accessed=2 * width * columns + 8 * rows * columns,
        transcendentals=0,
    )
    if last:
        return pl.pallas_call(
            project_last_kernel,
            in_specs=[SMEM_SPEC] + [VMEM_SPEC] * 3,
            out_specs=[VMEM_SPEC] * heads,
            out_shape=[jax.ShapeDtypeStruct((rows, HD), jnp.bfloat16)] * heads,
            compiler_params=params([features, weight, total, total]),
            cost_estimate=cost,
        )(me, features, weight, acc)
    operands = (features, weight) + (() if acc is None else (acc,))
    return pl.pallas_call(
        functools.partial(project_kernel, acc is None),
        in_specs=[VMEM_SPEC] * len(operands),
        out_specs=VMEM_SPEC,
        out_shape=total,
        compiler_params=params([features, weight, total, total]),
        cost_estimate=cost,
    )(*operands)


def at_or_before(q0, k0, shape):
    key = lax.broadcasted_iota(jnp.int32, shape, 0)
    return key <= q0 - k0 + lax.broadcasted_iota(jnp.int32, (1, shape[1]), 1)


def block_sizes(total):
    return (
        (block_size(total, 256), block_size(total, 256)),
        (block_size(total, 256), block_size(total, 256)),
    )


def plan_size(total, bq, bk):
    return sum(((q + 1) * bq + bk - 1) // bk for q in range(total // bq)) + 2


def fill_plan(lows, total, bq, bk, own, plan_q, plan_k, count_ref):
    def put(qi):
        def at(ki, count):
            plan_q[count] = qi
            plan_k[count] = ki
            return count + 1

        return at

    spans = []
    for qi, low in enumerate(lows):
        low, high = low // bk, ((qi + 1) * bq + bk - 1) // bk
        if own is not None:
            wanted = ((qi + 1) * bq > own[0]) & (qi * bq < own[1])
            low = jnp.where(wanted, low, jnp.maximum(low, own[0] // bk))
            high = jnp.where(wanted, high, jnp.minimum(high, (own[1] + bk - 1) // bk))
        whole = jnp.maximum(low, jnp.minimum(high, qi * bq // bk))
        spans.append((low, whole, high))
    count = 0
    for qi, (low, whole, high) in enumerate(spans):
        count = lax.fori_loop(low, whole, put(qi), count)
    count_ref[0] = jnp.maximum(count - 1, 0) // 2
    for qi, (low, whole, high) in enumerate(spans):
        count = lax.fori_loop(whole, high, put(qi), count)
    count_ref[1] = (count + 1) // 2
    for spare in range(2):
        plan_q[count + spare] = 0
        plan_k[count + spare] = total // bk - 1


def pipelined(plan_q, plan_k, count_ref, early, late, buffers):
    early(0, plan_q[0], plan_k[0], buffers[0], True)

    def turns(diagonal):
        def body(i, carry):
            for turn in range(2):
                now = 2 * i + turn
                late(now, plan_q[now], plan_k[now], buffers[turn])
                early(now + 1, plan_q[now + 1], plan_k[now + 1], buffers[1 - turn], diagonal)
            return carry

        return body

    lax.fori_loop(0, count_ref[0], turns(False), 0)
    lax.fori_loop(count_ref[0], count_ref[1], turns(True), 0)


def forward_kernel(peers, heads, rows, bq, bk, kept, me_s, *refs):
    blocks = refs[:peers]
    if kept:
        p_list, top_list = refs[peers + 6:peers + 8]
        refs = refs[:peers + 6] + refs[peers + 8:]
    v_ref, qx_ref, kx_ref, kt_ref, rows_ref, log_ref = refs[peers:peers + 6]
    plan_q, plan_k, count_ref, own_q, own_k, own_count = refs[peers + 6:peers + 12]
    vt_ref, out_ref, doc_ref, sum_ref, s0, top0, s1, top1 = refs[peers + 12:]
    total = v_ref.shape[0]
    factor = HD ** (-0.5) * math.log2(math.e)
    me = me_s[0]
    for d, block in enumerate(blocks):
        place = me ^ d
        for part, ref in enumerate((qx_ref.at[:, :HD], kx_ref.at[:, :HD], v_ref)):
            ref[aligned(place, rows), :] = block[part * rows:(part + 1) * rows, :]
        docs = block[3 * rows:, :].astype(jnp.float32)
        for t in range(rows // HD):
            doc_ref[:, aligned(place * (rows // HD) + t, HD)] = docs[t:t + 1, :]
    docs = doc_ref[...]
    first = jnp.zeros(docs.shape, jnp.float32)
    for value in range(1, DOC_VALUES):
        before = jnp.sum((docs < value).astype(jnp.float32))
        first = jnp.where(docs >= value, before, first)
    first = first.astype(jnp.int32)
    lows = [jnp.min(first[:, qi * bq:(qi + 1) * bq]) for qi in range(total // bq)]
    fill_plan(lows, total, bq, bk, None, own_q, own_k, own_count)
    group = (me // heads) * heads * rows
    own = None if heads == peers else (group, group + heads * rows)
    back_q, back_k = block_sizes(total)[1]
    lows = [jnp.min(first[:, qi * back_q:(qi + 1) * back_q]) for qi in range(total // back_q)]
    fill_plan(lows, total, back_q, back_k, own, plan_q, plan_k, count_ref)
    same = lax.broadcasted_iota(jnp.int32, (HD, total), 0).astype(jnp.float32) == docs
    ones = jnp.where(same, 1.0, 0.0).astype(jnp.bfloat16).T
    kx_ref[:, HD:] = ones
    qx_ref[:, HD:] = ((1.0 - ones.astype(jnp.float32)) * NEG_LARGE).astype(jnp.bfloat16)
    kt_ref[...] = kx_ref[:, :HD].T
    vt_ref[:HD, :] = v_ref[...].T
    vt_ref[HD:, :] = jnp.ones((ONES_ROWS, total), jnp.bfloat16)
    out_ref[...] = jnp.zeros_like(out_ref)
    log_ref[...] = jnp.full_like(log_ref, NEG_LARGE)
    sum_ref[...] = jnp.zeros_like(sum_ref)

    def early(now, qi, ki, buffer, diagonal):
        s_ref, top_ref = buffer
        keys, queries = aligned(ki, bk), aligned(qi, bq)
        top = jnp.full((8, bq), NEG_LARGE, jnp.float32)
        for strip in range(0, bk, STRIP):
            s = dot32(kx_ref[aligned(ki * (bk // STRIP) + strip // STRIP, STRIP), :], qx_ref[queries, :], NT)
            s = s * factor
            if diagonal:
                s = jnp.where(at_or_before(qi * bq, ki * bk + strip, (STRIP, bq)), s, NEG_LARGE)
            s_ref[strip:strip + STRIP, :] = s
            top = jnp.maximum(top, jnp.max(s.reshape(STRIP // 8, 8, bq), axis=0))
        top_ref[...] = jnp.max(top, axis=0, keepdims=True)

    def late(now, qi, ki, buffer):
        s_ref, top_ref = buffer
        keys, queries = aligned(ki, bk), aligned(qi, bq)
        top = log_ref[:, queries]
        new_top = jnp.maximum(top, top_ref[...])
        fix = jnp.exp2(top - new_top)
        vt = vt_ref[:, keys]
        if kept:
            for strip in range(0, bk, STRIP):
                part = slice(strip, strip + STRIP)
                p_list[now, part, :] = jnp.exp2(s_ref[part, :] - new_top).astype(jnp.bfloat16)
            top_list[now] = new_top
            sums = dot32(vt, p_list[now])
        else:
            p = jnp.exp2(s_ref[...] - new_top)
            high = p.astype(jnp.bfloat16)
            sums = dot32(vt, high) + dot32(vt, (p - high.astype(jnp.float32)).astype(jnp.bfloat16))
        out_ref[:, queries] = out_ref[:, queries] * fix + sums[:HD, :]
        sum_ref[:, queries] = sum_ref[:, queries] * fix + sums[HD:HD + 1, :]
        log_ref[:, queries] = new_top

    pipelined(own_q, own_k, own_count, early, late, ((s0, top0), (s1, top1)))
    total_p = sum_ref[...]
    rows_ref[...] = (out_ref[...] / total_p).T
    log_ref[...] = log_ref[...] + jnp.log2(total_p)


def backward_kernel(peers, heads, rows, bq, bk, kept, me_s, plan_q, plan_k, count_ref, v_ref,
                    qx_ref, kx_ref, kt_ref, rows_ref, log_ref, *refs):
    if kept:
        p_list, top_list = refs[:2]
        refs = refs[2:]
    blocks = refs[:peers]
    results = refs[peers:peers + heads]
    g_ref, dot_ref, dk_acc, dv_acc, dq_acc, p0, ds0, p1, ds1 = refs[peers + heads:]
    scale = HD ** (-0.5)
    factor = scale * math.log2(math.e)
    me = me_s[0]
    for d, block in enumerate(blocks):
        g_ref[aligned(me ^ d, rows), :] = block[...]
    ones = jnp.ones((ONES_ROWS, HD), jnp.bfloat16)
    for start in range(0, g_ref.shape[0], bq):
        part = slice(start, start + bq)
        left = g_ref[part, :].astype(jnp.float32) * rows_ref[part, :]
        dots = 0.0
        for _ in range(3):
            term = left.astype(jnp.bfloat16)
            left = left - term.astype(jnp.float32)
            dots = dots + dot32(ones, term, NT)
        dot_ref[:, part] = dots[:1, :]
    dk_acc[...] = jnp.zeros_like(dk_acc)
    dv_acc[...] = jnp.zeros_like(dv_acc)
    dq_acc[...] = jnp.zeros_like(dq_acc)

    def early(now, qi, ki, buffer, diagonal):
        p_ref, ds_ref = buffer
        queries = aligned(qi, bq)
        log_row, dot_row = log_ref[:, queries], dot_ref[:, queries]
        if kept:
            share = jnp.exp2(top_list[now] - log_row)
        for strip in range(0, bk, STRIP):
            part = slice(strip, strip + STRIP)
            keys = aligned(ki * (bk // STRIP) + strip // STRIP, STRIP)
            if kept:
                p = p_list[now, part, :].astype(jnp.float32) * share
            else:
                p = jnp.exp2(dot32(kx_ref[keys, :], qx_ref[queries, :], NT) * factor - log_row)
                if diagonal:
                    p = jnp.where(at_or_before(qi * bq, ki * bk + strip, (STRIP, bq)), p, 0.0)
            p_ref[part, :] = p.astype(jnp.bfloat16)
            dp = dot32(v_ref[keys, :], g_ref[queries, :], NT)
            ds_ref[part, :] = (p * (dp - dot_row)).astype(jnp.bfloat16)

    def late(now, qi, ki, buffer):
        p_ref, ds_ref = buffer
        keys, queries = aligned(ki, bk), aligned(qi, bq)
        dv_acc[keys, :] += dot32(p_ref[...], g_ref[queries, :])
        dk_acc[keys, :] += dot32(ds_ref[...], qx_ref[queries, :HD])
        dq_acc[:, queries] += dot32(kt_ref[:, keys], ds_ref[...])

    pipelined(plan_q, plan_k, count_ref, early, late, ((p0, ds0), (p1, ds1)))
    for d, result in enumerate(results):
        own = aligned(me ^ d, rows)
        result[:rows, :] = (scale * dq_acc[:, own]).astype(result.dtype).T
        result[rows:2 * rows, :] = (scale * dk_acc[own, :]).astype(result.dtype)
        result[2 * rows:, :] = dv_acc[own, :].astype(result.dtype)


def keeps_list(total, peers, heads):
    forward, backward = block_sizes(total)
    size = plan_size(total, *forward) * math.prod(forward) * 2
    return forward == backward and heads == peers and size <= LIST_BYTES


def attention_cost(total, products):
    return pl.CostEstimate(
        flops=products * total * total * HD // 2,
        bytes_accessed=16 * total * HD,
        transcendentals=total * total // 4,
    )


def attention_forward(me, blocks, rows, heads):
    peers = len(blocks)
    total = peers * rows
    (bq, bk), back = block_sizes(total)
    plan = [(plan_size(total, *back),)] * 2 + [(2,)]
    own_plan = [(plan_size(total, bq, bk),)] * 2 + [(2,)]
    vectors = [
        jax.ShapeDtypeStruct((total, HD), jnp.bfloat16),
        *[jax.ShapeDtypeStruct((total, 2 * HD), jnp.bfloat16)] * 2,
        jax.ShapeDtypeStruct((HD, total), jnp.bfloat16),
        jax.ShapeDtypeStruct((total, HD), jnp.float32),
        jax.ShapeDtypeStruct((1, total), jnp.float32),
    ]
    kept = keeps_list(total, peers, heads)
    if kept:
        vectors.append(jax.ShapeDtypeStruct((*own_plan[0], bk, bq), jnp.bfloat16))
        vectors.append(jax.ShapeDtypeStruct((*own_plan[0], 1, bq), jnp.float32))
    scratch = [
        pltpu.VMEM((HD + ONES_ROWS, total), jnp.bfloat16),
        pltpu.VMEM((HD, total), jnp.float32),
        pltpu.VMEM((1, total), jnp.float32),
        pltpu.VMEM((1, total), jnp.float32),
        *[pltpu.VMEM((bk, bq), jnp.float32), pltpu.VMEM((1, bq), jnp.float32)] * 2,
    ]
    return pl.pallas_call(
        functools.partial(forward_kernel, peers, heads, rows, bq, bk, kept),
        in_specs=[SMEM_SPEC] + [VMEM_SPEC] * peers,
        out_specs=[VMEM_SPEC] * len(vectors) + [SMEM_SPEC] * 3,
        out_shape=vectors + [jax.ShapeDtypeStruct(shape, jnp.int32) for shape in plan],
        scratch_shapes=[pltpu.SMEM(shape, jnp.int32) for shape in own_plan] + scratch,
        compiler_params=params([*blocks, *vectors], scratch),
        cost_estimate=attention_cost(total, 3),
    )(me, *blocks)


def attention_backward(me, heads, state, blocks):
    peers, rows = len(blocks), blocks[0].shape[0]
    total = peers * rows
    bq, bk = block_sizes(total)[1]
    vectors, plan = state[:-3], state[-3:]
    kept = keeps_list(total, peers, heads)
    out_shape = [jax.ShapeDtypeStruct((3 * rows, HD), jnp.bfloat16)] * heads
    scratch = [
        pltpu.VMEM((total, HD), jnp.bfloat16),
        pltpu.VMEM((1, total), jnp.float32),
        pltpu.VMEM((total, HD), jnp.float32),
        pltpu.VMEM((total, HD), jnp.float32),
        pltpu.VMEM((HD, total), jnp.float32),
        *[pltpu.VMEM((bk, bq), jnp.bfloat16)] * 4,
    ]
    return pl.pallas_call(
        functools.partial(backward_kernel, peers, heads, rows, bq, bk, kept),
        in_specs=[SMEM_SPEC] * 4 + [VMEM_SPEC] * (len(vectors) + peers),
        out_specs=[VMEM_SPEC] * heads,
        out_shape=out_shape,
        scratch_shapes=scratch,
        compiler_params=params([*vectors, *blocks, *out_shape], scratch),
        cost_estimate=attention_cost(total, 5),
    )(me, *plan, *vectors, *blocks)


def per_device(peers, groups, queries, keys_in, values, out_grad, out_weight, doc_ids):
    rows, width = queries.shape
    heads = width // HD
    me = lax.axis_index("seq")
    me_vector = me.reshape(1)

    def exchange(x, d):
        return x if d == 0 else lax.ppermute(x, "seq", [(i, i ^ d) for i in range(peers)])

    def pass_on(x):
        return lax.ppermute(x, "head", [(i, (i + 1) % groups) for i in range(groups)])

    order = [*range(2, peers, 2), *range(peers - 1, 0, -2)]

    def exchange_all(blocks, wanted):
        moved = {d: exchange(blocks[d % heads], d) for d in order if d < wanted}
        return [blocks[0]] + [moved[d] for d in range(1, wanted)]

    packed = list(pack_heads(me_vector, queries, keys_in, values, doc_ids))
    received = exchange_all(packed, peers)

    def share(step):
        return len(order) * step * (step + 1) // ((groups - 2) * (groups - 1))

    after = lax.optimization_barrier
    features, acc = out_grad, None
    weights = []
    for step in range(groups):
        block = lax.rem(lax.axis_index("head") + groups - step, groups)
        weights.append(lax.dynamic_slice_in_dim(out_weight, block * width, width, 1))
    for step in range(groups):
        last = step == groups - 1
        if not last:
            passed = pass_on(features)
        if step == groups - 2:
            received[0], features = after((received[0], features))
            state = list(attention_forward(me_vector, received, rows, heads))
            features, state[1] = after((features, state[1]))
        acc = project(me_vector, weights[step], features, acc, last)
        if not last:
            features = passed
            if step < groups - 2:
                batch = order[share(step):share(step + 1)]
                here = [received[d] for d in batch]
                features, acc, here, weights[2:] = after((features, acc, here, weights[2:]))
                for d, block in zip(batch, here):
                    received[d] = block
    grads = exchange_all(acc, peers)

    results = attention_backward(me_vector, heads, state, grads)
    returned = exchange_all(results, heads)
    return tuple(unpack_heads(me_vector, returned, rows))


def solution(mesh):
    in_specs = (
        P("seq", "head"),
        P("seq", "head"),
        P("seq", "head"),
        P("seq", "head"),
        P("head", None),
        P("seq"),
    )
    out_specs = (P("seq", "head"), P("seq", "head"), P("seq", "head"))
    return jax.shard_map(
        functools.partial(per_device, mesh.shape["seq"], mesh.shape["head"]),
        mesh=mesh, in_specs=in_specs, out_specs=out_specs, check_vma=False,
    )
```

```python
import functools
import math

import jax
import jax.numpy as jnp
from jax import lax
from jax.experimental import pallas as pl
from jax.experimental.pallas import tpu as pltpu
from jax.sharding import PartitionSpec as P

HD = 128
DOC_VALUES = 8
DOC_ROWS = 16
ONES_ROWS = 16
STRIP = 64
NEG_LARGE = -1e30
VMEM_SPARE = 6 * 1024 * 1024
LIST_BYTES = 16 * 1024 * 1024

NN = (((1,), (0,)), ((), ()))
NT = (((1,), (1,)), ((), ()))
SMEM_SPEC = pl.BlockSpec(memory_space=pltpu.SMEM)
VMEM_SPEC = pl.BlockSpec(memory_space=pltpu.VMEM)


def dot32(a, b, dims=NN):
    return lax.dot_general(a, b, dims, preferred_element_type=jnp.float32)


def block_size(total, wanted):
    size = min(wanted, total)
    while total % size or size % 128:
        size -= 128
    return size


def aligned(index, size):
    return pl.ds(pl.multiple_of(index * size, size), size)


def params(arrays, scratch=()):
    total = sum(math.prod(a.shape) * jnp.dtype(a.dtype).itemsize for a in (*arrays, *scratch))
    return pltpu.CompilerParams(vmem_limit_bytes=total + VMEM_SPARE)


def pack_kernel(heads, rows, me_s, q_ref, k_ref, v_ref, doc_ref, *refs):
    outs, done = refs[:heads], refs[heads]
    own = lax.rem(me_s[0], heads)
    copies = []
    for d, out in enumerate(outs):
        columns = aligned(own ^ d, HD)
        for part, ref in enumerate((q_ref, k_ref, v_ref)):
            place = out.at[pl.ds(part * rows, rows), :]
            copies.append(pltpu.make_async_copy(ref.at[:, columns], place, done.at[d, part]))
            copies[-1].start()
    docs = doc_ref[...].astype(jnp.float32)
    docs = jnp.concatenate([docs, jnp.zeros((DOC_ROWS - docs.shape[0], HD), jnp.float32)], axis=0)
    docs = docs.astype(jnp.bfloat16)
    for out in outs:
        out[3 * rows:, :] = docs
    for copy in copies:
        copy.wait()


def pack_heads(me, q, k, v, doc_ids):
    rows, width = q.shape
    heads = width // HD
    out_shape = [jax.ShapeDtypeStruct((3 * rows + DOC_ROWS, HD), q.dtype)] * heads
    return pl.pallas_call(
        functools.partial(pack_kernel, heads, rows),
        in_specs=[SMEM_SPEC] + [pl.BlockSpec(memory_space=pltpu.HBM)] * 3 + [VMEM_SPEC],
        out_specs=[VMEM_SPEC] * heads,
        out_shape=out_shape,
        scratch_shapes=[pltpu.SemaphoreType.DMA((heads, 3))],
        compiler_params=params(out_shape),
    )(me, q, k, v, doc_ids.reshape(rows // HD, HD))


def unpack_kernel(listed, rows, me_s, *refs):
    heads = len(listed)
    own = lax.rem(me_s[0], heads)
    for d, block in zip(listed, refs):
        columns = aligned(own ^ d, HD)
        for part in range(3):
            refs[heads + part][:, columns] = block[part * rows:(part + 1) * rows, :]


def unpack_heads(me, listed, blocks, rows):
    heads = len(blocks)
    return pl.pallas_call(
        functools.partial(unpack_kernel, listed, rows),
        in_specs=[SMEM_SPEC] + [VMEM_SPEC] * heads,
        out_specs=[VMEM_SPEC] * 3,
        out_shape=[jax.ShapeDtypeStruct((rows, heads * HD), blocks[0].dtype)] * 3,
        compiler_params=params([*blocks, *blocks]),
    )(me, *blocks)


def project_kernel(first, o_ref, w_ref, *refs):
    out_ref = refs[-1]
    for pair in range(w_ref.shape[0] // (2 * HD)):
        part = slice(pair * 2 * HD, (pair + 1) * 2 * HD)
        both = dot32(o_ref[...], w_ref[part, :], NT)
        out_ref[:, part] = both if first else refs[0][:, part] + both


def project_last_kernel(me_s, o_ref, w_ref, acc_ref, *outs):
    pairs = len(outs) // 2
    odd = lax.rem(me_s[0], 2) == 1
    for j in range(pairs):
        part = aligned(lax.rem(me_s[0] // 2, pairs) ^ j, 2 * HD)
        both = (acc_ref[:, part] + dot32(o_ref[...], w_ref[part, :], NT)).astype(jnp.bfloat16)
        outs[2 * j][...] = jnp.where(odd, both[:, HD:], both[:, :HD])
        outs[2 * j + 1][...] = jnp.where(odd, both[:, :HD], both[:, HD:])


def project(me, weight, features, acc, last):
    rows, width = features.shape
    columns = weight.shape[0]
    heads = columns // HD
    total = jax.ShapeDtypeStruct((rows, columns), jnp.float32)
    cost = pl.CostEstimate(
        flops=2 * rows * width * columns,
        bytes_accessed=2 * width * columns + 8 * rows * columns,
        transcendentals=0,
    )
    if last:
        return pl.pallas_call(
            project_last_kernel,
            in_specs=[SMEM_SPEC] + [VMEM_SPEC] * 3,
            out_specs=[VMEM_SPEC] * heads,
            out_shape=[jax.ShapeDtypeStruct((rows, HD), jnp.bfloat16)] * heads,
            compiler_params=params([features, weight, total, total]),
            cost_estimate=cost,
        )(me, features, weight, acc)
    operands = (features, weight) + (() if acc is None else (acc,))
    return pl.pallas_call(
        functools.partial(project_kernel, acc is None),
        in_specs=[VMEM_SPEC] * len(operands),
        out_specs=VMEM_SPEC,
        out_shape=total,
        compiler_params=params([features, weight, total, total]),
        cost_estimate=cost,
    )(*operands)


def at_or_before(q0, k0, shape):
    key = lax.broadcasted_iota(jnp.int32, shape, 0)
    return key <= q0 - k0 + lax.broadcasted_iota(jnp.int32, (1, shape[1]), 1)


def block_sizes(total):
    return (
        (block_size(total, 256), block_size(total, 256)),
        (block_size(total, 256), block_size(total, 256)),
    )


def plan_size(total, bq, bk):
    return sum(((q + 1) * bq + bk - 1) // bk for q in range(total // bq)) + 2


def fill_plan(lows, total, bq, bk, own, plan_q, plan_k, count_ref):
    def put(qi):
        def at(ki, count):
            plan_q[count] = qi
            plan_k[count] = ki
            return count + 1

        return at

    spans = []
    for qi, low in enumerate(lows):
        low, high = low // bk, ((qi + 1) * bq + bk - 1) // bk
        if own is not None:
            wanted = ((qi + 1) * bq > own[0]) & (qi * bq < own[1])
            low = jnp.where(wanted, low, jnp.maximum(low, own[0] // bk))
            high = jnp.where(wanted, high, jnp.minimum(high, (own[1] + bk - 1) // bk))
        whole = jnp.maximum(low, jnp.minimum(high, qi * bq // bk))
        spans.append((low, whole, high))
    count = 0
    for qi, (low, whole, high) in enumerate(spans):
        count = lax.fori_loop(low, whole, put(qi), count)
    count_ref[0] = jnp.maximum(count - 1, 0) // 2
    for qi, (low, whole, high) in enumerate(spans):
        count = lax.fori_loop(whole, high, put(qi), count)
    count_ref[1] = (count + 1) // 2
    for spare in range(2):
        plan_q[count + spare] = 0
        plan_k[count + spare] = total // bk - 1


def pipelined(plan_q, plan_k, count_ref, early, late, buffers):
    early(0, plan_q[0], plan_k[0], buffers[0], True)

    def turns(diagonal):
        def body(i, carry):
            for turn in range(2):
                now = 2 * i + turn
                late(now, plan_q[now], plan_k[now], buffers[turn])
                early(now + 1, plan_q[now + 1], plan_k[now + 1], buffers[1 - turn], diagonal)
            return carry

        return body

    lax.fori_loop(0, count_ref[0], turns(False), 0)
    lax.fori_loop(count_ref[0], count_ref[1], turns(True), 0)


def forward_kernel(peers, heads, rows, bq, bk, kept, me_s, *refs):
    blocks = refs[:peers]
    if kept:
        p_list, top_list = refs[peers + 6:peers + 8]
        refs = refs[:peers + 6] + refs[peers + 8:]
    v_ref, qx_ref, kx_ref, kt_ref, rows_ref, log_ref = refs[peers:peers + 6]
    plan_q, plan_k, count_ref, own_q, own_k, own_count = refs[peers + 6:peers + 12]
    vt_ref, out_ref, doc_ref, sum_ref, s0, top0, s1, top1 = refs[peers + 12:]
    total = v_ref.shape[0]
    factor = HD ** (-0.5) * math.log2(math.e)
    me = me_s[0]
    for d, block in enumerate(blocks):
        place = me ^ d
        for part, ref in enumerate((qx_ref.at[:, :HD], kx_ref.at[:, :HD], v_ref)):
            ref[aligned(place, rows), :] = block[part * rows:(part + 1) * rows, :]
        docs = block[3 * rows:, :].astype(jnp.float32)
        for t in range(rows // HD):
            doc_ref[:, aligned(place * (rows // HD) + t, HD)] = docs[t:t + 1, :]
    docs = doc_ref[...]
    first = jnp.zeros(docs.shape, jnp.float32)
    for value in range(1, DOC_VALUES):
        before = jnp.sum((docs < value).astype(jnp.float32))
        first = jnp.where(docs >= value, before, first)
    first = first.astype(jnp.int32)
    back_q, back_k = block_sizes(total)[1]
    lows = [jnp.min(first[:, qi * back_q:(qi + 1) * back_q]) for qi in range(total // back_q)]
    group = (me // heads) * heads * rows
    own = None if heads == peers else (group, group + heads * rows)
    fill_plan(lows, total, back_q, back_k, own, plan_q, plan_k, count_ref)
    if kept:
        own_q, own_k, own_count = plan_q, plan_k, count_ref
    else:
        lows = [jnp.min(first[:, qi * bq:(qi + 1) * bq]) for qi in range(total // bq)]
        fill_plan(lows, total, bq, bk, None, own_q, own_k, own_count)
    same = lax.broadcasted_iota(jnp.int32, (HD, total), 0).astype(jnp.float32) == docs
    ones = jnp.where(same, 1.0, 0.0).astype(jnp.bfloat16).T
    kx_ref[:, HD:] = ones
    qx_ref[:, HD:] = ((1.0 - ones.astype(jnp.float32)) * NEG_LARGE).astype(jnp.bfloat16)
    kt_ref[...] = kx_ref[:, :HD].T
    vt_ref[:HD, :] = v_ref[...].T
    vt_ref[HD:, :] = jnp.ones((ONES_ROWS, total), jnp.bfloat16)
    out_ref[...] = jnp.zeros_like(out_ref)
    log_ref[...] = jnp.full_like(log_ref, NEG_LARGE)
    sum_ref[...] = jnp.zeros_like(sum_ref)

    def early(now, qi, ki, buffer, diagonal):
        s_ref, top_ref = buffer
        keys, queries = aligned(ki, bk), aligned(qi, bq)
        s = dot32(kx_ref[keys, :], qx_ref[queries, :], NT) * factor
        if diagonal:
            s = jnp.where(at_or_before(qi * bq, ki * bk, (bk, bq)), s, NEG_LARGE)
        s_ref[...] = s
        top_ref[...] = jnp.max(s, axis=0, keepdims=True)

    def late(now, qi, ki, buffer):
        s_ref, top_ref = buffer
        keys, queries = aligned(ki, bk), aligned(qi, bq)
        top = log_ref[:, queries]
        new_top = jnp.maximum(top, top_ref[...])
        fix = jnp.exp2(top - new_top)
        vt = vt_ref[:, keys]
        p = jnp.exp2(s_ref[...] - new_top)
        high = p.astype(jnp.bfloat16)
        sums = dot32(vt, high)
        if kept:
            p_list[now] = high
            top_list[now] = new_top
        else:
            sums = sums + dot32(vt, (p - high.astype(jnp.float32)).astype(jnp.bfloat16))
        out_ref[:, queries] = out_ref[:, queries] * fix + sums[:HD, :]
        sum_ref[:, queries] = sum_ref[:, queries] * fix + sums[HD:HD + 1, :]
        log_ref[:, queries] = new_top

    pipelined(own_q, own_k, own_count, early, late, ((s0, top0), (s1, top1)))
    total_p = sum_ref[...]
    rows_ref[...] = (out_ref[...] / total_p).T
    log_ref[...] = log_ref[...] + jnp.log2(total_p)


def backward_kernel(listed, heads, rows, bq, bk, kept, me_s, plan_q, plan_k, count_ref, v_ref,
                    qx_ref, kx_ref, kt_ref, rows_ref, log_ref, *refs):
    if kept:
        p_list, top_list = refs[:2]
        refs = refs[2:]
    peers = len(listed)
    blocks = refs[:peers]
    results = refs[peers:peers + heads]
    g_ref, dot_ref, dk_acc, dv_acc, dq_acc, p0, ds0, p1, ds1 = refs[peers + heads:]
    scale = HD ** (-0.5)
    factor = scale * math.log2(math.e)
    me = me_s[0]
    for d, block in zip(listed, blocks):
        g_ref[aligned(me ^ d, rows), :] = block[...]
    ones = jnp.ones((ONES_ROWS, HD), jnp.bfloat16)
    for start in range(0, g_ref.shape[0], bq):
        part = slice(start, start + bq)
        left = g_ref[part, :].astype(jnp.float32) * rows_ref[part, :]
        dots = 0.0
        for _ in range(3):
            term = left.astype(jnp.bfloat16)
            left = left - term.astype(jnp.float32)
            dots = dots + dot32(ones, term, NT)
        dot_ref[:, part] = dots[:1, :]
    dk_acc[...] = jnp.zeros_like(dk_acc)
    dv_acc[...] = jnp.zeros_like(dv_acc)
    dq_acc[...] = jnp.zeros_like(dq_acc)

    def early(now, qi, ki, buffer, diagonal):
        p_ref, ds_ref = buffer
        queries = aligned(qi, bq)
        log_row, dot_row = log_ref[:, queries], dot_ref[:, queries]
        if kept:
            share = jnp.exp2(top_list[now] - log_row)
        for strip in range(0, bk, STRIP):
            part = slice(strip, strip + STRIP)
            keys = aligned(ki * (bk // STRIP) + strip // STRIP, STRIP)
            if kept:
                p = p_list[now, part, :].astype(jnp.float32) * share
            else:
                p = jnp.exp2(dot32(kx_ref[keys, :], qx_ref[queries, :], NT) * factor - log_row)
                if diagonal:
                    p = jnp.where(at_or_before(qi * bq, ki * bk + strip, (STRIP, bq)), p, 0.0)
            p_ref[part, :] = p.astype(jnp.bfloat16)
            dp = dot32(v_ref[keys, :], g_ref[queries, :], NT)
            ds_ref[part, :] = (p * (dp - dot_row)).astype(jnp.bfloat16)

    def late(now, qi, ki, buffer):
        p_ref, ds_ref = buffer
        keys, queries = aligned(ki, bk), aligned(qi, bq)
        dv_acc[keys, :] += dot32(p_ref[...], g_ref[queries, :])
        dk_acc[keys, :] += dot32(ds_ref[...], qx_ref[queries, :HD])
        dq_acc[:, queries] += dot32(kt_ref[:, keys], ds_ref[...])

    pipelined(plan_q, plan_k, count_ref, early, late, ((p0, ds0), (p1, ds1)))
    for d, result in enumerate(results):
        own = aligned(me ^ d, rows)
        result[:rows, :] = (scale * dq_acc[:, own]).astype(result.dtype).T
        result[rows:2 * rows, :] = (scale * dk_acc[own, :]).astype(result.dtype)
        result[2 * rows:, :] = dv_acc[own, :].astype(result.dtype)


def keeps_list(total, peers, heads):
    forward, backward = block_sizes(total)
    size = plan_size(total, *forward) * math.prod(forward) * 2
    return forward == backward and heads == peers and size <= LIST_BYTES


def attention_cost(total, products):
    return pl.CostEstimate(
        flops=products * total * total * HD // 2,
        bytes_accessed=16 * total * HD,
        transcendentals=total * total // 4,
    )


def attention_forward(me, blocks, rows, heads):
    peers = len(blocks)
    total = peers * rows
    (bq, bk), back = block_sizes(total)
    plan = [(plan_size(total, *back),)] * 2 + [(2,)]
    own_plan = [(plan_size(total, bq, bk),)] * 2 + [(2,)]
    vectors = [
        jax.ShapeDtypeStruct((total, HD), jnp.bfloat16),
        *[jax.ShapeDtypeStruct((total, 2 * HD), jnp.bfloat16)] * 2,
        jax.ShapeDtypeStruct((HD, total), jnp.bfloat16),
        jax.ShapeDtypeStruct((total, HD), jnp.float32),
        jax.ShapeDtypeStruct((1, total), jnp.float32),
    ]
    kept = keeps_list(total, peers, heads)
    if kept:
        vectors.append(jax.ShapeDtypeStruct((*own_plan[0], bk, bq), jnp.bfloat16))
        vectors.append(jax.ShapeDtypeStruct((*own_plan[0], 1, bq), jnp.float32))
    scratch = [
        pltpu.VMEM((HD + ONES_ROWS, total), jnp.bfloat16),
        pltpu.VMEM((HD, total), jnp.float32),
        pltpu.VMEM((1, total), jnp.float32),
        pltpu.VMEM((1, total), jnp.float32),
        *[pltpu.VMEM((bk, bq), jnp.float32), pltpu.VMEM((1, bq), jnp.float32)] * 2,
    ]
    return pl.pallas_call(
        functools.partial(forward_kernel, peers, heads, rows, bq, bk, kept),
        in_specs=[SMEM_SPEC] + [VMEM_SPEC] * peers,
        out_specs=[VMEM_SPEC] * len(vectors) + [SMEM_SPEC] * 3,
        out_shape=vectors + [jax.ShapeDtypeStruct(shape, jnp.int32) for shape in plan],
        scratch_shapes=[pltpu.SMEM(shape, jnp.int32) for shape in own_plan] + scratch,
        compiler_params=params([*blocks, *vectors], scratch),
        cost_estimate=attention_cost(total, 3),
    )(me, *blocks)


def attention_backward(me, heads, state, listed, blocks):
    peers, rows = len(blocks), blocks[0].shape[0]
    total = peers * rows
    bq, bk = block_sizes(total)[1]
    vectors, plan = state[:-3], state[-3:]
    kept = keeps_list(total, peers, heads)
    out_shape = [jax.ShapeDtypeStruct((3 * rows, HD), jnp.bfloat16)] * heads
    scratch = [
        pltpu.VMEM((total, HD), jnp.bfloat16),
        pltpu.VMEM((1, total), jnp.float32),
        pltpu.VMEM((total, HD), jnp.float32),
        pltpu.VMEM((total, HD), jnp.float32),
        pltpu.VMEM((HD, total), jnp.float32),
        *[pltpu.VMEM((bk, bq), jnp.bfloat16)] * 4,
    ]
    return pl.pallas_call(
        functools.partial(backward_kernel, listed, heads, rows, bq, bk, kept),
        in_specs=[SMEM_SPEC] * 4 + [VMEM_SPEC] * (len(vectors) + peers),
        out_specs=[VMEM_SPEC] * heads,
        out_shape=out_shape,
        scratch_shapes=scratch,
        compiler_params=params([*vectors, *blocks, *out_shape], scratch),
        cost_estimate=attention_cost(total, 5),
    )(me, *plan, *vectors, *blocks)


def per_device(peers, groups, queries, keys_in, values, out_grad, out_weight, doc_ids):
    rows, width = queries.shape
    heads = width // HD
    me = lax.axis_index("seq")
    me_vector = me.reshape(1)

    def exchange(x, d):
        return x if d == 0 else lax.ppermute(x, "seq", [(i, i ^ d) for i in range(peers)])

    def pass_on(x):
        return lax.ppermute(x, "head", [(i, (i + 1) % groups) for i in range(groups)])

    order = [*range(2, peers, 2), *range(peers - 1, 0, -2)]

    far_first = sorted(range(peers), key=lambda d: (-bin(d >> 1).count("1"), d & 1, d))
    returning = [d for d in far_first if d < heads]

    def exchange_all(blocks, listed):
        return [exchange(blocks[d % heads], d) for d in listed]

    packed = list(pack_heads(me_vector, queries, keys_in, values, doc_ids))
    received = exchange_all(packed, range(peers))

    def share(step):
        return len(order) * step * (step + 1) // ((groups - 2) * (groups - 1))

    after = lax.optimization_barrier
    features, acc = out_grad, None
    weights = []
    for step in range(groups):
        block = lax.rem(lax.axis_index("head") + groups - step, groups)
        weights.append(lax.dynamic_slice_in_dim(out_weight, block * width, width, 1))
    for step in range(groups):
        last = step == groups - 1
        if not last:
            passed = pass_on(features)
        if step == groups - 2:
            received[0], features = after((received[0], features))
            state = list(attention_forward(me_vector, received, rows, heads))
            features, state[1] = after((features, state[1]))
        acc = project(me_vector, weights[step], features, acc, last)
        if not last:
            features = passed
            if step < groups - 2:
                batch = order[share(step):share(step + 1)]
                here = [received[d] for d in batch]
                features, acc, here, weights[2:] = after((features, acc, here, weights[2:]))
                for d, block in zip(batch, here):
                    received[d] = block
    grads = exchange_all(acc, far_first)

    results = attention_backward(me_vector, heads, state, far_first, grads)
    returned = exchange_all(results, returning)
    return tuple(unpack_heads(me_vector, returning, returned, rows))


def solution(mesh):
    in_specs = (
        P("seq", "head"),
        P("seq", "head"),
        P("seq", "head"),
        P("seq", "head"),
        P("head", None),
        P("seq"),
    )
    out_specs = (P("seq", "head"), P("seq", "head"), P("seq", "head"))
    return jax.shard_map(
        functools.partial(per_device, mesh.shape["seq"], mesh.shape["head"]),
        mesh=mesh, in_specs=in_specs, out_specs=out_specs, check_vma=False,
    )
```

```python
import functools
import math

import jax
import jax.numpy as jnp
from jax import lax
from jax.experimental import pallas as pl
from jax.experimental.pallas import tpu as pltpu
from jax.sharding import PartitionSpec as P

HD = 128
DOC_VALUES = 8
DOC_ROWS = 16
ONES_ROWS = 16
STRIP = 64
NEG_LARGE = -1e30
VMEM_SPARE = 6 * 1024 * 1024
LIST_BYTES = 16 * 1024 * 1024

NN = (((1,), (0,)), ((), ()))
NT = (((1,), (1,)), ((), ()))
SMEM_SPEC = pl.BlockSpec(memory_space=pltpu.SMEM)
VMEM_SPEC = pl.BlockSpec(memory_space=pltpu.VMEM)


def dot32(a, b, dims=NN):
    return lax.dot_general(a, b, dims, preferred_element_type=jnp.float32)


def block_size(total, wanted):
    size = min(wanted, total)
    while total % size or size % 128:
        size -= 128
    return size


def aligned(index, size):
    return pl.ds(pl.multiple_of(index * size, size), size)


def params(arrays, scratch=()):
    total = sum(math.prod(a.shape) * jnp.dtype(a.dtype).itemsize for a in (*arrays, *scratch))
    return pltpu.CompilerParams(vmem_limit_bytes=total + VMEM_SPARE)


def pack_kernel(heads, rows, me_s, q_ref, k_ref, v_ref, doc_ref, *refs):
    outs, done = refs[:heads], refs[heads]
    own = lax.rem(me_s[0], heads)
    copies = []
    for d, out in enumerate(outs):
        columns = aligned(own ^ d, HD)
        for part, ref in enumerate((q_ref, k_ref, v_ref)):
            place = out.at[pl.ds(part * rows, rows), :]
            copies.append(pltpu.make_async_copy(ref.at[:, columns], place, done.at[d, part]))
            copies[-1].start()
    docs = doc_ref[...].astype(jnp.float32)
    docs = jnp.concatenate([docs, jnp.zeros((DOC_ROWS - docs.shape[0], HD), jnp.float32)], axis=0)
    docs = docs.astype(jnp.bfloat16)
    for out in outs:
        out[3 * rows:, :] = docs
    for copy in copies:
        copy.wait()


def pack_heads(me, q, k, v, doc_ids):
    rows, width = q.shape
    heads = width // HD
    out_shape = [jax.ShapeDtypeStruct((3 * rows + DOC_ROWS, HD), q.dtype)] * heads
    return pl.pallas_call(
        functools.partial(pack_kernel, heads, rows),
        in_specs=[SMEM_SPEC] + [pl.BlockSpec(memory_space=pltpu.HBM)] * 3 + [VMEM_SPEC],
        out_specs=[VMEM_SPEC] * heads,
        out_shape=out_shape,
        scratch_shapes=[pltpu.SemaphoreType.DMA((heads, 3))],
        compiler_params=params(out_shape),
    )(me, q, k, v, doc_ids.reshape(rows // HD, HD))


def unpack_kernel(listed, rows, me_s, *refs):
    heads = len(listed)
    own = lax.rem(me_s[0], heads)
    for d, block in zip(listed, refs):
        columns = aligned(own ^ d, HD)
        for part in range(3):
            refs[heads + part][:, columns] = block[part * rows:(part + 1) * rows, :]


def unpack_heads(me, listed, blocks, rows):
    heads = len(blocks)
    return pl.pallas_call(
        functools.partial(unpack_kernel, listed, rows),
        in_specs=[SMEM_SPEC] + [VMEM_SPEC] * heads,
        out_specs=[VMEM_SPEC] * 3,
        out_shape=[jax.ShapeDtypeStruct((rows, heads * HD), blocks[0].dtype)] * 3,
        compiler_params=params([*blocks, *blocks]),
    )(me, *blocks)


def project_kernel(first, o_ref, w_ref, *refs):
    out_ref = refs[-1]
    for pair in range(w_ref.shape[0] // (2 * HD)):
        part = slice(pair * 2 * HD, (pair + 1) * 2 * HD)
        both = dot32(o_ref[...], w_ref[part, :], NT)
        out_ref[:, part] = both if first else refs[0][:, part] + both


def project_last_kernel(me_s, o_ref, w_ref, acc_ref, *outs):
    pairs = len(outs) // 2
    odd = lax.rem(me_s[0], 2) == 1
    for j in range(pairs):
        part = aligned(lax.rem(me_s[0] // 2, pairs) ^ j, 2 * HD)
        both = (acc_ref[:, part] + dot32(o_ref[...], w_ref[part, :], NT)).astype(jnp.bfloat16)
        outs[2 * j][...] = jnp.where(odd, both[:, HD:], both[:, :HD])
        outs[2 * j + 1][...] = jnp.where(odd, both[:, :HD], both[:, HD:])


def project(me, weight, features, acc, last):
    rows, width = features.shape
    columns = weight.shape[0]
    heads = columns // HD
    total = jax.ShapeDtypeStruct((rows, columns), jnp.float32)
    cost = pl.CostEstimate(
        flops=2 * rows * width * columns,
        bytes_accessed=2 * width * columns + 8 * rows * columns,
        transcendentals=0,
    )
    if last:
        return pl.pallas_call(
            project_last_kernel,
            in_specs=[SMEM_SPEC] + [VMEM_SPEC] * 3,
            out_specs=[VMEM_SPEC] * heads,
            out_shape=[jax.ShapeDtypeStruct((rows, HD), jnp.bfloat16)] * heads,
            compiler_params=params([features, weight, total, total]),
            cost_estimate=cost,
        )(me, features, weight, acc)
    operands = (features, weight) + (() if acc is None else (acc,))
    return pl.pallas_call(
        functools.partial(project_kernel, acc is None),
        in_specs=[VMEM_SPEC] * len(operands),
        out_specs=VMEM_SPEC,
        out_shape=total,
        compiler_params=params([features, weight, total, total]),
        cost_estimate=cost,
    )(*operands)


def at_or_before(q0, k0, shape):
    key = lax.broadcasted_iota(jnp.int32, shape, 0)
    return key <= q0 - k0 + lax.broadcasted_iota(jnp.int32, (1, shape[1]), 1)


def block_sizes(total):
    return (
        (block_size(total, 256), block_size(total, 256)),
        (block_size(total, 256), block_size(total, 256)),
    )


def plan_size(total, bq, bk):
    return sum(((q + 1) * bq + bk - 1) // bk for q in range(total // bq)) + 2


def fill_plan(lows, total, bq, bk, own, plan_q, plan_k, count_ref):
    def put(qi):
        def at(ki, count):
            plan_q[count] = qi
            plan_k[count] = ki
            return count + 1

        return at

    spans = []
    for qi, low in enumerate(lows):
        low, high = low // bk, ((qi + 1) * bq + bk - 1) // bk
        if own is not None:
            wanted = ((qi + 1) * bq > own[0]) & (qi * bq < own[1])
            low = jnp.where(wanted, low, jnp.maximum(low, own[0] // bk))
            high = jnp.where(wanted, high, jnp.minimum(high, (own[1] + bk - 1) // bk))
        whole = jnp.maximum(low, jnp.minimum(high, qi * bq // bk))
        spans.append((low, whole, high))
    count = 0
    for qi, (low, whole, high) in enumerate(spans):
        count = lax.fori_loop(low, whole, put(qi), count)
    count_ref[0] = jnp.maximum(count - 1, 0) // 2
    for qi, (low, whole, high) in enumerate(spans):
        count = lax.fori_loop(whole, high, put(qi), count)
    count_ref[1] = (count + 1) // 2
    for spare in range(2):
        plan_q[count + spare] = 0
        plan_k[count + spare] = total // bk - 1


def pipelined(plan_q, plan_k, count_ref, early, late, buffers):
    early(0, plan_q[0], plan_k[0], buffers[0], True)

    def turns(diagonal):
        def body(i, carry):
            for turn in range(2):
                now = 2 * i + turn
                late(now, plan_q[now], plan_k[now], buffers[turn])
                early(now + 1, plan_q[now + 1], plan_k[now + 1], buffers[1 - turn], diagonal)
            return carry

        return body

    lax.fori_loop(0, count_ref[0], turns(False), 0)
    lax.fori_loop(count_ref[0], count_ref[1], turns(True), 0)


def forward_kernel(peers, heads, rows, bq, bk, kept, me_s, *refs):
    blocks = refs[:peers]
    if kept:
        p_list, top_list = refs[peers + 6], refs[-1]
        refs = refs[:peers + 6] + refs[peers + 7:-1]
    v_ref, qx_ref, kx_ref, kt_ref, rows_ref, log_ref = refs[peers:peers + 6]
    plan_q, plan_k, count_ref, own_q, own_k, own_count = refs[peers + 6:peers + 12]
    vt_ref, out_ref, doc_ref, sum_ref, s0, top0, s1, top1 = refs[peers + 12:]
    total = v_ref.shape[0]
    factor = HD ** (-0.5) * math.log2(math.e)
    me = me_s[0]
    for d, block in enumerate(blocks):
        place = me ^ d
        for part, ref in enumerate((qx_ref.at[:, :HD], kx_ref.at[:, :HD], v_ref)):
            ref[aligned(place, rows), :] = block[part * rows:(part + 1) * rows, :]
        docs = block[3 * rows:, :].astype(jnp.float32)
        for t in range(rows // HD):
            doc_ref[:, aligned(place * (rows // HD) + t, HD)] = docs[t:t + 1, :]
    docs = doc_ref[...]
    first = jnp.zeros(docs.shape, jnp.float32)
    for value in range(1, DOC_VALUES):
        before = jnp.sum((docs < value).astype(jnp.float32))
        first = jnp.where(docs >= value, before, first)
    first = first.astype(jnp.int32)
    back_q, back_k = block_sizes(total)[1]
    lows = [jnp.min(first[:, qi * back_q:(qi + 1) * back_q]) for qi in range(total // back_q)]
    group = (me // heads) * heads * rows
    own = None if heads == peers else (group, group + heads * rows)
    fill_plan(lows, total, back_q, back_k, own, plan_q, plan_k, count_ref)
    if kept:
        own_q, own_k, own_count = plan_q, plan_k, count_ref
    else:
        lows = [jnp.min(first[:, qi * bq:(qi + 1) * bq]) for qi in range(total // bq)]
        fill_plan(lows, total, bq, bk, None, own_q, own_k, own_count)
    same = lax.broadcasted_iota(jnp.int32, (HD, total), 0).astype(jnp.float32) == docs
    ones = jnp.where(same, 1.0, 0.0).astype(jnp.bfloat16).T
    kx_ref[:, HD:] = ones
    qx_ref[:, HD:] = ((1.0 - ones.astype(jnp.float32)) * NEG_LARGE).astype(jnp.bfloat16)
    kt_ref[...] = kx_ref[:, :HD].T
    vt_ref[:HD, :] = v_ref[...].T
    vt_ref[HD:, :] = jnp.ones((ONES_ROWS, total), jnp.bfloat16)
    out_ref[...] = jnp.zeros_like(out_ref)
    log_ref[...] = jnp.full_like(log_ref, NEG_LARGE)
    sum_ref[...] = jnp.zeros_like(sum_ref)

    def early(now, qi, ki, buffer, diagonal):
        s_ref, top_ref = buffer
        keys, queries = aligned(ki, bk), aligned(qi, bq)
        s = dot32(kx_ref[keys, :], qx_ref[queries, :], NT) * factor
        if diagonal:
            s = jnp.where(at_or_before(qi * bq, ki * bk, (bk, bq)), s, NEG_LARGE)
        s_ref[...] = s
        top_ref[...] = jnp.max(s, axis=0, keepdims=True)

    def late(now, qi, ki, buffer):
        s_ref, top_ref = buffer
        keys, queries = aligned(ki, bk), aligned(qi, bq)
        top = log_ref[:, queries]
        new_top = jnp.maximum(top, top_ref[...])
        fix = jnp.exp2(top - new_top)
        vt = vt_ref[:, keys]
        p = jnp.exp2(s_ref[...] - new_top)
        high = p.astype(jnp.bfloat16)
        sums = dot32(vt, high)
        if kept:
            p_list[now] = high
            top_list[now] = new_top
        else:
            sums = sums + dot32(vt, (p - high.astype(jnp.float32)).astype(jnp.bfloat16))
        out_ref[:, queries] = out_ref[:, queries] * fix + sums[:HD, :]
        sum_ref[:, queries] = sum_ref[:, queries] * fix + sums[HD:HD + 1, :]
        log_ref[:, queries] = new_top

    pipelined(own_q, own_k, own_count, early, late, ((s0, top0), (s1, top1)))
    total_p = sum_ref[...]
    rows_ref[...] = (out_ref[...] / total_p).T
    log_ref[...] = log_ref[...] + jnp.log2(total_p)
    if kept:

        @pl.loop(0, 2 * count_ref[1])
        def _(now):
            share = jnp.exp2(top_list[now] - log_ref[:, aligned(plan_q[now], bq)])
            for strip in range(0, bk, STRIP):
                part = slice(strip, strip + STRIP)
                p_list[now, part, :] = (p_list[now, part, :].astype(jnp.float32) * share).astype(jnp.bfloat16)


def backward_kernel(listed, heads, rows, bq, bk, kept, me_s, plan_q, plan_k, count_ref, v_ref,
                    qx_ref, kx_ref, kt_ref, rows_ref, log_ref, *refs):
    if kept:
        p_list, refs = refs[0], refs[1:]
    peers = len(listed)
    blocks = refs[:peers]
    results = refs[peers:peers + heads]
    g_ref, dot_ref, dk_acc, dv_acc, dq_acc, p0, ds0, p1, ds1 = refs[peers + heads:]
    scale = HD ** (-0.5)
    factor = scale * math.log2(math.e)
    me = me_s[0]
    for d, block in zip(listed, blocks):
        g_ref[aligned(me ^ d, rows), :] = block[...]
    ones = jnp.ones((ONES_ROWS, HD), jnp.bfloat16)
    for start in range(0, g_ref.shape[0], bq):
        part = slice(start, start + bq)
        left = g_ref[part, :].astype(jnp.float32) * rows_ref[part, :]
        dots = 0.0
        for _ in range(3):
            term = left.astype(jnp.bfloat16)
            left = left - term.astype(jnp.float32)
            dots = dots + dot32(ones, term, NT)
        dot_ref[:, part] = dots[:1, :]
    dk_acc[...] = jnp.zeros_like(dk_acc)
    dv_acc[...] = jnp.zeros_like(dv_acc)
    dq_acc[...] = jnp.zeros_like(dq_acc)

    def early(now, qi, ki, buffer, diagonal):
        p_ref, ds_ref = buffer
        queries = aligned(qi, bq)
        log_row, dot_row = log_ref[:, queries], dot_ref[:, queries]
        for strip in range(0, bk, STRIP):
            part = slice(strip, strip + STRIP)
            keys = aligned(ki * (bk // STRIP) + strip // STRIP, STRIP)
            if kept:
                p = p_list[now, part, :].astype(jnp.float32)
            else:
                p = jnp.exp2(dot32(kx_ref[keys, :], qx_ref[queries, :], NT) * factor - log_row)
                if diagonal:
                    p = jnp.where(at_or_before(qi * bq, ki * bk + strip, (STRIP, bq)), p, 0.0)
                p_ref[part, :] = p.astype(jnp.bfloat16)
            dp = dot32(v_ref[keys, :], g_ref[queries, :], NT)
            ds_ref[part, :] = (p * (dp - dot_row)).astype(jnp.bfloat16)

    def late(now, qi, ki, buffer):
        p_ref, ds_ref = buffer
        keys, queries = aligned(ki, bk), aligned(qi, bq)
        dv_acc[keys, :] += dot32(p_list[now] if kept else p_ref[...], g_ref[queries, :])
        dk_acc[keys, :] += dot32(ds_ref[...], qx_ref[queries, :HD])
        dq_acc[:, queries] += dot32(kt_ref[:, keys], ds_ref[...])

    pipelined(plan_q, plan_k, count_ref, early, late, ((p0, ds0), (p1, ds1)))
    for d, result in enumerate(results):
        own = aligned(me ^ d, rows)
        result[:rows, :] = (scale * dq_acc[:, own]).astype(result.dtype).T
        result[rows:2 * rows, :] = (scale * dk_acc[own, :]).astype(result.dtype)
        result[2 * rows:, :] = dv_acc[own, :].astype(result.dtype)


def keeps_list(total, peers, heads):
    forward, backward = block_sizes(total)
    size = plan_size(total, *forward) * math.prod(forward) * 2
    return forward == backward and heads == peers and size <= LIST_BYTES


def attention_cost(total, products):
    return pl.CostEstimate(
        flops=products * total * total * HD // 2,
        bytes_accessed=16 * total * HD,
        transcendentals=total * total // 4,
    )


def attention_forward(me, blocks, rows, heads):
    peers = len(blocks)
    total = peers * rows
    (bq, bk), back = block_sizes(total)
    plan = [(plan_size(total, *back),)] * 2 + [(2,)]
    own_plan = [(plan_size(total, bq, bk),)] * 2 + [(2,)]
    vectors = [
        jax.ShapeDtypeStruct((total, HD), jnp.bfloat16),
        *[jax.ShapeDtypeStruct((total, 2 * HD), jnp.bfloat16)] * 2,
        jax.ShapeDtypeStruct((HD, total), jnp.bfloat16),
        jax.ShapeDtypeStruct((total, HD), jnp.float32),
        jax.ShapeDtypeStruct((1, total), jnp.float32),
    ]
    scratch = [
        pltpu.VMEM((HD + ONES_ROWS, total), jnp.bfloat16),
        pltpu.VMEM((HD, total), jnp.float32),
        pltpu.VMEM((1, total), jnp.float32),
        pltpu.VMEM((1, total), jnp.float32),
        *[pltpu.VMEM((bk, bq), jnp.float32), pltpu.VMEM((1, bq), jnp.float32)] * 2,
    ]
    kept = keeps_list(total, peers, heads)
    if kept:
        vectors.append(jax.ShapeDtypeStruct((*own_plan[0], bk, bq), jnp.bfloat16))
        scratch.append(pltpu.VMEM((*own_plan[0], 1, bq), jnp.float32))
    return pl.pallas_call(
        functools.partial(forward_kernel, peers, heads, rows, bq, bk, kept),
        in_specs=[SMEM_SPEC] + [VMEM_SPEC] * peers,
        out_specs=[VMEM_SPEC] * len(vectors) + [SMEM_SPEC] * 3,
        out_shape=vectors + [jax.ShapeDtypeStruct(shape, jnp.int32) for shape in plan],
        scratch_shapes=[pltpu.SMEM(shape, jnp.int32) for shape in own_plan] + scratch,
        compiler_params=params([*blocks, *vectors], scratch),
        cost_estimate=attention_cost(total, 3),
    )(me, *blocks)


def attention_backward(me, heads, state, listed, blocks):
    peers, rows = len(blocks), blocks[0].shape[0]
    total = peers * rows
    bq, bk = block_sizes(total)[1]
    vectors, plan = state[:-3], state[-3:]
    kept = keeps_list(total, peers, heads)
    out_shape = [jax.ShapeDtypeStruct((3 * rows, HD), jnp.bfloat16)] * heads
    scratch = [
        pltpu.VMEM((total, HD), jnp.bfloat16),
        pltpu.VMEM((1, total), jnp.float32),
        pltpu.VMEM((total, HD), jnp.float32),
        pltpu.VMEM((total, HD), jnp.float32),
        pltpu.VMEM((HD, total), jnp.float32),
        *[pltpu.VMEM((bk, bq), jnp.bfloat16)] * 4,
    ]
    return pl.pallas_call(
        functools.partial(backward_kernel, listed, heads, rows, bq, bk, kept),
        in_specs=[SMEM_SPEC] * 4 + [VMEM_SPEC] * (len(vectors) + peers),
        out_specs=[VMEM_SPEC] * heads,
        out_shape=out_shape,
        scratch_shapes=scratch,
        compiler_params=params([*vectors, *blocks, *out_shape], scratch),
        cost_estimate=attention_cost(total, 5),
    )(me, *plan, *vectors, *blocks)


def per_device(peers, groups, queries, keys_in, values, out_grad, out_weight, doc_ids):
    rows, width = queries.shape
    heads = width // HD
    me = lax.axis_index("seq")
    me_vector = me.reshape(1)

    def exchange(x, d):
        return x if d == 0 else lax.ppermute(x, "seq", [(i, i ^ d) for i in range(peers)])

    def pass_on(x):
        return lax.ppermute(x, "head", [(i, (i + 1) % groups) for i in range(groups)])

    order = [*range(2, peers, 2), *range(peers - 1, 0, -2)]

    far_first = sorted(range(peers), key=lambda d: (-bin(d >> 1).count("1"), d & 1, d))
    returning = [d for d in far_first if d < heads]

    def exchange_all(blocks, listed):
        return [exchange(blocks[d % heads], d) for d in listed]

    packed = list(pack_heads(me_vector, queries, keys_in, values, doc_ids))
    received = exchange_all(packed, range(peers))

    def share(step):
        return len(order) * step * (step + 1) // ((groups - 2) * (groups - 1))

    after = lax.optimization_barrier
    features, acc = out_grad, None
    weights = []
    for step in range(groups):
        block = lax.rem(lax.axis_index("head") + groups - step, groups)
        weights.append(lax.dynamic_slice_in_dim(out_weight, block * width, width, 1))
    for step in range(groups):
        last = step == groups - 1
        if not last:
            passed = pass_on(features)
        if step == groups - 2:
            received[0], features = after((received[0], features))
            state = list(attention_forward(me_vector, received, rows, heads))
            features, state[1] = after((features, state[1]))
        acc = project(me_vector, weights[step], features, acc, last)
        if not last:
            features = passed
            if step < groups - 2:
                batch = order[share(step):share(step + 1)]
                here = [received[d] for d in batch]
                features, acc, here, weights[2:] = after((features, acc, here, weights[2:]))
                for d, block in zip(batch, here):
                    received[d] = block
    grads = exchange_all(acc, far_first)

    results = attention_backward(me_vector, heads, state, far_first, grads)
    returned = exchange_all(results, returning)
    return tuple(unpack_heads(me_vector, returning, returned, rows))


def solution(mesh):
    in_specs = (
        P("seq", "head"),
        P("seq", "head"),
        P("seq", "head"),
        P("seq", "head"),
        P("head", None),
        P("seq"),
    )
    out_specs = (P("seq", "head"), P("seq", "head"), P("seq", "head"))
    return jax.shard_map(
        functools.partial(per_device, mesh.shape["seq"], mesh.shape["head"]),
        mesh=mesh, in_specs=in_specs, out_specs=out_specs, check_vma=False,
    )
```

```python
import functools
import math

import jax
import jax.numpy as jnp
from jax import lax
from jax.experimental import pallas as pl
from jax.experimental.pallas import tpu as pltpu
from jax.sharding import PartitionSpec as P

HD = 128
DOC_VALUES = 8
DOC_ROWS = 16
ONES_ROWS = 16
STRIP = 64
NEG_LARGE = -1e30
VMEM_SPARE = 6 * 1024 * 1024
VMEM_MOST = 56 * 1024 * 1024
LIST_BYTES = 16 * 1024 * 1024

NN = (((1,), (0,)), ((), ()))
NT = (((1,), (1,)), ((), ()))
SMEM_SPEC = pl.BlockSpec(memory_space=pltpu.SMEM)
VMEM_SPEC = pl.BlockSpec(memory_space=pltpu.VMEM)
ANY_SPEC = pl.BlockSpec(memory_space=pl.ANY)


def dot32(a, b, dims=NN):
    return lax.dot_general(a, b, dims, preferred_element_type=jnp.float32)


def block_size(total, wanted):
    size = min(wanted, total)
    while total % size or size % 128:
        size -= 128
    return size


def aligned(index, size):
    return pl.ds(pl.multiple_of(index * size, size), size)


def params(arrays, scratch=()):
    total = sum(math.prod(a.shape) * jnp.dtype(a.dtype).itemsize for a in (*arrays, *scratch))
    return pltpu.CompilerParams(vmem_limit_bytes=total + VMEM_SPARE)


def pack_kernel(heads, rows, me_s, q_ref, k_ref, v_ref, doc_ref, *refs):
    outs, doc_block, done, doc_done = refs[:heads], refs[heads], refs[heads + 1], refs[heads + 2]
    own = lax.rem(me_s[0], heads)
    copies = []
    for d, out in enumerate(outs):
        columns = aligned(own ^ d, HD)
        for part, ref in enumerate((q_ref, k_ref, v_ref)):
            place = out.at[pl.ds(part * rows, rows), :]
            copies.append(pltpu.make_async_copy(ref.at[:, columns], place, done.at[d, part]))
            copies[-1].start()
    docs = doc_ref[...].astype(jnp.float32)
    docs = jnp.concatenate([docs, jnp.zeros((DOC_ROWS - docs.shape[0], HD), jnp.float32)], axis=0)
    doc_block[...] = docs.astype(jnp.bfloat16)
    for d, out in enumerate(outs):
        copies.append(pltpu.make_async_copy(doc_block, out.at[pl.ds(3 * rows, DOC_ROWS), :], doc_done.at[d]))
        copies[-1].start()
    for copy in copies:
        copy.wait()


def pack_heads(me, q, k, v, doc_ids):
    rows, width = q.shape
    heads = width // HD
    return pl.pallas_call(
        functools.partial(pack_kernel, heads, rows),
        in_specs=[SMEM_SPEC] + [ANY_SPEC] * 3 + [VMEM_SPEC],
        out_specs=[ANY_SPEC] * heads,
        out_shape=[jax.ShapeDtypeStruct((3 * rows + DOC_ROWS, HD), q.dtype)] * heads,
        scratch_shapes=[
            pltpu.VMEM((DOC_ROWS, HD), jnp.bfloat16),
            pltpu.SemaphoreType.DMA((heads, 3)),
            pltpu.SemaphoreType.DMA((heads,)),
        ],
        compiler_params=pltpu.CompilerParams(vmem_limit_bytes=VMEM_MOST),
    )(me, q, k, v, doc_ids.reshape(rows // HD, HD))


def unpack_kernel(listed, heads, rows, me_s, *refs):
    outs, done = refs[-4:-1], refs[-1]
    own = lax.rem(me_s[0], heads)
    copies = []
    for place, (d, block) in enumerate(zip(listed, refs)):
        columns = aligned(own ^ d, HD)
        for part, out in enumerate(outs):
            source = block.at[pl.ds(part * rows, rows), :]
            copies.append(pltpu.make_async_copy(source, out.at[:, columns], done.at[place, part]))
            copies[-1].start()
    for copy in copies:
        copy.wait()


def unpack_heads(me, listed, blocks, rows, heads, partial=()):
    count = len(blocks)
    return pl.pallas_call(
        functools.partial(unpack_kernel, listed, heads, rows),
        in_specs=[SMEM_SPEC] + [VMEM_SPEC] * count + [ANY_SPEC] * len(partial),
        out_specs=[ANY_SPEC] * 3,
        out_shape=[jax.ShapeDtypeStruct((rows, heads * HD), blocks[0].dtype)] * 3,
        scratch_shapes=[pltpu.SemaphoreType.DMA((count, 3))],
        input_output_aliases={1 + count + i: i for i in range(len(partial))},
        compiler_params=params([*blocks]),
    )(me, *blocks, *partial)


def project_kernel(first, o_ref, w_ref, *refs):
    out_ref = refs[-1]
    for pair in range(w_ref.shape[0] // (2 * HD)):
        part = slice(pair * 2 * HD, (pair + 1) * 2 * HD)
        both = dot32(o_ref[...], w_ref[part, :], NT)
        out_ref[:, part] = both if first else refs[0][:, part] + both


def project_last_kernel(me_s, o_ref, w_ref, acc_ref, *outs):
    pairs = len(outs) // 2
    odd = lax.rem(me_s[0], 2) == 1
    for j in range(pairs):
        part = aligned(lax.rem(me_s[0] // 2, pairs) ^ j, 2 * HD)
        both = (acc_ref[:, part] + dot32(o_ref[...], w_ref[part, :], NT)).astype(jnp.bfloat16)
        outs[2 * j][...] = jnp.where(odd, both[:, HD:], both[:, :HD])
        outs[2 * j + 1][...] = jnp.where(odd, both[:, :HD], both[:, HD:])


def project(me, weight, features, acc, last):
    rows, width = features.shape
    columns = weight.shape[0]
    heads = columns // HD
    total = jax.ShapeDtypeStruct((rows, columns), jnp.float32)
    cost = pl.CostEstimate(
        flops=2 * rows * width * columns,
        bytes_accessed=2 * width * columns + 8 * rows * columns,
        transcendentals=0,
    )
    if last:
        return pl.pallas_call(
            project_last_kernel,
            in_specs=[SMEM_SPEC] + [VMEM_SPEC] * 3,
            out_specs=[VMEM_SPEC] * heads,
            out_shape=[jax.ShapeDtypeStruct((rows, HD), jnp.bfloat16)] * heads,
            compiler_params=params([features, weight, total, total]),
            cost_estimate=cost,
        )(me, features, weight, acc)
    operands = (features, weight) + (() if acc is None else (acc,))
    return pl.pallas_call(
        functools.partial(project_kernel, acc is None),
        in_specs=[VMEM_SPEC] * len(operands),
        out_specs=VMEM_SPEC,
        out_shape=total,
        compiler_params=params([features, weight, total, total]),
        cost_estimate=cost,
    )(*operands)


def at_or_before(q0, k0, shape):
    key = lax.broadcasted_iota(jnp.int32, shape, 0)
    return key <= q0 - k0 + lax.broadcasted_iota(jnp.int32, (1, shape[1]), 1)


def block_sizes(total):
    return (
        (block_size(total, 256), block_size(total, 256)),
        (block_size(total, 256), block_size(total, 256)),
    )


def plan_size(total, bq, bk):
    return sum(((q + 1) * bq + bk - 1) // bk for q in range(total // bq)) + 2


def fill_plan(lows, total, bq, bk, own, plan_q, plan_k, count_ref):
    def put(qi):
        def at(ki, count):
            plan_q[count] = qi
            plan_k[count] = ki
            return count + 1

        return at

    spans = []
    for qi, low in enumerate(lows):
        low, high = low // bk, ((qi + 1) * bq + bk - 1) // bk
        if own is not None:
            wanted = ((qi + 1) * bq > own[0]) & (qi * bq < own[1])
            low = jnp.where(wanted, low, jnp.maximum(low, own[0] // bk))
            high = jnp.where(wanted, high, jnp.minimum(high, (own[1] + bk - 1) // bk))
        whole = jnp.maximum(low, jnp.minimum(high, qi * bq // bk))
        spans.append((low, whole, high))
    count = 0
    for qi, (low, whole, high) in enumerate(spans):
        count = lax.fori_loop(low, whole, put(qi), count)
    count_ref[0] = jnp.maximum(count - 1, 0) // 2
    for qi, (low, whole, high) in enumerate(spans):
        count = lax.fori_loop(whole, high, put(qi), count)
    count_ref[1] = (count + 1) // 2
    for spare in range(2):
        plan_q[count + spare] = 0
        plan_k[count + spare] = total // bk - 1


def pipelined(plan_q, plan_k, count_ref, early, late, buffers):
    early(0, plan_q[0], plan_k[0], buffers[0], True)

    def turns(diagonal):
        def body(i, carry):
            for turn in range(2):
                now = 2 * i + turn
                late(now, plan_q[now], plan_k[now], buffers[turn])
                early(now + 1, plan_q[now + 1], plan_k[now + 1], buffers[1 - turn], diagonal)
            return carry

        return body

    lax.fori_loop(0, count_ref[0], turns(False), 0)
    lax.fori_loop(count_ref[0], count_ref[1], turns(True), 0)


def forward_kernel(peers, heads, rows, bq, bk, kept, me_s, *refs):
    blocks = refs[:peers]
    if kept:
        p_list, top_list = refs[peers + 6:peers + 8]
        refs = refs[:peers + 6] + refs[peers + 8:]
    v_ref, qx_ref, kx_ref, kt_ref, rows_ref, log_ref = refs[peers:peers + 6]
    plan_q, plan_k, count_ref, own_q, own_k, own_count = refs[peers + 6:peers + 12]
    vt_ref, out_ref, doc_ref, sum_ref, s0, top0, s1, top1 = refs[peers + 12:]
    total = v_ref.shape[0]
    factor = HD ** (-0.5) * math.log2(math.e)
    me = me_s[0]
    for d, block in enumerate(blocks):
        place = me ^ d
        for part, ref in enumerate((qx_ref.at[:, :HD], kx_ref.at[:, :HD], v_ref)):
            ref[aligned(place, rows), :] = block[part * rows:(part + 1) * rows, :]
        docs = block[3 * rows:, :].astype(jnp.float32)
        for t in range(rows // HD):
            doc_ref[:, aligned(place * (rows // HD) + t, HD)] = docs[t:t + 1, :]
    docs = doc_ref[...]
    first = jnp.zeros(docs.shape, jnp.float32)
    for value in range(1, DOC_VALUES):
        before = jnp.sum((docs < value).astype(jnp.float32))
        first = jnp.where(docs >= value, before, first)
    first = first.astype(jnp.int32)
    back_q, back_k = block_sizes(total)[1]
    lows = [jnp.min(first[:, qi * back_q:(qi + 1) * back_q]) for qi in range(total // back_q)]
    group = (me // heads) * heads * rows
    own = None if heads == peers else (group, group + heads * rows)
    fill_plan(lows, total, back_q, back_k, own, plan_q, plan_k, count_ref)
    if kept:
        own_q, own_k, own_count = plan_q, plan_k, count_ref
    else:
        lows = [jnp.min(first[:, qi * bq:(qi + 1) * bq]) for qi in range(total // bq)]
        fill_plan(lows, total, bq, bk, None, own_q, own_k, own_count)
    same = lax.broadcasted_iota(jnp.int32, (HD, total), 0).astype(jnp.float32) == docs
    ones = jnp.where(same, 1.0, 0.0).astype(jnp.bfloat16).T
    kx_ref[:, HD:] = ones
    qx_ref[:, HD:] = ((1.0 - ones.astype(jnp.float32)) * NEG_LARGE).astype(jnp.bfloat16)
    kt_ref[...] = kx_ref[:, :HD].T
    vt_ref[:HD, :] = v_ref[...].T
    vt_ref[HD:, :] = jnp.ones((ONES_ROWS, total), jnp.bfloat16)
    out_ref[...] = jnp.zeros_like(out_ref)
    log_ref[...] = jnp.full_like(log_ref, NEG_LARGE)
    sum_ref[...] = jnp.zeros_like(sum_ref)

    def early(now, qi, ki, buffer, diagonal):
        s_ref, top_ref = buffer
        keys, queries = aligned(ki, bk), aligned(qi, bq)
        s = dot32(kx_ref[keys, :], qx_ref[queries, :], NT) * factor
        if diagonal:
            s = jnp.where(at_or_before(qi * bq, ki * bk, (bk, bq)), s, NEG_LARGE)
        s_ref[...] = s
        top_ref[...] = jnp.max(s, axis=0, keepdims=True)

    def late(now, qi, ki, buffer):
        s_ref, top_ref = buffer
        keys, queries = aligned(ki, bk), aligned(qi, bq)
        top = log_ref[:, queries]
        new_top = jnp.maximum(top, top_ref[...])
        fix = jnp.exp2(top - new_top)
        vt = vt_ref[:, keys]
        p = jnp.exp2(s_ref[...] - new_top)
        high = p.astype(jnp.bfloat16)
        sums = dot32(vt, high)
        if kept:
            p_list[now] = high
            top_list[now] = new_top
        else:
            sums = sums + dot32(vt, (p - high.astype(jnp.float32)).astype(jnp.bfloat16))
        out_ref[:, queries] = out_ref[:, queries] * fix + sums[:HD, :]
        sum_ref[:, queries] = sum_ref[:, queries] * fix + sums[HD:HD + 1, :]
        log_ref[:, queries] = new_top

    pipelined(own_q, own_k, own_count, early, late, ((s0, top0), (s1, top1)))
    total_p = sum_ref[...]
    rows_ref[...] = (out_ref[...] / total_p).T
    log_ref[...] = log_ref[...] + jnp.log2(total_p)


def backward_kernel(listed, heads, rows, bq, bk, kept, me_s, plan_q, plan_k, count_ref, v_ref,
                    qx_ref, kx_ref, kt_ref, rows_ref, log_ref, *refs):
    if kept:
        p_list, top_list = refs[:2]
        refs = refs[2:]
    peers = len(listed)
    blocks = refs[:peers]
    results = refs[peers:peers + heads]
    g_ref, dot_ref, dk_acc, dv_acc, dq_acc, p0, ds0, p1, ds1 = refs[peers + heads:]
    scale = HD ** (-0.5)
    factor = scale * math.log2(math.e)
    me = me_s[0]
    for d, block in zip(listed, blocks):
        g_ref[aligned(me ^ d, rows), :] = block[...]
    ones = jnp.ones((ONES_ROWS, HD), jnp.bfloat16)
    for start in range(0, g_ref.shape[0], bq):
        part = slice(start, start + bq)
        left = g_ref[part, :].astype(jnp.float32) * rows_ref[part, :]
        dots = 0.0
        for _ in range(3):
            term = left.astype(jnp.bfloat16)
            left = left - term.astype(jnp.float32)
            dots = dots + dot32(ones, term, NT)
        dot_ref[:, part] = dots[:1, :]
    dk_acc[...] = jnp.zeros_like(dk_acc)
    dv_acc[...] = jnp.zeros_like(dv_acc)
    dq_acc[...] = jnp.zeros_like(dq_acc)

    def early(now, qi, ki, buffer, diagonal):
        p_ref, ds_ref = buffer
        queries = aligned(qi, bq)
        log_row, dot_row = log_ref[:, queries], dot_ref[:, queries]
        if kept:
            share = jnp.exp2(top_list[now] - log_row)
        for strip in range(0, bk, STRIP):
            part = slice(strip, strip + STRIP)
            keys = aligned(ki * (bk // STRIP) + strip // STRIP, STRIP)
            if kept:
                p = p_list[now, part, :].astype(jnp.float32) * share
            else:
                p = jnp.exp2(dot32(kx_ref[keys, :], qx_ref[queries, :], NT) * factor - log_row)
                if diagonal:
                    p = jnp.where(at_or_before(qi * bq, ki * bk + strip, (STRIP, bq)), p, 0.0)
            p_ref[part, :] = p.astype(jnp.bfloat16)
            dp = dot32(v_ref[keys, :], g_ref[queries, :], NT)
            ds_ref[part, :] = (p * (dp - dot_row)).astype(jnp.bfloat16)

    def late(now, qi, ki, buffer):
        p_ref, ds_ref = buffer
        keys, queries = aligned(ki, bk), aligned(qi, bq)
        dv_acc[keys, :] += dot32(p_ref[...], g_ref[queries, :])
        dk_acc[keys, :] += dot32(ds_ref[...], qx_ref[queries, :HD])
        dq_acc[:, queries] += dot32(kt_ref[:, keys], ds_ref[...])

    pipelined(plan_q, plan_k, count_ref, early, late, ((p0, ds0), (p1, ds1)))
    for d, result in enumerate(results):
        own = aligned(me ^ d, rows)
        result[:rows, :] = (scale * dq_acc[:, own]).astype(result.dtype).T
        result[rows:2 * rows, :] = (scale * dk_acc[own, :]).astype(result.dtype)
        result[2 * rows:, :] = dv_acc[own, :].astype(result.dtype)


def keeps_list(total, peers, heads):
    forward, backward = block_sizes(total)
    size = plan_size(total, *forward) * math.prod(forward) * 2
    return forward == backward and heads == peers and size <= LIST_BYTES


def attention_cost(total, products):
    return pl.CostEstimate(
        flops=products * total * total * HD // 2,
        bytes_accessed=16 * total * HD,
        transcendentals=total * total // 4,
    )


def attention_forward(me, blocks, rows, heads):
    peers = len(blocks)
    total = peers * rows
    (bq, bk), back = block_sizes(total)
    plan = [(plan_size(total, *back),)] * 2 + [(2,)]
    own_plan = [(plan_size(total, bq, bk),)] * 2 + [(2,)]
    vectors = [
        jax.ShapeDtypeStruct((total, HD), jnp.bfloat16),
        *[jax.ShapeDtypeStruct((total, 2 * HD), jnp.bfloat16)] * 2,
        jax.ShapeDtypeStruct((HD, total), jnp.bfloat16),
        jax.ShapeDtypeStruct((total, HD), jnp.float32),
        jax.ShapeDtypeStruct((1, total), jnp.float32),
    ]
    kept = keeps_list(total, peers, heads)
    if kept:
        vectors.append(jax.ShapeDtypeStruct((*own_plan[0], bk, bq), jnp.bfloat16))
        vectors.append(jax.ShapeDtypeStruct((*own_plan[0], 1, bq), jnp.float32))
    scratch = [
        pltpu.VMEM((HD + ONES_ROWS, total), jnp.bfloat16),
        pltpu.VMEM((HD, total), jnp.float32),
        pltpu.VMEM((1, total), jnp.float32),
        pltpu.VMEM((1, total), jnp.float32),
        *[pltpu.VMEM((bk, bq), jnp.float32), pltpu.VMEM((1, bq), jnp.float32)] * 2,
    ]
    return pl.pallas_call(
        functools.partial(forward_kernel, peers, heads, rows, bq, bk, kept),
        in_specs=[SMEM_SPEC] + [VMEM_SPEC] * peers,
        out_specs=[VMEM_SPEC] * len(vectors) + [SMEM_SPEC] * 3,
        out_shape=vectors + [jax.ShapeDtypeStruct(shape, jnp.int32) for shape in plan],
        scratch_shapes=[pltpu.SMEM(shape, jnp.int32) for shape in own_plan] + scratch,
        compiler_params=params([*blocks, *vectors], scratch),
        cost_estimate=attention_cost(total, 3),
    )(me, *blocks)


def attention_backward(me, heads, state, listed, blocks):
    peers, rows = len(blocks), blocks[0].shape[0]
    total = peers * rows
    bq, bk = block_sizes(total)[1]
    vectors, plan = state[:-3], state[-3:]
    kept = keeps_list(total, peers, heads)
    out_shape = [jax.ShapeDtypeStruct((3 * rows, HD), jnp.bfloat16)] * heads
    scratch = [
        pltpu.VMEM((total, HD), jnp.bfloat16),
        pltpu.VMEM((1, total), jnp.float32),
        pltpu.VMEM((total, HD), jnp.float32),
        pltpu.VMEM((total, HD), jnp.float32),
        pltpu.VMEM((HD, total), jnp.float32),
        *[pltpu.VMEM((bk, bq), jnp.bfloat16)] * 4,
    ]
    return pl.pallas_call(
        functools.partial(backward_kernel, listed, heads, rows, bq, bk, kept),
        in_specs=[SMEM_SPEC] * 4 + [VMEM_SPEC] * (len(vectors) + peers),
        out_specs=[VMEM_SPEC] * heads,
        out_shape=out_shape,
        scratch_shapes=scratch,
        compiler_params=params([*vectors, *blocks, *out_shape], scratch),
        cost_estimate=attention_cost(total, 5),
    )(me, *plan, *vectors, *blocks)


def per_device(peers, groups, queries, keys_in, values, out_grad, out_weight, doc_ids):
    rows, width = queries.shape
    heads = width // HD
    me = lax.axis_index("seq")
    me_vector = me.reshape(1)

    def exchange(x, d):
        return x if d == 0 else lax.ppermute(x, "seq", [(i, i ^ d) for i in range(peers)])

    def pass_on(x):
        return lax.ppermute(x, "head", [(i, (i + 1) % groups) for i in range(groups)])

    order = [*range(2, peers, 2), *range(peers - 1, 0, -2)]

    far_first = sorted(range(peers), key=lambda d: (-bin(d >> 1).count("1"), d & 1, d))
    returning = [d for d in far_first if d < heads]

    def exchange_all(blocks, listed):
        return [exchange(blocks[d % heads], d) for d in listed]

    packed = list(pack_heads(me_vector, queries, keys_in, values, doc_ids))
    received = exchange_all(packed, range(peers))

    def share(step):
        return len(order) * step * (step + 1) // ((groups - 2) * (groups - 1))

    after = lax.optimization_barrier
    features, acc = out_grad, None
    weights = []
    for step in range(groups):
        block = lax.rem(lax.axis_index("head") + groups - step, groups)
        weights.append(lax.dynamic_slice_in_dim(out_weight, block * width, width, 1))
    for step in range(groups):
        last = step == groups - 1
        if not last:
            passed = pass_on(features)
        if step == groups - 2:
            received[0], features = after((received[0], features))
            state = list(attention_forward(me_vector, received, rows, heads))
            features, state[1] = after((features, state[1]))
        acc = project(me_vector, weights[step], features, acc, last)
        if not last:
            features = passed
            if step < groups - 2:
                batch = order[share(step):share(step + 1)]
                here = [received[d] for d in batch]
                features, acc, here, weights[2:] = after((features, acc, here, weights[2:]))
                for d, block in zip(batch, here):
                    received[d] = block
    grads = exchange_all(acc, far_first)

    results = attention_backward(me_vector, heads, state, far_first, grads)
    returned = exchange_all(results, returning)
    early = [d for d in returning if d == 0 or bin(d >> 1).count("1") > 1]
    late = [d for d in returning if d not in early]
    block_of = dict(zip(returning, returned))
    partial = unpack_heads(me_vector, early, [block_of[d] for d in early], rows, heads)
    return tuple(unpack_heads(me_vector, late, [block_of[d] for d in late], rows, heads, partial))


def solution(mesh):
    in_specs = (
        P("seq", "head"),
        P("seq", "head"),
        P("seq", "head"),
        P("seq", "head"),
        P("head", None),
        P("seq"),
    )
    out_specs = (P("seq", "head"), P("seq", "head"), P("seq", "head"))
    return jax.shard_map(
        functools.partial(per_device, mesh.shape["seq"], mesh.shape["head"]),
        mesh=mesh, in_specs=in_specs, out_specs=out_specs, check_vma=False,
    )
```

```python
import functools
import math

import jax
import jax.numpy as jnp
from jax import lax
from jax.experimental import pallas as pl
from jax.experimental.pallas import tpu as pltpu
from jax.sharding import PartitionSpec as P

HD = 128
DOC_VALUES = 8
DOC_ROWS = 16
ONES_ROWS = 16
STRIP = 64
NEG_LARGE = -1e30
VMEM_SPARE = 6 * 1024 * 1024
VMEM_MOST = 56 * 1024 * 1024
LIST_BYTES = 16 * 1024 * 1024

NN = (((1,), (0,)), ((), ()))
NT = (((1,), (1,)), ((), ()))
SMEM_SPEC = pl.BlockSpec(memory_space=pltpu.SMEM)
VMEM_SPEC = pl.BlockSpec(memory_space=pltpu.VMEM)
ANY_SPEC = pl.BlockSpec(memory_space=pl.ANY)


def dot32(a, b, dims=NN):
    return lax.dot_general(a, b, dims, preferred_element_type=jnp.float32)


def block_size(total, wanted):
    size = min(wanted, total)
    while total % size or size % 128:
        size -= 128
    return size


def aligned(index, size):
    return pl.ds(pl.multiple_of(index * size, size), size)


def params(arrays, scratch=()):
    total = sum(math.prod(a.shape) * jnp.dtype(a.dtype).itemsize for a in (*arrays, *scratch))
    return pltpu.CompilerParams(vmem_limit_bytes=total + VMEM_SPARE)


def pack_kernel(heads, rows, me_s, q_ref, k_ref, v_ref, doc_ref, *outs):
    own = lax.rem(me_s[0], heads)
    docs = doc_ref[...].astype(jnp.float32)
    docs = jnp.concatenate([docs, jnp.zeros((DOC_ROWS - docs.shape[0], HD), jnp.float32)], axis=0)
    docs = docs.astype(jnp.bfloat16)
    for d, out in enumerate(outs):
        columns = aligned(own ^ d, HD)
        for part, ref in enumerate((q_ref, k_ref, v_ref)):
            out[part * rows:(part + 1) * rows, :] = ref[:, columns]
        out[3 * rows:, :] = docs


def pack_heads(me, q, k, v, doc_ids):
    rows, width = q.shape
    heads = width // HD
    return pl.pallas_call(
        functools.partial(pack_kernel, heads, rows),
        in_specs=[SMEM_SPEC] + [VMEM_SPEC] * 4,
        out_specs=[VMEM_SPEC] * heads,
        out_shape=[jax.ShapeDtypeStruct((3 * rows + DOC_ROWS, HD), q.dtype)] * heads,
        compiler_params=pltpu.CompilerParams(vmem_limit_bytes=VMEM_MOST),
    )(me, q, k, v, doc_ids.reshape(rows // HD, HD))


def unpack_kernel(listed, heads, rows, me_s, *refs):
    outs, done = refs[-4:-1], refs[-1]
    own = lax.rem(me_s[0], heads)
    copies = []
    for place, (d, block) in enumerate(zip(listed, refs)):
        columns = aligned(own ^ d, HD)
        for part, out in enumerate(outs):
            source = block.at[pl.ds(part * rows, rows), :]
            copies.append(pltpu.make_async_copy(source, out.at[:, columns], done.at[place, part]))
            copies[-1].start()
    for copy in copies:
        copy.wait()


def unpack_heads(me, listed, blocks, rows, heads, partial=()):
    count = len(blocks)
    return pl.pallas_call(
        functools.partial(unpack_kernel, listed, heads, rows),
        in_specs=[SMEM_SPEC] + [VMEM_SPEC] * count + [ANY_SPEC] * len(partial),
        out_specs=[ANY_SPEC] * 3,
        out_shape=[jax.ShapeDtypeStruct((rows, heads * HD), blocks[0].dtype)] * 3,
        scratch_shapes=[pltpu.SemaphoreType.DMA((count, 3))],
        input_output_aliases={1 + count + i: i for i in range(len(partial))},
        compiler_params=params([*blocks]),
    )(me, *blocks, *partial)


def project_kernel(first, o_ref, w_ref, *refs):
    out_ref = refs[-1]
    for pair in range(w_ref.shape[0] // (2 * HD)):
        part = slice(pair * 2 * HD, (pair + 1) * 2 * HD)
        both = dot32(o_ref[...], w_ref[part, :], NT)
        out_ref[:, part] = both if first else refs[0][:, part] + both


def project_last_kernel(me_s, o_ref, w_ref, acc_ref, *outs):
    pairs = len(outs) // 2
    odd = lax.rem(me_s[0], 2) == 1
    for j in range(pairs):
        part = aligned(lax.rem(me_s[0] // 2, pairs) ^ j, 2 * HD)
        both = (acc_ref[:, part] + dot32(o_ref[...], w_ref[part, :], NT)).astype(jnp.bfloat16)
        outs[2 * j][...] = jnp.where(odd, both[:, HD:], both[:, :HD])
        outs[2 * j + 1][...] = jnp.where(odd, both[:, :HD], both[:, HD:])


def project(me, weight, features, acc, last):
    rows, width = features.shape
    columns = weight.shape[0]
    heads = columns // HD
    total = jax.ShapeDtypeStruct((rows, columns), jnp.float32)
    cost = pl.CostEstimate(
        flops=2 * rows * width * columns,
        bytes_accessed=2 * width * columns + 8 * rows * columns,
        transcendentals=0,
    )
    if last:
        return pl.pallas_call(
            project_last_kernel,
            in_specs=[SMEM_SPEC] + [VMEM_SPEC] * 3,
            out_specs=[VMEM_SPEC] * heads,
            out_shape=[jax.ShapeDtypeStruct((rows, HD), jnp.bfloat16)] * heads,
            compiler_params=params([features, weight, total, total]),
            cost_estimate=cost,
        )(me, features, weight, acc)
    operands = (features, weight) + (() if acc is None else (acc,))
    return pl.pallas_call(
        functools.partial(project_kernel, acc is None),
        in_specs=[VMEM_SPEC] * len(operands),
        out_specs=VMEM_SPEC,
        out_shape=total,
        compiler_params=params([features, weight, total, total]),
        cost_estimate=cost,
    )(*operands)


def at_or_before(q0, k0, shape):
    key = lax.broadcasted_iota(jnp.int32, shape, 0)
    return key <= q0 - k0 + lax.broadcasted_iota(jnp.int32, (1, shape[1]), 1)


def block_sizes(total):
    return (
        (block_size(total, 256), block_size(total, 256)),
        (block_size(total, 256), block_size(total, 256)),
    )


def plan_size(total, bq, bk):
    return sum(((q + 1) * bq + bk - 1) // bk for q in range(total // bq)) + 2


def fill_plan(lows, total, bq, bk, own, plan_q, plan_k, count_ref):
    def put(qi):
        def at(ki, count):
            plan_q[count] = qi
            plan_k[count] = ki
            return count + 1

        return at

    spans = []
    for qi, low in enumerate(lows):
        low, high = low // bk, ((qi + 1) * bq + bk - 1) // bk
        if own is not None:
            wanted = ((qi + 1) * bq > own[0]) & (qi * bq < own[1])
            low = jnp.where(wanted, low, jnp.maximum(low, own[0] // bk))
            high = jnp.where(wanted, high, jnp.minimum(high, (own[1] + bk - 1) // bk))
        whole = jnp.maximum(low, jnp.minimum(high, qi * bq // bk))
        spans.append((low, whole, high))
    count = 0
    for qi, (low, whole, high) in enumerate(spans):
        count = lax.fori_loop(low, whole, put(qi), count)
    count_ref[0] = jnp.maximum(count - 1, 0) // 2
    for qi, (low, whole, high) in enumerate(spans):
        count = lax.fori_loop(whole, high, put(qi), count)
    count_ref[1] = (count + 1) // 2
    for spare in range(2):
        plan_q[count + spare] = 0
        plan_k[count + spare] = total // bk - 1


def pipelined(plan_q, plan_k, count_ref, early, late, buffers):
    early(0, plan_q[0], plan_k[0], buffers[0], True)

    def turns(diagonal):
        def body(i, carry):
            for turn in range(2):
                now = 2 * i + turn
                late(now, plan_q[now], plan_k[now], buffers[turn])
                early(now + 1, plan_q[now + 1], plan_k[now + 1], buffers[1 - turn], diagonal)
            return carry

        return body

    lax.fori_loop(0, count_ref[0], turns(False), 0)
    lax.fori_loop(count_ref[0], count_ref[1], turns(True), 0)


def forward_kernel(peers, heads, rows, bq, bk, kept, me_s, *refs):
    blocks = refs[:peers]
    if kept:
        p_list, top_list = refs[peers + 6:peers + 8]
        refs = refs[:peers + 6] + refs[peers + 8:]
    v_ref, qx_ref, kx_ref, kt_ref, rows_ref, log_ref = refs[peers:peers + 6]
    plan_q, plan_k, count_ref, own_q, own_k, own_count = refs[peers + 6:peers + 12]
    vt_ref, out_ref, doc_ref, sum_ref, s0, top0, s1, top1 = refs[peers + 12:]
    total = v_ref.shape[0]
    factor = HD ** (-0.5) * math.log2(math.e)
    me = me_s[0]
    for d, block in enumerate(blocks):
        place = me ^ d
        for part, ref in enumerate((qx_ref.at[:, :HD], kx_ref.at[:, :HD], v_ref)):
            ref[aligned(place, rows), :] = block[part * rows:(part + 1) * rows, :]
        docs = block[3 * rows:, :].astype(jnp.float32)
        for t in range(rows // HD):
            doc_ref[:, aligned(place * (rows // HD) + t, HD)] = docs[t:t + 1, :]
    docs = doc_ref[...]
    first = jnp.zeros(docs.shape, jnp.float32)
    for value in range(1, DOC_VALUES):
        before = jnp.sum((docs < value).astype(jnp.float32))
        first = jnp.where(docs >= value, before, first)
    first = first.astype(jnp.int32)
    back_q, back_k = block_sizes(total)[1]
    lows = [jnp.min(first[:, qi * back_q:(qi + 1) * back_q]) for qi in range(total // back_q)]
    group = (me // heads) * heads * rows
    own = None if heads == peers else (group, group + heads * rows)
    fill_plan(lows, total, back_q, back_k, own, plan_q, plan_k, count_ref)
    if kept:
        own_q, own_k, own_count = plan_q, plan_k, count_ref
    else:
        lows = [jnp.min(first[:, qi * bq:(qi + 1) * bq]) for qi in range(total // bq)]
        fill_plan(lows, total, bq, bk, None, own_q, own_k, own_count)
    same = lax.broadcasted_iota(jnp.int32, (HD, total), 0).astype(jnp.float32) == docs
    ones = jnp.where(same, 1.0, 0.0).astype(jnp.bfloat16).T
    kx_ref[:, HD:] = ones
    qx_ref[:, HD:] = ((1.0 - ones.astype(jnp.float32)) * NEG_LARGE).astype(jnp.bfloat16)
    kt_ref[...] = kx_ref[:, :HD].T
    vt_ref[:HD, :] = v_ref[...].T
    vt_ref[HD:, :] = jnp.ones((ONES_ROWS, total), jnp.bfloat16)
    out_ref[...] = jnp.zeros_like(out_ref)
    log_ref[...] = jnp.full_like(log_ref, NEG_LARGE)
    sum_ref[...] = jnp.zeros_like(sum_ref)

    def early(now, qi, ki, buffer, diagonal):
        s_ref, top_ref = buffer
        keys, queries = aligned(ki, bk), aligned(qi, bq)
        s = dot32(kx_ref[keys, :], qx_ref[queries, :], NT) * factor
        if diagonal:
            s = jnp.where(at_or_before(qi * bq, ki * bk, (bk, bq)), s, NEG_LARGE)
        s_ref[...] = s
        top_ref[...] = jnp.max(s, axis=0, keepdims=True)

    def late(now, qi, ki, buffer):
        s_ref, top_ref = buffer
        keys, queries = aligned(ki, bk), aligned(qi, bq)
        top = log_ref[:, queries]
        new_top = jnp.maximum(top, top_ref[...])
        fix = jnp.exp2(top - new_top)
        vt = vt_ref[:, keys]
        p = jnp.exp2(s_ref[...] - new_top)
        high = p.astype(jnp.bfloat16)
        sums = dot32(vt, high)
        if kept:
            p_list[now] = high
            top_list[now] = new_top
        else:
            sums = sums + dot32(vt, (p - high.astype(jnp.float32)).astype(jnp.bfloat16))
        out_ref[:, queries] = out_ref[:, queries] * fix + sums[:HD, :]
        sum_ref[:, queries] = sum_ref[:, queries] * fix + sums[HD:HD + 1, :]
        log_ref[:, queries] = new_top

    pipelined(own_q, own_k, own_count, early, late, ((s0, top0), (s1, top1)))
    total_p = sum_ref[...]
    rows_ref[...] = (out_ref[...] / total_p).T
    log_ref[...] = log_ref[...] + jnp.log2(total_p)


def backward_kernel(listed, heads, rows, bq, bk, kept, me_s, plan_q, plan_k, count_ref, v_ref,
                    qx_ref, kx_ref, kt_ref, rows_ref, log_ref, *refs):
    if kept:
        p_list, top_list = refs[:2]
        refs = refs[2:]
    peers = len(listed)
    blocks = refs[:peers]
    results = refs[peers:peers + heads]
    g_ref, dot_ref, dk_acc, dv_acc, dq_acc, p0, ds0, p1, ds1 = refs[peers + heads:]
    scale = HD ** (-0.5)
    factor = scale * math.log2(math.e)
    me = me_s[0]
    for d, block in zip(listed, blocks):
        g_ref[aligned(me ^ d, rows), :] = block[...]
    ones = jnp.ones((ONES_ROWS, HD), jnp.bfloat16)
    for start in range(0, g_ref.shape[0], bq):
        part = slice(start, start + bq)
        left = g_ref[part, :].astype(jnp.float32) * rows_ref[part, :]
        dots = 0.0
        for _ in range(3):
            term = left.astype(jnp.bfloat16)
            left = left - term.astype(jnp.float32)
            dots = dots + dot32(ones, term, NT)
        dot_ref[:, part] = dots[:1, :]
    dk_acc[...] = jnp.zeros_like(dk_acc)
    dv_acc[...] = jnp.zeros_like(dv_acc)
    dq_acc[...] = jnp.zeros_like(dq_acc)

    def early(now, qi, ki, buffer, diagonal):
        p_ref, ds_ref = buffer
        queries = aligned(qi, bq)
        log_row, dot_row = log_ref[:, queries], dot_ref[:, queries]
        if kept:
            share = jnp.exp2(top_list[now] - log_row)
        for strip in range(0, bk, STRIP):
            part = slice(strip, strip + STRIP)
            keys = aligned(ki * (bk // STRIP) + strip // STRIP, STRIP)
            if kept:
                p = p_list[now, part, :].astype(jnp.float32) * share
            else:
                p = jnp.exp2(dot32(kx_ref[keys, :], qx_ref[queries, :], NT) * factor - log_row)
                if diagonal:
                    p = jnp.where(at_or_before(qi * bq, ki * bk + strip, (STRIP, bq)), p, 0.0)
            p_ref[part, :] = p.astype(jnp.bfloat16)
            dp = dot32(v_ref[keys, :], g_ref[queries, :], NT)
            ds_ref[part, :] = (p * (dp - dot_row)).astype(jnp.bfloat16)

    def late(now, qi, ki, buffer):
        p_ref, ds_ref = buffer
        keys, queries = aligned(ki, bk), aligned(qi, bq)
        dv_acc[keys, :] += dot32(p_ref[...], g_ref[queries, :])
        dk_acc[keys, :] += dot32(ds_ref[...], qx_ref[queries, :HD])
        dq_acc[:, queries] += dot32(kt_ref[:, keys], ds_ref[...])

    pipelined(plan_q, plan_k, count_ref, early, late, ((p0, ds0), (p1, ds1)))
    for d, result in enumerate(results):
        own = aligned(me ^ d, rows)
        result[:rows, :] = (scale * dq_acc[:, own]).astype(result.dtype).T
        result[rows:2 * rows, :] = (scale * dk_acc[own, :]).astype(result.dtype)
        result[2 * rows:, :] = dv_acc[own, :].astype(result.dtype)


def keeps_list(total, peers, heads):
    forward, backward = block_sizes(total)
    size = plan_size(total, *forward) * math.prod(forward) * 2
    return forward == backward and heads == peers and size <= LIST_BYTES


def attention_cost(total, products):
    return pl.CostEstimate(
        flops=products * total * total * HD // 2,
        bytes_accessed=16 * total * HD,
        transcendentals=total * total // 4,
    )


def attention_forward(me, blocks, rows, heads):
    peers = len(blocks)
    total = peers * rows
    (bq, bk), back = block_sizes(total)
    plan = [(plan_size(total, *back),)] * 2 + [(2,)]
    own_plan = [(plan_size(total, bq, bk),)] * 2 + [(2,)]
    vectors = [
        jax.ShapeDtypeStruct((total, HD), jnp.bfloat16),
        *[jax.ShapeDtypeStruct((total, 2 * HD), jnp.bfloat16)] * 2,
        jax.ShapeDtypeStruct((HD, total), jnp.bfloat16),
        jax.ShapeDtypeStruct((total, HD), jnp.float32),
        jax.ShapeDtypeStruct((1, total), jnp.float32),
    ]
    kept = keeps_list(total, peers, heads)
    if kept:
        vectors.append(jax.ShapeDtypeStruct((*own_plan[0], bk, bq), jnp.bfloat16))
        vectors.append(jax.ShapeDtypeStruct((*own_plan[0], 1, bq), jnp.float32))
    scratch = [
        pltpu.VMEM((HD + ONES_ROWS, total), jnp.bfloat16),
        pltpu.VMEM((HD, total), jnp.float32),
        pltpu.VMEM((1, total), jnp.float32),
        pltpu.VMEM((1, total), jnp.float32),
        *[pltpu.VMEM((bk, bq), jnp.float32), pltpu.VMEM((1, bq), jnp.float32)] * 2,
    ]
    return pl.pallas_call(
        functools.partial(forward_kernel, peers, heads, rows, bq, bk, kept),
        in_specs=[SMEM_SPEC] + [VMEM_SPEC] * peers,
        out_specs=[VMEM_SPEC] * len(vectors) + [SMEM_SPEC] * 3,
        out_shape=vectors + [jax.ShapeDtypeStruct(shape, jnp.int32) for shape in plan],
        scratch_shapes=[pltpu.SMEM(shape, jnp.int32) for shape in own_plan] + scratch,
        compiler_params=params([*blocks, *vectors], scratch),
        cost_estimate=attention_cost(total, 3),
    )(me, *blocks)


def attention_backward(me, heads, state, listed, blocks):
    peers, rows = len(blocks), blocks[0].shape[0]
    total = peers * rows
    bq, bk = block_sizes(total)[1]
    vectors, plan = state[:-3], state[-3:]
    kept = keeps_list(total, peers, heads)
    out_shape = [jax.ShapeDtypeStruct((3 * rows, HD), jnp.bfloat16)] * heads
    scratch = [
        pltpu.VMEM((total, HD), jnp.bfloat16),
        pltpu.VMEM((1, total), jnp.float32),
        pltpu.VMEM((total, HD), jnp.float32),
        pltpu.VMEM((total, HD), jnp.float32),
        pltpu.VMEM((HD, total), jnp.float32),
        *[pltpu.VMEM((bk, bq), jnp.bfloat16)] * 4,
    ]
    return pl.pallas_call(
        functools.partial(backward_kernel, listed, heads, rows, bq, bk, kept),
        in_specs=[SMEM_SPEC] * 4 + [VMEM_SPEC] * (len(vectors) + peers),
        out_specs=[VMEM_SPEC] * heads,
        out_shape=out_shape,
        scratch_shapes=scratch,
        compiler_params=params([*vectors, *blocks, *out_shape], scratch),
        cost_estimate=attention_cost(total, 5),
    )(me, *plan, *vectors, *blocks)


def per_device(peers, groups, queries, keys_in, values, out_grad, out_weight, doc_ids):
    rows, width = queries.shape
    heads = width // HD
    me = lax.axis_index("seq")
    me_vector = me.reshape(1)

    def exchange(x, d):
        return x if d == 0 else lax.ppermute(x, "seq", [(i, i ^ d) for i in range(peers)])

    def pass_on(x):
        return lax.ppermute(x, "head", [(i, (i + 1) % groups) for i in range(groups)])

    order = [*range(2, peers, 2), *range(peers - 1, 0, -2)]

    far_first = sorted(range(peers), key=lambda d: (-bin(d >> 1).count("1"), d & 1, d))
    returning = [d for d in far_first if d < heads]

    def exchange_all(blocks, listed):
        return [exchange(blocks[d % heads], d) for d in listed]

    packed = list(pack_heads(me_vector, queries, keys_in, values, doc_ids))
    received = exchange_all(packed, range(peers))

    def share(step):
        return len(order) * step * (step + 1) // ((groups - 2) * (groups - 1))

    after = lax.optimization_barrier
    features, acc = out_grad, None
    weights = []
    for step in range(groups):
        block = lax.rem(lax.axis_index("head") + groups - step, groups)
        weights.append(lax.dynamic_slice_in_dim(out_weight, block * width, width, 1))
    for step in range(groups):
        last = step == groups - 1
        if not last:
            passed = pass_on(features)
        if step == groups - 2:
            received[0], features = after((received[0], features))
            state = list(attention_forward(me_vector, received, rows, heads))
            features, state[1] = after((features, state[1]))
        acc = project(me_vector, weights[step], features, acc, last)
        if not last:
            features = passed
            if step < groups - 2:
                batch = order[share(step):share(step + 1)]
                here = [received[d] for d in batch]
                features, acc, here, weights[2:] = after((features, acc, here, weights[2:]))
                for d, block in zip(batch, here):
                    received[d] = block
    grads = exchange_all(acc, far_first)

    results = attention_backward(me_vector, heads, state, far_first, grads)
    returned = exchange_all(results, returning)
    early = [d for d in returning if d == 0 or bin(d >> 1).count("1") > 1]
    late = [d for d in returning if d not in early]
    block_of = dict(zip(returning, returned))
    partial = unpack_heads(me_vector, early, [block_of[d] for d in early], rows, heads)
    return tuple(unpack_heads(me_vector, late, [block_of[d] for d in late], rows, heads, partial))


def solution(mesh):
    in_specs = (
        P("seq", "head"),
        P("seq", "head"),
        P("seq", "head"),
        P("seq", "head"),
        P("head", None),
        P("seq"),
    )
    out_specs = (P("seq", "head"), P("seq", "head"), P("seq", "head"))
    return jax.shard_map(
        functools.partial(per_device, mesh.shape["seq"], mesh.shape["head"]),
        mesh=mesh, in_specs=in_specs, out_specs=out_specs, check_vma=False,
    )
```

```python
import functools
import math

import jax
import jax.numpy as jnp
from jax import lax
from jax.experimental import pallas as pl
from jax.experimental.pallas import tpu as pltpu
from jax.sharding import PartitionSpec as P

HD = 128
DOC_VALUES = 8
DOC_ROWS = 16
ONES_ROWS = 16
STRIP = 128
NEG_LARGE = -1e30
VMEM_SPARE = 6 * 1024 * 1024
VMEM_MOST = 56 * 1024 * 1024
LIST_BYTES = 16 * 1024 * 1024

NN = (((1,), (0,)), ((), ()))
NT = (((1,), (1,)), ((), ()))
SMEM_SPEC = pl.BlockSpec(memory_space=pltpu.SMEM)
VMEM_SPEC = pl.BlockSpec(memory_space=pltpu.VMEM)
ANY_SPEC = pl.BlockSpec(memory_space=pl.ANY)


def dot32(a, b, dims=NN):
    return lax.dot_general(a, b, dims, preferred_element_type=jnp.float32)


def block_size(total, wanted):
    size = min(wanted, total)
    while total % size or size % 128:
        size -= 128
    return size


def aligned(index, size):
    return pl.ds(pl.multiple_of(index * size, size), size)


def params(arrays, scratch=()):
    total = sum(math.prod(a.shape) * jnp.dtype(a.dtype).itemsize for a in (*arrays, *scratch))
    return pltpu.CompilerParams(vmem_limit_bytes=total + VMEM_SPARE)


def pack_kernel(heads, rows, me_s, q_ref, k_ref, v_ref, doc_ref, *outs):
    own = lax.rem(me_s[0], heads)
    docs = doc_ref[...].astype(jnp.float32)
    docs = jnp.concatenate([docs, jnp.zeros((DOC_ROWS - docs.shape[0], HD), jnp.float32)], axis=0)
    docs = docs.astype(jnp.bfloat16)
    for d, out in enumerate(outs):
        columns = aligned(own ^ d, HD)
        for part, ref in enumerate((q_ref, k_ref, v_ref)):
            out[part * rows:(part + 1) * rows, :] = ref[:, columns]
        out[3 * rows:, :] = docs


def pack_heads(me, q, k, v, doc_ids):
    rows, width = q.shape
    heads = width // HD
    return pl.pallas_call(
        functools.partial(pack_kernel, heads, rows),
        in_specs=[SMEM_SPEC] + [VMEM_SPEC] * 4,
        out_specs=[VMEM_SPEC] * heads,
        out_shape=[jax.ShapeDtypeStruct((3 * rows + DOC_ROWS, HD), q.dtype)] * heads,
        compiler_params=pltpu.CompilerParams(vmem_limit_bytes=VMEM_MOST),
    )(me, q, k, v, doc_ids.reshape(rows // HD, HD))


def unpack_kernel(listed, heads, rows, me_s, *refs):
    outs, done = refs[-4:-1], refs[-1]
    own = lax.rem(me_s[0], heads)
    copies = []
    for place, (d, block) in enumerate(zip(listed, refs)):
        columns = aligned(own ^ d, HD)
        for part, out in enumerate(outs):
            source = block.at[pl.ds(part * rows, rows), :]
            copies.append(pltpu.make_async_copy(source, out.at[:, columns], done.at[place, part]))
            copies[-1].start()
    for copy in copies:
        copy.wait()


def unpack_heads(me, listed, blocks, rows, heads, partial=()):
    count = len(blocks)
    return pl.pallas_call(
        functools.partial(unpack_kernel, listed, heads, rows),
        in_specs=[SMEM_SPEC] + [VMEM_SPEC] * count + [ANY_SPEC] * len(partial),
        out_specs=[ANY_SPEC] * 3,
        out_shape=[jax.ShapeDtypeStruct((rows, heads * HD), blocks[0].dtype)] * 3,
        scratch_shapes=[pltpu.SemaphoreType.DMA((count, 3))],
        input_output_aliases={1 + count + i: i for i in range(len(partial))},
        compiler_params=params([*blocks]),
    )(me, *blocks, *partial)


def project_kernel(first, o_ref, w_ref, *refs):
    out_ref = refs[-1]
    for pair in range(w_ref.shape[0] // (2 * HD)):
        part = slice(pair * 2 * HD, (pair + 1) * 2 * HD)
        both = dot32(o_ref[...], w_ref[part, :], NT)
        out_ref[:, part] = both if first else refs[0][:, part] + both


def project_last_kernel(me_s, o_ref, w_ref, acc_ref, *outs):
    pairs = len(outs) // 2
    odd = lax.rem(me_s[0], 2) == 1
    for j in range(pairs):
        part = aligned(lax.rem(me_s[0] // 2, pairs) ^ j, 2 * HD)
        both = (acc_ref[:, part] + dot32(o_ref[...], w_ref[part, :], NT)).astype(jnp.bfloat16)
        outs[2 * j][...] = jnp.where(odd, both[:, HD:], both[:, :HD])
        outs[2 * j + 1][...] = jnp.where(odd, both[:, :HD], both[:, HD:])


def project(me, weight, features, acc, last):
    rows, width = features.shape
    columns = weight.shape[0]
    heads = columns // HD
    total = jax.ShapeDtypeStruct((rows, columns), jnp.float32)
    cost = pl.CostEstimate(
        flops=2 * rows * width * columns,
        bytes_accessed=2 * width * columns + 8 * rows * columns,
        transcendentals=0,
    )
    if last:
        return pl.pallas_call(
            project_last_kernel,
            in_specs=[SMEM_SPEC] + [VMEM_SPEC] * 3,
            out_specs=[VMEM_SPEC] * heads,
            out_shape=[jax.ShapeDtypeStruct((rows, HD), jnp.bfloat16)] * heads,
            compiler_params=params([features, weight, total, total]),
            cost_estimate=cost,
        )(me, features, weight, acc)
    operands = (features, weight) + (() if acc is None else (acc,))
    return pl.pallas_call(
        functools.partial(project_kernel, acc is None),
        in_specs=[VMEM_SPEC] * len(operands),
        out_specs=VMEM_SPEC,
        out_shape=total,
        compiler_params=params([features, weight, total, total]),
        cost_estimate=cost,
    )(*operands)


def at_or_before(q0, k0, shape):
    key = lax.broadcasted_iota(jnp.int32, shape, 0)
    return key <= q0 - k0 + lax.broadcasted_iota(jnp.int32, (1, shape[1]), 1)


def block_sizes(total):
    return (
        (block_size(total, 256), block_size(total, 256)),
        (block_size(total, 256), block_size(total, 256)),
    )


def plan_size(total, bq, bk):
    return sum(((q + 1) * bq + bk - 1) // bk for q in range(total // bq)) + 2


def fill_plan(lows, total, bq, bk, own, plan_q, plan_k, count_ref):
    def put(qi):
        def at(ki, count):
            plan_q[count] = qi
            plan_k[count] = ki
            return count + 1

        return at

    spans = []
    for qi, low in enumerate(lows):
        low, high = low // bk, ((qi + 1) * bq + bk - 1) // bk
        if own is not None:
            wanted = ((qi + 1) * bq > own[0]) & (qi * bq < own[1])
            low = jnp.where(wanted, low, jnp.maximum(low, own[0] // bk))
            high = jnp.where(wanted, high, jnp.minimum(high, (own[1] + bk - 1) // bk))
        whole = jnp.maximum(low, jnp.minimum(high, qi * bq // bk))
        spans.append((low, whole, high))
    count = 0
    for qi, (low, whole, high) in enumerate(spans):
        count = lax.fori_loop(low, whole, put(qi), count)
    count_ref[0] = jnp.maximum(count - 1, 0) // 2
    for qi, (low, whole, high) in enumerate(spans):
        count = lax.fori_loop(whole, high, put(qi), count)
    count_ref[1] = (count + 1) // 2
    for spare in range(2):
        plan_q[count + spare] = 0
        plan_k[count + spare] = total // bk - 1


def pipelined(plan_q, plan_k, count_ref, early, late, buffers):
    early(0, plan_q[0], plan_k[0], buffers[0], True)

    def turns(diagonal):
        def body(i, carry):
            for turn in range(2):
                now = 2 * i + turn
                late(now, plan_q[now], plan_k[now], buffers[turn])
                early(now + 1, plan_q[now + 1], plan_k[now + 1], buffers[1 - turn], diagonal)
            return carry

        return body

    lax.fori_loop(0, count_ref[0], turns(False), 0)
    lax.fori_loop(count_ref[0], count_ref[1], turns(True), 0)


def forward_kernel(peers, heads, rows, bq, bk, kept, me_s, *refs):
    blocks = refs[:peers]
    if kept:
        p_list, top_list = refs[peers + 6:peers + 8]
        refs = refs[:peers + 6] + refs[peers + 8:]
    v_ref, qx_ref, kx_ref, kt_ref, rows_ref, log_ref = refs[peers:peers + 6]
    plan_q, plan_k, count_ref, own_q, own_k, own_count = refs[peers + 6:peers + 12]
    vt_ref, out_ref, doc_ref, sum_ref, s0, top0, s1, top1 = refs[peers + 12:]
    total = v_ref.shape[0]
    factor = HD ** (-0.5) * math.log2(math.e)
    me = me_s[0]
    for d, block in enumerate(blocks):
        place = me ^ d
        for part, ref in enumerate((qx_ref.at[:, :HD], kx_ref.at[:, :HD], v_ref)):
            ref[aligned(place, rows), :] = block[part * rows:(part + 1) * rows, :]
        docs = block[3 * rows:, :].astype(jnp.float32)
        for t in range(rows // HD):
            doc_ref[:, aligned(place * (rows // HD) + t, HD)] = docs[t:t + 1, :]
    docs = doc_ref[...]
    first = jnp.zeros(docs.shape, jnp.float32)
    for value in range(1, DOC_VALUES):
        before = jnp.sum((docs < value).astype(jnp.float32))
        first = jnp.where(docs >= value, before, first)
    first = first.astype(jnp.int32)
    back_q, back_k = block_sizes(total)[1]
    lows = [jnp.min(first[:, qi * back_q:(qi + 1) * back_q]) for qi in range(total // back_q)]
    group = (me // heads) * heads * rows
    own = None if heads == peers else (group, group + heads * rows)
    fill_plan(lows, total, back_q, back_k, own, plan_q, plan_k, count_ref)
    if kept:
        own_q, own_k, own_count = plan_q, plan_k, count_ref
    else:
        lows = [jnp.min(first[:, qi * bq:(qi + 1) * bq]) for qi in range(total // bq)]
        fill_plan(lows, total, bq, bk, None, own_q, own_k, own_count)
    same = lax.broadcasted_iota(jnp.int32, (HD, total), 0).astype(jnp.float32) == docs
    ones = jnp.where(same, 1.0, 0.0).astype(jnp.bfloat16).T
    kx_ref[:, HD:] = ones
    qx_ref[:, HD:] = ((1.0 - ones.astype(jnp.float32)) * NEG_LARGE).astype(jnp.bfloat16)
    kt_ref[...] = kx_ref[:, :HD].T
    vt_ref[:HD, :] = v_ref[...].T
    vt_ref[HD:, :] = jnp.ones((ONES_ROWS, total), jnp.bfloat16)
    out_ref[...] = jnp.zeros_like(out_ref)
    log_ref[...] = jnp.full_like(log_ref, NEG_LARGE)
    sum_ref[...] = jnp.zeros_like(sum_ref)

    def early(now, qi, ki, buffer, diagonal):
        s_ref, top_ref = buffer
        keys, queries = aligned(ki, bk), aligned(qi, bq)
        s = dot32(kx_ref[keys, :], qx_ref[queries, :], NT) * factor
        if diagonal:
            s = jnp.where(at_or_before(qi * bq, ki * bk, (bk, bq)), s, NEG_LARGE)
        s_ref[...] = s
        top_ref[...] = jnp.max(s, axis=0, keepdims=True)

    def late(now, qi, ki, buffer):
        s_ref, top_ref = buffer
        keys, queries = aligned(ki, bk), aligned(qi, bq)
        top = log_ref[:, queries]
        new_top = jnp.maximum(top, top_ref[...])
        fix = jnp.exp2(top - new_top)
        vt = vt_ref[:, keys]
        p = jnp.exp2(s_ref[...] - new_top)
        high = p.astype(jnp.bfloat16)
        sums = dot32(vt, high)
        if kept:
            p_list[now] = high
            top_list[now] = new_top
        else:
            sums = sums + dot32(vt, (p - high.astype(jnp.float32)).astype(jnp.bfloat16))
        out_ref[:, queries] = out_ref[:, queries] * fix + sums[:HD, :]
        sum_ref[:, queries] = sum_ref[:, queries] * fix + sums[HD:HD + 1, :]
        log_ref[:, queries] = new_top

    pipelined(own_q, own_k, own_count, early, late, ((s0, top0), (s1, top1)))
    total_p = sum_ref[...]
    rows_ref[...] = (out_ref[...] / total_p).T
    log_ref[...] = log_ref[...] + jnp.log2(total_p)


def backward_kernel(listed, heads, rows, bq, bk, kept, me_s, plan_q, plan_k, count_ref, v_ref,
                    qx_ref, kx_ref, kt_ref, rows_ref, log_ref, *refs):
    if kept:
        p_list, top_list = refs[:2]
        refs = refs[2:]
    peers = len(listed)
    blocks = refs[:peers]
    results = refs[peers:peers + heads]
    g_ref, dot_ref, dk_acc, dv_acc, dq_acc, p0, ds0, p1, ds1 = refs[peers + heads:]
    scale = HD ** (-0.5)
    factor = scale * math.log2(math.e)
    me = me_s[0]
    for d, block in zip(listed, blocks):
        g_ref[aligned(me ^ d, rows), :] = block[...]
    ones = jnp.ones((ONES_ROWS, HD), jnp.bfloat16)
    for start in range(0, g_ref.shape[0], bq):
        part = slice(start, start + bq)
        left = g_ref[part, :].astype(jnp.float32) * rows_ref[part, :]
        dots = 0.0
        for _ in range(3):
            term = left.astype(jnp.bfloat16)
            left = left - term.astype(jnp.float32)
            dots = dots + dot32(ones, term, NT)
        dot_ref[:, part] = dots[:1, :]
    dk_acc[...] = jnp.zeros_like(dk_acc)
    dv_acc[...] = jnp.zeros_like(dv_acc)
    dq_acc[...] = jnp.zeros_like(dq_acc)

    def early(now, qi, ki, buffer, diagonal):
        p_ref, ds_ref = buffer
        queries = aligned(qi, bq)
        log_row, dot_row = log_ref[:, queries], dot_ref[:, queries]
        if kept:
            share = jnp.exp2(top_list[now] - log_row)
        for strip in range(0, bk, STRIP):
            part = slice(strip, strip + STRIP)
            keys = aligned(ki * (bk // STRIP) + strip // STRIP, STRIP)
            if kept:
                p = p_list[now, part, :].astype(jnp.float32) * share
            else:
                p = jnp.exp2(dot32(kx_ref[keys, :], qx_ref[queries, :], NT) * factor - log_row)
                if diagonal:
                    p = jnp.where(at_or_before(qi * bq, ki * bk + strip, (STRIP, bq)), p, 0.0)
            p_ref[part, :] = p.astype(jnp.bfloat16)
            dp = dot32(v_ref[keys, :], g_ref[queries, :], NT)
            ds_ref[part, :] = (p * (dp - dot_row)).astype(jnp.bfloat16)

    def late(now, qi, ki, buffer):
        p_ref, ds_ref = buffer
        keys, queries = aligned(ki, bk), aligned(qi, bq)
        dv_acc[keys, :] += dot32(p_ref[...], g_ref[queries, :])
        dk_acc[keys, :] += dot32(ds_ref[...], qx_ref[queries, :HD])
        dq_acc[:, queries] += dot32(kt_ref[:, keys], ds_ref[...])

    pipelined(plan_q, plan_k, count_ref, early, late, ((p0, ds0), (p1, ds1)))
    for d, result in enumerate(results):
        own = aligned(me ^ d, rows)
        result[:rows, :] = (scale * dq_acc[:, own]).astype(result.dtype).T
        result[rows:2 * rows, :] = (scale * dk_acc[own, :]).astype(result.dtype)
        result[2 * rows:, :] = dv_acc[own, :].astype(result.dtype)


def keeps_list(total, peers, heads):
    forward, backward = block_sizes(total)
    size = plan_size(total, *forward) * math.prod(forward) * 2
    return forward == backward and heads == peers and size <= LIST_BYTES


def attention_cost(total, products):
    return pl.CostEstimate(
        flops=products * total * total * HD // 2,
        bytes_accessed=16 * total * HD,
        transcendentals=total * total // 4,
    )


def attention_forward(me, blocks, rows, heads):
    peers = len(blocks)
    total = peers * rows
    (bq, bk), back = block_sizes(total)
    plan = [(plan_size(total, *back),)] * 2 + [(2,)]
    own_plan = [(plan_size(total, bq, bk),)] * 2 + [(2,)]
    vectors = [
        jax.ShapeDtypeStruct((total, HD), jnp.bfloat16),
        *[jax.ShapeDtypeStruct((total, 2 * HD), jnp.bfloat16)] * 2,
        jax.ShapeDtypeStruct((HD, total), jnp.bfloat16),
        jax.ShapeDtypeStruct((total, HD), jnp.float32),
        jax.ShapeDtypeStruct((1, total), jnp.float32),
    ]
    kept = keeps_list(total, peers, heads)
    if kept:
        vectors.append(jax.ShapeDtypeStruct((*own_plan[0], bk, bq), jnp.bfloat16))
        vectors.append(jax.ShapeDtypeStruct((*own_plan[0], 1, bq), jnp.float32))
    scratch = [
        pltpu.VMEM((HD + ONES_ROWS, total), jnp.bfloat16),
        pltpu.VMEM((HD, total), jnp.float32),
        pltpu.VMEM((1, total), jnp.float32),
        pltpu.VMEM((1, total), jnp.float32),
        *[pltpu.VMEM((bk, bq), jnp.float32), pltpu.VMEM((1, bq), jnp.float32)] * 2,
    ]
    return pl.pallas_call(
        functools.partial(forward_kernel, peers, heads, rows, bq, bk, kept),
        in_specs=[SMEM_SPEC] + [VMEM_SPEC] * peers,
        out_specs=[VMEM_SPEC] * len(vectors) + [SMEM_SPEC] * 3,
        out_shape=vectors + [jax.ShapeDtypeStruct(shape, jnp.int32) for shape in plan],
        scratch_shapes=[pltpu.SMEM(shape, jnp.int32) for shape in own_plan] + scratch,
        compiler_params=params([*blocks, *vectors], scratch),
        cost_estimate=attention_cost(total, 3),
    )(me, *blocks)


def attention_backward(me, heads, state, listed, blocks):
    peers, rows = len(blocks), blocks[0].shape[0]
    total = peers * rows
    bq, bk = block_sizes(total)[1]
    vectors, plan = state[:-3], state[-3:]
    kept = keeps_list(total, peers, heads)
    out_shape = [jax.ShapeDtypeStruct((3 * rows, HD), jnp.bfloat16)] * heads
    scratch = [
        pltpu.VMEM((total, HD), jnp.bfloat16),
        pltpu.VMEM((1, total), jnp.float32),
        pltpu.VMEM((total, HD), jnp.float32),
        pltpu.VMEM((total, HD), jnp.float32),
        pltpu.VMEM((HD, total), jnp.float32),
        *[pltpu.VMEM((bk, bq), jnp.bfloat16)] * 4,
    ]
    return pl.pallas_call(
        functools.partial(backward_kernel, listed, heads, rows, bq, bk, kept),
        in_specs=[SMEM_SPEC] * 4 + [VMEM_SPEC] * (len(vectors) + peers),
        out_specs=[VMEM_SPEC] * heads,
        out_shape=out_shape,
        scratch_shapes=scratch,
        compiler_params=params([*vectors, *blocks, *out_shape], scratch),
        cost_estimate=attention_cost(total, 5),
    )(me, *plan, *vectors, *blocks)


def per_device(peers, groups, queries, keys_in, values, out_grad, out_weight, doc_ids):
    rows, width = queries.shape
    heads = width // HD
    me = lax.axis_index("seq")
    me_vector = me.reshape(1)

    def exchange(x, d):
        return x if d == 0 else lax.ppermute(x, "seq", [(i, i ^ d) for i in range(peers)])

    def pass_on(x):
        return lax.ppermute(x, "head", [(i, (i + 1) % groups) for i in range(groups)])

    order = [*range(2, peers, 2), *range(peers - 1, 0, -2)]

    far_first = sorted(range(peers), key=lambda d: (-bin(d >> 1).count("1"), d & 1, d))
    returning = [d for d in far_first if d < heads]

    def exchange_all(blocks, listed):
        return [exchange(blocks[d % heads], d) for d in listed]

    packed = list(pack_heads(me_vector, queries, keys_in, values, doc_ids))
    received = exchange_all(packed, range(peers))

    def share(step):
        return len(order) * step // (groups - 2)

    after = lax.optimization_barrier
    features, acc = out_grad, None
    weights = []
    for step in range(groups):
        block = lax.rem(lax.axis_index("head") + groups - step, groups)
        weights.append(lax.dynamic_slice_in_dim(out_weight, block * width, width, 1))
    for step in range(groups):
        last = step == groups - 1
        if not last:
            passed = pass_on(features)
        if step == groups - 2:
            received[0], features = after((received[0], features))
            state = list(attention_forward(me_vector, received, rows, heads))
            features, state[1] = after((features, state[1]))
        acc = project(me_vector, weights[step], features, acc, last)
        if not last:
            features = passed
            if step < groups - 2:
                batch = order[share(step):share(step + 1)]
                here = [received[d] for d in batch]
                features, acc, here, weights[2:] = after((features, acc, here, weights[2:]))
                for d, block in zip(batch, here):
                    received[d] = block
    grads = exchange_all(acc, far_first)

    results = attention_backward(me_vector, heads, state, far_first, grads)
    returned = exchange_all(results, returning)
    early = [d for d in returning if d == 0 or bin(d >> 1).count("1") > 1]
    late = [d for d in returning if d not in early]
    block_of = dict(zip(returning, returned))
    partial = unpack_heads(me_vector, early, [block_of[d] for d in early], rows, heads)
    return tuple(unpack_heads(me_vector, late, [block_of[d] for d in late], rows, heads, partial))


def solution(mesh):
    in_specs = (
        P("seq", "head"),
        P("seq", "head"),
        P("seq", "head"),
        P("seq", "head"),
        P("head", None),
        P("seq"),
    )
    out_specs = (P("seq", "head"), P("seq", "head"), P("seq", "head"))
    return jax.shard_map(
        functools.partial(per_device, mesh.shape["seq"], mesh.shape["head"]),
        mesh=mesh, in_specs=in_specs, out_specs=out_specs, check_vma=False,
    )
```

```python
import functools
import math

import jax
import jax.numpy as jnp
from jax import lax
from jax.experimental import pallas as pl
from jax.experimental.pallas import tpu as pltpu
from jax.sharding import PartitionSpec as P

HD = 128
DOC_VALUES = 8
DOC_ROWS = 16
ONES_ROWS = 16
STRIP = 128
NEG_LARGE = -1e30
VMEM_SPARE = 6 * 1024 * 1024
VMEM_MOST = 56 * 1024 * 1024
LIST_BYTES = 16 * 1024 * 1024

NN = (((1,), (0,)), ((), ()))
NT = (((1,), (1,)), ((), ()))
SMEM_SPEC = pl.BlockSpec(memory_space=pltpu.SMEM)
VMEM_SPEC = pl.BlockSpec(memory_space=pltpu.VMEM)
ANY_SPEC = pl.BlockSpec(memory_space=pl.ANY)


def dot32(a, b, dims=NN):
    return lax.dot_general(a, b, dims, preferred_element_type=jnp.float32)


def block_size(total, wanted):
    size = min(wanted, total)
    while total % size or size % 128:
        size -= 128
    return size


def aligned(index, size):
    return pl.ds(pl.multiple_of(index * size, size), size)


def params(arrays, scratch=()):
    total = sum(math.prod(a.shape) * jnp.dtype(a.dtype).itemsize for a in (*arrays, *scratch))
    return pltpu.CompilerParams(vmem_limit_bytes=total + VMEM_SPARE)


def pack_kernel(heads, rows, me_s, q_ref, k_ref, v_ref, doc_ref, *outs):
    own = lax.rem(me_s[0], heads)
    docs = doc_ref[...].astype(jnp.float32)
    docs = jnp.concatenate([docs, jnp.zeros((DOC_ROWS - docs.shape[0], HD), jnp.float32)], axis=0)
    docs = docs.astype(jnp.bfloat16)
    for d, out in enumerate(outs):
        columns = aligned(own ^ d, HD)
        for part, ref in enumerate((q_ref, k_ref, v_ref)):
            out[part * rows:(part + 1) * rows, :] = ref[:, columns]
        out[3 * rows:, :] = docs


def pack_heads(me, q, k, v, doc_ids):
    rows, width = q.shape
    heads = width // HD
    return pl.pallas_call(
        functools.partial(pack_kernel, heads, rows),
        in_specs=[SMEM_SPEC] + [VMEM_SPEC] * 4,
        out_specs=[VMEM_SPEC] * heads,
        out_shape=[jax.ShapeDtypeStruct((3 * rows + DOC_ROWS, HD), q.dtype)] * heads,
        compiler_params=pltpu.CompilerParams(vmem_limit_bytes=VMEM_MOST),
    )(me, q, k, v, doc_ids.reshape(rows // HD, HD))


def unpack_kernel(listed, heads, rows, me_s, *refs):
    outs, done = refs[-4:-1], refs[-1]
    own = lax.rem(me_s[0], heads)
    copies = []
    for place, (d, block) in enumerate(zip(listed, refs)):
        columns = aligned(own ^ d, HD)
        for part, out in enumerate(outs):
            source = block.at[pl.ds(part * rows, rows), :]
            copies.append(pltpu.make_async_copy(source, out.at[:, columns], done.at[place, part]))
            copies[-1].start()
    for copy in copies:
        copy.wait()


def unpack_heads(me, listed, blocks, rows, heads, partial=()):
    count = len(blocks)
    return pl.pallas_call(
        functools.partial(unpack_kernel, listed, heads, rows),
        in_specs=[SMEM_SPEC] + [VMEM_SPEC] * count + [ANY_SPEC] * len(partial),
        out_specs=[ANY_SPEC] * 3,
        out_shape=[jax.ShapeDtypeStruct((rows, heads * HD), blocks[0].dtype)] * 3,
        scratch_shapes=[pltpu.SemaphoreType.DMA((count, 3))],
        input_output_aliases={1 + count + i: i for i in range(len(partial))},
        compiler_params=params([*blocks]),
    )(me, *blocks, *partial)


def project_kernel(first, o_ref, w_ref, *refs):
    out_ref = refs[-1]
    for pair in range(w_ref.shape[0] // (2 * HD)):
        part = slice(pair * 2 * HD, (pair + 1) * 2 * HD)
        both = dot32(o_ref[...], w_ref[part, :], NT)
        out_ref[:, part] = both if first else refs[0][:, part] + both


def project_last_kernel(me_s, o_ref, w_ref, acc_ref, *outs):
    pairs = len(outs) // 2
    odd = lax.rem(me_s[0], 2) == 1
    for j in range(pairs):
        part = aligned(lax.rem(me_s[0] // 2, pairs) ^ j, 2 * HD)
        both = (acc_ref[:, part] + dot32(o_ref[...], w_ref[part, :], NT)).astype(jnp.bfloat16)
        outs[2 * j][...] = jnp.where(odd, both[:, HD:], both[:, :HD])
        outs[2 * j + 1][...] = jnp.where(odd, both[:, :HD], both[:, HD:])


def project(me, weight, features, acc, last):
    rows, width = features.shape
    columns = weight.shape[0]
    heads = columns // HD
    total = jax.ShapeDtypeStruct((rows, columns), jnp.float32)
    cost = pl.CostEstimate(
        flops=2 * rows * width * columns,
        bytes_accessed=2 * width * columns + 8 * rows * columns,
        transcendentals=0,
    )
    if last:
        return pl.pallas_call(
            project_last_kernel,
            in_specs=[SMEM_SPEC] + [VMEM_SPEC] * 3,
            out_specs=[VMEM_SPEC] * heads,
            out_shape=[jax.ShapeDtypeStruct((rows, HD), jnp.bfloat16)] * heads,
            compiler_params=params([features, weight, total, total]),
            cost_estimate=cost,
        )(me, features, weight, acc)
    operands = (features, weight) + (() if acc is None else (acc,))
    return pl.pallas_call(
        functools.partial(project_kernel, acc is None),
        in_specs=[VMEM_SPEC] * len(operands),
        out_specs=VMEM_SPEC,
        out_shape=total,
        compiler_params=params([features, weight, total, total]),
        cost_estimate=cost,
    )(*operands)


def at_or_before(q0, k0, shape):
    key = lax.broadcasted_iota(jnp.int32, shape, 0)
    return key <= q0 - k0 + lax.broadcasted_iota(jnp.int32, (1, shape[1]), 1)


def block_sizes(total):
    return (
        (block_size(total, 256), block_size(total, 256)),
        (block_size(total, 256), block_size(total, 256)),
    )


def plan_size(total, bq, bk):
    return sum(((q + 1) * bq + bk - 1) // bk for q in range(total // bq)) + 2


def fill_plan(lows, total, bq, bk, own, plan_q, plan_k, count_ref):
    def put(qi):
        def at(ki, count):
            plan_q[count] = qi
            plan_k[count] = ki
            return count + 1

        return at

    spans = []
    for qi, low in enumerate(lows):
        low, high = low // bk, ((qi + 1) * bq + bk - 1) // bk
        if own is not None:
            wanted = ((qi + 1) * bq > own[0]) & (qi * bq < own[1])
            low = jnp.where(wanted, low, jnp.maximum(low, own[0] // bk))
            high = jnp.where(wanted, high, jnp.minimum(high, (own[1] + bk - 1) // bk))
        whole = jnp.maximum(low, jnp.minimum(high, qi * bq // bk))
        spans.append((low, whole, high))
    count = 0
    for qi, (low, whole, high) in enumerate(spans):
        count = lax.fori_loop(low, whole, put(qi), count)
    count_ref[0] = jnp.maximum(count - 1, 0) // 2
    for qi, (low, whole, high) in enumerate(spans):
        count = lax.fori_loop(whole, high, put(qi), count)
    count_ref[1] = (count + 1) // 2
    for spare in range(2):
        plan_q[count + spare] = 0
        plan_k[count + spare] = total // bk - 1


def pipelined(plan_q, plan_k, count_ref, early, late, buffers):
    early(0, plan_q[0], plan_k[0], buffers[0], True)

    def turns(diagonal):
        def body(i, carry):
            for turn in range(2):
                now = 2 * i + turn
                late(now, plan_q[now], plan_k[now], buffers[turn])
                early(now + 1, plan_q[now + 1], plan_k[now + 1], buffers[1 - turn], diagonal)
            return carry

        return body

    lax.fori_loop(0, count_ref[0], turns(False), 0)
    lax.fori_loop(count_ref[0], count_ref[1], turns(True), 0)


def forward_kernel(peers, heads, rows, bq, bk, kept, me_s, *refs):
    blocks = refs[:peers]
    if kept:
        p_list, top_list = refs[peers + 6:peers + 8]
        refs = refs[:peers + 6] + refs[peers + 8:]
    v_ref, qx_ref, kx_ref, kt_ref, rows_ref, log_ref = refs[peers:peers + 6]
    plan_q, plan_k, count_ref, own_q, own_k, own_count = refs[peers + 6:peers + 12]
    vt_ref, out_ref, doc_ref, sum_ref, s0, top0, s1, top1 = refs[peers + 12:]
    total = v_ref.shape[0]
    factor = HD ** (-0.5) * math.log2(math.e)
    me = me_s[0]
    for d, block in enumerate(blocks):
        place = me ^ d
        for part, ref in enumerate((qx_ref.at[:, :HD], kx_ref.at[:, :HD], v_ref)):
            ref[aligned(place, rows), :] = block[part * rows:(part + 1) * rows, :]
        docs = block[3 * rows:, :].astype(jnp.float32)
        for t in range(rows // HD):
            doc_ref[:, aligned(place * (rows // HD) + t, HD)] = docs[t:t + 1, :]
    docs = doc_ref[...]
    first = jnp.zeros(docs.shape, jnp.float32)
    for value in range(1, DOC_VALUES):
        before = jnp.sum((docs < value).astype(jnp.float32))
        first = jnp.where(docs >= value, before, first)
    first = first.astype(jnp.int32)
    back_q, back_k = block_sizes(total)[1]
    lows = [jnp.min(first[:, qi * back_q:(qi + 1) * back_q]) for qi in range(total // back_q)]
    group = (me // heads) * heads * rows
    own = None if heads == peers else (group, group + heads * rows)
    fill_plan(lows, total, back_q, back_k, own, plan_q, plan_k, count_ref)
    if kept:
        own_q, own_k, own_count = plan_q, plan_k, count_ref
    else:
        lows = [jnp.min(first[:, qi * bq:(qi + 1) * bq]) for qi in range(total // bq)]
        fill_plan(lows, total, bq, bk, None, own_q, own_k, own_count)
    same = lax.broadcasted_iota(jnp.int32, (HD, total), 0).astype(jnp.float32) == docs
    ones = jnp.where(same, 1.0, 0.0).astype(jnp.bfloat16).T
    kx_ref[:, HD:] = ones
    qx_ref[:, HD:] = ((1.0 - ones.astype(jnp.float32)) * NEG_LARGE).astype(jnp.bfloat16)
    kt_ref[...] = kx_ref[:, :HD].T
    vt_ref[:HD, :] = v_ref[...].T
    vt_ref[HD:, :] = jnp.ones((ONES_ROWS, total), jnp.bfloat16)
    out_ref[...] = jnp.zeros_like(out_ref)
    log_ref[...] = jnp.full_like(log_ref, NEG_LARGE)
    sum_ref[...] = jnp.zeros_like(sum_ref)

    def early(now, qi, ki, buffer, diagonal):
        s_ref, top_ref = buffer
        keys, queries = aligned(ki, bk), aligned(qi, bq)
        s = dot32(kx_ref[keys, :], qx_ref[queries, :], NT) * factor
        if diagonal:
            s = jnp.where(at_or_before(qi * bq, ki * bk, (bk, bq)), s, NEG_LARGE)
        s_ref[...] = s
        top_ref[...] = jnp.max(s, axis=0, keepdims=True)

    def late(now, qi, ki, buffer):
        s_ref, top_ref = buffer
        keys, queries = aligned(ki, bk), aligned(qi, bq)
        top = log_ref[:, queries]
        new_top = jnp.maximum(top, top_ref[...])
        fix = jnp.exp2(top - new_top)
        vt = vt_ref[:, keys]
        p = jnp.exp2(s_ref[...] - new_top)
        high = p.astype(jnp.bfloat16)
        sums = dot32(vt, high)
        if kept:
            p_list[now] = high
            top_list[now] = new_top
        else:
            sums = sums + dot32(vt, (p - high.astype(jnp.float32)).astype(jnp.bfloat16))
        out_ref[:, queries] = out_ref[:, queries] * fix + sums[:HD, :]
        sum_ref[:, queries] = sum_ref[:, queries] * fix + sums[HD:HD + 1, :]
        log_ref[:, queries] = new_top

    pipelined(own_q, own_k, own_count, early, late, ((s0, top0), (s1, top1)))
    total_p = sum_ref[...]
    rows_ref[...] = (out_ref[...] / total_p).T
    log_ref[...] = log_ref[...] + jnp.log2(total_p)


def backward_kernel(listed, heads, rows, bq, bk, kept, me_s, plan_q, plan_k, count_ref, v_ref,
                    qx_ref, kx_ref, kt_ref, rows_ref, log_ref, *refs):
    if kept:
        p_list, top_list = refs[:2]
        refs = refs[2:]
    peers = len(listed)
    blocks = refs[:peers]
    dq_acc, dk_acc, dv_acc, g_ref, dot_ref, p0, ds0, p1, ds1 = refs[peers:]
    scale = HD ** (-0.5)
    factor = scale * math.log2(math.e)
    me = me_s[0]
    for d, block in zip(listed, blocks):
        g_ref[aligned(me ^ d, rows), :] = block[...]
    ones = jnp.ones((ONES_ROWS, HD), jnp.bfloat16)
    for start in range(0, g_ref.shape[0], bq):
        part = slice(start, start + bq)
        left = g_ref[part, :].astype(jnp.float32) * rows_ref[part, :]
        dots = 0.0
        for _ in range(3):
            term = left.astype(jnp.bfloat16)
            left = left - term.astype(jnp.float32)
            dots = dots + dot32(ones, term, NT)
        dot_ref[:, part] = dots[:1, :]
    dk_acc[...] = jnp.zeros_like(dk_acc)
    dv_acc[...] = jnp.zeros_like(dv_acc)
    dq_acc[...] = jnp.zeros_like(dq_acc)

    def early(now, qi, ki, buffer, diagonal):
        p_ref, ds_ref = buffer
        queries = aligned(qi, bq)
        log_row, dot_row = log_ref[:, queries], dot_ref[:, queries]
        if kept:
            share = jnp.exp2(top_list[now] - log_row)
        for strip in range(0, bk, STRIP):
            part = slice(strip, strip + STRIP)
            keys = aligned(ki * (bk // STRIP) + strip // STRIP, STRIP)
            if kept:
                p = p_list[now, part, :].astype(jnp.float32) * share
            else:
                p = jnp.exp2(dot32(kx_ref[keys, :], qx_ref[queries, :], NT) * factor - log_row)
                if diagonal:
                    p = jnp.where(at_or_before(qi * bq, ki * bk + strip, (STRIP, bq)), p, 0.0)
            p_ref[part, :] = p.astype(jnp.bfloat16)
            dp = dot32(v_ref[keys, :], g_ref[queries, :], NT)
            ds_ref[part, :] = (p * (dp - dot_row)).astype(jnp.bfloat16)

    def late(now, qi, ki, buffer):
        p_ref, ds_ref = buffer
        keys, queries = aligned(ki, bk), aligned(qi, bq)
        dv_acc[keys, :] += dot32(p_ref[...], g_ref[queries, :])
        dk_acc[keys, :] += dot32(ds_ref[...], qx_ref[queries, :HD])
        dq_acc[:, queries] += dot32(kt_ref[:, keys], ds_ref[...])

    pipelined(plan_q, plan_k, count_ref, early, late, ((p0, ds0), (p1, ds1)))


def finish_kernel(listed, rows, me_s, dq_ref, dk_ref, dv_ref, *results):
    scale = HD ** (-0.5)
    for d, result in zip(listed, results):
        own = aligned(me_s[0] ^ d, rows)
        result[:rows, :] = (scale * dq_ref[:, own]).astype(result.dtype).T
        result[rows:2 * rows, :] = (scale * dk_ref[own, :]).astype(result.dtype)
        result[2 * rows:, :] = dv_ref[own, :].astype(result.dtype)


def finish(me, listed, totals, rows):
    out_shape = [jax.ShapeDtypeStruct((3 * rows, HD), jnp.bfloat16)] * len(listed)
    results = pl.pallas_call(
        functools.partial(finish_kernel, listed, rows),
        in_specs=[SMEM_SPEC] + [VMEM_SPEC] * 3,
        out_specs=[VMEM_SPEC] * len(listed),
        out_shape=out_shape,
        compiler_params=params([*totals, *out_shape]),
    )(me, *totals)
    return dict(zip(listed, results))


def keeps_list(total, peers, heads):
    forward, backward = block_sizes(total)
    size = plan_size(total, *forward) * math.prod(forward) * 2
    return forward == backward and heads == peers and size <= LIST_BYTES


def attention_cost(total, products):
    return pl.CostEstimate(
        flops=products * total * total * HD // 2,
        bytes_accessed=16 * total * HD,
        transcendentals=total * total // 4,
    )


def attention_forward(me, blocks, rows, heads):
    peers = len(blocks)
    total = peers * rows
    (bq, bk), back = block_sizes(total)
    plan = [(plan_size(total, *back),)] * 2 + [(2,)]
    own_plan = [(plan_size(total, bq, bk),)] * 2 + [(2,)]
    vectors = [
        jax.ShapeDtypeStruct((total, HD), jnp.bfloat16),
        *[jax.ShapeDtypeStruct((total, 2 * HD), jnp.bfloat16)] * 2,
        jax.ShapeDtypeStruct((HD, total), jnp.bfloat16),
        jax.ShapeDtypeStruct((total, HD), jnp.float32),
        jax.ShapeDtypeStruct((1, total), jnp.float32),
    ]
    kept = keeps_list(total, peers, heads)
    if kept:
        vectors.append(jax.ShapeDtypeStruct((*own_plan[0], bk, bq), jnp.bfloat16))
        vectors.append(jax.ShapeDtypeStruct((*own_plan[0], 1, bq), jnp.float32))
    scratch = [
        pltpu.VMEM((HD + ONES_ROWS, total), jnp.bfloat16),
        pltpu.VMEM((HD, total), jnp.float32),
        pltpu.VMEM((1, total), jnp.float32),
        pltpu.VMEM((1, total), jnp.float32),
        *[pltpu.VMEM((bk, bq), jnp.float32), pltpu.VMEM((1, bq), jnp.float32)] * 2,
    ]
    return pl.pallas_call(
        functools.partial(forward_kernel, peers, heads, rows, bq, bk, kept),
        in_specs=[SMEM_SPEC] + [VMEM_SPEC] * peers,
        out_specs=[VMEM_SPEC] * len(vectors) + [SMEM_SPEC] * 3,
        out_shape=vectors + [jax.ShapeDtypeStruct(shape, jnp.int32) for shape in plan],
        scratch_shapes=[pltpu.SMEM(shape, jnp.int32) for shape in own_plan] + scratch,
        compiler_params=params([*blocks, *vectors], scratch),
        cost_estimate=attention_cost(total, 3),
    )(me, *blocks)


def attention_backward(me, heads, state, listed, blocks):
    peers, rows = len(blocks), blocks[0].shape[0]
    total = peers * rows
    bq, bk = block_sizes(total)[1]
    vectors, plan = state[:-3], state[-3:]
    kept = keeps_list(total, peers, heads)
    shapes = [(HD, total), (total, HD), (total, HD)]
    out_shape = [jax.ShapeDtypeStruct(shape, jnp.float32) for shape in shapes]
    scratch = [
        pltpu.VMEM((total, HD), jnp.bfloat16),
        pltpu.VMEM((1, total), jnp.float32),
        *[pltpu.VMEM((bk, bq), jnp.bfloat16)] * 4,
    ]
    return pl.pallas_call(
        functools.partial(backward_kernel, listed, heads, rows, bq, bk, kept),
        in_specs=[SMEM_SPEC] * 4 + [VMEM_SPEC] * (len(vectors) + peers),
        out_specs=[VMEM_SPEC] * 3,
        out_shape=out_shape,
        scratch_shapes=scratch,
        compiler_params=params([*vectors, *blocks, *out_shape], scratch),
        cost_estimate=attention_cost(total, 5),
    )(me, *plan, *vectors, *blocks)


def per_device(peers, groups, queries, keys_in, values, out_grad, out_weight, doc_ids):
    rows, width = queries.shape
    heads = width // HD
    me = lax.axis_index("seq")
    me_vector = me.reshape(1)

    def exchange(x, d):
        return x if d == 0 else lax.ppermute(x, "seq", [(i, i ^ d) for i in range(peers)])

    def pass_on(x):
        return lax.ppermute(x, "head", [(i, (i + 1) % groups) for i in range(groups)])

    order = [*range(2, peers, 2), *range(peers - 1, 0, -2)]

    far_first = sorted(range(peers), key=lambda d: (-bin(d >> 1).count("1"), d & 1, d))
    returning = [d for d in far_first if d < heads]

    def exchange_all(blocks, listed):
        return [exchange(blocks[d % heads], d) for d in listed]

    packed = list(pack_heads(me_vector, queries, keys_in, values, doc_ids))
    received = exchange_all(packed, range(peers))

    def share(step):
        return len(order) * step // (groups - 2)

    after = lax.optimization_barrier
    features, acc = out_grad, None
    weights = []
    for step in range(groups):
        block = lax.rem(lax.axis_index("head") + groups - step, groups)
        weights.append(lax.dynamic_slice_in_dim(out_weight, block * width, width, 1))
    for step in range(groups):
        last = step == groups - 1
        if not last:
            passed = pass_on(features)
        if step == groups - 2:
            received[0], features = after((received[0], features))
            state = list(attention_forward(me_vector, received, rows, heads))
            features, state[1] = after((features, state[1]))
        acc = project(me_vector, weights[step], features, acc, last)
        if not last:
            features = passed
            if step < groups - 2:
                batch = order[share(step):share(step + 1)]
                here = [received[d] for d in batch]
                features, acc, here, weights[2:] = after((features, acc, here, weights[2:]))
                for d, block in zip(batch, here):
                    received[d] = block
    grads = exchange_all(acc, far_first)

    totals = attention_backward(me_vector, heads, state, far_first, grads)

    far = [d for d in returning if bin(d >> 1).count("1") > 1]
    near = [d for d in returning if d not in far]
    results = {**(finish(me_vector, far, totals, rows) if far else {}), **finish(me_vector, near, totals, rows)}
    returned = {d: exchange(results[d], d) for d in returning}
    early, late = [*far, 0], [d for d in near if d > 0]
    partial = unpack_heads(me_vector, early, [returned[d] for d in early], rows, heads)
    return tuple(unpack_heads(me_vector, late, [returned[d] for d in late], rows, heads, partial))


def solution(mesh):
    in_specs = (
        P("seq", "head"),
        P("seq", "head"),
        P("seq", "head"),
        P("seq", "head"),
        P("head", None),
        P("seq"),
    )
    out_specs = (P("seq", "head"), P("seq", "head"), P("seq", "head"))
    return jax.shard_map(
        functools.partial(per_device, mesh.shape["seq"], mesh.shape["head"]),
        mesh=mesh, in_specs=in_specs, out_specs=out_specs, check_vma=False,
    )
```

```python
import functools
import math

import jax
import jax.numpy as jnp
from jax import lax
from jax.experimental import pallas as pl
from jax.experimental.pallas import tpu as pltpu
from jax.sharding import PartitionSpec as P

HD = 128
DOC_VALUES = 8
DOC_ROWS = 16
ONES_ROWS = 16
STRIP = 128
NEG_LARGE = -1e30
VMEM_SPARE = 6 * 1024 * 1024
VMEM_MOST = 56 * 1024 * 1024
LIST_BYTES = 16 * 1024 * 1024

NN = (((1,), (0,)), ((), ()))
NT = (((1,), (1,)), ((), ()))
SMEM_SPEC = pl.BlockSpec(memory_space=pltpu.SMEM)
VMEM_SPEC = pl.BlockSpec(memory_space=pltpu.VMEM)
ANY_SPEC = pl.BlockSpec(memory_space=pl.ANY)


def dot32(a, b, dims=NN):
    return lax.dot_general(a, b, dims, preferred_element_type=jnp.float32)


def block_size(total, wanted):
    size = min(wanted, total)
    while total % size or size % 128:
        size -= 128
    return size


def aligned(index, size):
    return pl.ds(pl.multiple_of(index * size, size), size)


def params(arrays, scratch=()):
    total = sum(math.prod(a.shape) * jnp.dtype(a.dtype).itemsize for a in (*arrays, *scratch))
    return pltpu.CompilerParams(vmem_limit_bytes=total + VMEM_SPARE)


def pack_kernel(heads, rows, me_s, q_ref, k_ref, v_ref, doc_ref, *outs):
    own = lax.rem(me_s[0], heads)
    docs = doc_ref[...].astype(jnp.float32)
    docs = jnp.concatenate([docs, jnp.zeros((DOC_ROWS - docs.shape[0], HD), jnp.float32)], axis=0)
    docs = docs.astype(jnp.bfloat16)
    for d, out in enumerate(outs):
        columns = aligned(own ^ d, HD)
        for part, ref in enumerate((q_ref, k_ref, v_ref)):
            out[part * rows:(part + 1) * rows, :] = ref[:, columns]
        out[3 * rows:, :] = docs


def pack_heads(me, q, k, v, doc_ids):
    rows, width = q.shape
    heads = width // HD
    return pl.pallas_call(
        functools.partial(pack_kernel, heads, rows),
        in_specs=[SMEM_SPEC] + [VMEM_SPEC] * 4,
        out_specs=[VMEM_SPEC] * heads,
        out_shape=[jax.ShapeDtypeStruct((3 * rows + DOC_ROWS, HD), q.dtype)] * heads,
        compiler_params=pltpu.CompilerParams(vmem_limit_bytes=VMEM_MOST),
    )(me, q, k, v, doc_ids.reshape(rows // HD, HD))


def unpack_kernel(listed, heads, rows, me_s, *refs):
    outs, done = refs[-4:-1], refs[-1]
    own = lax.rem(me_s[0], heads)
    copies = []
    for place, (d, block) in enumerate(zip(listed, refs)):
        columns = aligned(own ^ d, HD)
        for part, out in enumerate(outs):
            source = block.at[pl.ds(part * rows, rows), :]
            copies.append(pltpu.make_async_copy(source, out.at[:, columns], done.at[place, part]))
            copies[-1].start()
    for copy in copies:
        copy.wait()


def unpack_heads(me, listed, blocks, rows, heads, partial=()):
    count = len(blocks)
    return pl.pallas_call(
        functools.partial(unpack_kernel, listed, heads, rows),
        in_specs=[SMEM_SPEC] + [VMEM_SPEC] * count + [ANY_SPEC] * len(partial),
        out_specs=[ANY_SPEC] * 3,
        out_shape=[jax.ShapeDtypeStruct((rows, heads * HD), blocks[0].dtype)] * 3,
        scratch_shapes=[pltpu.SemaphoreType.DMA((count, 3))],
        input_output_aliases={1 + count + i: i for i in range(len(partial))},
        compiler_params=params([*blocks]),
    )(me, *blocks, *partial)


def project_kernel(first, o_ref, w_ref, *refs):
    out_ref = refs[-1]
    for pair in range(w_ref.shape[0] // (2 * HD)):
        part = slice(pair * 2 * HD, (pair + 1) * 2 * HD)
        both = dot32(o_ref[...], w_ref[part, :], NT)
        out_ref[:, part] = both if first else refs[0][:, part] + both


def project_last_kernel(me_s, o_ref, w_ref, acc_ref, *outs):
    pairs = len(outs) // 2
    odd = lax.rem(me_s[0], 2) == 1
    for j in range(pairs):
        part = aligned(lax.rem(me_s[0] // 2, pairs) ^ j, 2 * HD)
        both = (acc_ref[:, part] + dot32(o_ref[...], w_ref[part, :], NT)).astype(jnp.bfloat16)
        outs[2 * j][...] = jnp.where(odd, both[:, HD:], both[:, :HD])
        outs[2 * j + 1][...] = jnp.where(odd, both[:, :HD], both[:, HD:])


def project(me, weight, features, acc, last):
    rows, width = features.shape
    columns = weight.shape[0]
    heads = columns // HD
    total = jax.ShapeDtypeStruct((rows, columns), jnp.float32)
    cost = pl.CostEstimate(
        flops=2 * rows * width * columns,
        bytes_accessed=2 * width * columns + 8 * rows * columns,
        transcendentals=0,
    )
    if last:
        return pl.pallas_call(
            project_last_kernel,
            in_specs=[SMEM_SPEC] + [VMEM_SPEC] * 3,
            out_specs=[VMEM_SPEC] * heads,
            out_shape=[jax.ShapeDtypeStruct((rows, HD), jnp.bfloat16)] * heads,
            compiler_params=params([features, weight, total, total]),
            cost_estimate=cost,
        )(me, features, weight, acc)
    operands = (features, weight) + (() if acc is None else (acc,))
    return pl.pallas_call(
        functools.partial(project_kernel, acc is None),
        in_specs=[VMEM_SPEC] * len(operands),
        out_specs=VMEM_SPEC,
        out_shape=total,
        compiler_params=params([features, weight, total, total]),
        cost_estimate=cost,
    )(*operands)


def at_or_before(q0, k0, shape):
    key = lax.broadcasted_iota(jnp.int32, shape, 0)
    return key <= q0 - k0 + lax.broadcasted_iota(jnp.int32, (1, shape[1]), 1)


def block_sizes(total):
    return (
        (block_size(total, 256), block_size(total, 256)),
        (block_size(total, 256), block_size(total, 256)),
    )


def plan_size(total, bq, bk):
    return sum(((q + 1) * bq + bk - 1) // bk for q in range(total // bq)) + 2


def fill_plan(lows, total, bq, bk, own, plan_q, plan_k, count_ref):
    def put(qi):
        def at(ki, count):
            plan_q[count] = qi
            plan_k[count] = ki
            return count + 1

        return at

    spans = []
    for qi, low in enumerate(lows):
        low, high = low // bk, ((qi + 1) * bq + bk - 1) // bk
        if own is not None:
            wanted = ((qi + 1) * bq > own[0]) & (qi * bq < own[1])
            low = jnp.where(wanted, low, jnp.maximum(low, own[0] // bk))
            high = jnp.where(wanted, high, jnp.minimum(high, (own[1] + bk - 1) // bk))
        whole = jnp.maximum(low, jnp.minimum(high, qi * bq // bk))
        spans.append((low, whole, high))
    count = 0
    for qi, (low, whole, high) in enumerate(spans):
        count = lax.fori_loop(low, whole, put(qi), count)
    count_ref[0] = jnp.maximum(count - 1, 0) // 2
    for qi, (low, whole, high) in enumerate(spans):
        count = lax.fori_loop(whole, high, put(qi), count)
    count_ref[1] = (count + 1) // 2
    for spare in range(2):
        plan_q[count + spare] = 0
        plan_k[count + spare] = total // bk - 1


def pipelined(plan_q, plan_k, count_ref, early, late, buffers):
    early(0, plan_q[0], plan_k[0], buffers[0], True)

    def turns(diagonal):
        def body(i, carry):
            for turn in range(2):
                now = 2 * i + turn
                late(now, plan_q[now], plan_k[now], buffers[turn])
                early(now + 1, plan_q[now + 1], plan_k[now + 1], buffers[1 - turn], diagonal)
            return carry

        return body

    lax.fori_loop(0, count_ref[0], turns(False), 0)
    lax.fori_loop(count_ref[0], count_ref[1], turns(True), 0)


def forward_kernel(peers, heads, rows, bq, bk, kept, me_s, *refs):
    blocks = refs[:peers]
    if kept:
        p_list, top_list = refs[peers + 6:peers + 8]
        refs = refs[:peers + 6] + refs[peers + 8:]
    v_ref, qx_ref, kx_ref, kt_ref, rows_ref, log_ref = refs[peers:peers + 6]
    plan_q, plan_k, count_ref, own_q, own_k, own_count = refs[peers + 6:peers + 12]
    vt_ref, out_ref, doc_ref, sum_ref, s0, top0, s1, top1 = refs[peers + 12:]
    total = v_ref.shape[0]
    factor = HD ** (-0.5) * math.log2(math.e)
    me = me_s[0]
    for d, block in enumerate(blocks):
        place = me ^ d
        for part, ref in enumerate((qx_ref.at[:, :HD], kx_ref.at[:, :HD], v_ref)):
            ref[aligned(place, rows), :] = block[part * rows:(part + 1) * rows, :]
        docs = block[3 * rows:, :].astype(jnp.float32)
        for t in range(rows // HD):
            doc_ref[:, aligned(place * (rows // HD) + t, HD)] = docs[t:t + 1, :]
    docs = doc_ref[...]
    first = jnp.zeros(docs.shape, jnp.float32)
    for value in range(1, DOC_VALUES):
        before = jnp.sum((docs < value).astype(jnp.float32))
        first = jnp.where(docs >= value, before, first)
    first = first.astype(jnp.int32)
    back_q, back_k = block_sizes(total)[1]
    lows = [jnp.min(first[:, qi * back_q:(qi + 1) * back_q]) for qi in range(total // back_q)]
    group = (me // heads) * heads * rows
    own = None if heads == peers else (group, group + heads * rows)
    fill_plan(lows, total, back_q, back_k, own, plan_q, plan_k, count_ref)
    if kept:
        own_q, own_k, own_count = plan_q, plan_k, count_ref
    else:
        lows = [jnp.min(first[:, qi * bq:(qi + 1) * bq]) for qi in range(total // bq)]
        fill_plan(lows, total, bq, bk, None, own_q, own_k, own_count)
    same = lax.broadcasted_iota(jnp.int32, (HD, total), 0).astype(jnp.float32) == docs
    ones = jnp.where(same, 1.0, 0.0).astype(jnp.bfloat16).T
    kx_ref[:, HD:] = ones
    qx_ref[:, HD:] = ((1.0 - ones.astype(jnp.float32)) * NEG_LARGE).astype(jnp.bfloat16)
    kt_ref[...] = kx_ref[:, :HD].T
    vt_ref[:HD, :] = v_ref[...].T
    vt_ref[HD:, :] = jnp.ones((ONES_ROWS, total), jnp.bfloat16)
    out_ref[...] = jnp.zeros_like(out_ref)
    log_ref[...] = jnp.full_like(log_ref, NEG_LARGE)
    sum_ref[...] = jnp.zeros_like(sum_ref)

    def early(now, qi, ki, buffer, diagonal):
        s_ref, top_ref = buffer
        keys, queries = aligned(ki, bk), aligned(qi, bq)
        s = dot32(kx_ref[keys, :], qx_ref[queries, :], NT) * factor
        if diagonal:
            s = jnp.where(at_or_before(qi * bq, ki * bk, (bk, bq)), s, NEG_LARGE)
        s_ref[...] = s
        top_ref[...] = jnp.max(s, axis=0, keepdims=True)

    def late(now, qi, ki, buffer):
        s_ref, top_ref = buffer
        keys, queries = aligned(ki, bk), aligned(qi, bq)
        top = log_ref[:, queries]
        new_top = jnp.maximum(top, top_ref[...])
        fix = jnp.exp2(top - new_top)
        vt = vt_ref[:, keys]
        p = jnp.exp2(s_ref[...] - new_top)
        high = p.astype(jnp.bfloat16)
        sums = dot32(vt, high)
        if kept:
            p_list[now] = high
            top_list[now] = new_top
        else:
            sums = sums + dot32(vt, (p - high.astype(jnp.float32)).astype(jnp.bfloat16))
        out_ref[:, queries] = out_ref[:, queries] * fix + sums[:HD, :]
        sum_ref[:, queries] = sum_ref[:, queries] * fix + sums[HD:HD + 1, :]
        log_ref[:, queries] = new_top

    pipelined(own_q, own_k, own_count, early, late, ((s0, top0), (s1, top1)))
    total_p = sum_ref[...]
    rows_ref[...] = (out_ref[...] / total_p).T
    log_ref[...] = log_ref[...] + jnp.log2(total_p)


def backward_kernel(listed, heads, rows, bq, bk, kept, me_s, plan_q, plan_k, count_ref, v_ref,
                    qx_ref, kx_ref, kt_ref, rows_ref, log_ref, *refs):
    if kept:
        p_list, refs = refs[0], refs[1:]
    peers = len(listed)
    if kept:
        refs = refs[3:]
    blocks = refs[:peers]
    dq_acc, dk_acc, dv_acc, g_ref, dot_ref, p0, ds0, p1, ds1 = refs[peers:]
    scale = HD ** (-0.5)
    factor = scale * math.log2(math.e)
    me = me_s[0]
    for d, block in zip(listed, blocks):
        g_ref[aligned(me ^ d, rows), :] = block[...]
    ones = jnp.ones((ONES_ROWS, HD), jnp.bfloat16)
    for start in range(0, g_ref.shape[0], bq):
        part = slice(start, start + bq)
        left = g_ref[part, :].astype(jnp.float32) * rows_ref[part, :]
        dots = 0.0
        for _ in range(3):
            term = left.astype(jnp.bfloat16)
            left = left - term.astype(jnp.float32)
            dots = dots + dot32(ones, term, NT)
        dot_ref[:, part] = dots[:1, :]
    if not kept:
        for ref in (dq_acc, dk_acc, dv_acc):
            ref[...] = jnp.zeros_like(ref)

    def early(now, qi, ki, buffer, diagonal):
        p_ref, ds_ref = buffer
        queries = aligned(qi, bq)
        log_row, dot_row = log_ref[:, queries], dot_ref[:, queries]
        for strip in range(0, bk, STRIP):
            part = slice(strip, strip + STRIP)
            keys = aligned(ki * (bk // STRIP) + strip // STRIP, STRIP)
            if kept:
                p = p_list[now, part, :].astype(jnp.float32)
            else:
                p = jnp.exp2(dot32(kx_ref[keys, :], qx_ref[queries, :], NT) * factor - log_row)
                if diagonal:
                    p = jnp.where(at_or_before(qi * bq, ki * bk + strip, (STRIP, bq)), p, 0.0)
                p_ref[part, :] = p.astype(jnp.bfloat16)
            dp = dot32(v_ref[keys, :], g_ref[queries, :], NT)
            ds_ref[part, :] = (p * (dp - dot_row)).astype(jnp.bfloat16)

    def late(now, qi, ki, buffer):
        p_ref, ds_ref = buffer
        keys, queries = aligned(ki, bk), aligned(qi, bq)
        dv_acc[keys, :] += dot32(p_list[now] if kept else p_ref[...], g_ref[queries, :])
        dk_acc[keys, :] += dot32(ds_ref[...], qx_ref[queries, :HD])
        dq_acc[:, queries] += dot32(kt_ref[:, keys], ds_ref[...])

    pipelined(plan_q, plan_k, count_ref, early, late, ((p0, ds0), (p1, ds1)))


def prepare_kernel(bq, bk, plan_q, count_ref, log_ref, top_list, p_list, p_out, *totals):
    for total in totals:
        total[...] = jnp.zeros_like(total)

    @pl.loop(0, 2 * count_ref[1])
    def _(now):
        share = jnp.exp2(top_list[now] - log_ref[:, aligned(plan_q[now], bq)])
        for strip in range(0, bk, STRIP):
            part = slice(strip, strip + STRIP)
            p_out[now, part, :] = (p_list[now, part, :].astype(jnp.float32) * share).astype(jnp.bfloat16)


def finish_kernel(listed, rows, me_s, dq_ref, dk_ref, dv_ref, *results):
    scale = HD ** (-0.5)
    for d, result in zip(listed, results):
        own = aligned(me_s[0] ^ d, rows)
        result[:rows, :] = (scale * dq_ref[:, own]).astype(result.dtype).T
        result[rows:2 * rows, :] = (scale * dk_ref[own, :]).astype(result.dtype)
        result[2 * rows:, :] = dv_ref[own, :].astype(result.dtype)


def finish(me, listed, totals, rows):
    out_shape = [jax.ShapeDtypeStruct((3 * rows, HD), jnp.bfloat16)] * len(listed)
    results = pl.pallas_call(
        functools.partial(finish_kernel, listed, rows),
        in_specs=[SMEM_SPEC] + [VMEM_SPEC] * 3,
        out_specs=[VMEM_SPEC] * len(listed),
        out_shape=out_shape,
        compiler_params=params([*totals, *out_shape]),
    )(me, *totals)
    return dict(zip(listed, results))


def keeps_list(total, peers, heads):
    forward, backward = block_sizes(total)
    size = plan_size(total, *forward) * math.prod(forward) * 2
    return forward == backward and heads == peers and size <= LIST_BYTES


def attention_cost(total, products):
    return pl.CostEstimate(
        flops=products * total * total * HD // 2,
        bytes_accessed=16 * total * HD,
        transcendentals=total * total // 4,
    )


def attention_forward(me, blocks, rows, heads):
    peers = len(blocks)
    total = peers * rows
    (bq, bk), back = block_sizes(total)
    plan = [(plan_size(total, *back),)] * 2 + [(2,)]
    own_plan = [(plan_size(total, bq, bk),)] * 2 + [(2,)]
    vectors = [
        jax.ShapeDtypeStruct((total, HD), jnp.bfloat16),
        *[jax.ShapeDtypeStruct((total, 2 * HD), jnp.bfloat16)] * 2,
        jax.ShapeDtypeStruct((HD, total), jnp.bfloat16),
        jax.ShapeDtypeStruct((total, HD), jnp.float32),
        jax.ShapeDtypeStruct((1, total), jnp.float32),
    ]
    kept = keeps_list(total, peers, heads)
    if kept:
        vectors.append(jax.ShapeDtypeStruct((*own_plan[0], bk, bq), jnp.bfloat16))
        vectors.append(jax.ShapeDtypeStruct((*own_plan[0], 1, bq), jnp.float32))
    scratch = [
        pltpu.VMEM((HD + ONES_ROWS, total), jnp.bfloat16),
        pltpu.VMEM((HD, total), jnp.float32),
        pltpu.VMEM((1, total), jnp.float32),
        pltpu.VMEM((1, total), jnp.float32),
        *[pltpu.VMEM((bk, bq), jnp.float32), pltpu.VMEM((1, bq), jnp.float32)] * 2,
    ]
    return pl.pallas_call(
        functools.partial(forward_kernel, peers, heads, rows, bq, bk, kept),
        in_specs=[SMEM_SPEC] + [VMEM_SPEC] * peers,
        out_specs=[VMEM_SPEC] * len(vectors) + [SMEM_SPEC] * 3,
        out_shape=vectors + [jax.ShapeDtypeStruct(shape, jnp.int32) for shape in plan],
        scratch_shapes=[pltpu.SMEM(shape, jnp.int32) for shape in own_plan] + scratch,
        compiler_params=params([*blocks, *vectors], scratch),
        cost_estimate=attention_cost(total, 3),
    )(me, *blocks)


def total_shapes(total):
    shapes = [(HD, total), (total, HD), (total, HD)]
    return [jax.ShapeDtypeStruct(shape, jnp.float32) for shape in shapes]


def prepare(log_total, p_list, top_list, plan_q, count):
    bk, bq = p_list.shape[1:]
    out_shape = [jax.ShapeDtypeStruct(p_list.shape, p_list.dtype)] + total_shapes(log_total.shape[1])
    return pl.pallas_call(
        functools.partial(prepare_kernel, bq, bk),
        in_specs=[SMEM_SPEC] * 2 + [VMEM_SPEC] * 3,
        out_specs=[VMEM_SPEC] * len(out_shape),
        out_shape=out_shape,
        input_output_aliases={4: 0},
        compiler_params=params([log_total, top_list, *out_shape[1:]]),
    )(plan_q, count, log_total, top_list, p_list)


def attention_backward(me, heads, state, listed, blocks, ready=()):
    peers, rows = len(blocks), blocks[0].shape[0]
    total = peers * rows
    bq, bk = block_sizes(total)[1]
    kept = bool(ready)
    vectors, plan = [*state[:6], *ready], state[-3:]
    out_shape = total_shapes(total)
    scratch = [
        pltpu.VMEM((total, HD), jnp.bfloat16),
        pltpu.VMEM((1, total), jnp.float32),
        *[pltpu.VMEM((bk, bq), jnp.bfloat16)] * 4,
    ]
    return pl.pallas_call(
        functools.partial(backward_kernel, listed, heads, rows, bq, bk, kept),
        in_specs=[SMEM_SPEC] * 4 + [VMEM_SPEC] * (len(vectors) + peers),
        out_specs=[VMEM_SPEC] * 3,
        out_shape=out_shape,
        scratch_shapes=scratch,
        input_output_aliases={4 + 7 + i: i for i in range(3)} if kept else {},
        compiler_params=params([*vectors[:6], *blocks] if kept else [*vectors, *blocks, *out_shape], scratch),
        cost_estimate=attention_cost(total, 5),
    )(me, *plan, *vectors, *blocks)


def per_device(peers, groups, queries, keys_in, values, out_grad, out_weight, doc_ids):
    rows, width = queries.shape
    heads = width // HD
    me = lax.axis_index("seq")
    me_vector = me.reshape(1)

    def exchange(x, d):
        return x if d == 0 else lax.ppermute(x, "seq", [(i, i ^ d) for i in range(peers)])

    def pass_on(x):
        return lax.ppermute(x, "head", [(i, (i + 1) % groups) for i in range(groups)])

    order = [*range(2, peers, 2), *range(peers - 1, 0, -2)]

    far_first = sorted(range(peers), key=lambda d: (-bin(d >> 1).count("1"), d & 1, d))
    returning = [d for d in far_first if d < heads]

    def exchange_all(blocks, listed):
        return [exchange(blocks[d % heads], d) for d in listed]

    packed = list(pack_heads(me_vector, queries, keys_in, values, doc_ids))
    received = exchange_all(packed, range(peers))

    def share(step):
        return len(order) * step // (groups - 2)

    after = lax.optimization_barrier
    features, acc = out_grad, None
    weights = []
    for step in range(groups):
        block = lax.rem(lax.axis_index("head") + groups - step, groups)
        weights.append(lax.dynamic_slice_in_dim(out_weight, block * width, width, 1))
    for step in range(groups):
        last = step == groups - 1
        if not last:
            passed = pass_on(features)
        if step == groups - 2:
            received[0], features = after((received[0], features))
            state = list(attention_forward(me_vector, received, rows, heads))
            features, state[1] = after((features, state[1]))
        acc = project(me_vector, weights[step], features, acc, last)
        if not last:
            features = passed
            if step < groups - 2:
                batch = order[share(step):share(step + 1)]
                here = [received[d] for d in batch]
                features, acc, here, weights[2:] = after((features, acc, here, weights[2:]))
                for d, block in zip(batch, here):
                    received[d] = block
    grads = exchange_all(acc, far_first)

    ready = ()
    if len(state) > 9:
        p_list, grads[0] = after((state[6], grads[0]))
        ready = prepare(state[5], p_list, state[7], state[-3], state[-1])
    totals = attention_backward(me_vector, heads, state, far_first, grads, ready)

    far = [d for d in returning if bin(d >> 1).count("1") > 1]
    near = [d for d in returning if d not in far]
    results = {**(finish(me_vector, far, totals, rows) if far else {}), **finish(me_vector, near, totals, rows)}
    returned = {d: exchange(results[d], d) for d in returning}
    early, late = [*far, 0], [d for d in near if d > 0]
    partial = unpack_heads(me_vector, early, [returned[d] for d in early], rows, heads)
    return tuple(unpack_heads(me_vector, late, [returned[d] for d in late], rows, heads, partial))


def solution(mesh):
    in_specs = (
        P("seq", "head"),
        P("seq", "head"),
        P("seq", "head"),
        P("seq", "head"),
        P("head", None),
        P("seq"),
    )
    out_specs = (P("seq", "head"), P("seq", "head"), P("seq", "head"))
    return jax.shard_map(
        functools.partial(per_device, mesh.shape["seq"], mesh.shape["head"]),
        mesh=mesh, in_specs=in_specs, out_specs=out_specs, check_vma=False,
    )
```

```python
import functools
import math

import jax
import jax.numpy as jnp
from jax import lax
from jax.experimental import pallas as pl
from jax.experimental.pallas import tpu as pltpu
from jax.sharding import PartitionSpec as P

HD = 128
DOC_VALUES = 8
DOC_ROWS = 16
ONES_ROWS = 16
STRIP = 128
NEG_LARGE = -1e30
VMEM_SPARE = 6 * 1024 * 1024
VMEM_MOST = 56 * 1024 * 1024
LIST_BYTES = 16 * 1024 * 1024

NN = (((1,), (0,)), ((), ()))
NT = (((1,), (1,)), ((), ()))
SMEM_SPEC = pl.BlockSpec(memory_space=pltpu.SMEM)
VMEM_SPEC = pl.BlockSpec(memory_space=pltpu.VMEM)
ANY_SPEC = pl.BlockSpec(memory_space=pl.ANY)


def dot32(a, b, dims=NN):
    return lax.dot_general(a, b, dims, preferred_element_type=jnp.float32)


def block_size(total, wanted):
    size = min(wanted, total)
    while total % size or size % 128:
        size -= 128
    return size


def aligned(index, size):
    return pl.ds(pl.multiple_of(index * size, size), size)


def params(arrays, scratch=()):
    total = sum(math.prod(a.shape) * jnp.dtype(a.dtype).itemsize for a in (*arrays, *scratch))
    return pltpu.CompilerParams(vmem_limit_bytes=total + VMEM_SPARE)


def pack_kernel(heads, rows, me_s, q_ref, k_ref, v_ref, doc_ref, *outs):
    own = lax.rem(me_s[0], heads)
    docs = doc_ref[...].astype(jnp.float32)
    docs = jnp.concatenate([docs, jnp.zeros((DOC_ROWS - docs.shape[0], HD), jnp.float32)], axis=0)
    docs = docs.astype(jnp.bfloat16)
    for d, out in enumerate(outs):
        columns = aligned(own ^ d, HD)
        for part, ref in enumerate((q_ref, k_ref, v_ref)):
            out[part * rows:(part + 1) * rows, :] = ref[:, columns]
        out[3 * rows:, :] = docs


def pack_heads(me, q, k, v, doc_ids):
    rows, width = q.shape
    heads = width // HD
    return pl.pallas_call(
        functools.partial(pack_kernel, heads, rows),
        in_specs=[SMEM_SPEC] + [VMEM_SPEC] * 4,
        out_specs=[VMEM_SPEC] * heads,
        out_shape=[jax.ShapeDtypeStruct((3 * rows + DOC_ROWS, HD), q.dtype)] * heads,
        compiler_params=pltpu.CompilerParams(vmem_limit_bytes=VMEM_MOST),
    )(me, q, k, v, doc_ids.reshape(rows // HD, HD))


def unpack_kernel(listed, heads, rows, me_s, *refs):
    outs, done = refs[-4:-1], refs[-1]
    own = lax.rem(me_s[0], heads)
    copies = []
    for place, (d, block) in enumerate(zip(listed, refs)):
        columns = aligned(own ^ d, HD)
        for part, out in enumerate(outs):
            source = block.at[pl.ds(part * rows, rows), :]
            copies.append(pltpu.make_async_copy(source, out.at[:, columns], done.at[place, part]))
            copies[-1].start()
    for copy in copies:
        copy.wait()


def unpack_heads(me, listed, blocks, rows, heads, partial=()):
    count = len(blocks)
    return pl.pallas_call(
        functools.partial(unpack_kernel, listed, heads, rows),
        in_specs=[SMEM_SPEC] + [VMEM_SPEC] * count + [ANY_SPEC] * len(partial),
        out_specs=[ANY_SPEC] * 3,
        out_shape=[jax.ShapeDtypeStruct((rows, heads * HD), blocks[0].dtype)] * 3,
        scratch_shapes=[pltpu.SemaphoreType.DMA((count, 3))],
        input_output_aliases={1 + count + i: i for i in range(len(partial))},
        compiler_params=params([*blocks]),
    )(me, *blocks, *partial)


def project_kernel(first, o_ref, w_ref, *refs):
    out_ref = refs[-1]
    for pair in range(w_ref.shape[0] // (2 * HD)):
        part = slice(pair * 2 * HD, (pair + 1) * 2 * HD)
        both = dot32(o_ref[...], w_ref[part, :], NT)
        out_ref[:, part] = both if first else refs[0][:, part] + both


def project_last_kernel(me_s, o_ref, w_ref, acc_ref, *outs):
    pairs = len(outs) // 2
    odd = lax.rem(me_s[0], 2) == 1
    for j in range(pairs):
        part = aligned(lax.rem(me_s[0] // 2, pairs) ^ j, 2 * HD)
        both = (acc_ref[:, part] + dot32(o_ref[...], w_ref[part, :], NT)).astype(jnp.bfloat16)
        outs[2 * j][...] = jnp.where(odd, both[:, HD:], both[:, :HD])
        outs[2 * j + 1][...] = jnp.where(odd, both[:, :HD], both[:, HD:])


def project(me, weight, features, acc, last):
    rows, width = features.shape
    columns = weight.shape[0]
    heads = columns // HD
    total = jax.ShapeDtypeStruct((rows, columns), jnp.float32)
    cost = pl.CostEstimate(
        flops=2 * rows * width * columns,
        bytes_accessed=2 * width * columns + 8 * rows * columns,
        transcendentals=0,
    )
    if last:
        return pl.pallas_call(
            project_last_kernel,
            in_specs=[SMEM_SPEC] + [VMEM_SPEC] * 3,
            out_specs=[VMEM_SPEC] * heads,
            out_shape=[jax.ShapeDtypeStruct((rows, HD), jnp.bfloat16)] * heads,
            compiler_params=params([features, weight, total, total]),
            cost_estimate=cost,
        )(me, features, weight, acc)
    operands = (features, weight) + (() if acc is None else (acc,))
    return pl.pallas_call(
        functools.partial(project_kernel, acc is None),
        in_specs=[VMEM_SPEC] * len(operands),
        out_specs=VMEM_SPEC,
        out_shape=total,
        compiler_params=params([features, weight, total, total]),
        cost_estimate=cost,
    )(*operands)


def at_or_before(q0, k0, shape):
    key = lax.broadcasted_iota(jnp.int32, shape, 0)
    return key <= q0 - k0 + lax.broadcasted_iota(jnp.int32, (1, shape[1]), 1)


def block_sizes(total):
    return (
        (block_size(total, 256), block_size(total, 256)),
        (block_size(total, 256), block_size(total, 256)),
    )


def plan_size(total, bq, bk):
    return sum(((q + 1) * bq + bk - 1) // bk for q in range(total // bq)) + 2


def fill_plan(lows, total, bq, bk, own, plan_q, plan_k, count_ref):
    def put(qi):
        def at(ki, count):
            plan_q[count] = qi
            plan_k[count] = ki
            return count + 1

        return at

    spans = []
    for qi, low in enumerate(lows):
        low, high = low // bk, ((qi + 1) * bq + bk - 1) // bk
        if own is not None:
            wanted = ((qi + 1) * bq > own[0]) & (qi * bq < own[1])
            low = jnp.where(wanted, low, jnp.maximum(low, own[0] // bk))
            high = jnp.where(wanted, high, jnp.minimum(high, (own[1] + bk - 1) // bk))
        whole = jnp.maximum(low, jnp.minimum(high, qi * bq // bk))
        spans.append((low, whole, high))
    count = 0
    for qi, (low, whole, high) in enumerate(spans):
        count = lax.fori_loop(low, whole, put(qi), count)
    count_ref[0] = jnp.maximum(count - 1, 0) // 2
    for qi, (low, whole, high) in enumerate(spans):
        count = lax.fori_loop(whole, high, put(qi), count)
    count_ref[1] = (count + 1) // 2
    for spare in range(2):
        plan_q[count + spare] = 0
        plan_k[count + spare] = total // bk - 1


def pipelined(plan_q, plan_k, count_ref, early, late, buffers):
    early(0, plan_q[0], plan_k[0], buffers[0], True)

    def turns(base, count, diagonal):
        for turn in range(2 * count):
            now = 2 * base + turn
            late(now, plan_q[now], plan_k[now], buffers[turn % 2])
            early(now + 1, plan_q[now + 1], plan_k[now + 1], buffers[1 - turn % 2], diagonal)

    def run(start, stop, diagonal):
        doubles = (stop - start) // 2

        @pl.loop(0, doubles)
        def _(i):
            turns(start + 2 * i, 2, diagonal)

        @pl.loop(start + 2 * doubles, stop)
        def _(i):
            turns(i, 1, diagonal)

    run(0, count_ref[0], False)
    run(count_ref[0], count_ref[1], True)


def forward_kernel(peers, heads, rows, bq, bk, kept, me_s, *refs):
    blocks = refs[:peers]
    if kept:
        p_list, top_list = refs[peers + 6:peers + 8]
        refs = refs[:peers + 6] + refs[peers + 8:]
    v_ref, qx_ref, kx_ref, kt_ref, rows_ref, log_ref = refs[peers:peers + 6]
    plan_q, plan_k, count_ref, own_q, own_k, own_count = refs[peers + 6:peers + 12]
    vt_ref, out_ref, doc_ref, sum_ref, s0, top0, s1, top1 = refs[peers + 12:]
    total = v_ref.shape[0]
    factor = HD ** (-0.5) * math.log2(math.e)
    me = me_s[0]
    for d, block in enumerate(blocks):
        place = me ^ d
        for part, ref in enumerate((qx_ref.at[:, :HD], kx_ref.at[:, :HD], v_ref)):
            ref[aligned(place, rows), :] = block[part * rows:(part + 1) * rows, :]
        docs = block[3 * rows:, :].astype(jnp.float32)
        for t in range(rows // HD):
            doc_ref[:, aligned(place * (rows // HD) + t, HD)] = docs[t:t + 1, :]
    docs = doc_ref[...]
    first = jnp.zeros(docs.shape, jnp.float32)
    for value in range(1, DOC_VALUES):
        before = jnp.sum((docs < value).astype(jnp.float32))
        first = jnp.where(docs >= value, before, first)
    first = first.astype(jnp.int32)
    back_q, back_k = block_sizes(total)[1]
    lows = [jnp.min(first[:, qi * back_q:(qi + 1) * back_q]) for qi in range(total // back_q)]
    group = (me // heads) * heads * rows
    own = None if heads == peers else (group, group + heads * rows)
    fill_plan(lows, total, back_q, back_k, own, plan_q, plan_k, count_ref)
    if kept:
        own_q, own_k, own_count = plan_q, plan_k, count_ref
    else:
        lows = [jnp.min(first[:, qi * bq:(qi + 1) * bq]) for qi in range(total // bq)]
        fill_plan(lows, total, bq, bk, None, own_q, own_k, own_count)
    same = lax.broadcasted_iota(jnp.int32, (HD, total), 0).astype(jnp.float32) == docs
    ones = jnp.where(same, 1.0, 0.0).astype(jnp.bfloat16).T
    kx_ref[:, HD:] = ones
    qx_ref[:, HD:] = ((1.0 - ones.astype(jnp.float32)) * NEG_LARGE).astype(jnp.bfloat16)
    kt_ref[...] = kx_ref[:, :HD].T
    vt_ref[:HD, :] = v_ref[...].T
    vt_ref[HD:, :] = jnp.ones((ONES_ROWS, total), jnp.bfloat16)
    out_ref[...] = jnp.zeros_like(out_ref)
    log_ref[...] = jnp.full_like(log_ref, NEG_LARGE)
    sum_ref[...] = jnp.zeros_like(sum_ref)

    def early(now, qi, ki, buffer, diagonal):
        s_ref, top_ref = buffer
        keys, queries = aligned(ki, bk), aligned(qi, bq)
        s = dot32(kx_ref[keys, :], qx_ref[queries, :], NT) * factor
        if diagonal:
            s = jnp.where(at_or_before(qi * bq, ki * bk, (bk, bq)), s, NEG_LARGE)
        s_ref[...] = s
        top_ref[...] = jnp.max(s, axis=0, keepdims=True)

    def late(now, qi, ki, buffer):
        s_ref, top_ref = buffer
        keys, queries = aligned(ki, bk), aligned(qi, bq)
        top = log_ref[:, queries]
        new_top = jnp.maximum(top, top_ref[...])
        fix = jnp.exp2(top - new_top)
        vt = vt_ref[:, keys]
        p = jnp.exp2(s_ref[...] - new_top)
        high = p.astype(jnp.bfloat16)
        sums = dot32(vt, high)
        if kept:
            p_list[now] = high
            top_list[now] = new_top
        else:
            sums = sums + dot32(vt, (p - high.astype(jnp.float32)).astype(jnp.bfloat16))
        out_ref[:, queries] = out_ref[:, queries] * fix + sums[:HD, :]
        sum_ref[:, queries] = sum_ref[:, queries] * fix + sums[HD:HD + 1, :]
        log_ref[:, queries] = new_top

    pipelined(own_q, own_k, own_count, early, late, ((s0, top0), (s1, top1)))
    total_p = sum_ref[...]
    rows_ref[...] = (out_ref[...] / total_p).T
    log_ref[...] = log_ref[...] + jnp.log2(total_p)


def backward_kernel(listed, heads, rows, bq, bk, kept, me_s, plan_q, plan_k, count_ref, v_ref,
                    qx_ref, kx_ref, kt_ref, rows_ref, log_ref, *refs):
    if kept:
        p_list, refs = refs[0], refs[1:]
    peers = len(listed)
    if kept:
        refs = refs[3:]
    blocks = refs[:peers]
    dq_acc, dk_acc, dv_acc, g_ref, dot_ref, p0, ds0, p1, ds1 = refs[peers:]
    scale = HD ** (-0.5)
    factor = scale * math.log2(math.e)
    me = me_s[0]
    for d, block in zip(listed, blocks):
        g_ref[aligned(me ^ d, rows), :] = block[...]
    ones = jnp.ones((ONES_ROWS, HD), jnp.bfloat16)
    for start in range(0, g_ref.shape[0], bq):
        part = slice(start, start + bq)
        left = g_ref[part, :].astype(jnp.float32) * rows_ref[part, :]
        dots = 0.0
        for _ in range(3):
            term = left.astype(jnp.bfloat16)
            left = left - term.astype(jnp.float32)
            dots = dots + dot32(ones, term, NT)
        dot_ref[:, part] = dots[:1, :]
    if not kept:
        for ref in (dq_acc, dk_acc, dv_acc):
            ref[...] = jnp.zeros_like(ref)

    def early(now, qi, ki, buffer, diagonal):
        p_ref, ds_ref = buffer
        queries = aligned(qi, bq)
        log_row, dot_row = log_ref[:, queries], dot_ref[:, queries]
        for strip in range(0, bk, STRIP):
            part = slice(strip, strip + STRIP)
            keys = aligned(ki * (bk // STRIP) + strip // STRIP, STRIP)
            if kept:
                p = p_list[now, part, :].astype(jnp.float32)
            else:
                p = jnp.exp2(dot32(kx_ref[keys, :], qx_ref[queries, :], NT) * factor - log_row)
                if diagonal:
                    p = jnp.where(at_or_before(qi * bq, ki * bk + strip, (STRIP, bq)), p, 0.0)
                p_ref[part, :] = p.astype(jnp.bfloat16)
            dp = dot32(v_ref[keys, :], g_ref[queries, :], NT)
            ds_ref[part, :] = (p * (dp - dot_row)).astype(jnp.bfloat16)

    def late(now, qi, ki, buffer):
        p_ref, ds_ref = buffer
        keys, queries = aligned(ki, bk), aligned(qi, bq)
        dv_acc[keys, :] += dot32(p_list[now] if kept else p_ref[...], g_ref[queries, :])
        dk_acc[keys, :] += dot32(ds_ref[...], qx_ref[queries, :HD])
        dq_acc[:, queries] += dot32(kt_ref[:, keys], ds_ref[...])

    pipelined(plan_q, plan_k, count_ref, early, late, ((p0, ds0), (p1, ds1)))


def prepare_kernel(bq, bk, plan_q, count_ref, log_ref, top_list, p_list, p_out, *totals):
    for total in totals:
        total[...] = jnp.zeros_like(total)

    @pl.loop(0, 2 * count_ref[1])
    def _(now):
        share = jnp.exp2(top_list[now] - log_ref[:, aligned(plan_q[now], bq)])
        for strip in range(0, bk, STRIP):
            part = slice(strip, strip + STRIP)
            p_out[now, part, :] = (p_list[now, part, :].astype(jnp.float32) * share).astype(jnp.bfloat16)


def finish_kernel(listed, rows, me_s, dq_ref, dk_ref, dv_ref, *results):
    scale = HD ** (-0.5)
    for d, result in zip(listed, results):
        own = aligned(me_s[0] ^ d, rows)
        result[:rows, :] = (scale * dq_ref[:, own]).astype(result.dtype).T
        result[rows:2 * rows, :] = (scale * dk_ref[own, :]).astype(result.dtype)
        result[2 * rows:, :] = dv_ref[own, :].astype(result.dtype)


def finish(me, listed, totals, rows):
    out_shape = [jax.ShapeDtypeStruct((3 * rows, HD), jnp.bfloat16)] * len(listed)
    results = pl.pallas_call(
        functools.partial(finish_kernel, listed, rows),
        in_specs=[SMEM_SPEC] + [VMEM_SPEC] * 3,
        out_specs=[VMEM_SPEC] * len(listed),
        out_shape=out_shape,
        compiler_params=params([*totals, *out_shape]),
    )(me, *totals)
    return dict(zip(listed, results))


def keeps_list(total, peers, heads):
    forward, backward = block_sizes(total)
    size = plan_size(total, *forward) * math.prod(forward) * 2
    return forward == backward and heads == peers and size <= LIST_BYTES


def attention_cost(total, products):
    return pl.CostEstimate(
        flops=products * total * total * HD // 2,
        bytes_accessed=16 * total * HD,
        transcendentals=total * total // 4,
    )


def attention_forward(me, blocks, rows, heads):
    peers = len(blocks)
    total = peers * rows
    (bq, bk), back = block_sizes(total)
    plan = [(plan_size(total, *back),)] * 2 + [(2,)]
    own_plan = [(plan_size(total, bq, bk),)] * 2 + [(2,)]
    vectors = [
        jax.ShapeDtypeStruct((total, HD), jnp.bfloat16),
        *[jax.ShapeDtypeStruct((total, 2 * HD), jnp.bfloat16)] * 2,
        jax.ShapeDtypeStruct((HD, total), jnp.bfloat16),
        jax.ShapeDtypeStruct((total, HD), jnp.float32),
        jax.ShapeDtypeStruct((1, total), jnp.float32),
    ]
    kept = keeps_list(total, peers, heads)
    if kept:
        vectors.append(jax.ShapeDtypeStruct((*own_plan[0], bk, bq), jnp.bfloat16))
        vectors.append(jax.ShapeDtypeStruct((*own_plan[0], 1, bq), jnp.float32))
    scratch = [
        pltpu.VMEM((HD + ONES_ROWS, total), jnp.bfloat16),
        pltpu.VMEM((HD, total), jnp.float32),
        pltpu.VMEM((1, total), jnp.float32),
        pltpu.VMEM((1, total), jnp.float32),
        *[pltpu.VMEM((bk, bq), jnp.float32), pltpu.VMEM((1, bq), jnp.float32)] * 2,
    ]
    return pl.pallas_call(
        functools.partial(forward_kernel, peers, heads, rows, bq, bk, kept),
        in_specs=[SMEM_SPEC] + [VMEM_SPEC] * peers,
        out_specs=[VMEM_SPEC] * len(vectors) + [SMEM_SPEC] * 3,
        out_shape=vectors + [jax.ShapeDtypeStruct(shape, jnp.int32) for shape in plan],
        scratch_shapes=[pltpu.SMEM(shape, jnp.int32) for shape in own_plan] + scratch,
        compiler_params=params([*blocks, *vectors], scratch),
        cost_estimate=attention_cost(total, 3),
    )(me, *blocks)


def total_shapes(total):
    shapes = [(HD, total), (total, HD), (total, HD)]
    return [jax.ShapeDtypeStruct(shape, jnp.float32) for shape in shapes]


def prepare(log_total, p_list, top_list, plan_q, count):
    bk, bq = p_list.shape[1:]
    out_shape = [jax.ShapeDtypeStruct(p_list.shape, p_list.dtype)] + total_shapes(log_total.shape[1])
    return pl.pallas_call(
        functools.partial(prepare_kernel, bq, bk),
        in_specs=[SMEM_SPEC] * 2 + [VMEM_SPEC] * 3,
        out_specs=[VMEM_SPEC] * len(out_shape),
        out_shape=out_shape,
        input_output_aliases={4: 0},
        compiler_params=params([log_total, top_list, *out_shape[1:]]),
    )(plan_q, count, log_total, top_list, p_list)


def attention_backward(me, heads, state, listed, blocks, ready=()):
    peers, rows = len(blocks), blocks[0].shape[0]
    total = peers * rows
    bq, bk = block_sizes(total)[1]
    kept = bool(ready)
    vectors, plan = [*state[:6], *ready], state[-3:]
    out_shape = total_shapes(total)
    scratch = [
        pltpu.VMEM((total, HD), jnp.bfloat16),
        pltpu.VMEM((1, total), jnp.float32),
        *[pltpu.VMEM((bk, bq), jnp.bfloat16)] * 4,
    ]
    return pl.pallas_call(
        functools.partial(backward_kernel, listed, heads, rows, bq, bk, kept),
        in_specs=[SMEM_SPEC] * 4 + [VMEM_SPEC] * (len(vectors) + peers),
        out_specs=[VMEM_SPEC] * 3,
        out_shape=out_shape,
        scratch_shapes=scratch,
        input_output_aliases={4 + 7 + i: i for i in range(3)} if kept else {},
        compiler_params=params([*vectors[:6], *blocks] if kept else [*vectors, *blocks, *out_shape], scratch),
        cost_estimate=attention_cost(total, 5),
    )(me, *plan, *vectors, *blocks)


def per_device(peers, groups, queries, keys_in, values, out_grad, out_weight, doc_ids):
    rows, width = queries.shape
    heads = width // HD
    me = lax.axis_index("seq")
    me_vector = me.reshape(1)

    def exchange(x, d):
        return x if d == 0 else lax.ppermute(x, "seq", [(i, i ^ d) for i in range(peers)])

    def pass_on(x):
        return lax.ppermute(x, "head", [(i, (i + 1) % groups) for i in range(groups)])

    order = [*range(2, peers, 2), *range(peers - 1, 0, -2)]

    far_first = sorted(range(peers), key=lambda d: (-bin(d >> 1).count("1"), d & 1, d))
    returning = [d for d in far_first if d < heads]

    def exchange_all(blocks, listed):
        return [exchange(blocks[d % heads], d) for d in listed]

    packed = list(pack_heads(me_vector, queries, keys_in, values, doc_ids))
    received = exchange_all(packed, range(peers))

    def share(step):
        return len(order) * step // (groups - 2)

    after = lax.optimization_barrier
    features, acc = out_grad, None
    weights = []
    for step in range(groups):
        block = lax.rem(lax.axis_index("head") + groups - step, groups)
        weights.append(lax.dynamic_slice_in_dim(out_weight, block * width, width, 1))
    for step in range(groups):
        last = step == groups - 1
        if not last:
            passed = pass_on(features)
        if step == groups - 2:
            received[0], features = after((received[0], features))
            state = list(attention_forward(me_vector, received, rows, heads))
            features, state[1] = after((features, state[1]))
        acc = project(me_vector, weights[step], features, acc, last)
        if not last:
            features = passed
            if step < groups - 2:
                batch = order[share(step):share(step + 1)]
                here = [received[d] for d in batch]
                features, acc, here, weights[2:] = after((features, acc, here, weights[2:]))
                for d, block in zip(batch, here):
                    received[d] = block
    grads = exchange_all(acc, far_first)

    ready = ()
    if len(state) > 9:
        p_list, grads[0] = after((state[6], grads[0]))
        ready = prepare(state[5], p_list, state[7], state[-3], state[-1])
    totals = attention_backward(me_vector, heads, state, far_first, grads, ready)

    far = [d for d in returning if bin(d >> 1).count("1") > 1]
    near = [d for d in returning if d not in far]
    results = {**(finish(me_vector, far, totals, rows) if far else {}), **finish(me_vector, near, totals, rows)}
    returned = {d: exchange(results[d], d) for d in returning}
    early, late = [*far, 0], [d for d in near if d > 0]
    partial = unpack_heads(me_vector, early, [returned[d] for d in early], rows, heads)
    return tuple(unpack_heads(me_vector, late, [returned[d] for d in late], rows, heads, partial))


def solution(mesh):
    in_specs = (
        P("seq", "head"),
        P("seq", "head"),
        P("seq", "head"),
        P("seq", "head"),
        P("head", None),
        P("seq"),
    )
    out_specs = (P("seq", "head"), P("seq", "head"), P("seq", "head"))
    return jax.shard_map(
        functools.partial(per_device, mesh.shape["seq"], mesh.shape["head"]),
        mesh=mesh, in_specs=in_specs, out_specs=out_specs, check_vma=False,
    )
```

```python
import functools
import math

import jax
import jax.numpy as jnp
from jax import lax
from jax.experimental import pallas as pl
from jax.experimental.pallas import tpu as pltpu
from jax.sharding import PartitionSpec as P

HD = 128
DOC_VALUES = 8
DOC_ROWS = 16
ONES_ROWS = 16
STRIP = 128
LOOP_TURNS = 4
NEG_LARGE = -1e30
VMEM_SPARE = 6 * 1024 * 1024
VMEM_MOST = 56 * 1024 * 1024
LIST_BYTES = 16 * 1024 * 1024

NN = (((1,), (0,)), ((), ()))
NT = (((1,), (1,)), ((), ()))
SMEM_SPEC = pl.BlockSpec(memory_space=pltpu.SMEM)
VMEM_SPEC = pl.BlockSpec(memory_space=pltpu.VMEM)
ANY_SPEC = pl.BlockSpec(memory_space=pl.ANY)


def dot32(a, b, dims=NN):
    return lax.dot_general(a, b, dims, preferred_element_type=jnp.float32)


def block_size(total, wanted):
    size = min(wanted, total)
    while total % size or size % 128:
        size -= 128
    return size


def aligned(index, size):
    return pl.ds(pl.multiple_of(index * size, size), size)


def params(arrays, scratch=()):
    total = sum(math.prod(a.shape) * jnp.dtype(a.dtype).itemsize for a in (*arrays, *scratch))
    return pltpu.CompilerParams(vmem_limit_bytes=total + VMEM_SPARE)


def pack_kernel(heads, rows, me_s, q_ref, k_ref, v_ref, doc_ref, *outs):
    own = lax.rem(me_s[0], heads)
    docs = doc_ref[...].astype(jnp.float32)
    docs = jnp.concatenate([docs, jnp.zeros((DOC_ROWS - docs.shape[0], HD), jnp.float32)], axis=0)
    docs = docs.astype(jnp.bfloat16)
    for d, out in enumerate(outs):
        columns = aligned(own ^ d, HD)
        for part, ref in enumerate((q_ref, k_ref, v_ref)):
            out[part * rows:(part + 1) * rows, :] = ref[:, columns]
        out[3 * rows:, :] = docs


def pack_heads(me, q, k, v, doc_ids):
    rows, width = q.shape
    heads = width // HD
    return pl.pallas_call(
        functools.partial(pack_kernel, heads, rows),
        in_specs=[SMEM_SPEC] + [VMEM_SPEC] * 4,
        out_specs=[VMEM_SPEC] * heads,
        out_shape=[jax.ShapeDtypeStruct((3 * rows + DOC_ROWS, HD), q.dtype)] * heads,
        compiler_params=pltpu.CompilerParams(vmem_limit_bytes=VMEM_MOST),
    )(me, q, k, v, doc_ids.reshape(rows // HD, HD))


def unpack_kernel(listed, heads, rows, me_s, *refs):
    outs, done = refs[-4:-1], refs[-1]
    own = lax.rem(me_s[0], heads)
    copies = []
    for place, (d, block) in enumerate(zip(listed, refs)):
        columns = aligned(own ^ d, HD)
        for part, out in enumerate(outs):
            source = block.at[pl.ds(part * rows, rows), :]
            copies.append(pltpu.make_async_copy(source, out.at[:, columns], done.at[place, part]))
            copies[-1].start()
    for copy in copies:
        copy.wait()


def unpack_heads(me, listed, blocks, rows, heads, partial=()):
    count = len(blocks)
    return pl.pallas_call(
        functools.partial(unpack_kernel, listed, heads, rows),
        in_specs=[SMEM_SPEC] + [VMEM_SPEC] * count + [ANY_SPEC] * len(partial),
        out_specs=[ANY_SPEC] * 3,
        out_shape=[jax.ShapeDtypeStruct((rows, heads * HD), blocks[0].dtype)] * 3,
        scratch_shapes=[pltpu.SemaphoreType.DMA((count, 3))],
        input_output_aliases={1 + count + i: i for i in range(len(partial))},
        compiler_params=params([*blocks]),
    )(me, *blocks, *partial)


def project_kernel(first, o_ref, w_ref, *refs):
    out_ref = refs[-1]
    for pair in range(w_ref.shape[0] // (2 * HD)):
        part = slice(pair * 2 * HD, (pair + 1) * 2 * HD)
        both = dot32(o_ref[...], w_ref[part, :], NT)
        out_ref[:, part] = both if first else refs[0][:, part] + both


def project_last_kernel(me_s, o_ref, w_ref, acc_ref, *outs):
    pairs = len(outs) // 2
    odd = lax.rem(me_s[0], 2) == 1
    for j in range(pairs):
        part = aligned(lax.rem(me_s[0] // 2, pairs) ^ j, 2 * HD)
        both = (acc_ref[:, part] + dot32(o_ref[...], w_ref[part, :], NT)).astype(jnp.bfloat16)
        outs[2 * j][...] = jnp.where(odd, both[:, HD:], both[:, :HD])
        outs[2 * j + 1][...] = jnp.where(odd, both[:, :HD], both[:, HD:])


def project(me, weight, features, acc, last):
    rows, width = features.shape
    columns = weight.shape[0]
    heads = columns // HD
    total = jax.ShapeDtypeStruct((rows, columns), jnp.float32)
    cost = pl.CostEstimate(
        flops=2 * rows * width * columns,
        bytes_accessed=2 * width * columns + 8 * rows * columns,
        transcendentals=0,
    )
    if last:
        return pl.pallas_call(
            project_last_kernel,
            in_specs=[SMEM_SPEC] + [VMEM_SPEC] * 3,
            out_specs=[VMEM_SPEC] * heads,
            out_shape=[jax.ShapeDtypeStruct((rows, HD), jnp.bfloat16)] * heads,
            compiler_params=params([features, weight, total, total]),
            cost_estimate=cost,
        )(me, features, weight, acc)
    operands = (features, weight) + (() if acc is None else (acc,))
    return pl.pallas_call(
        functools.partial(project_kernel, acc is None),
        in_specs=[VMEM_SPEC] * len(operands),
        out_specs=VMEM_SPEC,
        out_shape=total,
        compiler_params=params([features, weight, total, total]),
        cost_estimate=cost,
    )(*operands)


def at_or_before(q0, k0, shape):
    key = lax.broadcasted_iota(jnp.int32, shape, 0)
    return key <= q0 - k0 + lax.broadcasted_iota(jnp.int32, (1, shape[1]), 1)


def block_sizes(total):
    return (
        (block_size(total, 256), block_size(total, 256)),
        (block_size(total, 256), block_size(total, 256)),
    )


def plan_size(total, bq, bk):
    return sum(((q + 1) * bq + bk - 1) // bk for q in range(total // bq)) + 2


def fill_plan(lows, total, bq, bk, own, plan_q, plan_k, count_ref):
    def put(qi):
        def at(ki, count):
            plan_q[count] = qi
            plan_k[count] = ki
            return count + 1

        return at

    spans = []
    for qi, low in enumerate(lows):
        low, high = low // bk, ((qi + 1) * bq + bk - 1) // bk
        if own is not None:
            wanted = ((qi + 1) * bq > own[0]) & (qi * bq < own[1])
            low = jnp.where(wanted, low, jnp.maximum(low, own[0] // bk))
            high = jnp.where(wanted, high, jnp.minimum(high, (own[1] + bk - 1) // bk))
        whole = jnp.maximum(low, jnp.minimum(high, qi * bq // bk))
        spans.append((low, whole, high))
    count = 0
    for qi, (low, whole, high) in enumerate(spans):
        count = lax.fori_loop(low, whole, put(qi), count)
    count_ref[0] = jnp.maximum(count - 1, 0) // 2
    for qi, (low, whole, high) in enumerate(spans):
        count = lax.fori_loop(whole, high, put(qi), count)
    count_ref[1] = (count + 1) // 2
    for spare in range(2):
        plan_q[count + spare] = 0
        plan_k[count + spare] = total // bk - 1


def pipelined(plan_q, plan_k, count_ref, early, late, buffers):
    early(0, plan_q[0], plan_k[0], buffers[0], True)

    def turns(base, count, diagonal):
        for turn in range(2 * count):
            now = 2 * base + turn
            late(now, plan_q[now], plan_k[now], buffers[turn % 2])
            early(now + 1, plan_q[now + 1], plan_k[now + 1], buffers[1 - turn % 2], diagonal)

    def run(start, stop, diagonal):
        many = (stop - start) // LOOP_TURNS

        @pl.loop(0, many)
        def _(i):
            turns(start + LOOP_TURNS * i, LOOP_TURNS, diagonal)

        @pl.loop(start + LOOP_TURNS * many, stop)
        def _(i):
            turns(i, 1, diagonal)

    run(0, count_ref[0], False)
    run(count_ref[0], count_ref[1], True)


def forward_kernel(peers, heads, rows, bq, bk, kept, me_s, *refs):
    blocks = refs[:peers]
    if kept:
        p_list, top_list = refs[peers + 6:peers + 8]
        refs = refs[:peers + 6] + refs[peers + 8:]
    v_ref, qx_ref, kx_ref, kt_ref, rows_ref, log_ref = refs[peers:peers + 6]
    plan_q, plan_k, count_ref, own_q, own_k, own_count = refs[peers + 6:peers + 12]
    vt_ref, out_ref, doc_ref, sum_ref, s0, top0, s1, top1 = refs[peers + 12:]
    total = v_ref.shape[0]
    factor = HD ** (-0.5) * math.log2(math.e)
    me = me_s[0]
    for d, block in enumerate(blocks):
        place = me ^ d
        for part, ref in enumerate((qx_ref.at[:, :HD], kx_ref.at[:, :HD], v_ref)):
            ref[aligned(place, rows), :] = block[part * rows:(part + 1) * rows, :]
        docs = block[3 * rows:, :].astype(jnp.float32)
        for t in range(rows // HD):
            doc_ref[:, aligned(place * (rows // HD) + t, HD)] = docs[t:t + 1, :]
    docs = doc_ref[...]
    first = jnp.zeros(docs.shape, jnp.float32)
    for value in range(1, DOC_VALUES):
        before = jnp.sum((docs < value).astype(jnp.float32))
        first = jnp.where(docs >= value, before, first)
    first = first.astype(jnp.int32)
    back_q, back_k = block_sizes(total)[1]
    lows = [jnp.min(first[:, qi * back_q:(qi + 1) * back_q]) for qi in range(total // back_q)]
    group = (me // heads) * heads * rows
    own = None if heads == peers else (group, group + heads * rows)
    fill_plan(lows, total, back_q, back_k, own, plan_q, plan_k, count_ref)
    if kept:
        own_q, own_k, own_count = plan_q, plan_k, count_ref
    else:
        lows = [jnp.min(first[:, qi * bq:(qi + 1) * bq]) for qi in range(total // bq)]
        fill_plan(lows, total, bq, bk, None, own_q, own_k, own_count)
    same = lax.broadcasted_iota(jnp.int32, (HD, total), 0).astype(jnp.float32) == docs
    ones = jnp.where(same, 1.0, 0.0).astype(jnp.bfloat16).T
    kx_ref[:, HD:] = ones
    qx_ref[:, HD:] = ((1.0 - ones.astype(jnp.float32)) * NEG_LARGE).astype(jnp.bfloat16)
    kt_ref[...] = kx_ref[:, :HD].T
    vt_ref[:HD, :] = v_ref[...].T
    vt_ref[HD:, :] = jnp.ones((ONES_ROWS, total), jnp.bfloat16)
    out_ref[...] = jnp.zeros_like(out_ref)
    log_ref[...] = jnp.full_like(log_ref, NEG_LARGE)
    sum_ref[...] = jnp.zeros_like(sum_ref)

    def early(now, qi, ki, buffer, diagonal):
        s_ref, top_ref = buffer
        keys, queries = aligned(ki, bk), aligned(qi, bq)
        s = dot32(kx_ref[keys, :], qx_ref[queries, :], NT) * factor
        if diagonal:
            s = jnp.where(at_or_before(qi * bq, ki * bk, (bk, bq)), s, NEG_LARGE)
        s_ref[...] = s
        top_ref[...] = jnp.max(s, axis=0, keepdims=True)

    def late(now, qi, ki, buffer):
        s_ref, top_ref = buffer
        keys, queries = aligned(ki, bk), aligned(qi, bq)
        top = log_ref[:, queries]
        new_top = jnp.maximum(top, top_ref[...])
        fix = jnp.exp2(top - new_top)
        vt = vt_ref[:, keys]
        p = jnp.exp2(s_ref[...] - new_top)
        high = p.astype(jnp.bfloat16)
        sums = dot32(vt, high)
        if kept:
            p_list[now] = high
            top_list[now] = new_top
        else:
            sums = sums + dot32(vt, (p - high.astype(jnp.float32)).astype(jnp.bfloat16))
        out_ref[:, queries] = out_ref[:, queries] * fix + sums[:HD, :]
        sum_ref[:, queries] = sum_ref[:, queries] * fix + sums[HD:HD + 1, :]
        log_ref[:, queries] = new_top

    pipelined(own_q, own_k, own_count, early, late, ((s0, top0), (s1, top1)))
    total_p = sum_ref[...]
    rows_ref[...] = (out_ref[...] / total_p).T
    log_ref[...] = log_ref[...] + jnp.log2(total_p)


def backward_kernel(listed, heads, rows, bq, bk, kept, me_s, plan_q, plan_k, count_ref, v_ref,
                    qx_ref, kx_ref, kt_ref, rows_ref, log_ref, *refs):
    if kept:
        p_list, refs = refs[0], refs[1:]
    peers = len(listed)
    if kept:
        refs = refs[3:]
    blocks = refs[:peers]
    dq_acc, dk_acc, dv_acc, g_ref, dot_ref, p0, ds0, p1, ds1 = refs[peers:]
    scale = HD ** (-0.5)
    factor = scale * math.log2(math.e)
    me = me_s[0]
    for d, block in zip(listed, blocks):
        g_ref[aligned(me ^ d, rows), :] = block[...]
    ones = jnp.ones((ONES_ROWS, HD), jnp.bfloat16)
    for start in range(0, g_ref.shape[0], bq):
        part = slice(start, start + bq)
        left = g_ref[part, :].astype(jnp.float32) * rows_ref[part, :]
        dots = 0.0
        for _ in range(3):
            term = left.astype(jnp.bfloat16)
            left = left - term.astype(jnp.float32)
            dots = dots + dot32(ones, term, NT)
        dot_ref[:, part] = dots[:1, :]
    if not kept:
        for ref in (dq_acc, dk_acc, dv_acc):
            ref[...] = jnp.zeros_like(ref)

    def early(now, qi, ki, buffer, diagonal):
        p_ref, ds_ref = buffer
        queries = aligned(qi, bq)
        log_row, dot_row = log_ref[:, queries], dot_ref[:, queries]
        for strip in range(0, bk, STRIP):
            part = slice(strip, strip + STRIP)
            keys = aligned(ki * (bk // STRIP) + strip // STRIP, STRIP)
            if kept:
                p = p_list[now, part, :].astype(jnp.float32)
            else:
                p = jnp.exp2(dot32(kx_ref[keys, :], qx_ref[queries, :], NT) * factor - log_row)
                if diagonal:
                    p = jnp.where(at_or_before(qi * bq, ki * bk + strip, (STRIP, bq)), p, 0.0)
                p_ref[part, :] = p.astype(jnp.bfloat16)
            dp = dot32(v_ref[keys, :], g_ref[queries, :], NT)
            ds_ref[part, :] = (p * (dp - dot_row)).astype(jnp.bfloat16)

    def late(now, qi, ki, buffer):
        p_ref, ds_ref = buffer
        keys, queries = aligned(ki, bk), aligned(qi, bq)
        dv_acc[keys, :] += dot32(p_list[now] if kept else p_ref[...], g_ref[queries, :])
        dk_acc[keys, :] += dot32(ds_ref[...], qx_ref[queries, :HD])
        dq_acc[:, queries] += dot32(kt_ref[:, keys], ds_ref[...])

    pipelined(plan_q, plan_k, count_ref, early, late, ((p0, ds0), (p1, ds1)))


def prepare_kernel(bq, bk, plan_q, count_ref, log_ref, top_list, p_list, p_out, *totals):
    for total in totals:
        total[...] = jnp.zeros_like(total)

    @pl.loop(0, 2 * count_ref[1])
    def _(now):
        share = jnp.exp2(top_list[now] - log_ref[:, aligned(plan_q[now], bq)])
        for strip in range(0, bk, STRIP):
            part = slice(strip, strip + STRIP)
            p_out[now, part, :] = (p_list[now, part, :].astype(jnp.float32) * share).astype(jnp.bfloat16)


def finish_kernel(listed, rows, me_s, dq_ref, dk_ref, dv_ref, *results):
    scale = HD ** (-0.5)
    for d, result in zip(listed, results):
        own = aligned(me_s[0] ^ d, rows)
        result[:rows, :] = (scale * dq_ref[:, own]).astype(result.dtype).T
        result[rows:2 * rows, :] = (scale * dk_ref[own, :]).astype(result.dtype)
        result[2 * rows:, :] = dv_ref[own, :].astype(result.dtype)


def finish(me, listed, totals, rows):
    out_shape = [jax.ShapeDtypeStruct((3 * rows, HD), jnp.bfloat16)] * len(listed)
    results = pl.pallas_call(
        functools.partial(finish_kernel, listed, rows),
        in_specs=[SMEM_SPEC] + [VMEM_SPEC] * 3,
        out_specs=[VMEM_SPEC] * len(listed),
        out_shape=out_shape,
        compiler_params=params([*totals, *out_shape]),
    )(me, *totals)
    return dict(zip(listed, results))


def keeps_list(total, peers, heads):
    forward, backward = block_sizes(total)
    size = plan_size(total, *forward) * math.prod(forward) * 2
    return forward == backward and heads == peers and size <= LIST_BYTES


def attention_cost(total, products):
    return pl.CostEstimate(
        flops=products * total * total * HD // 2,
        bytes_accessed=16 * total * HD,
        transcendentals=total * total // 4,
    )


def attention_forward(me, blocks, rows, heads):
    peers = len(blocks)
    total = peers * rows
    (bq, bk), back = block_sizes(total)
    plan = [(plan_size(total, *back),)] * 2 + [(2,)]
    own_plan = [(plan_size(total, bq, bk),)] * 2 + [(2,)]
    vectors = [
        jax.ShapeDtypeStruct((total, HD), jnp.bfloat16),
        *[jax.ShapeDtypeStruct((total, 2 * HD), jnp.bfloat16)] * 2,
        jax.ShapeDtypeStruct((HD, total), jnp.bfloat16),
        jax.ShapeDtypeStruct((total, HD), jnp.float32),
        jax.ShapeDtypeStruct((1, total), jnp.float32),
    ]
    kept = keeps_list(total, peers, heads)
    if kept:
        vectors.append(jax.ShapeDtypeStruct((*own_plan[0], bk, bq), jnp.bfloat16))
        vectors.append(jax.ShapeDtypeStruct((*own_plan[0], 1, bq), jnp.float32))
    scratch = [
        pltpu.VMEM((HD + ONES_ROWS, total), jnp.bfloat16),
        pltpu.VMEM((HD, total), jnp.float32),
        pltpu.VMEM((1, total), jnp.float32),
        pltpu.VMEM((1, total), jnp.float32),
        *[pltpu.VMEM((bk, bq), jnp.float32), pltpu.VMEM((1, bq), jnp.float32)] * 2,
    ]
    return pl.pallas_call(
        functools.partial(forward_kernel, peers, heads, rows, bq, bk, kept),
        in_specs=[SMEM_SPEC] + [VMEM_SPEC] * peers,
        out_specs=[VMEM_SPEC] * len(vectors) + [SMEM_SPEC] * 3,
        out_shape=vectors + [jax.ShapeDtypeStruct(shape, jnp.int32) for shape in plan],
        scratch_shapes=[pltpu.SMEM(shape, jnp.int32) for shape in own_plan] + scratch,
        compiler_params=params([*blocks, *vectors], scratch),
        cost_estimate=attention_cost(total, 3),
    )(me, *blocks)


def total_shapes(total):
    shapes = [(HD, total), (total, HD), (total, HD)]
    return [jax.ShapeDtypeStruct(shape, jnp.float32) for shape in shapes]


def prepare(log_total, p_list, top_list, plan_q, count):
    bk, bq = p_list.shape[1:]
    out_shape = [jax.ShapeDtypeStruct(p_list.shape, p_list.dtype)] + total_shapes(log_total.shape[1])
    return pl.pallas_call(
        functools.partial(prepare_kernel, bq, bk),
        in_specs=[SMEM_SPEC] * 2 + [VMEM_SPEC] * 3,
        out_specs=[VMEM_SPEC] * len(out_shape),
        out_shape=out_shape,
        input_output_aliases={4: 0},
        compiler_params=params([log_total, top_list, *out_shape[1:]]),
    )(plan_q, count, log_total, top_list, p_list)


def attention_backward(me, heads, state, listed, blocks, ready=()):
    peers, rows = len(blocks), blocks[0].shape[0]
    total = peers * rows
    bq, bk = block_sizes(total)[1]
    kept = bool(ready)
    vectors, plan = [*state[:6], *ready], state[-3:]
    out_shape = total_shapes(total)
    scratch = [
        pltpu.VMEM((total, HD), jnp.bfloat16),
        pltpu.VMEM((1, total), jnp.float32),
        *[pltpu.VMEM((bk, bq), jnp.bfloat16)] * 4,
    ]
    return pl.pallas_call(
        functools.partial(backward_kernel, listed, heads, rows, bq, bk, kept),
        in_specs=[SMEM_SPEC] * 4 + [VMEM_SPEC] * (len(vectors) + peers),
        out_specs=[VMEM_SPEC] * 3,
        out_shape=out_shape,
        scratch_shapes=scratch,
        input_output_aliases={4 + 7 + i: i for i in range(3)} if kept else {},
        compiler_params=params([*vectors[:6], *blocks] if kept else [*vectors, *blocks, *out_shape], scratch),
        cost_estimate=attention_cost(total, 5),
    )(me, *plan, *vectors, *blocks)


def per_device(peers, groups, queries, keys_in, values, out_grad, out_weight, doc_ids):
    rows, width = queries.shape
    heads = width // HD
    me = lax.axis_index("seq")
    me_vector = me.reshape(1)

    def exchange(x, d):
        return x if d == 0 else lax.ppermute(x, "seq", [(i, i ^ d) for i in range(peers)])

    def pass_on(x):
        return lax.ppermute(x, "head", [(i, (i + 1) % groups) for i in range(groups)])

    order = [*range(2, peers, 2), *range(peers - 1, 0, -2)]

    far_first = sorted(range(peers), key=lambda d: (-bin(d >> 1).count("1"), d & 1, d))
    returning = [d for d in far_first if d < heads]

    def exchange_all(blocks, listed):
        return [exchange(blocks[d % heads], d) for d in listed]

    packed = list(pack_heads(me_vector, queries, keys_in, values, doc_ids))
    received = exchange_all(packed, range(peers))

    def share(step):
        return len(order) * step // (groups - 2)

    after = lax.optimization_barrier
    features, acc = out_grad, None
    weights = []
    for step in range(groups):
        block = lax.rem(lax.axis_index("head") + groups - step, groups)
        weights.append(lax.dynamic_slice_in_dim(out_weight, block * width, width, 1))
    for step in range(groups):
        last = step == groups - 1
        if not last:
            passed = pass_on(features)
        if step == groups - 2:
            received[0], features = after((received[0], features))
            state = list(attention_forward(me_vector, received, rows, heads))
            features, state[1] = after((features, state[1]))
        acc = project(me_vector, weights[step], features, acc, last)
        if not last:
            features = passed
            if step < groups - 2:
                batch = order[share(step):share(step + 1)]
                here = [received[d] for d in batch]
                features, acc, here, weights[2:] = after((features, acc, here, weights[2:]))
                for d, block in zip(batch, here):
                    received[d] = block
    grads = exchange_all(acc, far_first)

    ready = ()
    if len(state) > 9:
        p_list, grads[0] = after((state[6], grads[0]))
        ready = prepare(state[5], p_list, state[7], state[-3], state[-1])
    totals = attention_backward(me_vector, heads, state, far_first, grads, ready)

    far = [d for d in returning if bin(d >> 1).count("1") > 1]
    near = [d for d in returning if d not in far]
    results = {**(finish(me_vector, far, totals, rows) if far else {}), **finish(me_vector, near, totals, rows)}
    returned = {d: exchange(results[d], d) for d in returning}
    early, late = [*far, 0], [d for d in near if d > 0]
    partial = unpack_heads(me_vector, early, [returned[d] for d in early], rows, heads)
    return tuple(unpack_heads(me_vector, late, [returned[d] for d in late], rows, heads, partial))


def solution(mesh):
    in_specs = (
        P("seq", "head"),
        P("seq", "head"),
        P("seq", "head"),
        P("seq", "head"),
        P("head", None),
        P("seq"),
    )
    out_specs = (P("seq", "head"), P("seq", "head"), P("seq", "head"))
    return jax.shard_map(
        functools.partial(per_device, mesh.shape["seq"], mesh.shape["head"]),
        mesh=mesh, in_specs=in_specs, out_specs=out_specs, check_vma=False,
    )
```

```python
import functools
import math

import jax
import jax.numpy as jnp
from jax import lax
from jax.experimental import pallas as pl
from jax.experimental.pallas import tpu as pltpu
from jax.sharding import PartitionSpec as P

HD = 128
DOC_VALUES = 8
DOC_ROWS = 16
ONES_ROWS = 16
STRIP = 128
LOOP_TURNS = 4
NEG_LARGE = -1e30
VMEM_SPARE = 6 * 1024 * 1024
VMEM_MOST = 56 * 1024 * 1024
LIST_BYTES = 16 * 1024 * 1024

NN = (((1,), (0,)), ((), ()))
NT = (((1,), (1,)), ((), ()))
SMEM_SPEC = pl.BlockSpec(memory_space=pltpu.SMEM)
VMEM_SPEC = pl.BlockSpec(memory_space=pltpu.VMEM)
ANY_SPEC = pl.BlockSpec(memory_space=pl.ANY)


def dot32(a, b, dims=NN):
    return lax.dot_general(a, b, dims, preferred_element_type=jnp.float32)


def block_size(total, wanted):
    size = min(wanted, total)
    while total % size or size % 128:
        size -= 128
    return size


def aligned(index, size):
    return pl.ds(pl.multiple_of(index * size, size), size)


def params(arrays, scratch=()):
    total = sum(math.prod(a.shape) * jnp.dtype(a.dtype).itemsize for a in (*arrays, *scratch))
    return pltpu.CompilerParams(vmem_limit_bytes=total + VMEM_SPARE)


def pack_kernel(heads, rows, me_s, q_ref, k_ref, v_ref, doc_ref, *outs):
    own = lax.rem(me_s[0], heads)
    docs = doc_ref[...].astype(jnp.float32)
    docs = jnp.concatenate([docs, jnp.zeros((DOC_ROWS - docs.shape[0], HD), jnp.float32)], axis=0)
    docs = docs.astype(jnp.bfloat16)
    for d, out in enumerate(outs):
        columns = aligned(own ^ d, HD)
        for part, ref in enumerate((q_ref, k_ref, v_ref)):
            out[part * rows:(part + 1) * rows, :] = ref[:, columns]
        out[3 * rows:, :] = docs


def pack_heads(me, q, k, v, doc_ids):
    rows, width = q.shape
    heads = width // HD
    return pl.pallas_call(
        functools.partial(pack_kernel, heads, rows),
        in_specs=[SMEM_SPEC] + [VMEM_SPEC] * 4,
        out_specs=[VMEM_SPEC] * heads,
        out_shape=[jax.ShapeDtypeStruct((3 * rows + DOC_ROWS, HD), q.dtype)] * heads,
        compiler_params=pltpu.CompilerParams(vmem_limit_bytes=VMEM_MOST),
    )(me, q, k, v, doc_ids.reshape(rows // HD, HD))


def unpack_kernel(listed, heads, rows, me_s, *refs):
    outs, done = refs[-4:-1], refs[-1]
    own = lax.rem(me_s[0], heads)
    copies = []
    for place, (d, block) in enumerate(zip(listed, refs)):
        columns = aligned(own ^ d, HD)
        for part, out in enumerate(outs):
            source = block.at[pl.ds(part * rows, rows), :]
            copies.append(pltpu.make_async_copy(source, out.at[:, columns], done.at[place, part]))
            copies[-1].start()
    for copy in copies:
        copy.wait()


def unpack_heads(me, listed, blocks, rows, heads, partial=()):
    count = len(blocks)
    return pl.pallas_call(
        functools.partial(unpack_kernel, listed, heads, rows),
        in_specs=[SMEM_SPEC] + [VMEM_SPEC] * count + [ANY_SPEC] * len(partial),
        out_specs=[ANY_SPEC] * 3,
        out_shape=[jax.ShapeDtypeStruct((rows, heads * HD), blocks[0].dtype)] * 3,
        scratch_shapes=[pltpu.SemaphoreType.DMA((count, 3))],
        input_output_aliases={1 + count + i: i for i in range(len(partial))},
        compiler_params=params([*blocks]),
    )(me, *blocks, *partial)


def project_kernel(first, o_ref, w_ref, *refs):
    out_ref = refs[-1]
    for pair in range(w_ref.shape[0] // (2 * HD)):
        part = slice(pair * 2 * HD, (pair + 1) * 2 * HD)
        both = dot32(o_ref[...], w_ref[part, :], NT)
        out_ref[:, part] = both if first else refs[0][:, part] + both


def project_last_kernel(me_s, o_ref, w_ref, acc_ref, *outs):
    pairs = len(outs) // 2
    odd = lax.rem(me_s[0], 2) == 1
    for j in range(pairs):
        part = aligned(lax.rem(me_s[0] // 2, pairs) ^ j, 2 * HD)
        both = (acc_ref[:, part] + dot32(o_ref[...], w_ref[part, :], NT)).astype(jnp.bfloat16)
        outs[2 * j][...] = jnp.where(odd, both[:, HD:], both[:, :HD])
        outs[2 * j + 1][...] = jnp.where(odd, both[:, :HD], both[:, HD:])


def project(me, weight, features, acc, last):
    rows, width = features.shape
    columns = weight.shape[0]
    heads = columns // HD
    total = jax.ShapeDtypeStruct((rows, columns), jnp.float32)
    cost = pl.CostEstimate(
        flops=2 * rows * width * columns,
        bytes_accessed=2 * width * columns + 8 * rows * columns,
        transcendentals=0,
    )
    if last:
        return pl.pallas_call(
            project_last_kernel,
            in_specs=[SMEM_SPEC] + [VMEM_SPEC] * 3,
            out_specs=[VMEM_SPEC] * heads,
            out_shape=[jax.ShapeDtypeStruct((rows, HD), jnp.bfloat16)] * heads,
            compiler_params=params([features, weight, total, total]),
            cost_estimate=cost,
        )(me, features, weight, acc)
    operands = (features, weight) + (() if acc is None else (acc,))
    return pl.pallas_call(
        functools.partial(project_kernel, acc is None),
        in_specs=[VMEM_SPEC] * len(operands),
        out_specs=VMEM_SPEC,
        out_shape=total,
        compiler_params=params([features, weight, total, total]),
        cost_estimate=cost,
    )(*operands)


def at_or_before(q0, k0, shape):
    key = lax.broadcasted_iota(jnp.int32, shape, 0)
    return key <= q0 - k0 + lax.broadcasted_iota(jnp.int32, (1, shape[1]), 1)


def block_sizes(total):
    return (
        (block_size(total, 256), block_size(total, 256)),
        (block_size(total, 256), block_size(total, 256)),
    )


def plan_size(total, bq, bk):
    return sum(((q + 1) * bq + bk - 1) // bk for q in range(total // bq)) + 2


def fill_plan(lows, total, bq, bk, own, plan_q, plan_k, count_ref):
    def put(qi):
        def at(ki, count):
            plan_q[count] = qi
            plan_k[count] = ki
            return count + 1

        return at

    spans = []
    for qi, low in enumerate(lows):
        low, high = low // bk, ((qi + 1) * bq + bk - 1) // bk
        if own is not None:
            wanted = ((qi + 1) * bq > own[0]) & (qi * bq < own[1])
            low = jnp.where(wanted, low, jnp.maximum(low, own[0] // bk))
            high = jnp.where(wanted, high, jnp.minimum(high, (own[1] + bk - 1) // bk))
        whole = jnp.maximum(low, jnp.minimum(high, qi * bq // bk))
        spans.append((low, whole, high))
    count = 0
    for qi, (low, whole, high) in enumerate(spans):
        count = lax.fori_loop(low, whole, put(qi), count)
    count_ref[0] = jnp.maximum(count - 1, 0) // 2
    for qi, (low, whole, high) in enumerate(spans):
        count = lax.fori_loop(whole, high, put(qi), count)
    count_ref[1] = (count + 1) // 2
    for spare in range(2):
        plan_q[count + spare] = 0
        plan_k[count + spare] = total // bk - 1


def pipelined(plan_q, plan_k, count_ref, early, late, buffers, diagonals=True):
    early(0, plan_q[0], plan_k[0], buffers[0], True)

    def turns(base, count, diagonal):
        for turn in range(2 * count):
            now = 2 * base + turn
            late(now, plan_q[now], plan_k[now], buffers[turn % 2])
            early(now + 1, plan_q[now + 1], plan_k[now + 1], buffers[1 - turn % 2], diagonal)

    def run(start, stop, diagonal):
        many = (stop - start) // LOOP_TURNS

        @pl.loop(0, many)
        def _(i):
            turns(start + LOOP_TURNS * i, LOOP_TURNS, diagonal)

        @pl.loop(start + LOOP_TURNS * many, stop)
        def _(i):
            turns(i, 1, diagonal)

    if diagonals:
        run(0, count_ref[0], False)
        run(count_ref[0], count_ref[1], True)
    else:
        run(0, count_ref[1], False)


def forward_kernel(peers, heads, rows, bq, bk, kept, me_s, *refs):
    blocks = refs[:peers]
    if kept:
        p_list, top_list = refs[peers + 6:peers + 8]
        refs = refs[:peers + 6] + refs[peers + 8:]
    v_ref, qx_ref, kx_ref, kt_ref, rows_ref, log_ref = refs[peers:peers + 6]
    plan_q, plan_k, count_ref, own_q, own_k, own_count = refs[peers + 6:peers + 12]
    vt_ref, out_ref, doc_ref, sum_ref, s0, top0, s1, top1 = refs[peers + 12:]
    total = v_ref.shape[0]
    factor = HD ** (-0.5) * math.log2(math.e)
    me = me_s[0]
    for d, block in enumerate(blocks):
        place = me ^ d
        for part, ref in enumerate((qx_ref.at[:, :HD], kx_ref.at[:, :HD], v_ref)):
            ref[aligned(place, rows), :] = block[part * rows:(part + 1) * rows, :]
        docs = block[3 * rows:, :].astype(jnp.float32)
        for t in range(rows // HD):
            doc_ref[:, aligned(place * (rows // HD) + t, HD)] = docs[t:t + 1, :]
    docs = doc_ref[...]
    first = jnp.zeros(docs.shape, jnp.float32)
    for value in range(1, DOC_VALUES):
        before = jnp.sum((docs < value).astype(jnp.float32))
        first = jnp.where(docs >= value, before, first)
    first = first.astype(jnp.int32)
    back_q, back_k = block_sizes(total)[1]
    lows = [jnp.min(first[:, qi * back_q:(qi + 1) * back_q]) for qi in range(total // back_q)]
    group = (me // heads) * heads * rows
    own = None if heads == peers else (group, group + heads * rows)
    fill_plan(lows, total, back_q, back_k, own, plan_q, plan_k, count_ref)
    if kept:
        own_q, own_k, own_count = plan_q, plan_k, count_ref
    else:
        lows = [jnp.min(first[:, qi * bq:(qi + 1) * bq]) for qi in range(total // bq)]
        fill_plan(lows, total, bq, bk, None, own_q, own_k, own_count)
    same = lax.broadcasted_iota(jnp.int32, (HD, total), 0).astype(jnp.float32) == docs
    ones = jnp.where(same, 1.0, 0.0).astype(jnp.bfloat16).T
    kx_ref[:, HD:] = ones
    qx_ref[:, HD:] = ((1.0 - ones.astype(jnp.float32)) * NEG_LARGE).astype(jnp.bfloat16)
    kt_ref[...] = kx_ref[:, :HD].T
    vt_ref[:HD, :] = v_ref[...].T
    vt_ref[HD:, :] = jnp.ones((ONES_ROWS, total), jnp.bfloat16)
    out_ref[...] = jnp.zeros_like(out_ref)
    log_ref[...] = jnp.full_like(log_ref, NEG_LARGE)
    sum_ref[...] = jnp.zeros_like(sum_ref)

    def early(now, qi, ki, buffer, diagonal):
        s_ref, top_ref = buffer
        keys, queries = aligned(ki, bk), aligned(qi, bq)
        s = dot32(kx_ref[keys, :], qx_ref[queries, :], NT) * factor
        if diagonal:
            s = jnp.where(at_or_before(qi * bq, ki * bk, (bk, bq)), s, NEG_LARGE)
        s_ref[...] = s
        top_ref[...] = jnp.max(s, axis=0, keepdims=True)

    def late(now, qi, ki, buffer):
        s_ref, top_ref = buffer
        keys, queries = aligned(ki, bk), aligned(qi, bq)
        top = log_ref[:, queries]
        new_top = jnp.maximum(top, top_ref[...])
        fix = jnp.exp2(top - new_top)
        vt = vt_ref[:, keys]
        p = jnp.exp2(s_ref[...] - new_top)
        high = p.astype(jnp.bfloat16)
        sums = dot32(vt, high)
        if kept:
            p_list[now] = high
            top_list[now] = new_top
        else:
            sums = sums + dot32(vt, (p - high.astype(jnp.float32)).astype(jnp.bfloat16))
        out_ref[:, queries] = out_ref[:, queries] * fix + sums[:HD, :]
        sum_ref[:, queries] = sum_ref[:, queries] * fix + sums[HD:HD + 1, :]
        log_ref[:, queries] = new_top

    pipelined(own_q, own_k, own_count, early, late, ((s0, top0), (s1, top1)))
    total_p = sum_ref[...]
    rows_ref[...] = (out_ref[...] / total_p).T
    log_ref[...] = log_ref[...] + jnp.log2(total_p)


def backward_kernel(listed, heads, rows, bq, bk, kept, me_s, plan_q, plan_k, count_ref, v_ref,
                    qx_ref, kx_ref, kt_ref, rows_ref, log_ref, *refs):
    if kept:
        p_list, refs = refs[0], refs[1:]
    peers = len(listed)
    if kept:
        refs = refs[3:]
    blocks = refs[:peers]
    dq_acc, dk_acc, dv_acc, g_ref, dot_ref, p0, ds0, p1, ds1 = refs[peers:]
    scale = HD ** (-0.5)
    factor = scale * math.log2(math.e)
    me = me_s[0]
    for d, block in zip(listed, blocks):
        g_ref[aligned(me ^ d, rows), :] = block[...]
    ones = jnp.ones((ONES_ROWS, HD), jnp.bfloat16)
    for start in range(0, g_ref.shape[0], bq):
        part = slice(start, start + bq)
        left = g_ref[part, :].astype(jnp.float32) * rows_ref[part, :]
        dots = 0.0
        for _ in range(3):
            term = left.astype(jnp.bfloat16)
            left = left - term.astype(jnp.float32)
            dots = dots + dot32(ones, term, NT)
        dot_ref[:, part] = dots[:1, :]
    if not kept:
        for ref in (dq_acc, dk_acc, dv_acc):
            ref[...] = jnp.zeros_like(ref)

    def early(now, qi, ki, buffer, diagonal):
        p_ref, ds_ref = buffer
        queries = aligned(qi, bq)
        log_row, dot_row = log_ref[:, queries], dot_ref[:, queries]
        for strip in range(0, bk, STRIP):
            part = slice(strip, strip + STRIP)
            keys = aligned(ki * (bk // STRIP) + strip // STRIP, STRIP)
            if kept:
                p = p_list[now, part, :].astype(jnp.float32)
            else:
                p = jnp.exp2(dot32(kx_ref[keys, :], qx_ref[queries, :], NT) * factor - log_row)
                if diagonal:
                    p = jnp.where(at_or_before(qi * bq, ki * bk + strip, (STRIP, bq)), p, 0.0)
                p_ref[part, :] = p.astype(jnp.bfloat16)
            dp = dot32(v_ref[keys, :], g_ref[queries, :], NT)
            ds_ref[part, :] = (p * (dp - dot_row)).astype(jnp.bfloat16)

    def late(now, qi, ki, buffer):
        p_ref, ds_ref = buffer
        keys, queries = aligned(ki, bk), aligned(qi, bq)
        dv_acc[keys, :] += dot32(p_list[now] if kept else p_ref[...], g_ref[queries, :])
        dk_acc[keys, :] += dot32(ds_ref[...], qx_ref[queries, :HD])
        dq_acc[:, queries] += dot32(kt_ref[:, keys], ds_ref[...])

    pipelined(plan_q, plan_k, count_ref, early, late, ((p0, ds0), (p1, ds1)), diagonals=not kept)


def prepare_kernel(bq, bk, plan_q, count_ref, log_ref, top_list, p_list, p_out, *totals):
    for total in totals:
        total[...] = jnp.zeros_like(total)

    @pl.loop(0, 2 * count_ref[1])
    def _(now):
        share = jnp.exp2(top_list[now] - log_ref[:, aligned(plan_q[now], bq)])
        for strip in range(0, bk, STRIP):
            part = slice(strip, strip + STRIP)
            p_out[now, part, :] = (p_list[now, part, :].astype(jnp.float32) * share).astype(jnp.bfloat16)


def finish_kernel(listed, rows, me_s, dq_ref, dk_ref, dv_ref, *results):
    scale = HD ** (-0.5)
    for d, result in zip(listed, results):
        own = aligned(me_s[0] ^ d, rows)
        result[:rows, :] = (scale * dq_ref[:, own]).astype(result.dtype).T
        result[rows:2 * rows, :] = (scale * dk_ref[own, :]).astype(result.dtype)
        result[2 * rows:, :] = dv_ref[own, :].astype(result.dtype)


def finish(me, listed, totals, rows):
    out_shape = [jax.ShapeDtypeStruct((3 * rows, HD), jnp.bfloat16)] * len(listed)
    results = pl.pallas_call(
        functools.partial(finish_kernel, listed, rows),
        in_specs=[SMEM_SPEC] + [VMEM_SPEC] * 3,
        out_specs=[VMEM_SPEC] * len(listed),
        out_shape=out_shape,
        compiler_params=params([*totals, *out_shape]),
    )(me, *totals)
    return dict(zip(listed, results))


def keeps_list(total, peers, heads):
    forward, backward = block_sizes(total)
    size = plan_size(total, *forward) * math.prod(forward) * 2
    return forward == backward and heads == peers and size <= LIST_BYTES


def attention_cost(total, products):
    return pl.CostEstimate(
        flops=products * total * total * HD // 2,
        bytes_accessed=16 * total * HD,
        transcendentals=total * total // 4,
    )


def attention_forward(me, blocks, rows, heads):
    peers = len(blocks)
    total = peers * rows
    (bq, bk), back = block_sizes(total)
    plan = [(plan_size(total, *back),)] * 2 + [(2,)]
    own_plan = [(plan_size(total, bq, bk),)] * 2 + [(2,)]
    vectors = [
        jax.ShapeDtypeStruct((total, HD), jnp.bfloat16),
        *[jax.ShapeDtypeStruct((total, 2 * HD), jnp.bfloat16)] * 2,
        jax.ShapeDtypeStruct((HD, total), jnp.bfloat16),
        jax.ShapeDtypeStruct((total, HD), jnp.float32),
        jax.ShapeDtypeStruct((1, total), jnp.float32),
    ]
    kept = keeps_list(total, peers, heads)
    if kept:
        vectors.append(jax.ShapeDtypeStruct((*own_plan[0], bk, bq), jnp.bfloat16))
        vectors.append(jax.ShapeDtypeStruct((*own_plan[0], 1, bq), jnp.float32))
    scratch = [
        pltpu.VMEM((HD + ONES_ROWS, total), jnp.bfloat16),
        pltpu.VMEM((HD, total), jnp.float32),
        pltpu.VMEM((1, total), jnp.float32),
        pltpu.VMEM((1, total), jnp.float32),
        *[pltpu.VMEM((bk, bq), jnp.float32), pltpu.VMEM((1, bq), jnp.float32)] * 2,
    ]
    return pl.pallas_call(
        functools.partial(forward_kernel, peers, heads, rows, bq, bk, kept),
        in_specs=[SMEM_SPEC] + [VMEM_SPEC] * peers,
        out_specs=[VMEM_SPEC] * len(vectors) + [SMEM_SPEC] * 3,
        out_shape=vectors + [jax.ShapeDtypeStruct(shape, jnp.int32) for shape in plan],
        scratch_shapes=[pltpu.SMEM(shape, jnp.int32) for shape in own_plan] + scratch,
        compiler_params=params([*blocks, *vectors], scratch),
        cost_estimate=attention_cost(total, 3),
    )(me, *blocks)


def total_shapes(total):
    shapes = [(HD, total), (total, HD), (total, HD)]
    return [jax.ShapeDtypeStruct(shape, jnp.float32) for shape in shapes]


def prepare(log_total, p_list, top_list, plan_q, count):
    bk, bq = p_list.shape[1:]
    out_shape = [jax.ShapeDtypeStruct(p_list.shape, p_list.dtype)] + total_shapes(log_total.shape[1])
    return pl.pallas_call(
        functools.partial(prepare_kernel, bq, bk),
        in_specs=[SMEM_SPEC] * 2 + [VMEM_SPEC] * 3,
        out_specs=[VMEM_SPEC] * len(out_shape),
        out_shape=out_shape,
        input_output_aliases={4: 0},
        compiler_params=params([log_total, top_list, *out_shape[1:]]),
    )(plan_q, count, log_total, top_list, p_list)


def attention_backward(me, heads, state, listed, blocks, ready=()):
    peers, rows = len(blocks), blocks[0].shape[0]
    total = peers * rows
    bq, bk = block_sizes(total)[1]
    kept = bool(ready)
    vectors, plan = [*state[:6], *ready], state[-3:]
    out_shape = total_shapes(total)
    scratch = [
        pltpu.VMEM((total, HD), jnp.bfloat16),
        pltpu.VMEM((1, total), jnp.float32),
        *[pltpu.VMEM((bk, bq), jnp.bfloat16)] * 4,
    ]
    return pl.pallas_call(
        functools.partial(backward_kernel, listed, heads, rows, bq, bk, kept),
        in_specs=[SMEM_SPEC] * 4 + [VMEM_SPEC] * (len(vectors) + peers),
        out_specs=[VMEM_SPEC] * 3,
        out_shape=out_shape,
        scratch_shapes=scratch,
        input_output_aliases={4 + 7 + i: i for i in range(3)} if kept else {},
        compiler_params=params([*vectors[:6], *blocks] if kept else [*vectors, *blocks, *out_shape], scratch),
        cost_estimate=attention_cost(total, 5),
    )(me, *plan, *vectors, *blocks)


def per_device(peers, groups, queries, keys_in, values, out_grad, out_weight, doc_ids):
    rows, width = queries.shape
    heads = width // HD
    me = lax.axis_index("seq")
    me_vector = me.reshape(1)

    def exchange(x, d):
        return x if d == 0 else lax.ppermute(x, "seq", [(i, i ^ d) for i in range(peers)])

    def pass_on(x):
        return lax.ppermute(x, "head", [(i, (i + 1) % groups) for i in range(groups)])

    order = [*range(2, peers, 2), *range(peers - 1, 0, -2)]

    far_first = sorted(range(peers), key=lambda d: (-bin(d >> 1).count("1"), d & 1, d))
    returning = [d for d in far_first if d < heads]

    def exchange_all(blocks, listed):
        return [exchange(blocks[d % heads], d) for d in listed]

    packed = list(pack_heads(me_vector, queries, keys_in, values, doc_ids))
    received = exchange_all(packed, range(peers))

    def share(step):
        return len(order) * step // (groups - 2)

    after = lax.optimization_barrier
    features, acc = out_grad, None
    weights = []
    for step in range(groups):
        block = lax.rem(lax.axis_index("head") + groups - step, groups)
        weights.append(lax.dynamic_slice_in_dim(out_weight, block * width, width, 1))
    for step in range(groups):
        last = step == groups - 1
        if not last:
            passed = pass_on(features)
        if step == groups - 2:
            received[0], features = after((received[0], features))
            state = list(attention_forward(me_vector, received, rows, heads))
            features, state[1] = after((features, state[1]))
        acc = project(me_vector, weights[step], features, acc, last)
        if not last:
            features = passed
            if step < groups - 2:
                batch = order[share(step):share(step + 1)]
                here = [received[d] for d in batch]
                features, acc, here, weights[2:] = after((features, acc, here, weights[2:]))
                for d, block in zip(batch, here):
                    received[d] = block
    grads = exchange_all(acc, far_first)

    ready = ()
    if len(state) > 9:
        p_list, grads[0] = after((state[6], grads[0]))
        ready = prepare(state[5], p_list, state[7], state[-3], state[-1])
    totals = attention_backward(me_vector, heads, state, far_first, grads, ready)

    far = [d for d in returning if bin(d >> 1).count("1") > 1]
    near = [d for d in returning if d not in far]
    results = {**(finish(me_vector, far, totals, rows) if far else {}), **finish(me_vector, near, totals, rows)}
    returned = {d: exchange(results[d], d) for d in returning}
    early, late = [*far, 0], [d for d in near if d > 0]
    partial = unpack_heads(me_vector, early, [returned[d] for d in early], rows, heads)
    return tuple(unpack_heads(me_vector, late, [returned[d] for d in late], rows, heads, partial))


def solution(mesh):
    in_specs = (
        P("seq", "head"),
        P("seq", "head"),
        P("seq", "head"),
        P("seq", "head"),
        P("head", None),
        P("seq"),
    )
    out_specs = (P("seq", "head"), P("seq", "head"), P("seq", "head"))
    return jax.shard_map(
        functools.partial(per_device, mesh.shape["seq"], mesh.shape["head"]),
        mesh=mesh, in_specs=in_specs, out_specs=out_specs, check_vma=False,
    )
```

```python
import functools
import math

import jax
import jax.numpy as jnp
from jax import lax
from jax.experimental import pallas as pl
from jax.experimental.pallas import tpu as pltpu
from jax.sharding import PartitionSpec as P

HD = 128
DOC_VALUES = 8
DOC_ROWS = 16
ONES_ROWS = 16
STRIP = 128
LOOP_TURNS = 6
NEG_LARGE = -1e30
VMEM_SPARE = 6 * 1024 * 1024
VMEM_MOST = 56 * 1024 * 1024
LIST_BYTES = 16 * 1024 * 1024

NN = (((1,), (0,)), ((), ()))
NT = (((1,), (1,)), ((), ()))
SMEM_SPEC = pl.BlockSpec(memory_space=pltpu.SMEM)
VMEM_SPEC = pl.BlockSpec(memory_space=pltpu.VMEM)
ANY_SPEC = pl.BlockSpec(memory_space=pl.ANY)


def dot32(a, b, dims=NN):
    return lax.dot_general(a, b, dims, preferred_element_type=jnp.float32)


def block_size(total, wanted):
    size = min(wanted, total)
    while total % size or size % 128:
        size -= 128
    return size


def aligned(index, size):
    return pl.ds(pl.multiple_of(index * size, size), size)


def params(arrays, scratch=()):
    total = sum(math.prod(a.shape) * jnp.dtype(a.dtype).itemsize for a in (*arrays, *scratch))
    return pltpu.CompilerParams(vmem_limit_bytes=total + VMEM_SPARE)


def pack_kernel(heads, rows, me_s, q_ref, k_ref, v_ref, doc_ref, *outs):
    own = lax.rem(me_s[0], heads)
    docs = doc_ref[...].astype(jnp.float32)
    docs = jnp.concatenate([docs, jnp.zeros((DOC_ROWS - docs.shape[0], HD), jnp.float32)], axis=0)
    docs = docs.astype(jnp.bfloat16)
    for d, out in enumerate(outs):
        columns = aligned(own ^ d, HD)
        for part, ref in enumerate((q_ref, k_ref, v_ref)):
            out[part * rows:(part + 1) * rows, :] = ref[:, columns]
        out[3 * rows:, :] = docs


def pack_heads(me, q, k, v, doc_ids):
    rows, width = q.shape
    heads = width // HD
    return pl.pallas_call(
        functools.partial(pack_kernel, heads, rows),
        in_specs=[SMEM_SPEC] + [VMEM_SPEC] * 4,
        out_specs=[VMEM_SPEC] * heads,
        out_shape=[jax.ShapeDtypeStruct((3 * rows + DOC_ROWS, HD), q.dtype)] * heads,
        compiler_params=pltpu.CompilerParams(vmem_limit_bytes=VMEM_MOST),
    )(me, q, k, v, doc_ids.reshape(rows // HD, HD))


def unpack_kernel(listed, heads, rows, me_s, *refs):
    outs, done = refs[-4:-1], refs[-1]
    own = lax.rem(me_s[0], heads)
    copies = []
    for place, (d, block) in enumerate(zip(listed, refs)):
        columns = aligned(own ^ d, HD)
        for part, out in enumerate(outs):
            source = block.at[pl.ds(part * rows, rows), :]
            copies.append(pltpu.make_async_copy(source, out.at[:, columns], done.at[place, part]))
            copies[-1].start()
    for copy in copies:
        copy.wait()


def unpack_heads(me, listed, blocks, rows, heads, partial=()):
    count = len(blocks)
    return pl.pallas_call(
        functools.partial(unpack_kernel, listed, heads, rows),
        in_specs=[SMEM_SPEC] + [VMEM_SPEC] * count + [ANY_SPEC] * len(partial),
        out_specs=[ANY_SPEC] * 3,
        out_shape=[jax.ShapeDtypeStruct((rows, heads * HD), blocks[0].dtype)] * 3,
        scratch_shapes=[pltpu.SemaphoreType.DMA((count, 3))],
        input_output_aliases={1 + count + i: i for i in range(len(partial))},
        compiler_params=params([*blocks]),
    )(me, *blocks, *partial)


def project_kernel(first, o_ref, w_ref, *refs):
    out_ref = refs[-1]
    for pair in range(w_ref.shape[0] // (2 * HD)):
        part = slice(pair * 2 * HD, (pair + 1) * 2 * HD)
        both = dot32(o_ref[...], w_ref[part, :], NT)
        out_ref[:, part] = both if first else refs[0][:, part] + both


def project_last_kernel(me_s, o_ref, w_ref, acc_ref, *outs):
    pairs = len(outs) // 2
    odd = lax.rem(me_s[0], 2) == 1
    for j in range(pairs):
        part = aligned(lax.rem(me_s[0] // 2, pairs) ^ j, 2 * HD)
        both = (acc_ref[:, part] + dot32(o_ref[...], w_ref[part, :], NT)).astype(jnp.bfloat16)
        outs[2 * j][...] = jnp.where(odd, both[:, HD:], both[:, :HD])
        outs[2 * j + 1][...] = jnp.where(odd, both[:, :HD], both[:, HD:])


def project(me, weight, features, acc, last):
    rows, width = features.shape
    columns = weight.shape[0]
    heads = columns // HD
    total = jax.ShapeDtypeStruct((rows, columns), jnp.float32)
    cost = pl.CostEstimate(
        flops=2 * rows * width * columns,
        bytes_accessed=2 * width * columns + 8 * rows * columns,
        transcendentals=0,
    )
    if last:
        return pl.pallas_call(
            project_last_kernel,
            in_specs=[SMEM_SPEC] + [VMEM_SPEC] * 3,
            out_specs=[VMEM_SPEC] * heads,
            out_shape=[jax.ShapeDtypeStruct((rows, HD), jnp.bfloat16)] * heads,
            compiler_params=params([features, weight, total, total]),
            cost_estimate=cost,
        )(me, features, weight, acc)
    operands = (features, weight) + (() if acc is None else (acc,))
    return pl.pallas_call(
        functools.partial(project_kernel, acc is None),
        in_specs=[VMEM_SPEC] * len(operands),
        out_specs=VMEM_SPEC,
        out_shape=total,
        compiler_params=params([features, weight, total, total]),
        cost_estimate=cost,
    )(*operands)


def at_or_before(q0, k0, shape):
    key = lax.broadcasted_iota(jnp.int32, shape, 0)
    return key <= q0 - k0 + lax.broadcasted_iota(jnp.int32, (1, shape[1]), 1)


def block_sizes(total):
    return (
        (block_size(total, 256), block_size(total, 256)),
        (block_size(total, 256), block_size(total, 256)),
    )


def plan_size(total, bq, bk):
    return sum(((q + 1) * bq + bk - 1) // bk for q in range(total // bq)) + 2


def fill_plan(lows, total, bq, bk, own, plan_q, plan_k, count_ref):
    def put(qi):
        def at(ki, count):
            plan_q[count] = qi
            plan_k[count] = ki
            return count + 1

        return at

    spans = []
    for qi, low in enumerate(lows):
        low, high = low // bk, ((qi + 1) * bq + bk - 1) // bk
        if own is not None:
            wanted = ((qi + 1) * bq > own[0]) & (qi * bq < own[1])
            low = jnp.where(wanted, low, jnp.maximum(low, own[0] // bk))
            high = jnp.where(wanted, high, jnp.minimum(high, (own[1] + bk - 1) // bk))
        whole = jnp.maximum(low, jnp.minimum(high, qi * bq // bk))
        spans.append((low, whole, high))
    count = 0
    for qi, (low, whole, high) in enumerate(spans):
        count = lax.fori_loop(low, whole, put(qi), count)
    count_ref[0] = jnp.maximum(count - 1, 0) // 2
    for qi, (low, whole, high) in enumerate(spans):
        count = lax.fori_loop(whole, high, put(qi), count)
    count_ref[1] = (count + 1) // 2
    for spare in range(2):
        plan_q[count + spare] = 0
        plan_k[count + spare] = total // bk - 1


def pipelined(plan_q, plan_k, count_ref, early, late, buffers, diagonals=True):
    early(0, plan_q[0], plan_k[0], buffers[0], True)

    def turns(base, count, diagonal):
        for turn in range(2 * count):
            now = 2 * base + turn
            late(now, plan_q[now], plan_k[now], buffers[turn % 2])
            early(now + 1, plan_q[now + 1], plan_k[now + 1], buffers[1 - turn % 2], diagonal)

    def run(start, stop, diagonal):
        many = (stop - start) // LOOP_TURNS

        @pl.loop(0, many)
        def _(i):
            turns(start + LOOP_TURNS * i, LOOP_TURNS, diagonal)

        @pl.loop(start + LOOP_TURNS * many, stop)
        def _(i):
            turns(i, 1, diagonal)

    if diagonals:
        run(0, count_ref[0], False)
        run(count_ref[0], count_ref[1], True)
    else:
        run(0, count_ref[1], False)


def forward_kernel(peers, heads, rows, bq, bk, kept, me_s, *refs):
    blocks = refs[:peers]
    if kept:
        p_list, top_list = refs[peers + 6:peers + 8]
        refs = refs[:peers + 6] + refs[peers + 8:]
    v_ref, qx_ref, kx_ref, kt_ref, rows_ref, log_ref = refs[peers:peers + 6]
    plan_q, plan_k, count_ref, own_q, own_k, own_count = refs[peers + 6:peers + 12]
    vt_ref, out_ref, doc_ref, sum_ref, s0, top0, s1, top1 = refs[peers + 12:]
    total = v_ref.shape[0]
    factor = HD ** (-0.5) * math.log2(math.e)
    me = me_s[0]
    for d, block in enumerate(blocks):
        place = me ^ d
        for part, ref in enumerate((qx_ref.at[:, :HD], kx_ref.at[:, :HD], v_ref)):
            ref[aligned(place, rows), :] = block[part * rows:(part + 1) * rows, :]
        docs = block[3 * rows:, :].astype(jnp.float32)
        for t in range(rows // HD):
            doc_ref[:, aligned(place * (rows // HD) + t, HD)] = docs[t:t + 1, :]
    docs = doc_ref[...]
    first = jnp.zeros(docs.shape, jnp.float32)
    for value in range(1, DOC_VALUES):
        before = jnp.sum((docs < value).astype(jnp.float32))
        first = jnp.where(docs >= value, before, first)
    first = first.astype(jnp.int32)
    back_q, back_k = block_sizes(total)[1]
    lows = [jnp.min(first[:, qi * back_q:(qi + 1) * back_q]) for qi in range(total // back_q)]
    group = (me // heads) * heads * rows
    own = None if heads == peers else (group, group + heads * rows)
    fill_plan(lows, total, back_q, back_k, own, plan_q, plan_k, count_ref)
    if kept:
        own_q, own_k, own_count = plan_q, plan_k, count_ref
    else:
        lows = [jnp.min(first[:, qi * bq:(qi + 1) * bq]) for qi in range(total // bq)]
        fill_plan(lows, total, bq, bk, None, own_q, own_k, own_count)
    same = lax.broadcasted_iota(jnp.int32, (HD, total), 0).astype(jnp.float32) == docs
    ones = jnp.where(same, 1.0, 0.0).astype(jnp.bfloat16).T
    kx_ref[:, HD:] = ones
    qx_ref[:, HD:] = ((1.0 - ones.astype(jnp.float32)) * NEG_LARGE).astype(jnp.bfloat16)
    kt_ref[...] = kx_ref[:, :HD].T
    vt_ref[:HD, :] = v_ref[...].T
    vt_ref[HD:, :] = jnp.ones((ONES_ROWS, total), jnp.bfloat16)
    out_ref[...] = jnp.zeros_like(out_ref)
    log_ref[...] = jnp.full_like(log_ref, NEG_LARGE)
    sum_ref[...] = jnp.zeros_like(sum_ref)

    def early(now, qi, ki, buffer, diagonal):
        s_ref, top_ref = buffer
        keys, queries = aligned(ki, bk), aligned(qi, bq)
        s = dot32(kx_ref[keys, :], qx_ref[queries, :], NT) * factor
        if diagonal:
            s = jnp.where(at_or_before(qi * bq, ki * bk, (bk, bq)), s, NEG_LARGE)
        s_ref[...] = s
        top_ref[...] = jnp.max(s, axis=0, keepdims=True)

    def late(now, qi, ki, buffer):
        s_ref, top_ref = buffer
        keys, queries = aligned(ki, bk), aligned(qi, bq)
        top = log_ref[:, queries]
        new_top = jnp.maximum(top, top_ref[...])
        fix = jnp.exp2(top - new_top)
        vt = vt_ref[:, keys]
        p = jnp.exp2(s_ref[...] - new_top)
        high = p.astype(jnp.bfloat16)
        sums = dot32(vt, high)
        if kept:
            p_list[now] = high
            top_list[now] = new_top
        else:
            sums = sums + dot32(vt, (p - high.astype(jnp.float32)).astype(jnp.bfloat16))
        out_ref[:, queries] = out_ref[:, queries] * fix + sums[:HD, :]
        sum_ref[:, queries] = sum_ref[:, queries] * fix + sums[HD:HD + 1, :]
        log_ref[:, queries] = new_top

    pipelined(own_q, own_k, own_count, early, late, ((s0, top0), (s1, top1)))
    total_p = sum_ref[...]
    rows_ref[...] = (out_ref[...] / total_p).T
    log_ref[...] = log_ref[...] + jnp.log2(total_p)


def backward_kernel(listed, heads, rows, bq, bk, kept, me_s, plan_q, plan_k, count_ref, v_ref,
                    qx_ref, kx_ref, kt_ref, rows_ref, log_ref, *refs):
    if kept:
        p_list, refs = refs[0], refs[1:]
    peers = len(listed)
    if kept:
        refs = refs[3:]
    blocks = refs[:peers]
    dq_acc, dk_acc, dv_acc, g_ref, dot_ref, p0, ds0, p1, ds1 = refs[peers:]
    scale = HD ** (-0.5)
    factor = scale * math.log2(math.e)
    me = me_s[0]
    for d, block in zip(listed, blocks):
        g_ref[aligned(me ^ d, rows), :] = block[...]
    ones = jnp.ones((ONES_ROWS, HD), jnp.bfloat16)
    for start in range(0, g_ref.shape[0], bq):
        part = slice(start, start + bq)
        left = g_ref[part, :].astype(jnp.float32) * rows_ref[part, :]
        dots = 0.0
        for _ in range(3):
            term = left.astype(jnp.bfloat16)
            left = left - term.astype(jnp.float32)
            dots = dots + dot32(ones, term, NT)
        dot_ref[:, part] = dots[:1, :]
    if not kept:
        for ref in (dq_acc, dk_acc, dv_acc):
            ref[...] = jnp.zeros_like(ref)

    def early(now, qi, ki, buffer, diagonal):
        p_ref, ds_ref = buffer
        queries = aligned(qi, bq)
        log_row, dot_row = log_ref[:, queries], dot_ref[:, queries]
        for strip in range(0, bk, STRIP):
            part = slice(strip, strip + STRIP)
            keys = aligned(ki * (bk // STRIP) + strip // STRIP, STRIP)
            if kept:
                p = p_list[now, part, :].astype(jnp.float32)
            else:
                p = jnp.exp2(dot32(kx_ref[keys, :], qx_ref[queries, :], NT) * factor - log_row)
                if diagonal:
                    p = jnp.where(at_or_before(qi * bq, ki * bk + strip, (STRIP, bq)), p, 0.0)
                p_ref[part, :] = p.astype(jnp.bfloat16)
            dp = dot32(v_ref[keys, :], g_ref[queries, :], NT)
            ds_ref[part, :] = (p * (dp - dot_row)).astype(jnp.bfloat16)

    def late(now, qi, ki, buffer):
        p_ref, ds_ref = buffer
        keys, queries = aligned(ki, bk), aligned(qi, bq)
        dv_acc[keys, :] += dot32(p_list[now] if kept else p_ref[...], g_ref[queries, :])
        dk_acc[keys, :] += dot32(ds_ref[...], qx_ref[queries, :HD])
        dq_acc[:, queries] += dot32(kt_ref[:, keys], ds_ref[...])

    pipelined(plan_q, plan_k, count_ref, early, late, ((p0, ds0), (p1, ds1)), diagonals=not kept)


def prepare_kernel(bq, bk, plan_q, count_ref, log_ref, top_list, p_list, p_out, *totals):
    for total in totals:
        total[...] = jnp.zeros_like(total)

    @pl.loop(0, 2 * count_ref[1])
    def _(now):
        share = jnp.exp2(top_list[now] - log_ref[:, aligned(plan_q[now], bq)])
        for strip in range(0, bk, STRIP):
            part = slice(strip, strip + STRIP)
            p_out[now, part, :] = (p_list[now, part, :].astype(jnp.float32) * share).astype(jnp.bfloat16)


def finish_kernel(listed, rows, me_s, dq_ref, dk_ref, dv_ref, *results):
    scale = HD ** (-0.5)
    for d, result in zip(listed, results):
        own = aligned(me_s[0] ^ d, rows)
        result[:rows, :] = (scale * dq_ref[:, own]).astype(result.dtype).T
        result[rows:2 * rows, :] = (scale * dk_ref[own, :]).astype(result.dtype)
        result[2 * rows:, :] = dv_ref[own, :].astype(result.dtype)


def finish(me, listed, totals, rows):
    out_shape = [jax.ShapeDtypeStruct((3 * rows, HD), jnp.bfloat16)] * len(listed)
    results = pl.pallas_call(
        functools.partial(finish_kernel, listed, rows),
        in_specs=[SMEM_SPEC] + [VMEM_SPEC] * 3,
        out_specs=[VMEM_SPEC] * len(listed),
        out_shape=out_shape,
        compiler_params=params([*totals, *out_shape]),
    )(me, *totals)
    return dict(zip(listed, results))


def keeps_list(total, peers, heads):
    forward, backward = block_sizes(total)
    size = plan_size(total, *forward) * math.prod(forward) * 2
    return forward == backward and heads == peers and size <= LIST_BYTES


def attention_cost(total, products):
    return pl.CostEstimate(
        flops=products * total * total * HD // 2,
        bytes_accessed=16 * total * HD,
        transcendentals=total * total // 4,
    )


def attention_forward(me, blocks, rows, heads):
    peers = len(blocks)
    total = peers * rows
    (bq, bk), back = block_sizes(total)
    plan = [(plan_size(total, *back),)] * 2 + [(2,)]
    own_plan = [(plan_size(total, bq, bk),)] * 2 + [(2,)]
    vectors = [
        jax.ShapeDtypeStruct((total, HD), jnp.bfloat16),
        *[jax.ShapeDtypeStruct((total, 2 * HD), jnp.bfloat16)] * 2,
        jax.ShapeDtypeStruct((HD, total), jnp.bfloat16),
        jax.ShapeDtypeStruct((total, HD), jnp.float32),
        jax.ShapeDtypeStruct((1, total), jnp.float32),
    ]
    kept = keeps_list(total, peers, heads)
    if kept:
        vectors.append(jax.ShapeDtypeStruct((*own_plan[0], bk, bq), jnp.bfloat16))
        vectors.append(jax.ShapeDtypeStruct((*own_plan[0], 1, bq), jnp.float32))
    scratch = [
        pltpu.VMEM((HD + ONES_ROWS, total), jnp.bfloat16),
        pltpu.VMEM((HD, total), jnp.float32),
        pltpu.VMEM((1, total), jnp.float32),
        pltpu.VMEM((1, total), jnp.float32),
        *[pltpu.VMEM((bk, bq), jnp.float32), pltpu.VMEM((1, bq), jnp.float32)] * 2,
    ]
    return pl.pallas_call(
        functools.partial(forward_kernel, peers, heads, rows, bq, bk, kept),
        in_specs=[SMEM_SPEC] + [VMEM_SPEC] * peers,
        out_specs=[VMEM_SPEC] * len(vectors) + [SMEM_SPEC] * 3,
        out_shape=vectors + [jax.ShapeDtypeStruct(shape, jnp.int32) for shape in plan],
        scratch_shapes=[pltpu.SMEM(shape, jnp.int32) for shape in own_plan] + scratch,
        compiler_params=params([*blocks, *vectors], scratch),
        cost_estimate=attention_cost(total, 3),
    )(me, *blocks)


def total_shapes(total):
    shapes = [(HD, total), (total, HD), (total, HD)]
    return [jax.ShapeDtypeStruct(shape, jnp.float32) for shape in shapes]


def prepare(log_total, p_list, top_list, plan_q, count):
    bk, bq = p_list.shape[1:]
    out_shape = [jax.ShapeDtypeStruct(p_list.shape, p_list.dtype)] + total_shapes(log_total.shape[1])
    return pl.pallas_call(
        functools.partial(prepare_kernel, bq, bk),
        in_specs=[SMEM_SPEC] * 2 + [VMEM_SPEC] * 3,
        out_specs=[VMEM_SPEC] * len(out_shape),
        out_shape=out_shape,
        input_output_aliases={4: 0},
        compiler_params=params([log_total, top_list, *out_shape[1:]]),
    )(plan_q, count, log_total, top_list, p_list)


def attention_backward(me, heads, state, listed, blocks, ready=()):
    peers, rows = len(blocks), blocks[0].shape[0]
    total = peers * rows
    bq, bk = block_sizes(total)[1]
    kept = bool(ready)
    vectors, plan = [*state[:6], *ready], state[-3:]
    out_shape = total_shapes(total)
    scratch = [
        pltpu.VMEM((total, HD), jnp.bfloat16),
        pltpu.VMEM((1, total), jnp.float32),
        *[pltpu.VMEM((bk, bq), jnp.bfloat16)] * 4,
    ]
    return pl.pallas_call(
        functools.partial(backward_kernel, listed, heads, rows, bq, bk, kept),
        in_specs=[SMEM_SPEC] * 4 + [VMEM_SPEC] * (len(vectors) + peers),
        out_specs=[VMEM_SPEC] * 3,
        out_shape=out_shape,
        scratch_shapes=scratch,
        input_output_aliases={4 + 7 + i: i for i in range(3)} if kept else {},
        compiler_params=params([*vectors[:6], *blocks] if kept else [*vectors, *blocks, *out_shape], scratch),
        cost_estimate=attention_cost(total, 5),
    )(me, *plan, *vectors, *blocks)


def per_device(peers, groups, queries, keys_in, values, out_grad, out_weight, doc_ids):
    rows, width = queries.shape
    heads = width // HD
    me = lax.axis_index("seq")
    me_vector = me.reshape(1)

    def exchange(x, d):
        return x if d == 0 else lax.ppermute(x, "seq", [(i, i ^ d) for i in range(peers)])

    def pass_on(x):
        return lax.ppermute(x, "head", [(i, (i + 1) % groups) for i in range(groups)])

    order = [*range(2, peers, 2), *range(peers - 1, 0, -2)]

    far_first = sorted(range(peers), key=lambda d: (-bin(d >> 1).count("1"), d & 1, d))
    returning = [d for d in far_first if d < heads]

    def exchange_all(blocks, listed):
        return [exchange(blocks[d % heads], d) for d in listed]

    packed = list(pack_heads(me_vector, queries, keys_in, values, doc_ids))
    received = exchange_all(packed, range(peers))

    def share(step):
        return len(order) * step // (groups - 2)

    after = lax.optimization_barrier
    features, acc = out_grad, None
    weights = []
    for step in range(groups):
        block = lax.rem(lax.axis_index("head") + groups - step, groups)
        weights.append(lax.dynamic_slice_in_dim(out_weight, block * width, width, 1))
    for step in range(groups):
        last = step == groups - 1
        if not last:
            passed = pass_on(features)
        if step == groups - 2:
            received[0], features = after((received[0], features))
            state = list(attention_forward(me_vector, received, rows, heads))
            features, state[1] = after((features, state[1]))
        acc = project(me_vector, weights[step], features, acc, last)
        if not last:
            features = passed
            if step < groups - 2:
                batch = order[share(step):share(step + 1)]
                here = [received[d] for d in batch]
                features, acc, here, weights[2:] = after((features, acc, here, weights[2:]))
                for d, block in zip(batch, here):
                    received[d] = block
    grads = exchange_all(acc, far_first)

    ready = ()
    if len(state) > 9:
        p_list, grads[0] = after((state[6], grads[0]))
        ready = prepare(state[5], p_list, state[7], state[-3], state[-1])
    totals = attention_backward(me_vector, heads, state, far_first, grads, ready)

    far = [d for d in returning if bin(d >> 1).count("1") > 1]
    near = [d for d in returning if d not in far]
    results = {**(finish(me_vector, far, totals, rows) if far else {}), **finish(me_vector, near, totals, rows)}
    returned = {d: exchange(results[d], d) for d in returning}
    early, late = [*far, 0], [d for d in near if d > 0]
    partial = unpack_heads(me_vector, early, [returned[d] for d in early], rows, heads)
    return tuple(unpack_heads(me_vector, late, [returned[d] for d in late], rows, heads, partial))


def solution(mesh):
    in_specs = (
        P("seq", "head"),
        P("seq", "head"),
        P("seq", "head"),
        P("seq", "head"),
        P("head", None),
        P("seq"),
    )
    out_specs = (P("seq", "head"), P("seq", "head"), P("seq", "head"))
    return jax.shard_map(
        functools.partial(per_device, mesh.shape["seq"], mesh.shape["head"]),
        mesh=mesh, in_specs=in_specs, out_specs=out_specs, check_vma=False,
    )
```
